128 devices in a mesh: grp: 4 (over z_lo, core), blk: 32 (over y, x, z_hi).
Axes of the slice: x: 4, y: 4, z: 4 (z_hi: 2, z_lo: 2; z = z_hi * 2 + z_lo), core: 2. Of those that a mesh axis runs over, the one named last changes fastest.
Arguments:
- embeddings: float32 [4, 4, 32, 128, 768], P(None, 'grp', 'blk')
- cluster_ids: int32 [4, 16384], P('grp'), may hold values from 0 to 63, as said below
Outputs:
- best_match: float32 [4, 16384], P('grp', 'blk')
The draws below stay inside these ranges and needn't reach their ends.
Inputs may be any that keep to these rules, and one draw needn't show every extreme that they name: `cluster_ids`: along each group's row the ids never fall; group g holds clusters g * 16 to (g + 1) * 16 - 1, each with one point or more, and the largest of them has exactly 9216 points.
All inputs are finite; a program needn't handle non-finite values.
Results may differ from the reference program's by a relative error of at most 0.0003.
Values may be sent and summed in bfloat16 or wider, within the bound.
A program may use at most 128 MiB of HBM per device.

```python
import jax
import jax.numpy as jnp
from jax import lax

D = 768
ROWS_DEV = 512
CLUS_GRP = 16
SHARE = 128
GROUP_ROWS = 16384
BIG_CLUS = 9216
CLUSTERS = 64
N_GRP = 4


def cluster_layout(key):
    key = jax.random.fold_in(key, 11)
    keys = jax.random.split(key, N_GRP)
    rest = GROUP_ROWS - BIG_CLUS

    def one_group(group_key):
        key_cut, key_big = jax.random.split(group_key)
        order = jax.random.permutation(key_cut, rest - 1)
        cuts = jnp.sort(order[:CLUS_GRP - 2] + 1).astype(jnp.int32)
        bounds = jnp.concatenate([jnp.zeros((1,), jnp.int32), cuts, jnp.full((1,), rest, jnp.int32)])
        small_sizes = bounds[1:] - bounds[:-1]
        big_index = jax.random.randint(key_big, (), 0, CLUS_GRP).astype(jnp.int32)
        slots = jnp.arange(CLUS_GRP, dtype=jnp.int32)
        pick = jnp.clip(jnp.where(slots < big_index, slots, slots - 1), 0, CLUS_GRP - 2)
        sizes = jnp.where(slots == big_index, jnp.int32(BIG_CLUS), small_sizes[pick]).astype(jnp.int32)
        ends = jnp.cumsum(sizes).astype(jnp.int32)
        return (ends, (ends - sizes).astype(jnp.int32))
    ends, starts = jax.vmap(one_group)(keys)
    positions = jnp.arange(GROUP_ROWS, dtype=jnp.int32)
    local = jnp.sum((positions[None, :, None] >= ends[:, None, :]).astype(jnp.int32), axis=2)
    offsets = (jnp.arange(N_GRP, dtype=jnp.int32) * CLUS_GRP)[:, None]
    ids = offsets + local
    lower = jnp.take_along_axis(starts, local, axis=1)
    upper = jnp.take_along_axis(ends, local, axis=1)
    return (ids.astype(jnp.int32), lower.astype(jnp.int32), upper.astype(jnp.int32))


def draw_cluster_ids(key, part):
    ids, lower, upper = cluster_layout(key)
    return ids


def draw_embeddings(key, part):
    ids, lower, upper = cluster_layout(key)
    key = jax.random.fold_in(key, 5)
    key_cent, key_noise, key_pick, key_dup, key_small = jax.random.split(key, 5)
    centers = jax.random.normal(key_cent, (CLUSTERS, D), jnp.float32)
    noise = jax.random.normal(key_noise, (N_GRP, GROUP_ROWS, D), jnp.float32)
    base = 0.35 * centers[ids] + noise
    picks = jax.random.randint(key_pick, (N_GRP, GROUP_ROWS), 0, 1 << 20)
    partner = lower + picks % (upper - lower)
    copied = jnp.take_along_axis(base, partner[:, :, None], axis=1)
    small = jax.random.normal(key_small, (N_GRP, GROUP_ROWS, D), jnp.float32)
    is_dup = jax.random.randint(key_dup, (N_GRP, GROUP_ROWS, 1), 0, 3) == 0
    grouped = jnp.where(is_dup, copied + 0.25 * small, base)
    blocks = GROUP_ROWS // ROWS_DEV
    shaped = grouped.reshape(N_GRP, blocks, N_GRP, SHARE, D)
    return jnp.transpose(shaped, (0, 2, 1, 3, 4))


def setup_inputs(seed: int = 0) -> dict:
    key_list = jax.random.split(jax.random.key(seed), 3)
    return {
        "embeddings": draw_embeddings(jax.random.fold_in(key_list[2], 71), 0),
        "cluster_ids": draw_cluster_ids(jax.random.fold_in(key_list[2], 71), 0),
    }


def unit_vectors(vectors):
    total = lax.optimization_barrier(jnp.sum(vectors * vectors, axis=-1, keepdims=True))
    return (vectors / jnp.sqrt(total + 1e-06)).astype(jnp.bfloat16)

def group_best(grouped, group_ids):
    positions = jnp.arange(GROUP_ROWS, dtype=jnp.int32)

    def one_block(block_index):
        start = (block_index * ROWS_DEV).astype(jnp.int32)
        rows = lax.dynamic_slice_in_dim(grouped, start, ROWS_DEV, 0)
        row_ids = lax.dynamic_slice_in_dim(group_ids, start, ROWS_DEV, 0)
        row_pos = start + jnp.arange(ROWS_DEV, dtype=jnp.int32)
        similarity = jnp.dot(rows, grouped.T, preferred_element_type=jnp.float32)
        keep = (row_ids[:, None] == group_ids[None, :]) & (row_pos[:, None] != positions[None, :])
        return lax.optimization_barrier(jnp.max(jnp.where(keep, similarity, jnp.float32(-1.0)), axis=1))
    blocks = lax.map(one_block, jnp.arange(GROUP_ROWS // ROWS_DEV, dtype=jnp.int32))
    return blocks.reshape(GROUP_ROWS)

def reference(embeddings, cluster_ids):
    units = unit_vectors(embeddings)
    grouped = jnp.transpose(units, (0, 2, 1, 3, 4)).reshape(N_GRP, GROUP_ROWS, D)
    results = [group_best(grouped[g], cluster_ids[g]) for g in range(N_GRP)]
    return jnp.stack(results, axis=0)
```

```python
import functools

import jax
import jax.numpy as jnp
from jax import lax
from jax.experimental import pallas as pl
from jax.experimental.pallas import tpu as pltpu
from jax.sharding import PartitionSpec as P

MESH = pl.DeviceIdType.MESH
D = 768
SLOTS = 5
STEPS = 8

SRC = [[0, 3, 0, 0], [3, 0, 0, 0], [0, 0, 4, 0], [0, 0, 4, 0], [0, 4, 1, 0], [4, 0, 2, 0], [0, 3, 0, 0], [3, 0, 0, 0],
       [3, 0, 0, 3], [0, 3, 0, 3], [2, 4, 0, 0], [4, 1, 0, 0], [2, 0, 4, 0], [0, 1, 4, 0], [4, 0, 0, 3], [0, 4, 0, 3]]
DEP = [[1, 1, 1, 2], [1, 1, 1, 2], [1, 2, 1, 1], [2, 1, 1, 1], [1, 2, 2, 1], [2, 1, 2, 1], [1, 2, 1, 2], [2, 1, 1, 2],
       [2, 2, 1, 2], [2, 2, 1, 2], [2, 1, 2, 1], [1, 2, 2, 1], [2, 1, 1, 1], [1, 2, 1, 1], [2, 1, 1, 1], [1, 2, 1, 1]]
BLK = [[1, 3, 4, 8], [2, 0, 5, 9], [3, 5, 6, 14], [4, 2, 7, 15], [5, 11, 12, 0], [10, 4, 13, 1], [7, 1, 10, 14],
       [0, 6, 11, 15], [13, 7, 12, 5], [6, 12, 13, 4], [8, 9, 2, 6], [8, 9, 3, 7], [14, 15, 0, 8], [14, 15, 1, 9],
       [11, 13, 2, 10], [12, 10, 3, 11]]
IDX = [[1, 1, 1, 1], [1, 1, 1, 1], [2, 2, 1, 1], [2, 2, 1, 1], [3, 1, 1, 2], [1, 3, 1, 2], [2, 3, 2, 2], [3, 2, 2, 2],
       [2, 3, 2, 4], [3, 3, 3, 4], [2, 2, 3, 4], [3, 3, 3, 4], [3, 3, 4, 4], [4, 4, 4, 4], [3, 4, 4, 3], [4, 4, 4, 4]]
HOLD = [[0, 1, 4, 7, 12], [1, 0, 5, 6, 13], [2, 1, 3, 10, 14], [3, 0, 2, 11, 15], [4, 0, 3, 5, 9], [5, 1, 2, 4, 8],
        [6, 2, 7, 9, 10], [7, 3, 6, 8, 11], [8, 0, 10, 11, 12], [9, 1, 10, 11, 13], [10, 5, 6, 14, 15], [11, 4, 7, 14, 15],
        [12, 4, 8, 9, 15], [13, 5, 8, 9, 14], [14, 2, 6, 12, 13], [15, 3, 7, 12, 13]]
PAIRS = [[[(0, 2), (1, 2), (2, 4)], [(0, 3), (1, 4), (3, 4)]], [[(2, 0), (0, 1), (1, 4)], [(2, 1), (2, 4), (3, 4)]],
         [[(0, 3), (0, 2), (2, 3)], [(1, 3), (1, 2), (2, 4)]], [[(2, 0), (3, 4), (0, 1)], [(2, 3), (2, 1), (1, 3)]],
         [[(4, 1), (0, 2), (1, 2)], [(0, 1), (0, 3), (1, 3)]], [[(4, 2), (4, 1), (2, 3)], [(4, 0), (2, 1), (0, 1)]],
         [[(1, 3), (2, 1), (1, 4)], [(2, 0), (0, 4), (3, 4)]], [[(2, 0), (1, 2), (2, 4)], [(2, 3), (1, 0), (3, 4)]],
         [[(4, 2), (4, 1), (2, 3), (0, 1)], [(4, 0), (2, 0), (2, 1)]],
         [[(4, 1), (1, 0), (1, 3), (2, 3)], [(4, 0), (1, 2), (0, 2)]],
         [[(4, 0), (3, 1), (4, 1), (1, 0)], [(2, 0), (3, 0), (1, 2)]],
         [[(4, 0), (3, 4), (4, 2)], [(1, 0), (3, 2), (2, 0)]], [[(3, 4), (4, 2), (4, 1)], [(4, 0), (0, 2), (0, 1)]],
         [[(3, 4), (4, 1), (0, 2)], [(4, 0), (4, 2), (1, 2)]], [[(4, 2), (3, 1), (1, 2)], [(2, 0), (4, 1), (1, 0)]],
         [[(3, 4), (4, 1), (2, 1)], [(3, 1), (3, 2), (2, 0)]]]

REL = (0, 3, 1, 2)


def word(digits, base):
    total = 0
    for digit in reversed(digits):
        total = total * base + digit
    return total


def look_up(index, words):
    got = jnp.int32(words[0])
    for k in range(1, len(words)):
        got = jnp.where(index == k, jnp.int32(words[k]), got)
    return got


def digits_of(value, base, count):
    out = []
    for _ in range(count):
        out.append(value % base)
        value = value // base
    return out


def kernel(emb, ids_in, out, x, units, stage, ids_got, ids_rows, ids_cols, row_best, col_best, part, parts_got,
           load_sem, id_send, id_recv, z_send, z_recv, f_send, f_recv, c_send, c_recv, r_send, r_recv):
    grp, blk = lax.axis_index("grp"), lax.axis_index("blk")
    h, zl = grp % 2, grp // 2
    p, zh = blk // 2, blk % 2
    z = zh * 2 + zl
    px, py = p % 4, p // 4

    def device(z_of, core, chip):
        return ((z_of % 2) * 2 + core, chip * 2 + z_of // 2)

    def group_of(z_of):
        return (z_of % 2) * 2 + z_of // 2

    near = [py * 4 + (px + 1) % 4, py * 4 + (px + 3) % 4, ((py + 1) % 4) * 4 + px, ((py + 3) % 4) * 4 + px]
    first = look_up(p, [word(SRC[c], 8) + 4096 * word(DEP[c], 4) for c in range(16)])
    src = digits_of(first, 8, 4)
    dep = digits_of(first // 4096, 4, 4)
    held = [p] + digits_of(look_up(p, [word(BLK[c], 16) for c in range(16)]), 16, 4)
    third = look_up(p, [word(IDX[c], 8) + 4096 * word(HOLD[c][1:], 16) for c in range(16)])
    place = [jnp.int32(0)] + digits_of(third, 8, 4)
    holders = [p] + digits_of(third // 4096, 16, 4)
    lists = []
    for c in range(16):
        for core in range(2):
            flat = [slot for pair in PAIRS[c][core] for slot in pair]
            lists.append(len(PAIRS[c][core]) + 8 * word(flat + [0] * (8 - len(flat)), 8))
    todo = look_up(p * 2 + h, lists)
    pair_count = todo % 8
    todo = digits_of(todo // 8, 8, 8)

    sibling = device(z, 1 - h, p)
    owner_grp = zl * 2 + zh
    mine = h == zh

    loads = []
    for k, rel in enumerate((0, 1, 3, 2)):
        loads.append(pltpu.make_async_copy(emb.at[group_of((z + rel) % 4)], stage.at[k], load_sem.at[k]))
        loads[-1].start()

    barrier = pltpu.get_barrier_semaphore()
    for rel in (1, 3, 2):
        pl.semaphore_signal(barrier, inc=1, device_id=device((z + rel) % 4, h, p), device_id_type=MESH)
    for d in range(4):
        pl.semaphore_signal(barrier, inc=1, device_id=device(z, h, near[d]), device_id_type=MESH)
    pl.semaphore_signal(barrier, inc=1, device_id=sibling, device_id_type=MESH)
    from_z = 2 * h + zl
    for k in range(SLOTS):
        for core in range(2):
            def tell():
                pl.semaphore_signal(barrier, inc=1, device_id=device(from_z, core, holders[k]), device_id_type=MESH)
            if k == 0:
                pl.when(jnp.logical_not(jnp.logical_and(mine, h == core)))(tell)
            else:
                tell()

    def normalise(k):
        loads[k].wait()
        v = stage[k]
        total = jnp.sum(v * v, axis=-1, keepdims=True)
        return (v / jnp.sqrt(total + 1e-06)).astype(jnp.bfloat16)

    own_rows = pl.multiple_of(h * 128, 128)
    x[0, pl.ds(own_rows, 128), :] = normalise(0)
    for k in range(3):
        units[k] = normalise(k + 1)
    row_best[...] = jnp.full_like(row_best, -1.0)
    col_best[...] = jnp.full_like(col_best, -1.0)

    pl.semaphore_wait(barrier, jnp.where(mine, 17, 18))

    sends = []

    def remote(src_ref, dst_ref, send_sem, recv_sem, to):
        return pltpu.make_async_remote_copy(
            src_ref=src_ref, dst_ref=dst_ref, send_sem=send_sem, recv_sem=recv_sem, device_id=to, device_id_type=MESH)

    def part_rows(t):
        return pl.ds(pl.multiple_of((t // 2) * 256 + h * 128 + (t % 2) * 64, 64), 64)

    def forward(d, t):
        rows = part_rows(t)
        return remote(x.at[src[d], rows, :], x.at[1 + (d ^ 1), rows, :], f_send.at[d, t], f_recv.at[d ^ 1, t],
                      device(z, h, near[d]))

    def arrival(s, t):
        rows = part_rows(t)
        return remote(x.at[s, rows, :], x.at[s, rows, :], f_send.at[s - 1, t], f_recv.at[s - 1, t],
                      device(z, h, near[s - 1]))

    def swap(k):
        rows = pl.ds(pl.multiple_of(k * 256 + h * 128, 128), 128)
        return remote(units.at[k - 1], x.at[0, rows, :], z_send.at[k - 1], z_recv.at[k - 1],
                      device((z + (1, 3, 2)[k - 1]) % 4, h, p))

    def share(s, m):
        rows = pl.ds(pl.multiple_of(m * 256 + h * 128, 128), 128)
        return remote(x.at[s, rows, :], x.at[s, rows, :], c_send.at[s, m], c_recv.at[s, m], sibling)

    def shared(s, m):
        rows = pl.ds(pl.multiple_of(m * 256 + (1 - h) * 128, 128), 128)
        return remote(x.at[s, rows, :], x.at[s, rows, :], c_send.at[s, m], c_recv.at[s, m], sibling)

    def send_own(t):
        for d in range(4):
            @pl.when(src[d] == 0)
            def _():
                forward(d, t).start()

    def send_held(t):
        for d in range(4):
            @pl.when(src[d] != 0)
            def _():
                forward(d, t).start()

    send_own(0)
    swap(1).start()
    swap(2).start()
    send_own(1)
    swap(3).start()
    ids_copy = remote(ids_in, ids_got, id_send, id_recv, sibling)
    ids_copy.start()
    share(0, 0).start()

    ids_copy.wait_recv()
    ids_cols[...] = jnp.zeros_like(ids_cols)
    for s in range(SLOTS):
        for t in range(4):
            for core in range(2):
                unit = held[s] * 8 + 2 * ((z + REL[t]) % 4) + core
                got = jnp.where(mine, ids_in[pl.ds(unit, 1), :], ids_got[pl.ds(unit, 1), :])
                ids_cols[pl.ds(s * 8 + 2 * t + core, 1), :] = got.astype(jnp.float32)
    turned = ids_cols[...].T
    for j in range(SLOTS * 8):
        ids_rows[j] = jnp.broadcast_to(turned[:, j:j + 1], (128, 128))

    def tile(a, r, b, t, diagonal=False):
        lhs = x[a, 256 * r:256 * r + 256, :]
        rhs = x[b, 256 * t:256 * t + 256, :]
        sim = lax.dot_general(lhs, rhs, (((1,), (1,)), ((), ())), preferred_element_type=jnp.float32)
        row_ids = jnp.concatenate([ids_rows[a * 8 + 2 * r], ids_rows[a * 8 + 2 * r + 1]], axis=0)
        best = None
        for c in range(2):
            col_ids = ids_cols[pl.ds(b * 8 + 2 * t + c, 1), :]
            keep = row_ids == col_ids
            if diagonal:
                row = lax.broadcasted_iota(jnp.int32, (256, 128), 0)
                col = lax.broadcasted_iota(jnp.int32, (256, 128), 1) + 128 * c
                keep = jnp.logical_and(keep, row != col)
            kept = jnp.where(keep, sim[:, 128 * c:128 * c + 128], jnp.float32(-1.0))
            down = jnp.max(kept.reshape(32, 8, 128), axis=0)
            col_best[b * 8 + 2 * t + c] = jnp.maximum(col_best[b * 8 + 2 * t + c], down)
            best = kept if best is None else jnp.maximum(best, kept)
        for c in range(2):
            row_best[a * 8 + 2 * r + c] = jnp.maximum(row_best[a * 8 + 2 * r + c], best[128 * c:128 * c + 128])

    def compare(t):
        def one_pair(j, carry):
            a, b = todo[0], todo[1]
            for k in range(1, 4):
                a = jnp.where(j == k, todo[2 * k], a)
                b = jnp.where(j == k, todo[2 * k + 1], b)
            for r in range(t + 1):
                tile(a, r, b, t)
            for r in range(t):
                tile(b, r, a, t)
            return carry

        lax.fori_loop(0, pair_count, one_pair, 0)

        @pl.when(h == 1)
        def _():
            for r in range(t + 1):
                tile(0, r, 0, t, diagonal=r == t)

    def wait_shared(m):
        for s in range(SLOTS):
            shared(s, m).wait_recv()

    for step in range(STEPS + 2):
        for s in range(1, SLOTS):
            t = step - dep[s - 1]
            if 2 <= step <= STEPS:
                arrival(s, t).wait_recv()
            elif step == 1:
                pl.when(dep[s - 1] == 1)(lambda s=s: arrival(s, 0).wait_recv())
            elif step == STEPS + 1:
                pl.when(dep[s - 1] == 2)(lambda s=s: arrival(s, STEPS - 1).wait_recv())
        if 1 <= step <= STEPS:
            send_held(step - 1)
        for s in range(1, SLOTS):
            for links in (1, 2):
                t = step - links
                if t % 2 == 1 and 0 <= t < STEPS:
                    pl.when(dep[s - 1] == links)(lambda s=s, t=t: share(s, t // 2).start())
        if step in (4, 6, 8):
            wait_shared(step // 2 - 2)
            compare(step // 2 - 2)
        if step >= 1 and step + 1 < STEPS:
            if step % 2 == 1:
                swap((step + 1) // 2).wait_recv()
                share(0, (step + 1) // 2).start()
            send_own(step + 1)
    wait_shared(3)
    compare(3)

    for s in range(SLOTS):
        for t in range(4):
            z_of = (z + REL[t]) % 4
            for core in range(2):
                j = s * 8 + 2 * t + core
                both = jnp.maximum(jnp.max(row_best[j].T, axis=0, keepdims=True),
                                   jnp.max(col_best[j], axis=0, keepdims=True))
                part[s * 2 + z_of // 2, pl.ds(2 * (z_of % 2) + core, 1), :] = both
        for half in range(2):
            copy = remote(part.at[s * 2 + half], parts_got.at[place[s] * 2 + h], r_send.at[s * 2 + half],
                          r_recv.at[place[s] * 2 + h], (owner_grp, held[s] * 2 + half))
            if s == 0:
                keep_it = jnp.logical_and(mine, zh == half)
                pl.when(jnp.logical_not(keep_it))(copy.start)

                @pl.when(keep_it)
                def _():
                    parts_got[h] = part[half]
            else:
                copy.start()

    best = None
    for k in range(2 * SLOTS):
        got = remote(parts_got.at[k], parts_got.at[k], r_send.at[k], r_recv.at[k], sibling)
        if k < 2:
            pl.when(jnp.logical_not(jnp.logical_and(mine, h == k)))(got.wait_recv)
        else:
            got.wait_recv()
        best = parts_got[k] if best is None else jnp.maximum(best, parts_got[k])
    out[...] = best

    ids_copy.wait_send()
    for k in range(1, 4):
        swap(k).wait_send()
    for d in range(4):
        for t in range(STEPS):
            forward(d, t).wait_send()
    for s in range(SLOTS):
        for m in range(4):
            share(s, m).wait_send()
        for half in range(2):
            copy = remote(part.at[s * 2 + half], parts_got.at[place[s] * 2 + h], r_send.at[s * 2 + half],
                          r_recv.at[place[s] * 2 + h], (owner_grp, held[s] * 2 + half))
            if s == 0:
                pl.when(jnp.logical_not(jnp.logical_and(mine, zh == half)))(copy.wait_send)
            else:
                copy.wait_send()


def on_device(embeddings, cluster_ids):
    emb = embeddings.reshape(4, 128, D)
    ids = cluster_ids.reshape(128, 128)
    dma = pltpu.SemaphoreType.DMA
    best = pl.pallas_call(
        kernel,
        out_shape=jax.ShapeDtypeStruct((4, 128), jnp.float32),
        in_specs=[pl.BlockSpec(memory_space=pl.ANY), pl.BlockSpec(memory_space=pltpu.VMEM)],
        out_specs=pl.BlockSpec(memory_space=pltpu.VMEM),
        scratch_shapes=[
            pltpu.VMEM((SLOTS, 1024, D), jnp.bfloat16),
            pltpu.VMEM((3, 128, D), jnp.bfloat16),
            pltpu.VMEM((4, 128, D), jnp.float32),
            pltpu.VMEM((128, 128), jnp.int32),
            pltpu.VMEM((SLOTS * 8, 128, 128), jnp.float32),
            pltpu.VMEM((128, 128), jnp.float32),
            pltpu.VMEM((SLOTS * 8, 128, 128), jnp.float32),
            pltpu.VMEM((SLOTS * 8, 8, 128), jnp.float32),
            pltpu.VMEM((2 * SLOTS, 4, 128), jnp.float32),
            pltpu.VMEM((2 * SLOTS, 4, 128), jnp.float32),
            dma((4,)), dma, dma, dma((3,)), dma((3,)), dma((4, STEPS)), dma((4, STEPS)),
            dma((SLOTS, 4)), dma((SLOTS, 4)), dma((2 * SLOTS,)), dma((2 * SLOTS,)),
        ],
        compiler_params=pltpu.CompilerParams(
            collective_id=0, has_side_effects=True, vmem_limit_bytes=48 * 1024 * 1024),
        cost_estimate=pl.CostEstimate(flops=7 * 10**9, bytes_accessed=2 * 10**6, transcendentals=0),
        name="best_match",
    )(emb, ids)
    return best.reshape(1, 512)


def solution(mesh):
    placed = (P(None, "grp", "blk", None, None), P("grp", None))
    return jax.shard_map(
        on_device, mesh=mesh, in_specs=placed, out_specs=P("grp", "blk"), check_vma=False
    )
```

```python
import functools

import jax
import jax.numpy as jnp
from jax import lax
from jax.experimental import pallas as pl
from jax.experimental.pallas import tpu as pltpu
from jax.sharding import PartitionSpec as P

MESH = pl.DeviceIdType.MESH
D = 768
SLOTS = 5
STEPS = 8

SRC = [[0, 3, 0, 0], [3, 0, 0, 0], [0, 0, 4, 0], [0, 0, 4, 0], [0, 4, 1, 0], [4, 0, 2, 0], [0, 3, 0, 0], [3, 0, 0, 0],
       [3, 0, 0, 3], [0, 3, 0, 3], [2, 4, 0, 0], [4, 1, 0, 0], [2, 0, 4, 0], [0, 1, 4, 0], [4, 0, 0, 3], [0, 4, 0, 3]]
DEP = [[1, 1, 1, 2], [1, 1, 1, 2], [1, 2, 1, 1], [2, 1, 1, 1], [1, 2, 2, 1], [2, 1, 2, 1], [1, 2, 1, 2], [2, 1, 1, 2],
       [2, 2, 1, 2], [2, 2, 1, 2], [2, 1, 2, 1], [1, 2, 2, 1], [2, 1, 1, 1], [1, 2, 1, 1], [2, 1, 1, 1], [1, 2, 1, 1]]
BLK = [[1, 3, 4, 8], [2, 0, 5, 9], [3, 5, 6, 14], [4, 2, 7, 15], [5, 11, 12, 0], [10, 4, 13, 1], [7, 1, 10, 14],
       [0, 6, 11, 15], [13, 7, 12, 5], [6, 12, 13, 4], [8, 9, 2, 6], [8, 9, 3, 7], [14, 15, 0, 8], [14, 15, 1, 9],
       [11, 13, 2, 10], [12, 10, 3, 11]]
IDX = [[1, 1, 1, 1], [1, 1, 1, 1], [2, 2, 1, 1], [2, 2, 1, 1], [3, 1, 1, 2], [1, 3, 1, 2], [2, 3, 2, 2], [3, 2, 2, 2],
       [2, 3, 2, 4], [3, 3, 3, 4], [2, 2, 3, 4], [3, 3, 3, 4], [3, 3, 4, 4], [4, 4, 4, 4], [3, 4, 4, 3], [4, 4, 4, 4]]
HOLD = [[0, 1, 4, 7, 12], [1, 0, 5, 6, 13], [2, 1, 3, 10, 14], [3, 0, 2, 11, 15], [4, 0, 3, 5, 9], [5, 1, 2, 4, 8],
        [6, 2, 7, 9, 10], [7, 3, 6, 8, 11], [8, 0, 10, 11, 12], [9, 1, 10, 11, 13], [10, 5, 6, 14, 15], [11, 4, 7, 14, 15],
        [12, 4, 8, 9, 15], [13, 5, 8, 9, 14], [14, 2, 6, 12, 13], [15, 3, 7, 12, 13]]
PAIRS = [[[(0, 2), (1, 2), (2, 4)], [(0, 3), (1, 4), (3, 4)]], [[(2, 0), (0, 1), (1, 4)], [(2, 1), (2, 4), (3, 4)]],
         [[(0, 3), (0, 2), (2, 3)], [(1, 3), (1, 2), (2, 4)]], [[(2, 0), (3, 4), (0, 1)], [(2, 3), (2, 1), (1, 3)]],
         [[(4, 1), (0, 2), (1, 2)], [(0, 1), (0, 3), (1, 3)]], [[(4, 2), (4, 1), (2, 3)], [(4, 0), (2, 1), (0, 1)]],
         [[(1, 3), (2, 1), (1, 4)], [(2, 0), (0, 4), (3, 4)]], [[(2, 0), (1, 2), (2, 4)], [(2, 3), (1, 0), (3, 4)]],
         [[(4, 2), (4, 1), (2, 3), (0, 1)], [(4, 0), (2, 0), (2, 1)]],
         [[(4, 1), (1, 0), (1, 3), (2, 3)], [(4, 0), (1, 2), (0, 2)]],
         [[(4, 0), (3, 1), (4, 1), (1, 0)], [(2, 0), (3, 0), (1, 2)]],
         [[(4, 0), (3, 4), (4, 2)], [(1, 0), (3, 2), (2, 0)]], [[(3, 4), (4, 2), (4, 1)], [(4, 0), (0, 2), (0, 1)]],
         [[(3, 4), (4, 1), (0, 2)], [(4, 0), (4, 2), (1, 2)]], [[(4, 2), (3, 1), (1, 2)], [(2, 0), (4, 1), (1, 0)]],
         [[(3, 4), (4, 1), (2, 1)], [(3, 1), (3, 2), (2, 0)]]]

REL = (0, 3, 1, 2)


def word(digits, base):
    total = 0
    for digit in reversed(digits):
        total = total * base + digit
    return total


def look_up(index, words):
    got = jnp.int32(words[0])
    for k in range(1, len(words)):
        got = jnp.where(index == k, jnp.int32(words[k]), got)
    return got


def digits_of(value, base, count):
    out = []
    for _ in range(count):
        out.append(value % base)
        value = value // base
    return out


def kernel(emb, ids_in, out, x, units, stage, ids_got, ids_rows, ids_cols, row_best, col_best, part, parts_got,
           load_sem, id_send, id_recv, z_send, z_recv, f_send, f_recv, c_send, c_recv, r_send, r_recv):
    grp, blk = lax.axis_index("grp"), lax.axis_index("blk")
    h, zl = grp % 2, grp // 2
    p, zh = blk // 2, blk % 2
    z = zh * 2 + zl
    px, py = p % 4, p // 4

    def device(z_of, core, chip):
        return ((z_of % 2) * 2 + core, chip * 2 + z_of // 2)

    def group_of(z_of):
        return (z_of % 2) * 2 + z_of // 2

    near = [py * 4 + (px + 1) % 4, py * 4 + (px + 3) % 4, ((py + 1) % 4) * 4 + px, ((py + 3) % 4) * 4 + px]
    first = look_up(p, [word(SRC[c], 8) + 4096 * word(DEP[c], 4) for c in range(16)])
    src = digits_of(first, 8, 4)
    dep = digits_of(first // 4096, 4, 4)
    held = [p] + digits_of(look_up(p, [word(BLK[c], 16) for c in range(16)]), 16, 4)
    third = look_up(p, [word(IDX[c], 8) + 4096 * word(HOLD[c][1:], 16) for c in range(16)])
    place = [jnp.int32(0)] + digits_of(third, 8, 4)
    holders = [p] + digits_of(third // 4096, 16, 4)
    lists = []
    for c in range(16):
        for core in range(2):
            flat = [slot for pair in PAIRS[c][core] for slot in pair]
            lists.append(len(PAIRS[c][core]) + 8 * word(flat + [0] * (8 - len(flat)), 8))
    todo = look_up(p * 2 + h, lists)
    pair_count = todo % 8
    todo = digits_of(todo // 8, 8, 8)

    sibling = device(z, 1 - h, p)
    owner_grp = zl * 2 + zh
    mine = h == zh

    loads = []
    for k, rel in enumerate((0, 1, 3, 2)):
        loads.append(pltpu.make_async_copy(emb.at[group_of((z + rel) % 4)], stage.at[k], load_sem.at[k]))
        loads[-1].start()

    barrier = pltpu.get_barrier_semaphore()
    for rel in (1, 3, 2):
        pl.semaphore_signal(barrier, inc=1, device_id=device((z + rel) % 4, h, p), device_id_type=MESH)
    for d in range(4):
        pl.semaphore_signal(barrier, inc=1, device_id=device(z, h, near[d]), device_id_type=MESH)
    pl.semaphore_signal(barrier, inc=1, device_id=sibling, device_id_type=MESH)
    from_z = 2 * h + zl
    for k in range(SLOTS):
        for core in range(2):
            def tell():
                pl.semaphore_signal(barrier, inc=1, device_id=device(from_z, core, holders[k]), device_id_type=MESH)
            if k == 0:
                pl.when(jnp.logical_not(jnp.logical_and(mine, h == core)))(tell)
            else:
                tell()

    def normalise(k):
        loads[k].wait()
        v = stage[k]
        total = jnp.sum(v * v, axis=-1, keepdims=True)
        return (v / jnp.sqrt(total + 1e-06)).astype(jnp.bfloat16)

    own_rows = pl.multiple_of(h * 128, 128)
    x[0, pl.ds(own_rows, 128), :] = normalise(0)
    for k in range(3):
        units[k] = normalise(k + 1)
    row_best[...] = jnp.full_like(row_best, -1.0)
    col_best[...] = jnp.full_like(col_best, -1.0)

    pl.semaphore_wait(barrier, jnp.where(mine, 17, 18))

    sends = []

    def remote(src_ref, dst_ref, send_sem, recv_sem, to):
        return pltpu.make_async_remote_copy(
            src_ref=src_ref, dst_ref=dst_ref, send_sem=send_sem, recv_sem=recv_sem, device_id=to, device_id_type=MESH)

    def part_rows(t):
        return pl.ds(pl.multiple_of((t // 2) * 256 + h * 128 + (t % 2) * 64, 64), 64)

    def forward(d, t):
        rows = part_rows(t)
        return remote(x.at[src[d], rows, :], x.at[1 + (d ^ 1), rows, :], f_send.at[d, t], f_recv.at[d ^ 1, t],
                      device(z, h, near[d]))

    def arrival(s, t):
        rows = part_rows(t)
        return remote(x.at[s, rows, :], x.at[s, rows, :], f_send.at[s - 1, t], f_recv.at[s - 1, t],
                      device(z, h, near[s - 1]))

    def swap(k):
        rows = pl.ds(pl.multiple_of(k * 256 + h * 128, 128), 128)
        return remote(units.at[k - 1], x.at[0, rows, :], z_send.at[k - 1], z_recv.at[k - 1],
                      device((z + (1, 3, 2)[k - 1]) % 4, h, p))

    def share(s, m):
        rows = pl.ds(pl.multiple_of(m * 256 + h * 128, 128), 128)
        return remote(x.at[s, rows, :], x.at[s, rows, :], c_send.at[s, m], c_recv.at[s, m], sibling)

    def shared(s, m):
        rows = pl.ds(pl.multiple_of(m * 256 + (1 - h) * 128, 128), 128)
        return remote(x.at[s, rows, :], x.at[s, rows, :], c_send.at[s, m], c_recv.at[s, m], sibling)

    def send_own(t):
        for d in range(4):
            @pl.when(src[d] == 0)
            def _():
                forward(d, t).start()

    def send_held(t):
        for d in range(4):
            @pl.when(src[d] != 0)
            def _():
                forward(d, t).start()

    send_own(0)
    swap(1).start()
    swap(2).start()
    send_own(1)
    swap(3).start()
    ids_copy = remote(ids_in, ids_got, id_send, id_recv, sibling)
    ids_copy.start()
    share(0, 0).start()

    ids_copy.wait_recv()
    ids_cols[...] = jnp.zeros_like(ids_cols)
    for s in range(SLOTS):
        for t in range(4):
            for core in range(2):
                unit = held[s] * 8 + 2 * ((z + REL[t]) % 4) + core
                got = jnp.where(mine, ids_in[pl.ds(unit, 1), :], ids_got[pl.ds(unit, 1), :])
                ids_cols[pl.ds(s * 8 + 2 * t + core, 1), :] = got.astype(jnp.float32)
    turned = ids_cols[...].T
    for j in range(SLOTS * 8):
        ids_rows[j] = jnp.broadcast_to(turned[:, j:j + 1], (128, 128))

    def strip(a, t, b, count, diagonal=False):
        sim = lax.dot_general(x[a, 256 * t:256 * t + 256, :], x[b, 0:256 * count, :], (((1,), (1,)), ((), ())),
                              preferred_element_type=jnp.float32)
        for r in range(4):
            unit, first_row = a * 8 + 2 * t + r // 2, 64 * (r % 2)
            row_ids = ids_rows[unit, first_row:first_row + 64]
            best = row_best[unit, first_row:first_row + 64]
            for c in range(2 * count):
                keep = row_ids == ids_cols[pl.ds(b * 8 + c, 1), :]
                if diagonal and c // 2 == t:
                    row = lax.broadcasted_iota(jnp.int32, (64, 128), 0) + 64 * r
                    col = lax.broadcasted_iota(jnp.int32, (64, 128), 1) + 128 * (c % 2)
                    keep = jnp.logical_and(keep, row != col)
                kept = jnp.where(keep, sim[64 * r:64 * r + 64, 128 * c:128 * c + 128], jnp.float32(-1.0))
                down = jnp.max(kept.reshape(8, 8, 128), axis=0)
                col_best[b * 8 + c] = jnp.maximum(col_best[b * 8 + c], down)
                best = jnp.maximum(best, kept)
            row_best[unit, first_row:first_row + 64] = best

    def compare(t):
        def one_pair(j, carry):
            a, b = todo[0], todo[1]
            for k in range(1, 4):
                a = jnp.where(j == k, todo[2 * k], a)
                b = jnp.where(j == k, todo[2 * k + 1], b)
            strip(a, t, b, t + 1)
            if t:
                strip(b, t, a, t)
            return carry

        lax.fori_loop(0, pair_count, one_pair, 0)

        @pl.when(h == 1)
        def _():
            strip(0, t, 0, t + 1, diagonal=True)

    def wait_shared(m):
        for s in range(SLOTS):
            shared(s, m).wait_recv()

    for step in range(STEPS + 2):
        for s in range(1, SLOTS):
            t = step - dep[s - 1]
            if 2 <= step <= STEPS:
                arrival(s, t).wait_recv()
            elif step == 1:
                pl.when(dep[s - 1] == 1)(lambda s=s: arrival(s, 0).wait_recv())
            elif step == STEPS + 1:
                pl.when(dep[s - 1] == 2)(lambda s=s: arrival(s, STEPS - 1).wait_recv())
        if 1 <= step <= STEPS:
            send_held(step - 1)
        for s in range(1, SLOTS):
            for links in (1, 2):
                t = step - links
                if t % 2 == 1 and 0 <= t < STEPS:
                    pl.when(dep[s - 1] == links)(lambda s=s, t=t: share(s, t // 2).start())
        if step in (4, 6, 8):
            wait_shared(step // 2 - 2)
            compare(step // 2 - 2)
        if step >= 1 and step + 1 < STEPS:
            if step % 2 == 1:
                swap((step + 1) // 2).wait_recv()
                share(0, (step + 1) // 2).start()
            send_own(step + 1)
    wait_shared(3)
    compare(3)

    for s in range(SLOTS):
        for t in range(4):
            z_of = (z + REL[t]) % 4
            for core in range(2):
                j = s * 8 + 2 * t + core
                both = jnp.maximum(jnp.max(row_best[j].T, axis=0, keepdims=True),
                                   jnp.max(col_best[j], axis=0, keepdims=True))
                part[s * 2 + z_of // 2, pl.ds(2 * (z_of % 2) + core, 1), :] = both
        for half in range(2):
            copy = remote(part.at[s * 2 + half], parts_got.at[place[s] * 2 + h], r_send.at[s * 2 + half],
                          r_recv.at[place[s] * 2 + h], (owner_grp, held[s] * 2 + half))
            if s == 0:
                keep_it = jnp.logical_and(mine, zh == half)
                pl.when(jnp.logical_not(keep_it))(copy.start)

                @pl.when(keep_it)
                def _():
                    parts_got[h] = part[half]
            else:
                copy.start()

    best = None
    for k in range(2 * SLOTS):
        got = remote(parts_got.at[k], parts_got.at[k], r_send.at[k], r_recv.at[k], sibling)
        if k < 2:
            pl.when(jnp.logical_not(jnp.logical_and(mine, h == k)))(got.wait_recv)
        else:
            got.wait_recv()
        best = parts_got[k] if best is None else jnp.maximum(best, parts_got[k])
    out[...] = best

    ids_copy.wait_send()
    for k in range(1, 4):
        swap(k).wait_send()
    for d in range(4):
        for t in range(STEPS):
            forward(d, t).wait_send()
    for s in range(SLOTS):
        for m in range(4):
            share(s, m).wait_send()
        for half in range(2):
            copy = remote(part.at[s * 2 + half], parts_got.at[place[s] * 2 + h], r_send.at[s * 2 + half],
                          r_recv.at[place[s] * 2 + h], (owner_grp, held[s] * 2 + half))
            if s == 0:
                pl.when(jnp.logical_not(jnp.logical_and(mine, zh == half)))(copy.wait_send)
            else:
                copy.wait_send()


def on_device(embeddings, cluster_ids):
    emb = embeddings.reshape(4, 128, D)
    ids = cluster_ids.reshape(128, 128)
    dma = pltpu.SemaphoreType.DMA
    best = pl.pallas_call(
        kernel,
        out_shape=jax.ShapeDtypeStruct((4, 128), jnp.float32),
        in_specs=[pl.BlockSpec(memory_space=pl.ANY), pl.BlockSpec(memory_space=pltpu.VMEM)],
        out_specs=pl.BlockSpec(memory_space=pltpu.VMEM),
        scratch_shapes=[
            pltpu.VMEM((SLOTS, 1024, D), jnp.bfloat16),
            pltpu.VMEM((3, 128, D), jnp.bfloat16),
            pltpu.VMEM((4, 128, D), jnp.float32),
            pltpu.VMEM((128, 128), jnp.int32),
            pltpu.VMEM((SLOTS * 8, 128, 128), jnp.float32),
            pltpu.VMEM((128, 128), jnp.float32),
            pltpu.VMEM((SLOTS * 8, 128, 128), jnp.float32),
            pltpu.VMEM((SLOTS * 8, 8, 128), jnp.float32),
            pltpu.VMEM((2 * SLOTS, 4, 128), jnp.float32),
            pltpu.VMEM((2 * SLOTS, 4, 128), jnp.float32),
            dma((4,)), dma, dma, dma((3,)), dma((3,)), dma((4, STEPS)), dma((4, STEPS)),
            dma((SLOTS, 4)), dma((SLOTS, 4)), dma((2 * SLOTS,)), dma((2 * SLOTS,)),
        ],
        compiler_params=pltpu.CompilerParams(
            collective_id=0, has_side_effects=True, vmem_limit_bytes=60 * 1024 * 1024),
        cost_estimate=pl.CostEstimate(flops=7 * 10**9, bytes_accessed=2 * 10**6, transcendentals=0),
        name="best_match",
    )(emb, ids)
    return best.reshape(1, 512)


def solution(mesh):
    placed = (P(None, "grp", "blk", None, None), P("grp", None))
    return jax.shard_map(
        on_device, mesh=mesh, in_specs=placed, out_specs=P("grp", "blk"), check_vma=False
    )
```

```python
import functools

import jax
import jax.numpy as jnp
from jax import lax
from jax.experimental import pallas as pl
from jax.experimental.pallas import tpu as pltpu
from jax.sharding import PartitionSpec as P

MESH = pl.DeviceIdType.MESH
D = 768
SLOTS = 5
STEPS = 8

SRC = [[0, 3, 0, 0], [3, 0, 0, 0], [0, 0, 4, 0], [0, 0, 4, 0], [0, 4, 1, 0], [4, 0, 2, 0], [0, 3, 0, 0], [3, 0, 0, 0],
       [3, 0, 0, 3], [0, 3, 0, 3], [2, 4, 0, 0], [4, 1, 0, 0], [2, 0, 4, 0], [0, 1, 4, 0], [4, 0, 0, 3], [0, 4, 0, 3]]
DEP = [[1, 1, 1, 2], [1, 1, 1, 2], [1, 2, 1, 1], [2, 1, 1, 1], [1, 2, 2, 1], [2, 1, 2, 1], [1, 2, 1, 2], [2, 1, 1, 2],
       [2, 2, 1, 2], [2, 2, 1, 2], [2, 1, 2, 1], [1, 2, 2, 1], [2, 1, 1, 1], [1, 2, 1, 1], [2, 1, 1, 1], [1, 2, 1, 1]]
BLK = [[1, 3, 4, 8], [2, 0, 5, 9], [3, 5, 6, 14], [4, 2, 7, 15], [5, 11, 12, 0], [10, 4, 13, 1], [7, 1, 10, 14],
       [0, 6, 11, 15], [13, 7, 12, 5], [6, 12, 13, 4], [8, 9, 2, 6], [8, 9, 3, 7], [14, 15, 0, 8], [14, 15, 1, 9],
       [11, 13, 2, 10], [12, 10, 3, 11]]
IDX = [[1, 1, 1, 1], [1, 1, 1, 1], [2, 2, 1, 1], [2, 2, 1, 1], [3, 1, 1, 2], [1, 3, 1, 2], [2, 3, 2, 2], [3, 2, 2, 2],
       [2, 3, 2, 4], [3, 3, 3, 4], [2, 2, 3, 4], [3, 3, 3, 4], [3, 3, 4, 4], [4, 4, 4, 4], [3, 4, 4, 3], [4, 4, 4, 4]]
HOLD = [[0, 1, 4, 7, 12], [1, 0, 5, 6, 13], [2, 1, 3, 10, 14], [3, 0, 2, 11, 15], [4, 0, 3, 5, 9], [5, 1, 2, 4, 8],
        [6, 2, 7, 9, 10], [7, 3, 6, 8, 11], [8, 0, 10, 11, 12], [9, 1, 10, 11, 13], [10, 5, 6, 14, 15], [11, 4, 7, 14, 15],
        [12, 4, 8, 9, 15], [13, 5, 8, 9, 14], [14, 2, 6, 12, 13], [15, 3, 7, 12, 13]]
PAIRS = [[[(0, 2), (1, 2), (2, 4)], [(0, 3), (1, 4), (3, 4)]], [[(2, 0), (0, 1), (1, 4)], [(2, 1), (2, 4), (3, 4)]],
         [[(0, 3), (0, 2), (2, 3)], [(1, 3), (1, 2), (2, 4)]], [[(2, 0), (3, 4), (0, 1)], [(2, 3), (2, 1), (1, 3)]],
         [[(4, 1), (0, 2), (1, 2)], [(0, 1), (0, 3), (1, 3)]], [[(4, 2), (4, 1), (2, 3)], [(4, 0), (2, 1), (0, 1)]],
         [[(1, 3), (2, 1), (1, 4)], [(2, 0), (0, 4), (3, 4)]], [[(2, 0), (1, 2), (2, 4)], [(2, 3), (1, 0), (3, 4)]],
         [[(4, 2), (4, 1), (2, 3), (0, 1)], [(4, 0), (2, 0), (2, 1)]],
         [[(4, 1), (1, 0), (1, 3), (2, 3)], [(4, 0), (1, 2), (0, 2)]],
         [[(4, 0), (3, 1), (4, 1), (1, 0)], [(2, 0), (3, 0), (1, 2)]],
         [[(4, 0), (3, 4), (4, 2)], [(1, 0), (3, 2), (2, 0)]], [[(3, 4), (4, 2), (4, 1)], [(4, 0), (0, 2), (0, 1)]],
         [[(3, 4), (4, 1), (0, 2)], [(4, 0), (4, 2), (1, 2)]], [[(4, 2), (3, 1), (1, 2)], [(2, 0), (4, 1), (1, 0)]],
         [[(3, 4), (4, 1), (2, 1)], [(3, 1), (3, 2), (2, 0)]]]

REL = (0, 3, 1, 2)


def word(digits, base):
    total = 0
    for digit in reversed(digits):
        total = total * base + digit
    return total


def look_up(index, words):
    got = jnp.int32(words[0])
    for k in range(1, len(words)):
        got = jnp.where(index == k, jnp.int32(words[k]), got)
    return got


def digits_of(value, base, count):
    out = []
    for _ in range(count):
        out.append(value % base)
        value = value // base
    return out


def position():
    grp, blk = lax.axis_index("grp"), lax.axis_index("blk")
    h, zl = grp % 2, grp // 2
    p, zh = blk // 2, blk % 2
    return h, zl, zh, zh * 2 + zl, p


def device(z_of, core, chip):
    return ((z_of % 2) * 2 + core, chip * 2 + z_of // 2)


def blocks_of(p):
    return [p] + digits_of(look_up(p, [word(BLK[c], 16) for c in range(16)]), 16, 4)


def remote(src_ref, dst_ref, send_sem, recv_sem, to):
    return pltpu.make_async_remote_copy(
        src_ref=src_ref, dst_ref=dst_ref, send_sem=send_sem, recv_sem=recv_sem, device_id=to, device_id_type=MESH)


def exchange(emb, ids_in, x, ids_out, units, stage, load_sem, id_send, id_recv, z_send, z_recv, f_send, f_recv,
             c_send, c_recv):
    h, zl, zh, z, p = position()
    px, py = p % 4, p // 4
    near = [py * 4 + (px + 1) % 4, py * 4 + (px + 3) % 4, ((py + 1) % 4) * 4 + px, ((py + 3) % 4) * 4 + px]
    first = look_up(p, [word(SRC[c], 8) + 4096 * word(DEP[c], 4) for c in range(16)])
    src = digits_of(first, 8, 4)
    dep = digits_of(first // 4096, 4, 4)
    sibling = device(z, 1 - h, p)

    def group_of(z_of):
        return (z_of % 2) * 2 + z_of // 2

    loads = []
    for k, rel in enumerate((0, 1, 3, 2)):
        loads.append(pltpu.make_async_copy(emb.at[group_of((z + rel) % 4)], stage.at[k], load_sem.at[k]))
        loads[-1].start()

    barrier = pltpu.get_barrier_semaphore()
    for rel in (1, 3, 2):
        pl.semaphore_signal(barrier, inc=1, device_id=device((z + rel) % 4, h, p), device_id_type=MESH)
    for d in range(4):
        pl.semaphore_signal(barrier, inc=1, device_id=device(z, h, near[d]), device_id_type=MESH)
    pl.semaphore_signal(barrier, inc=1, device_id=sibling, device_id_type=MESH)

    def normalise(k):
        loads[k].wait()
        v = stage[k]
        total = jnp.sum(v * v, axis=-1, keepdims=True)
        return (v / jnp.sqrt(total + 1e-06)).astype(jnp.bfloat16)

    own_rows = pl.multiple_of(h * 128, 128)
    x[0, pl.ds(own_rows, 128), :] = normalise(0)
    for k in range(3):
        units[k] = normalise(k + 1)

    pl.semaphore_wait(barrier, 8)

    def part_rows(t):
        return pl.ds(pl.multiple_of((t // 2) * 256 + h * 128 + (t % 2) * 64, 64), 64)

    def forward(d, t):
        rows = part_rows(t)
        return remote(x.at[src[d], rows, :], x.at[1 + (d ^ 1), rows, :], f_send.at[d, t], f_recv.at[d ^ 1, t],
                      device(z, h, near[d]))

    def arrival(s, t):
        rows = part_rows(t)
        return remote(x.at[s, rows, :], x.at[s, rows, :], f_send.at[s - 1, t], f_recv.at[s - 1, t],
                      device(z, h, near[s - 1]))

    def swap(k):
        rows = pl.ds(pl.multiple_of(k * 256 + h * 128, 128), 128)
        return remote(units.at[k - 1], x.at[0, rows, :], z_send.at[k - 1], z_recv.at[k - 1],
                      device((z + (1, 3, 2)[k - 1]) % 4, h, p))

    def share(s, m):
        rows = pl.ds(pl.multiple_of(m * 256 + h * 128, 128), 128)
        return remote(x.at[s, rows, :], x.at[s, rows, :], c_send.at[s, m], c_recv.at[s, m], sibling)

    def shared(s, m):
        rows = pl.ds(pl.multiple_of(m * 256 + (1 - h) * 128, 128), 128)
        return remote(x.at[s, rows, :], x.at[s, rows, :], c_send.at[s, m], c_recv.at[s, m], sibling)

    def send_own(t):
        for d in range(4):
            @pl.when(src[d] == 0)
            def _():
                forward(d, t).start()

    def send_held(t):
        for d in range(4):
            @pl.when(src[d] != 0)
            def _():
                forward(d, t).start()

    send_own(0)
    swap(1).start()
    swap(2).start()
    send_own(1)
    swap(3).start()
    ids_copy = remote(ids_in, ids_out, id_send, id_recv, sibling)
    ids_copy.start()
    share(0, 0).start()

    for step in range(STEPS + 2):
        for s in range(1, SLOTS):
            t = step - dep[s - 1]
            if 2 <= step <= STEPS:
                arrival(s, t).wait_recv()
            elif step == 1:
                pl.when(dep[s - 1] == 1)(lambda s=s: arrival(s, 0).wait_recv())
            elif step == STEPS + 1:
                pl.when(dep[s - 1] == 2)(lambda s=s: arrival(s, STEPS - 1).wait_recv())
        if 1 <= step <= STEPS:
            send_held(step - 1)
        for s in range(1, SLOTS):
            for links in (1, 2):
                t = step - links
                if t % 2 == 1 and 0 <= t < STEPS:
                    pl.when(dep[s - 1] == links)(lambda s=s, t=t: share(s, t // 2).start())
        if step >= 1 and step + 1 < STEPS:
            if step % 2 == 1:
                swap((step + 1) // 2).wait_recv()
                share(0, (step + 1) // 2).start()
            send_own(step + 1)

    ids_copy.wait()
    for s in range(SLOTS):
        for m in range(4):
            shared(s, m).wait_recv()
            share(s, m).wait_send()
    for k in range(1, 4):
        swap(k).wait_send()
    for d in range(4):
        for t in range(STEPS):
            forward(d, t).wait_send()

    @pl.when(h == zh)
    def _():
        ids_out[...] = ids_in[...]


def compare(x, ids, ends, part, ids_rows, ids_cols, row_best, col_best):
    h, zl, zh, z, p = position()
    held = blocks_of(p)
    lists = []
    for c in range(16):
        for core in range(2):
            flat = [slot for pair in PAIRS[c][core] for slot in pair]
            lists.append(len(PAIRS[c][core]) + 8 * word(flat + [0] * (8 - len(flat)), 8))
    todo = look_up(p * 2 + h, lists)
    pair_count = todo % 8
    todo = digits_of(todo // 8, 8, 8)

    row_best[...] = jnp.full_like(row_best, -1.0)
    col_best[...] = jnp.full_like(col_best, -1.0)

    ids_cols[...] = jnp.zeros_like(ids_cols)
    for s in range(SLOTS):
        for t in range(4):
            for core in range(2):
                unit = held[s] * 8 + 2 * ((z + REL[t]) % 4) + core
                ids_cols[pl.ds(s * 8 + 2 * t + core, 1), :] = ids[pl.ds(unit, 1), :].astype(jnp.float32)
    turned = ids_cols[...].T
    for j in range(SLOTS * 8):
        ids_rows[j] = jnp.broadcast_to(turned[:, j:j + 1], (128, 128))

    def span(slot, t):
        block = held[0]
        for s in range(1, SLOTS):
            block = jnp.where(slot == s, held[s], block)
        unit = block * 8 + 2 * ((z + jnp.where(t == 1, 3, jnp.where(t == 2, 1, jnp.where(t == 3, 2, 0)))) % 4)
        return ends[unit, 0], ends[unit + 1, 127]

    def tile(a, t, b, u, diagonal=False):
        sim = lax.dot_general(x[a, pl.ds(pl.multiple_of(256 * t, 256), 256), :],
                              x[b, pl.ds(pl.multiple_of(256 * u, 256), 256), :],
                              (((1,), (1,)), ((), ())), preferred_element_type=jnp.float32)
        for r in range(4):
            unit, first_row = a * 8 + 2 * t + r // 2, 64 * (r % 2)
            row_ids = ids_rows[unit, first_row:first_row + 64]
            best = row_best[unit, first_row:first_row + 64]
            for c in range(2):
                keep = row_ids == ids_cols[pl.ds(b * 8 + 2 * u + c, 1), :]
                if diagonal:
                    row = lax.broadcasted_iota(jnp.int32, (64, 128), 0) + 64 * r
                    col = lax.broadcasted_iota(jnp.int32, (64, 128), 1) + 128 * c
                    keep = jnp.logical_and(keep, row != col)
                kept = jnp.where(keep, sim[64 * r:64 * r + 64, 128 * c:128 * c + 128], jnp.float32(-1.0))
                down = jnp.max(kept.reshape(8, 8, 128), axis=0)
                col_best[b * 8 + 2 * u + c] = jnp.maximum(col_best[b * 8 + 2 * u + c], down)
                best = jnp.maximum(best, kept)
            row_best[unit, first_row:first_row + 64] = best

    def one_tile(k, carry):
        j, t, u = k // 16, (k // 4) % 4, k % 4
        a, b = todo[0], todo[1]
        for i in range(1, 4):
            a = jnp.where(j == i, todo[2 * i], a)
            b = jnp.where(j == i, todo[2 * i + 1], b)
        a_first, a_last = span(a, t)
        b_first, b_last = span(b, u)

        @pl.when(jnp.logical_and(a_last >= b_first, b_last >= a_first))
        def _():
            tile(a, t, b, u)
        return carry

    lax.fori_loop(0, pair_count * 16, one_tile, 0)

    @pl.when(h == 1)
    def _():
        def own_tile(k, carry):
            t, u = k // 4, k % 4
            a_first, a_last = span(0, t)
            b_first, b_last = span(0, u)

            @pl.when(jnp.logical_and(t < u, jnp.logical_and(a_last >= b_first, b_last >= a_first)))
            def _():
                tile(0, t, 0, u)

            @pl.when(t == u)
            def _():
                tile(0, t, 0, u, diagonal=True)
            return carry

        lax.fori_loop(0, 16, own_tile, 0)

    for s in range(SLOTS):
        for t in range(4):
            z_of = (z + REL[t]) % 4
            for core in range(2):
                j = s * 8 + 2 * t + core
                both = jnp.maximum(jnp.max(row_best[j].T, axis=0, keepdims=True),
                                   jnp.max(col_best[j], axis=0, keepdims=True))
                part[s * 2 + z_of // 2, pl.ds(2 * (z_of % 2) + core, 1), :] = both


def combine(part, out, parts_got, r_send, r_recv):
    h, zl, zh, z, p = position()
    held = blocks_of(p)
    third = look_up(p, [word(IDX[c], 8) + 4096 * word(HOLD[c][1:], 16) for c in range(16)])
    place = [jnp.int32(0)] + digits_of(third, 8, 4)
    holders = [p] + digits_of(third // 4096, 16, 4)
    sibling = device(z, 1 - h, p)
    owner_grp = zl * 2 + zh
    mine = h == zh

    barrier = pltpu.get_barrier_semaphore()
    for k in range(SLOTS):
        for core in range(2):
            def tell():
                pl.semaphore_signal(barrier, inc=1, device_id=device(2 * h + zl, core, holders[k]), device_id_type=MESH)
            if k == 0:
                pl.when(jnp.logical_not(jnp.logical_and(mine, h == core)))(tell)
            else:
                tell()
    pl.semaphore_wait(barrier, jnp.where(mine, 9, 10))

    def deliver(s, half):
        return remote(part.at[s * 2 + half], parts_got.at[place[s] * 2 + h], r_send.at[s * 2 + half],
                      r_recv.at[place[s] * 2 + h], (owner_grp, held[s] * 2 + half))

    for s in range(SLOTS):
        for half in range(2):
            if s == 0:
                keep_it = jnp.logical_and(mine, zh == half)
                pl.when(jnp.logical_not(keep_it))(deliver(s, half).start)

                @pl.when(keep_it)
                def _():
                    parts_got[h] = part[half]
            else:
                deliver(s, half).start()

    best = None
    for k in range(2 * SLOTS):
        got = remote(parts_got.at[k], parts_got.at[k], r_send.at[k], r_recv.at[k], sibling)
        if k < 2:
            pl.when(jnp.logical_not(jnp.logical_and(mine, h == k)))(got.wait_recv)
        else:
            got.wait_recv()
        best = parts_got[k] if best is None else jnp.maximum(best, parts_got[k])
    out[...] = best
    for s in range(SLOTS):
        for half in range(2):
            if s == 0:
                pl.when(jnp.logical_not(jnp.logical_and(mine, zh == half)))(deliver(s, half).wait_send)
            else:
                deliver(s, half).wait_send()


def on_device(embeddings, cluster_ids):
    emb = embeddings.reshape(4, 128, D)
    ids = cluster_ids.reshape(128, 128)
    dma = pltpu.SemaphoreType.DMA
    vmem = pl.BlockSpec(memory_space=pltpu.VMEM)
    x, ids = pl.pallas_call(
        exchange,
        out_shape=(jax.ShapeDtypeStruct((SLOTS, 1024, D), jnp.bfloat16), jax.ShapeDtypeStruct((128, 128), jnp.int32)),
        in_specs=[pl.BlockSpec(memory_space=pl.ANY), vmem],
        out_specs=[vmem, vmem],
        scratch_shapes=[
            pltpu.VMEM((3, 128, D), jnp.bfloat16),
            pltpu.VMEM((4, 128, D), jnp.float32),
            dma((4,)), dma, dma, dma((3,)), dma((3,)), dma((4, STEPS)), dma((4, STEPS)),
            dma((SLOTS, 4)), dma((SLOTS, 4)),
        ],
        compiler_params=pltpu.CompilerParams(
            collective_id=0, has_side_effects=True, vmem_limit_bytes=48 * 1024 * 1024),
        name="exchange",
    )(emb, ids)
    part = pl.pallas_call(
        compare,
        out_shape=jax.ShapeDtypeStruct((2 * SLOTS, 4, 128), jnp.float32),
        in_specs=[vmem, vmem, pl.BlockSpec(memory_space=pltpu.SMEM)],
        out_specs=vmem,
        scratch_shapes=[
            pltpu.VMEM((SLOTS * 8, 128, 128), jnp.float32),
            pltpu.VMEM((128, 128), jnp.float32),
            pltpu.VMEM((SLOTS * 8, 128, 128), jnp.float32),
            pltpu.VMEM((SLOTS * 8, 8, 128), jnp.float32),
        ],
        compiler_params=pltpu.CompilerParams(vmem_limit_bytes=48 * 1024 * 1024),
        name="compare",
    )(x, ids, ids)
    best = pl.pallas_call(
        combine,
        out_shape=jax.ShapeDtypeStruct((4, 128), jnp.float32),
        in_specs=[vmem],
        out_specs=vmem,
        scratch_shapes=[pltpu.VMEM((2 * SLOTS, 4, 128), jnp.float32), dma((2 * SLOTS,)), dma((2 * SLOTS,))],
        compiler_params=pltpu.CompilerParams(collective_id=1, has_side_effects=True),
        name="combine",
    )(part)
    return best.reshape(1, 512)


def solution(mesh):
    placed = (P(None, "grp", "blk", None, None), P("grp", None))
    return jax.shard_map(
        on_device, mesh=mesh, in_specs=placed, out_specs=P("grp", "blk"), check_vma=False
    )
```

```python
import functools

import jax
import jax.numpy as jnp
from jax import lax
from jax.experimental import pallas as pl
from jax.experimental.pallas import tpu as pltpu
from jax.sharding import PartitionSpec as P

MESH = pl.DeviceIdType.MESH
D = 768
SLOTS = 5
STEPS = 8

SRC = [[0, 3, 0, 0], [3, 0, 0, 0], [0, 0, 4, 0], [0, 0, 4, 0], [0, 4, 1, 0], [4, 0, 2, 0], [0, 3, 0, 0], [3, 0, 0, 0],
       [3, 0, 0, 3], [0, 3, 0, 3], [2, 4, 0, 0], [4, 1, 0, 0], [2, 0, 4, 0], [0, 1, 4, 0], [4, 0, 0, 3], [0, 4, 0, 3]]
DEP = [[1, 1, 1, 2], [1, 1, 1, 2], [1, 2, 1, 1], [2, 1, 1, 1], [1, 2, 2, 1], [2, 1, 2, 1], [1, 2, 1, 2], [2, 1, 1, 2],
       [2, 2, 1, 2], [2, 2, 1, 2], [2, 1, 2, 1], [1, 2, 2, 1], [2, 1, 1, 1], [1, 2, 1, 1], [2, 1, 1, 1], [1, 2, 1, 1]]
BLK = [[1, 3, 4, 8], [2, 0, 5, 9], [3, 5, 6, 14], [4, 2, 7, 15], [5, 11, 12, 0], [10, 4, 13, 1], [7, 1, 10, 14],
       [0, 6, 11, 15], [13, 7, 12, 5], [6, 12, 13, 4], [8, 9, 2, 6], [8, 9, 3, 7], [14, 15, 0, 8], [14, 15, 1, 9],
       [11, 13, 2, 10], [12, 10, 3, 11]]
IDX = [[1, 1, 1, 1], [1, 1, 1, 1], [2, 2, 1, 1], [2, 2, 1, 1], [3, 1, 1, 2], [1, 3, 1, 2], [2, 3, 2, 2], [3, 2, 2, 2],
       [2, 3, 2, 4], [3, 3, 3, 4], [2, 2, 3, 4], [3, 3, 3, 4], [3, 3, 4, 4], [4, 4, 4, 4], [3, 4, 4, 3], [4, 4, 4, 4]]
HOLD = [[0, 1, 4, 7, 12], [1, 0, 5, 6, 13], [2, 1, 3, 10, 14], [3, 0, 2, 11, 15], [4, 0, 3, 5, 9], [5, 1, 2, 4, 8],
        [6, 2, 7, 9, 10], [7, 3, 6, 8, 11], [8, 0, 10, 11, 12], [9, 1, 10, 11, 13], [10, 5, 6, 14, 15], [11, 4, 7, 14, 15],
        [12, 4, 8, 9, 15], [13, 5, 8, 9, 14], [14, 2, 6, 12, 13], [15, 3, 7, 12, 13]]
PAIRS = [[[(1, 3), (1, 4), (3, 4)], [(0, 1), (0, 2), (1, 2)]], [[(2, 1), (2, 4), (1, 4)], [(0, 1), (0, 3), (3, 4)]],
         [[(1, 3), (3, 4), (2, 3), (2, 4)], [(0, 1), (0, 2), (1, 2)]],
         [[(2, 3), (2, 1), (1, 3)], [(0, 3), (3, 4), (0, 1)]], [[(4, 0), (4, 1), (0, 2), (1, 2)], [(0, 3), (1, 3)]],
         [[(2, 0), (4, 1), (2, 1)], [(0, 1), (0, 3), (1, 3)]], [[(1, 3), (1, 4), (3, 4)], [(0, 3), (2, 0), (2, 1)]],
         [[(2, 3), (2, 4), (3, 4)], [(2, 0), (1, 2), (1, 0)]],
         [[(2, 3), (2, 1), (0, 1), (3, 1)], [(4, 2), (4, 0), (2, 0)]],
         [[(4, 1), (4, 0), (4, 3), (1, 3)], [(1, 0), (1, 2), (0, 2)]],
         [[(3, 4), (3, 1), (4, 1)], [(2, 0), (1, 2), (1, 0)]], [[(1, 0), (3, 1), (3, 2)], [(4, 0), (4, 2), (2, 0)]],
         [[(3, 4), (4, 1), (0, 1)], [(4, 0), (4, 2), (0, 2)]], [[(3, 4), (4, 1), (1, 2)], [(4, 0), (4, 2), (0, 2)]],
         [[(3, 4), (3, 1), (4, 1)], [(2, 0), (1, 2), (1, 0)]], [[(3, 4), (3, 1), (4, 1)], [(3, 2), (2, 1), (2, 0)]]]
NEED = [[[1, 3, 4], [0, 1, 2]], [[1, 2, 4], [0, 1, 3, 4]], [[1, 2, 3, 4], [0, 1, 2]], [[1, 2, 3], [0, 1, 3, 4]],
        [[0, 1, 2, 4], [0, 1, 3]], [[0, 1, 2, 4], [0, 1, 3]], [[1, 3, 4], [0, 1, 2, 3]], [[2, 3, 4], [0, 1, 2]],
        [[0, 1, 2, 3], [0, 2, 4]], [[0, 1, 3, 4], [0, 1, 2]], [[1, 3, 4], [0, 1, 2]], [[0, 1, 2, 3], [0, 2, 4]],
        [[0, 1, 3, 4], [0, 2, 4]], [[1, 2, 3, 4], [0, 2, 4]], [[1, 3, 4], [0, 1, 2]], [[1, 3, 4], [0, 1, 2, 3]]]

REL = (0, 3, 1, 2)


def word(digits, base):
    total = 0
    for digit in reversed(digits):
        total = total * base + digit
    return total


def look_up(index, words):
    got = jnp.int32(words[0])
    for k in range(1, len(words)):
        got = jnp.where(index == k, jnp.int32(words[k]), got)
    return got


def digits_of(value, base, count):
    out = []
    for _ in range(count):
        out.append(value % base)
        value = value // base
    return out


def kernel(emb, ids_in, out, x, units, stage, ids_got, ids_rows, ids_cols, row_best, col_best, part, parts_got, relay,
           load_sem, id_send, id_recv, z_send, z_recv, relay_send, relay_recv, f_send, f_recv, c_send, c_recv, r_send, r_recv):
    grp, blk = lax.axis_index("grp"), lax.axis_index("blk")
    h, zl = grp % 2, grp // 2
    p, zh = blk // 2, blk % 2
    z = zh * 2 + zl
    px, py = p % 4, p // 4

    def device(z_of, core, chip):
        return ((z_of % 2) * 2 + core, chip * 2 + z_of // 2)

    def group_of(z_of):
        return (z_of % 2) * 2 + z_of // 2

    near = [py * 4 + (px + 1) % 4, py * 4 + (px + 3) % 4, ((py + 1) % 4) * 4 + px, ((py + 3) % 4) * 4 + px]
    first = look_up(p, [word(SRC[c], 8) + 4096 * word(DEP[c], 4) for c in range(16)])
    src = digits_of(first, 8, 4)
    dep = digits_of(first // 4096, 4, 4)
    held = [p] + digits_of(look_up(p, [word(BLK[c], 16) for c in range(16)]), 16, 4)
    third = look_up(p, [word(IDX[c], 8) + 4096 * word(HOLD[c][1:], 16) for c in range(16)])
    place = [jnp.int32(0)] + digits_of(third, 8, 4)
    holders = [p] + digits_of(third // 4096, 16, 4)
    lists = []
    for c in range(16):
        for core in range(2):
            flat = [slot for pair in PAIRS[c][core] for slot in pair]
            lists.append(len(PAIRS[c][core]) + 8 * word(flat + [0] * (8 - len(flat)), 8))
    todo = look_up(p * 2 + h, lists)
    pair_count = todo % 8
    todo = digits_of(todo // 8, 8, 8)

    needs = [[sum(1 << slot for slot in NEED[c][core]) for core in range(2)] for c in range(16)]
    need = digits_of(look_up(p * 2 + h, [needs[c][core] for c in range(16) for core in range(2)]), 2, SLOTS)
    sibling_need = digits_of(look_up(p * 2 + h, [needs[c][1 - core] for c in range(16) for core in range(2)]), 2, SLOTS)

    sibling = device(z, 1 - h, p)
    owner_grp = zl * 2 + zh
    mine = h == zh

    loads = []
    for k, rel in enumerate((0, 1, 3, 2)):
        loads.append(pltpu.make_async_copy(emb.at[group_of((z + rel) % 4)], stage.at[k], load_sem.at[k]))
        loads[-1].start()

    barrier = pltpu.get_barrier_semaphore()
    for rel in (1, 3):
        pl.semaphore_signal(barrier, inc=1, device_id=device((z + rel) % 4, h, p), device_id_type=MESH)
    for d in range(4):
        pl.semaphore_signal(barrier, inc=1, device_id=device(z, h, near[d]), device_id_type=MESH)
    pl.semaphore_signal(barrier, inc=1, device_id=sibling, device_id_type=MESH)
    from_z = 2 * h + zl
    for k in range(SLOTS):
        for core in range(2):
            def tell():
                pl.semaphore_signal(barrier, inc=1, device_id=device(from_z, core, holders[k]), device_id_type=MESH)
            if k == 0:
                pl.when(jnp.logical_not(jnp.logical_and(mine, h == core)))(tell)
            else:
                tell()

    def normalise(k):
        loads[k].wait()
        v = stage[k]
        total = jnp.sum(v * v, axis=-1, keepdims=True)
        return (v / jnp.sqrt(total + 1e-06)).astype(jnp.bfloat16)

    own_rows = pl.multiple_of(h * 128, 128)
    x[0, pl.ds(own_rows, 128), :] = normalise(0)
    for k in range(3):
        units[k] = normalise(k + 1)
    row_best[...] = jnp.full_like(row_best, -1.0)
    col_best[...] = jnp.full_like(col_best, -1.0)

    pl.semaphore_wait(barrier, jnp.where(mine, 16, 17))

    sends = []

    def remote(src_ref, dst_ref, send_sem, recv_sem, to):
        return pltpu.make_async_remote_copy(
            src_ref=src_ref, dst_ref=dst_ref, send_sem=send_sem, recv_sem=recv_sem, device_id=to, device_id_type=MESH)

    def part_rows(t):
        return pl.ds(pl.multiple_of((t // 2) * 256 + h * 128 + (t % 2) * 64, 64), 64)

    def forward(d, t):
        rows = part_rows(t)
        return remote(x.at[src[d], rows, :], x.at[1 + (d ^ 1), rows, :], f_send.at[d, t], f_recv.at[d ^ 1, t],
                      device(z, h, near[d]))

    def arrival(s, t):
        rows = part_rows(t)
        return remote(x.at[s, rows, :], x.at[s, rows, :], f_send.at[s - 1, t], f_recv.at[s - 1, t],
                      device(z, h, near[s - 1]))

    def swap(k):
        rows = pl.ds(pl.multiple_of(k * 256 + h * 128, 128), 128)
        return remote(units.at[k - 1], x.at[0, rows, :], z_send.at[k - 1], z_recv.at[k - 1],
                      device((z + (1, 3, 2)[k - 1]) % 4, h, p))

    between = device((z + jnp.where(h == 0, 1, 3)) % 4, h, p)
    third_rows = pl.ds(pl.multiple_of(3 * 256 + h * 128, 128), 128)
    relay_in = remote(units.at[2], relay, relay_send.at[0], relay_recv, between)
    relay_out = remote(relay, x.at[0, third_rows, :], relay_send.at[1], z_recv.at[2], between)

    def share(s, m):
        rows = pl.ds(pl.multiple_of(m * 256 + h * 128, 128), 128)
        return remote(x.at[s, rows, :], x.at[s, rows, :], c_send.at[s, m], c_recv.at[s, m], sibling)

    def shared(s, m):
        rows = pl.ds(pl.multiple_of(m * 256 + (1 - h) * 128, 128), 128)
        return remote(x.at[s, rows, :], x.at[s, rows, :], c_send.at[s, m], c_recv.at[s, m], sibling)

    def give(s, m):
        pl.when(sibling_need[s] == 1)(lambda: share(s, m).start())

    def send_own(t):
        for d in range(4):
            @pl.when(src[d] == 0)
            def _():
                forward(d, t).start()

    def send_held(t):
        for d in range(4):
            @pl.when(src[d] != 0)
            def _():
                forward(d, t).start()

    send_own(0)
    swap(1).start()
    swap(2).start()
    send_own(1)
    relay_in.start()
    ids_copy = remote(ids_in, ids_got, id_send, id_recv, sibling)
    ids_copy.start()
    give(0, 0)

    ids_copy.wait_recv()
    ids_cols[...] = jnp.zeros_like(ids_cols)
    for s in range(SLOTS):
        for t in range(4):
            for core in range(2):
                unit = held[s] * 8 + 2 * ((z + REL[t]) % 4) + core
                got = jnp.where(mine, ids_in[pl.ds(unit, 1), :], ids_got[pl.ds(unit, 1), :])
                ids_cols[pl.ds(s * 8 + 2 * t + core, 1), :] = got.astype(jnp.float32)
    turned = ids_cols[...].T
    for j in range(SLOTS * 8):
        ids_rows[j] = jnp.broadcast_to(turned[:, j:j + 1], (128, 128))

    def strip(a, t, b, count, diagonal=False):
        sim = lax.dot_general(x[a, 256 * t:256 * t + 256, :], x[b, 0:256 * count, :], (((1,), (1,)), ((), ())),
                              preferred_element_type=jnp.float32)
        for r in range(4):
            unit, first_row = a * 8 + 2 * t + r // 2, 64 * (r % 2)
            row_ids = ids_rows[unit, first_row:first_row + 64]
            best = row_best[unit, first_row:first_row + 64]
            for c in range(2 * count):
                keep = row_ids == ids_cols[pl.ds(b * 8 + c, 1), :]
                if diagonal and c // 2 == t:
                    row = lax.broadcasted_iota(jnp.int32, (64, 128), 0) + 64 * r
                    col = lax.broadcasted_iota(jnp.int32, (64, 128), 1) + 128 * (c % 2)
                    keep = jnp.logical_and(keep, row != col)
                kept = jnp.where(keep, sim[64 * r:64 * r + 64, 128 * c:128 * c + 128], jnp.float32(-1.0))
                down = jnp.max(kept.reshape(8, 8, 128), axis=0)
                col_best[b * 8 + c] = jnp.maximum(col_best[b * 8 + c], down)
                best = jnp.maximum(best, kept)
            row_best[unit, first_row:first_row + 64] = best

    def compare(t):
        def one_pair(j, carry):
            a, b = todo[0], todo[1]
            for k in range(1, 4):
                a = jnp.where(j == k, todo[2 * k], a)
                b = jnp.where(j == k, todo[2 * k + 1], b)
            strip(a, t, b, t + 1)
            if t:
                strip(b, t, a, t)
            return carry

        lax.fori_loop(0, pair_count, one_pair, 0)

        @pl.when(h == 1)
        def _():
            strip(0, t, 0, t + 1, diagonal=True)

    def wait_shared(m):
        for s in range(SLOTS):
            pl.when(need[s] == 1)(lambda s=s: shared(s, m).wait_recv())

    for step in range(STEPS + 2):
        for s in range(1, SLOTS):
            t = step - dep[s - 1]
            if 2 <= step <= STEPS:
                arrival(s, t).wait_recv()
            elif step == 1:
                pl.when(dep[s - 1] == 1)(lambda s=s: arrival(s, 0).wait_recv())
            elif step == STEPS + 1:
                pl.when(dep[s - 1] == 2)(lambda s=s: arrival(s, STEPS - 1).wait_recv())
        if 1 <= step <= STEPS:
            send_held(step - 1)
        for s in range(1, SLOTS):
            for links in (1, 2):
                t = step - links
                if t % 2 == 1 and 0 <= t < STEPS:
                    pl.when(dep[s - 1] == links)(lambda s=s, t=t: give(s, t // 2))
        if step in (4, 6, 8):
            wait_shared(step // 2 - 2)
            compare(step // 2 - 2)
        if step in (1, 3, 5):
            m = (step + 1) // 2
            if m == 3:
                relay_out.wait_recv()
            else:
                swap(m).wait_recv()
            send_own(2 * m)
            send_own(2 * m + 1)
            give(0, m)
        if step == 2:
            relay_in.wait_recv()
            relay_out.start()
    wait_shared(3)
    compare(3)

    for s in range(SLOTS):
        for t in range(4):
            z_of = (z + REL[t]) % 4
            for core in range(2):
                j = s * 8 + 2 * t + core
                both = jnp.maximum(jnp.max(row_best[j].T, axis=0, keepdims=True),
                                   jnp.max(col_best[j], axis=0, keepdims=True))
                part[s * 2 + z_of // 2, pl.ds(2 * (z_of % 2) + core, 1), :] = both
        for half in range(2):
            copy = remote(part.at[s * 2 + half], parts_got.at[place[s] * 2 + h], r_send.at[s * 2 + half],
                          r_recv.at[place[s] * 2 + h], (owner_grp, held[s] * 2 + half))
            if s == 0:
                keep_it = jnp.logical_and(mine, zh == half)
                pl.when(jnp.logical_not(keep_it))(copy.start)

                @pl.when(keep_it)
                def _():
                    parts_got[h] = part[half]
            else:
                copy.start()

    best = None
    for k in range(2 * SLOTS):
        got = remote(parts_got.at[k], parts_got.at[k], r_send.at[k], r_recv.at[k], sibling)
        if k < 2:
            pl.when(jnp.logical_not(jnp.logical_and(mine, h == k)))(got.wait_recv)
        else:
            got.wait_recv()
        best = parts_got[k] if best is None else jnp.maximum(best, parts_got[k])
    out[...] = best

    ids_copy.wait_send()
    for copy in (swap(1), swap(2), relay_in, relay_out):
        copy.wait_send()
    for d in range(4):
        for t in range(STEPS):
            forward(d, t).wait_send()
    for s in range(SLOTS):
        for m in range(4):
            pl.when(sibling_need[s] == 1)(lambda s=s, m=m: share(s, m).wait_send())
        for half in range(2):
            copy = remote(part.at[s * 2 + half], parts_got.at[place[s] * 2 + h], r_send.at[s * 2 + half],
                          r_recv.at[place[s] * 2 + h], (owner_grp, held[s] * 2 + half))
            if s == 0:
                pl.when(jnp.logical_not(jnp.logical_and(mine, zh == half)))(copy.wait_send)
            else:
                copy.wait_send()


def on_device(embeddings, cluster_ids):
    emb = embeddings.reshape(4, 128, D)
    ids = cluster_ids.reshape(128, 128)
    dma = pltpu.SemaphoreType.DMA
    best = pl.pallas_call(
        kernel,
        out_shape=jax.ShapeDtypeStruct((4, 128), jnp.float32),
        in_specs=[pl.BlockSpec(memory_space=pl.ANY), pl.BlockSpec(memory_space=pltpu.VMEM)],
        out_specs=pl.BlockSpec(memory_space=pltpu.VMEM),
        scratch_shapes=[
            pltpu.VMEM((SLOTS, 1024, D), jnp.bfloat16),
            pltpu.VMEM((3, 128, D), jnp.bfloat16),
            pltpu.VMEM((4, 128, D), jnp.float32),
            pltpu.VMEM((128, 128), jnp.int32),
            pltpu.VMEM((SLOTS * 8, 128, 128), jnp.float32),
            pltpu.VMEM((128, 128), jnp.float32),
            pltpu.VMEM((SLOTS * 8, 128, 128), jnp.float32),
            pltpu.VMEM((SLOTS * 8, 8, 128), jnp.float32),
            pltpu.VMEM((2 * SLOTS, 4, 128), jnp.float32),
            pltpu.VMEM((2 * SLOTS, 4, 128), jnp.float32),
            pltpu.VMEM((128, D), jnp.bfloat16),
            dma((4,)), dma, dma, dma((3,)), dma((3,)), dma((2,)), dma, dma((4, STEPS)), dma((4, STEPS)),
            dma((SLOTS, 4)), dma((SLOTS, 4)), dma((2 * SLOTS,)), dma((2 * SLOTS,)),
        ],
        compiler_params=pltpu.CompilerParams(
            collective_id=0, has_side_effects=True, vmem_limit_bytes=60 * 1024 * 1024),
        cost_estimate=pl.CostEstimate(flops=7 * 10**9, bytes_accessed=2 * 10**6, transcendentals=0),
        name="best_match",
    )(emb, ids)
    return best.reshape(1, 512)


def solution(mesh):
    placed = (P(None, "grp", "blk", None, None), P("grp", None))
    return jax.shard_map(
        on_device, mesh=mesh, in_specs=placed, out_specs=P("grp", "blk"), check_vma=False
    )
```

```python
import functools

import jax
import jax.numpy as jnp
from jax import lax
from jax.experimental import pallas as pl
from jax.experimental.pallas import tpu as pltpu
from jax.sharding import PartitionSpec as P

MESH = pl.DeviceIdType.MESH
D = 768
SLOTS = 5
STEPS = 8

SRC = [[0, 3, 0, 0], [3, 0, 0, 0], [0, 0, 4, 0], [0, 0, 4, 0], [0, 4, 1, 0], [4, 0, 2, 0], [0, 3, 0, 0], [3, 0, 0, 0],
       [3, 0, 0, 3], [0, 3, 0, 3], [2, 4, 0, 0], [4, 1, 0, 0], [2, 0, 4, 0], [0, 1, 4, 0], [4, 0, 0, 3], [0, 4, 0, 3]]
DEP = [[1, 1, 1, 2], [1, 1, 1, 2], [1, 2, 1, 1], [2, 1, 1, 1], [1, 2, 2, 1], [2, 1, 2, 1], [1, 2, 1, 2], [2, 1, 1, 2],
       [2, 2, 1, 2], [2, 2, 1, 2], [2, 1, 2, 1], [1, 2, 2, 1], [2, 1, 1, 1], [1, 2, 1, 1], [2, 1, 1, 1], [1, 2, 1, 1]]
BLK = [[1, 3, 4, 8], [2, 0, 5, 9], [3, 5, 6, 14], [4, 2, 7, 15], [5, 11, 12, 0], [10, 4, 13, 1], [7, 1, 10, 14],
       [0, 6, 11, 15], [13, 7, 12, 5], [6, 12, 13, 4], [8, 9, 2, 6], [8, 9, 3, 7], [14, 15, 0, 8], [14, 15, 1, 9],
       [11, 13, 2, 10], [12, 10, 3, 11]]
IDX = [[1, 1, 1, 1], [1, 1, 1, 1], [2, 2, 1, 1], [2, 2, 1, 1], [3, 1, 1, 2], [1, 3, 1, 2], [2, 3, 2, 2], [3, 2, 2, 2],
       [2, 3, 2, 4], [3, 3, 3, 4], [2, 2, 3, 4], [3, 3, 3, 4], [3, 3, 4, 4], [4, 4, 4, 4], [3, 4, 4, 3], [4, 4, 4, 4]]
HOLD = [[0, 1, 4, 7, 12], [1, 0, 5, 6, 13], [2, 1, 3, 10, 14], [3, 0, 2, 11, 15], [4, 0, 3, 5, 9], [5, 1, 2, 4, 8],
        [6, 2, 7, 9, 10], [7, 3, 6, 8, 11], [8, 0, 10, 11, 12], [9, 1, 10, 11, 13], [10, 5, 6, 14, 15], [11, 4, 7, 14, 15],
        [12, 4, 8, 9, 15], [13, 5, 8, 9, 14], [14, 2, 6, 12, 13], [15, 3, 7, 12, 13]]
PAIRS = [[[(1, 3), (1, 4), (3, 4)], [(0, 1), (0, 2), (1, 2)]], [[(2, 1), (2, 4), (1, 4)], [(0, 1), (0, 3), (3, 4)]],
         [[(1, 3), (3, 4), (2, 3), (2, 4)], [(0, 1), (0, 2), (1, 2)]],
         [[(2, 3), (2, 1), (1, 3)], [(0, 3), (3, 4), (0, 1)]], [[(4, 0), (4, 1), (0, 2), (1, 2)], [(0, 3), (1, 3)]],
         [[(2, 0), (4, 1), (2, 1)], [(0, 1), (0, 3), (1, 3)]], [[(1, 3), (1, 4), (3, 4)], [(0, 3), (2, 0), (2, 1)]],
         [[(2, 3), (2, 4), (3, 4)], [(2, 0), (1, 2), (1, 0)]],
         [[(2, 3), (2, 1), (0, 1), (3, 1)], [(4, 2), (4, 0), (2, 0)]],
         [[(4, 1), (4, 0), (4, 3), (1, 3)], [(1, 0), (1, 2), (0, 2)]],
         [[(3, 4), (3, 1), (4, 1)], [(2, 0), (1, 2), (1, 0)]], [[(1, 0), (3, 1), (3, 2)], [(4, 0), (4, 2), (2, 0)]],
         [[(3, 4), (4, 1), (0, 1)], [(4, 0), (4, 2), (0, 2)]], [[(3, 4), (4, 1), (1, 2)], [(4, 0), (4, 2), (0, 2)]],
         [[(3, 4), (3, 1), (4, 1)], [(2, 0), (1, 2), (1, 0)]], [[(3, 4), (3, 1), (4, 1)], [(3, 2), (2, 1), (2, 0)]]]
NEED = [[[1, 3, 4], [0, 1, 2]], [[1, 2, 4], [0, 1, 3, 4]], [[1, 2, 3, 4], [0, 1, 2]], [[1, 2, 3], [0, 1, 3, 4]],
        [[0, 1, 2, 4], [0, 1, 3]], [[0, 1, 2, 4], [0, 1, 3]], [[1, 3, 4], [0, 1, 2, 3]], [[2, 3, 4], [0, 1, 2]],
        [[0, 1, 2, 3], [0, 2, 4]], [[0, 1, 3, 4], [0, 1, 2]], [[1, 3, 4], [0, 1, 2]], [[0, 1, 2, 3], [0, 2, 4]],
        [[0, 1, 3, 4], [0, 2, 4]], [[1, 2, 3, 4], [0, 2, 4]], [[1, 3, 4], [0, 1, 2]], [[1, 3, 4], [0, 1, 2, 3]]]

REL = (0, 3, 1, 2)


def word(digits, base):
    total = 0
    for digit in reversed(digits):
        total = total * base + digit
    return total


def look_up(index, words):
    got = jnp.int32(words[0])
    for k in range(1, len(words)):
        got = jnp.where(index == k, jnp.int32(words[k]), got)
    return got


def digits_of(value, base, count):
    out = []
    for _ in range(count):
        out.append(value % base)
        value = value // base
    return out


def kernel(emb, ids_in, out, x, units, stage, ids_got, ids_rows, ids_cols, row_best, col_best, part, parts_got, relay,
           load_sem, id_send, id_recv, z_send, z_recv, relay_send, relay_recv, f_send, f_recv, c_send, c_recv, r_send, r_recv):
    grp, blk = lax.axis_index("grp"), lax.axis_index("blk")
    h, zl = grp % 2, grp // 2
    p, zh = blk // 2, blk % 2
    z = zh * 2 + zl
    px, py = p % 4, p // 4

    def device(z_of, core, chip):
        return ((z_of % 2) * 2 + core, chip * 2 + z_of // 2)

    def group_of(z_of):
        return (z_of % 2) * 2 + z_of // 2

    near = [py * 4 + (px + 1) % 4, py * 4 + (px + 3) % 4, ((py + 1) % 4) * 4 + px, ((py + 3) % 4) * 4 + px]
    first = look_up(p, [word(SRC[c], 8) + 4096 * word(DEP[c], 4) for c in range(16)])
    src = digits_of(first, 8, 4)
    dep = digits_of(first // 4096, 4, 4)
    held = [p] + digits_of(look_up(p, [word(BLK[c], 16) for c in range(16)]), 16, 4)
    third = look_up(p, [word(IDX[c], 8) + 4096 * word(HOLD[c][1:], 16) for c in range(16)])
    place = [jnp.int32(0)] + digits_of(third, 8, 4)
    holders = [p] + digits_of(third // 4096, 16, 4)
    lists = []
    for c in range(16):
        for core in range(2):
            flat = [slot for pair in PAIRS[c][core] for slot in pair]
            lists.append(len(PAIRS[c][core]) + 8 * word(flat + [0] * (8 - len(flat)), 8))
    todo = look_up(p * 2 + h, lists)
    pair_count = todo % 8
    todo = digits_of(todo // 8, 8, 8)

    needs = [[sum(1 << slot for slot in NEED[c][core]) for core in range(2)] for c in range(16)]
    need = digits_of(look_up(p * 2 + h, [needs[c][core] for c in range(16) for core in range(2)]), 2, SLOTS)
    sibling_need = digits_of(look_up(p * 2 + h, [needs[c][1 - core] for c in range(16) for core in range(2)]), 2, SLOTS)

    sibling = device(z, 1 - h, p)
    owner_grp = zl * 2 + zh
    mine = h == zh

    loads = []
    for k, rel in enumerate((0, 1, 3, 2)):
        loads.append(pltpu.make_async_copy(emb.at[group_of((z + rel) % 4)], stage.at[k], load_sem.at[k]))
        loads[-1].start()

    barrier = pltpu.get_barrier_semaphore()
    for rel in (1, 3):
        pl.semaphore_signal(barrier, inc=1, device_id=device((z + rel) % 4, h, p), device_id_type=MESH)
    for d in range(4):
        pl.semaphore_signal(barrier, inc=1, device_id=device(z, h, near[d]), device_id_type=MESH)
    pl.semaphore_signal(barrier, inc=1, device_id=sibling, device_id_type=MESH)
    from_z = 2 * h + zl
    for k in range(SLOTS):
        for core in range(2):
            def tell():
                pl.semaphore_signal(barrier, inc=1, device_id=device(from_z, core, holders[k]), device_id_type=MESH)
            if k == 0:
                pl.when(jnp.logical_not(jnp.logical_and(mine, h == core)))(tell)
            else:
                tell()

    def normalise(k):
        loads[k].wait()
        v = stage[k]
        total = jnp.sum(v * v, axis=-1, keepdims=True)
        return (v / jnp.sqrt(total + 1e-06)).astype(jnp.bfloat16)

    own_rows = pl.multiple_of(h * 128, 128)
    x[0, pl.ds(own_rows, 128), :] = normalise(0)
    for k in range(3):
        units[k] = normalise(k + 1)
    row_best[...] = jnp.full_like(row_best, -1.0)
    col_best[...] = jnp.full_like(col_best, -1.0)

    pl.semaphore_wait(barrier, jnp.where(mine, 16, 17))

    sends = []

    def remote(src_ref, dst_ref, send_sem, recv_sem, to):
        return pltpu.make_async_remote_copy(
            src_ref=src_ref, dst_ref=dst_ref, send_sem=send_sem, recv_sem=recv_sem, device_id=to, device_id_type=MESH)

    def part_rows(t):
        return pl.ds(pl.multiple_of((t // 2) * 256 + h * 128 + (t % 2) * 64, 64), 64)

    def forward(d, t):
        rows = part_rows(t)
        return remote(x.at[src[d], rows, :], x.at[1 + (d ^ 1), rows, :], f_send.at[d, t], f_recv.at[d ^ 1, t],
                      device(z, h, near[d]))

    def arrival(s, t):
        rows = part_rows(t)
        return remote(x.at[s, rows, :], x.at[s, rows, :], f_send.at[s - 1, t], f_recv.at[s - 1, t],
                      device(z, h, near[s - 1]))

    def swap(k, half):
        rows = pl.ds(pl.multiple_of(k * 256 + h * 128 + half * 64, 64), 64)
        return remote(units.at[k - 1, pl.ds(half * 64, 64), :], x.at[0, rows, :], z_send.at[k - 1, half],
                      z_recv.at[k - 1, half], device((z + (1, 3, 2)[k - 1]) % 4, h, p))

    between = device((z + jnp.where(h == 0, 1, 3)) % 4, h, p)

    def relay_in(half):
        rows = pl.ds(half * 64, 64)
        return remote(units.at[2, rows, :], relay.at[rows, :], relay_send.at[0, half], relay_recv.at[half], between)

    def relay_out(half):
        rows = pl.ds(pl.multiple_of(3 * 256 + h * 128 + half * 64, 64), 64)
        return remote(relay.at[pl.ds(half * 64, 64), :], x.at[0, rows, :], relay_send.at[1, half], z_recv.at[2, half],
                      between)

    def share(s, m):
        rows = pl.ds(pl.multiple_of(m * 256 + h * 128, 128), 128)
        return remote(x.at[s, rows, :], x.at[s, rows, :], c_send.at[s, m], c_recv.at[s, m], sibling)

    def shared(s, m):
        rows = pl.ds(pl.multiple_of(m * 256 + (1 - h) * 128, 128), 128)
        return remote(x.at[s, rows, :], x.at[s, rows, :], c_send.at[s, m], c_recv.at[s, m], sibling)

    def give(s, m):
        pl.when(sibling_need[s] == 1)(lambda: share(s, m).start())

    def send_own(t):
        for d in range(4):
            pl.when(src[d] == 0)(lambda d=d: forward(d, t).start())

    def send_held(t):
        for d in range(4):
            pl.when(src[d] != 0)(lambda d=d: forward(d, t).start())

    def receive(links, t):
        for s in range(1, SLOTS):
            pl.when(dep[s - 1] == links)(lambda s=s: arrival(s, t).wait_recv())

    def give_held(links, t):
        if t % 2 == 1:
            for s in range(1, SLOTS):
                pl.when(dep[s - 1] == links)(lambda s=s: give(s, t // 2))

    send_own(0)
    send_own(1)
    for half in range(2):
        swap(1, half).start()
        swap(2, half).start()
    for half in range(2):
        relay_in(half).start()
    ids_copy = remote(ids_in, ids_got, id_send, id_recv, sibling)
    ids_copy.start()
    give(0, 0)

    ids_copy.wait_recv()
    ids_cols[...] = jnp.zeros_like(ids_cols)
    for s in range(SLOTS):
        for t in range(4):
            for core in range(2):
                unit = held[s] * 8 + 2 * ((z + REL[t]) % 4) + core
                got = jnp.where(mine, ids_in[pl.ds(unit, 1), :], ids_got[pl.ds(unit, 1), :])
                ids_cols[pl.ds(s * 8 + 2 * t + core, 1), :] = got.astype(jnp.float32)
    turned = ids_cols[...].T
    for j in range(SLOTS * 8):
        ids_rows[j] = jnp.broadcast_to(turned[:, j:j + 1], (128, 128))

    def strip(a, t, b, count, diagonal=False):
        sim = lax.dot_general(x[a, 256 * t:256 * t + 256, :], x[b, 0:256 * count, :], (((1,), (1,)), ((), ())),
                              preferred_element_type=jnp.float32)
        for r in range(4):
            unit, first_row = a * 8 + 2 * t + r // 2, 64 * (r % 2)
            row_ids = ids_rows[unit, first_row:first_row + 64]
            best = row_best[unit, first_row:first_row + 64]
            for c in range(2 * count):
                keep = row_ids == ids_cols[pl.ds(b * 8 + c, 1), :]
                if diagonal and c // 2 == t:
                    row = lax.broadcasted_iota(jnp.int32, (64, 128), 0) + 64 * r
                    col = lax.broadcasted_iota(jnp.int32, (64, 128), 1) + 128 * (c % 2)
                    keep = jnp.logical_and(keep, row != col)
                kept = jnp.where(keep, sim[64 * r:64 * r + 64, 128 * c:128 * c + 128], jnp.float32(-1.0))
                down = jnp.max(kept.reshape(8, 8, 128), axis=0)
                col_best[b * 8 + c] = jnp.maximum(col_best[b * 8 + c], down)
                best = jnp.maximum(best, kept)
            row_best[unit, first_row:first_row + 64] = best

    def compare(t, first, last, own):
        def one_pair(j, carry):
            a, b = todo[0], todo[1]
            for k in range(1, 4):
                a = jnp.where(j == k, todo[2 * k], a)
                b = jnp.where(j == k, todo[2 * k + 1], b)
            strip(a, t, b, t + 1)
            if t:
                strip(b, t, a, t)
            return carry

        lax.fori_loop(first, last, one_pair, 0)
        if own:
            pl.when(h == 1)(lambda: strip(0, t, 0, t + 1, diagonal=True))

    def wait_shared(m):
        for s in range(SLOTS):
            pl.when(need[s] == 1)(lambda s=s: shared(s, m).wait_recv())

    for step in range(1, STEPS + 1):
        receive(1, step - 1)
        send_held(step - 1)
        give_held(1, step - 1)
        if step == 1:
            swap(1, 0).wait_recv()
            send_own(2)
        elif step == 2:
            swap(1, 1).wait_recv()
            send_own(3)
            give(0, 1)
            swap(2, 0).wait_recv()
            send_own(4)
        elif step == 3:
            for half in range(2):
                relay_in(half).wait_recv()
                relay_out(half).start()
            swap(2, 1).wait_recv()
            send_own(5)
            give(0, 2)
        elif step == 5:
            for half in range(2):
                relay_out(half).wait_recv()
                send_own(6 + half)
            give(0, 3)
        if step in (4, 6, 8):
            wait_shared(step // 2 - 2)
            compare(step // 2 - 2, 0, 2, False)
        elif step in (5, 7):
            compare(step // 2 - 2, 2, pair_count, True)
        if step >= 2:
            receive(2, step - 2)
            give_held(2, step - 2)
    compare(2, 2, pair_count, True)
    receive(2, STEPS - 1)
    give_held(2, STEPS - 1)
    wait_shared(3)
    compare(3, 0, pair_count, True)

    for s in range(SLOTS):
        for t in range(4):
            z_of = (z + REL[t]) % 4
            for core in range(2):
                j = s * 8 + 2 * t + core
                both = jnp.maximum(jnp.max(row_best[j].T, axis=0, keepdims=True),
                                   jnp.max(col_best[j], axis=0, keepdims=True))
                part[s * 2 + z_of // 2, pl.ds(2 * (z_of % 2) + core, 1), :] = both
        for half in range(2):
            copy = remote(part.at[s * 2 + half], parts_got.at[place[s] * 2 + h], r_send.at[s * 2 + half],
                          r_recv.at[place[s] * 2 + h], (owner_grp, held[s] * 2 + half))
            if s == 0:
                keep_it = jnp.logical_and(mine, zh == half)
                pl.when(jnp.logical_not(keep_it))(copy.start)

                @pl.when(keep_it)
                def _():
                    parts_got[h] = part[half]
            else:
                copy.start()

    best = None
    for k in range(2 * SLOTS):
        got = remote(parts_got.at[k], parts_got.at[k], r_send.at[k], r_recv.at[k], sibling)
        if k < 2:
            pl.when(jnp.logical_not(jnp.logical_and(mine, h == k)))(got.wait_recv)
        else:
            got.wait_recv()
        best = parts_got[k] if best is None else jnp.maximum(best, parts_got[k])
    out[...] = best

    ids_copy.wait_send()
    for half in range(2):
        for copy in (swap(1, half), swap(2, half), relay_in(half), relay_out(half)):
            copy.wait_send()
    for d in range(4):
        for t in range(STEPS):
            forward(d, t).wait_send()
    for s in range(SLOTS):
        for m in range(4):
            pl.when(sibling_need[s] == 1)(lambda s=s, m=m: share(s, m).wait_send())
        for half in range(2):
            copy = remote(part.at[s * 2 + half], parts_got.at[place[s] * 2 + h], r_send.at[s * 2 + half],
                          r_recv.at[place[s] * 2 + h], (owner_grp, held[s] * 2 + half))
            if s == 0:
                pl.when(jnp.logical_not(jnp.logical_and(mine, zh == half)))(copy.wait_send)
            else:
                copy.wait_send()


def on_device(embeddings, cluster_ids):
    emb = embeddings.reshape(4, 128, D)
    ids = cluster_ids.reshape(128, 128)
    dma = pltpu.SemaphoreType.DMA
    best = pl.pallas_call(
        kernel,
        out_shape=jax.ShapeDtypeStruct((4, 128), jnp.float32),
        in_specs=[pl.BlockSpec(memory_space=pl.ANY), pl.BlockSpec(memory_space=pltpu.VMEM)],
        out_specs=pl.BlockSpec(memory_space=pltpu.VMEM),
        scratch_shapes=[
            pltpu.VMEM((SLOTS, 1024, D), jnp.bfloat16),
            pltpu.VMEM((3, 128, D), jnp.bfloat16),
            pltpu.VMEM((4, 128, D), jnp.float32),
            pltpu.VMEM((128, 128), jnp.int32),
            pltpu.VMEM((SLOTS * 8, 128, 128), jnp.float32),
            pltpu.VMEM((128, 128), jnp.float32),
            pltpu.VMEM((SLOTS * 8, 128, 128), jnp.float32),
            pltpu.VMEM((SLOTS * 8, 8, 128), jnp.float32),
            pltpu.VMEM((2 * SLOTS, 4, 128), jnp.float32),
            pltpu.VMEM((2 * SLOTS, 4, 128), jnp.float32),
            pltpu.VMEM((128, D), jnp.bfloat16),
            dma((4,)), dma, dma, dma((3, 2)), dma((3, 2)), dma((2, 2)), dma((2,)), dma((4, STEPS)), dma((4, STEPS)),
            dma((SLOTS, 4)), dma((SLOTS, 4)), dma((2 * SLOTS,)), dma((2 * SLOTS,)),
        ],
        compiler_params=pltpu.CompilerParams(
            collective_id=0, has_side_effects=True, vmem_limit_bytes=60 * 1024 * 1024),
        cost_estimate=pl.CostEstimate(flops=7 * 10**9, bytes_accessed=2 * 10**6, transcendentals=0),
        name="best_match",
    )(emb, ids)
    return best.reshape(1, 512)


def solution(mesh):
    placed = (P(None, "grp", "blk", None, None), P("grp", None))
    return jax.shard_map(
        on_device, mesh=mesh, in_specs=placed, out_specs=P("grp", "blk"), check_vma=False
    )
```

```python
import functools

import jax
import jax.numpy as jnp
from jax import lax
from jax.experimental import pallas as pl
from jax.experimental.pallas import tpu as pltpu
from jax.sharding import PartitionSpec as P

MESH = pl.DeviceIdType.MESH
D = 768
SLOTS = 5
PIECE = 32
STEPS = 16

SRC = [[0, 3, 0, 0], [3, 0, 0, 0], [0, 0, 4, 0], [0, 0, 4, 0], [0, 4, 1, 0], [4, 0, 2, 0], [0, 3, 0, 0], [3, 0, 0, 0],
       [3, 0, 0, 3], [0, 3, 0, 3], [2, 4, 0, 0], [4, 1, 0, 0], [2, 0, 4, 0], [0, 1, 4, 0], [4, 0, 0, 3], [0, 4, 0, 3]]
DEP = [[1, 1, 1, 2], [1, 1, 1, 2], [1, 2, 1, 1], [2, 1, 1, 1], [1, 2, 2, 1], [2, 1, 2, 1], [1, 2, 1, 2], [2, 1, 1, 2],
       [2, 2, 1, 2], [2, 2, 1, 2], [2, 1, 2, 1], [1, 2, 2, 1], [2, 1, 1, 1], [1, 2, 1, 1], [2, 1, 1, 1], [1, 2, 1, 1]]
BLK = [[1, 3, 4, 8], [2, 0, 5, 9], [3, 5, 6, 14], [4, 2, 7, 15], [5, 11, 12, 0], [10, 4, 13, 1], [7, 1, 10, 14],
       [0, 6, 11, 15], [13, 7, 12, 5], [6, 12, 13, 4], [8, 9, 2, 6], [8, 9, 3, 7], [14, 15, 0, 8], [14, 15, 1, 9],
       [11, 13, 2, 10], [12, 10, 3, 11]]
IDX = [[1, 1, 1, 1], [1, 1, 1, 1], [2, 2, 1, 1], [2, 2, 1, 1], [3, 1, 1, 2], [1, 3, 1, 2], [2, 3, 2, 2], [3, 2, 2, 2],
       [2, 3, 2, 4], [3, 3, 3, 4], [2, 2, 3, 4], [3, 3, 3, 4], [3, 3, 4, 4], [4, 4, 4, 4], [3, 4, 4, 3], [4, 4, 4, 4]]
HOLD = [[0, 1, 4, 7, 12], [1, 0, 5, 6, 13], [2, 1, 3, 10, 14], [3, 0, 2, 11, 15], [4, 0, 3, 5, 9], [5, 1, 2, 4, 8],
        [6, 2, 7, 9, 10], [7, 3, 6, 8, 11], [8, 0, 10, 11, 12], [9, 1, 10, 11, 13], [10, 5, 6, 14, 15], [11, 4, 7, 14, 15],
        [12, 4, 8, 9, 15], [13, 5, 8, 9, 14], [14, 2, 6, 12, 13], [15, 3, 7, 12, 13]]
PAIRS = [[[(1, 3), (1, 4), (3, 4)], [(0, 1), (0, 2), (1, 2)]], [[(2, 1), (2, 4), (1, 4)], [(0, 1), (0, 3), (3, 4)]],
         [[(1, 3), (3, 4), (2, 3), (2, 4)], [(0, 1), (0, 2), (1, 2)]],
         [[(2, 3), (2, 1), (1, 3)], [(0, 3), (3, 4), (0, 1)]], [[(4, 0), (4, 1), (0, 2), (1, 2)], [(0, 3), (1, 3)]],
         [[(2, 0), (4, 1), (2, 1)], [(0, 1), (0, 3), (1, 3)]], [[(1, 3), (1, 4), (3, 4)], [(0, 3), (2, 0), (2, 1)]],
         [[(2, 3), (2, 4), (3, 4)], [(2, 0), (1, 2), (1, 0)]],
         [[(2, 3), (2, 1), (0, 1), (3, 1)], [(4, 2), (4, 0), (2, 0)]],
         [[(4, 1), (4, 0), (4, 3), (1, 3)], [(1, 0), (1, 2), (0, 2)]],
         [[(3, 4), (3, 1), (4, 1)], [(2, 0), (1, 2), (1, 0)]], [[(1, 0), (3, 1), (3, 2)], [(4, 0), (4, 2), (2, 0)]],
         [[(3, 4), (4, 1), (0, 1)], [(4, 0), (4, 2), (0, 2)]], [[(3, 4), (4, 1), (1, 2)], [(4, 0), (4, 2), (0, 2)]],
         [[(3, 4), (3, 1), (4, 1)], [(2, 0), (1, 2), (1, 0)]], [[(3, 4), (3, 1), (4, 1)], [(3, 2), (2, 1), (2, 0)]]]
NEED = [[[1, 3, 4], [0, 1, 2]], [[1, 2, 4], [0, 1, 3, 4]], [[1, 2, 3, 4], [0, 1, 2]], [[1, 2, 3], [0, 1, 3, 4]],
        [[0, 1, 2, 4], [0, 1, 3]], [[0, 1, 2, 4], [0, 1, 3]], [[1, 3, 4], [0, 1, 2, 3]], [[2, 3, 4], [0, 1, 2]],
        [[0, 1, 2, 3], [0, 2, 4]], [[0, 1, 3, 4], [0, 1, 2]], [[1, 3, 4], [0, 1, 2]], [[0, 1, 2, 3], [0, 2, 4]],
        [[0, 1, 3, 4], [0, 2, 4]], [[1, 2, 3, 4], [0, 2, 4]], [[1, 3, 4], [0, 1, 2]], [[1, 3, 4], [0, 1, 2, 3]]]

REL = (0, 3, 1, 2)


def word(digits, base):
    total = 0
    for digit in reversed(digits):
        total = total * base + digit
    return total


def look_up(index, words):
    got = jnp.int32(words[0])
    for k in range(1, len(words)):
        got = jnp.where(index == k, jnp.int32(words[k]), got)
    return got


def digits_of(value, base, count):
    out = []
    for _ in range(count):
        out.append(value % base)
        value = value // base
    return out


def kernel(emb, ids_in, out, x, units, stage, ids_got, ids_rows, ids_cols, row_best, col_best, row_line, part, parts_got,
           relay,
           load_sem, id_send, id_recv, z_send, z_recv, relay_send, relay_recv, f_send, f_recv, c_send, c_recv, r_send, r_recv):
    grp, blk = lax.axis_index("grp"), lax.axis_index("blk")
    h, zl = grp % 2, grp // 2
    p, zh = blk // 2, blk % 2
    z = zh * 2 + zl
    px, py = p % 4, p // 4

    def device(z_of, core, chip):
        return ((z_of % 2) * 2 + core, chip * 2 + z_of // 2)

    def group_of(z_of):
        return (z_of % 2) * 2 + z_of // 2

    near = [py * 4 + (px + 1) % 4, py * 4 + (px + 3) % 4, ((py + 1) % 4) * 4 + px, ((py + 3) % 4) * 4 + px]
    first = look_up(p, [word(SRC[c], 8) + 4096 * word(DEP[c], 4) for c in range(16)])
    src = digits_of(first, 8, 4)
    dep = digits_of(first // 4096, 4, 4)
    held = [p] + digits_of(look_up(p, [word(BLK[c], 16) for c in range(16)]), 16, 4)
    third = look_up(p, [word(IDX[c], 8) + 4096 * word(HOLD[c][1:], 16) for c in range(16)])
    place = [jnp.int32(0)] + digits_of(third, 8, 4)
    holders = [p] + digits_of(third // 4096, 16, 4)
    lists = []
    for c in range(16):
        for core in range(2):
            flat = [slot for pair in PAIRS[c][core] for slot in pair]
            lists.append(len(PAIRS[c][core]) + 8 * word(flat + [0] * (8 - len(flat)), 8))
    todo = look_up(p * 2 + h, lists)
    pair_count = todo % 8
    todo = digits_of(todo // 8, 8, 8)

    needs = [[sum(1 << slot for slot in NEED[c][core]) for core in range(2)] for c in range(16)]
    need = digits_of(look_up(p * 2 + h, [needs[c][core] for c in range(16) for core in range(2)]), 2, SLOTS)
    sibling_need = digits_of(look_up(p * 2 + h, [needs[c][1 - core] for c in range(16) for core in range(2)]), 2, SLOTS)

    sibling = device(z, 1 - h, p)
    owner_grp = zl * 2 + zh
    mine = h == zh

    loads = []
    for k, rel in enumerate((0, 1, 3, 2)):
        loads.append(pltpu.make_async_copy(emb.at[group_of((z + rel) % 4)], stage.at[k], load_sem.at[k]))
        loads[-1].start()

    barrier = pltpu.get_barrier_semaphore()
    for rel in (1, 3):
        pl.semaphore_signal(barrier, inc=1, device_id=device((z + rel) % 4, h, p), device_id_type=MESH)
    for d in range(4):
        pl.semaphore_signal(barrier, inc=1, device_id=device(z, h, near[d]), device_id_type=MESH)
    pl.semaphore_signal(barrier, inc=1, device_id=sibling, device_id_type=MESH)
    from_z = 2 * h + zl
    for k in range(SLOTS):
        for core in range(2):
            def tell():
                pl.semaphore_signal(barrier, inc=1, device_id=device(from_z, core, holders[k]), device_id_type=MESH)
            if k == 0:
                pl.when(jnp.logical_not(jnp.logical_and(mine, h == core)))(tell)
            else:
                tell()

    def normalise(k):
        loads[k].wait()
        v = stage[k]
        total = jnp.sum(v * v, axis=-1, keepdims=True)
        return (v / jnp.sqrt(total + 1e-06)).astype(jnp.bfloat16)

    own_rows = pl.multiple_of(h * 128, 128)
    x[0, pl.ds(own_rows, 128), :] = normalise(0)
    pl.semaphore_wait(barrier, jnp.where(mine, 16, 17))

    def remote(src_ref, dst_ref, send_sem, recv_sem, to):
        return pltpu.make_async_remote_copy(
            src_ref=src_ref, dst_ref=dst_ref, send_sem=send_sem, recv_sem=recv_sem, device_id=to, device_id_type=MESH)

    def part_rows(t):
        return pl.ds(pl.multiple_of((t // 4) * 256 + h * 128 + (t % 4) * PIECE, PIECE), PIECE)

    def forward(d, t):
        rows = part_rows(t)
        return remote(x.at[src[d], rows, :], x.at[1 + (d ^ 1), rows, :], f_send.at[d, t], f_recv.at[d ^ 1, t],
                      device(z, h, near[d]))

    def arrival(s, t):
        rows = part_rows(t)
        return remote(x.at[s, rows, :], x.at[s, rows, :], f_send.at[s - 1, t], f_recv.at[s - 1, t],
                      device(z, h, near[s - 1]))

    def swap(k, half):
        rows = pl.ds(pl.multiple_of(k * 256 + h * 128 + half * 64, 64), 64)
        return remote(units.at[k - 1, pl.ds(half * 64, 64), :], x.at[0, rows, :], z_send.at[k - 1, half],
                      z_recv.at[k - 1, half], device((z + (1, 3, 2)[k - 1]) % 4, h, p))

    between = device((z + jnp.where(h == 0, 1, 3)) % 4, h, p)

    def relay_in(half):
        rows = pl.ds(half * 64, 64)
        return remote(units.at[2, rows, :], relay.at[rows, :], relay_send.at[0, half], relay_recv.at[half], between)

    def relay_out(half):
        rows = pl.ds(pl.multiple_of(3 * 256 + h * 128 + half * 64, 64), 64)
        return remote(relay.at[pl.ds(half * 64, 64), :], x.at[0, rows, :], relay_send.at[1, half], z_recv.at[2, half],
                      between)

    def share_rows(t, core):
        return pl.ds(pl.multiple_of((t // 2) * 256 + core * 128 + (t % 2) * 64, 64), 64)

    def share(s, t):
        rows = share_rows(t, h)
        return remote(x.at[s, rows, :], x.at[s, rows, :], c_send.at[s, t], c_recv.at[s, t], sibling)

    def shared(s, t):
        rows = share_rows(t, 1 - h)
        return remote(x.at[s, rows, :], x.at[s, rows, :], c_send.at[s, t], c_recv.at[s, t], sibling)

    def give(s, t):
        pl.when(sibling_need[s] == 1)(lambda: share(s, t).start())

    def send_own(t):
        for d in range(4):
            pl.when(src[d] == 0)(lambda d=d: forward(d, t).start())

    def send_held(t):
        for d in range(4):
            pl.when(src[d] != 0)(lambda d=d: forward(d, t).start())

    def receive(links, t):
        for s in range(1, SLOTS):
            pl.when(dep[s - 1] == links)(lambda s=s: arrival(s, t).wait_recv())

    def give_held(links, t):
        for s in range(1, SLOTS):
            pl.when(dep[s - 1] == links)(lambda s=s: give(s, t // 2))

    for t in range(4):
        send_own(t)
    units[0] = normalise(1)
    for half in range(2):
        swap(1, half).start()
    units[1] = normalise(2)
    for half in range(2):
        swap(2, half).start()
    units[2] = normalise(3)
    for half in range(2):
        relay_in(half).start()
    ids_copy = remote(ids_in, ids_got, id_send, id_recv, sibling)
    ids_copy.start()
    give(0, 0)
    give(0, 1)
    row_best[...] = jnp.full_like(row_best, -1.0)
    col_best[...] = jnp.full_like(col_best, -1.0)
    row_line[...] = jnp.full_like(row_line, -1.0)

    ids_copy.wait_recv()
    ids_cols[...] = jnp.zeros_like(ids_cols)
    for s in range(SLOTS):
        for t in range(4):
            for core in range(2):
                unit = held[s] * 8 + 2 * ((z + REL[t]) % 4) + core
                got = jnp.where(mine, ids_in[pl.ds(unit, 1), :], ids_got[pl.ds(unit, 1), :])
                ids_cols[pl.ds(s * 8 + 2 * t + core, 1), :] = got.astype(jnp.float32)
    turned = ids_cols[...].T
    for j in range(SLOTS * 8):
        ids_rows[j] = jnp.broadcast_to(turned[:, j:j + 1], (128, 128))

    def strip(a, t, b, count, diagonal=False):
        sim = lax.dot_general(x[a, 256 * t:256 * t + 256, :], x[b, 0:256 * count, :], (((1,), (1,)), ((), ())),
                              preferred_element_type=jnp.float32)
        for r in range(4):
            unit, first_row = a * 8 + 2 * t + r // 2, 64 * (r % 2)
            row_ids = ids_rows[unit, first_row:first_row + 64]
            best = row_best[unit, first_row:first_row + 64]
            for c in range(2 * count):
                keep = row_ids == ids_cols[pl.ds(b * 8 + c, 1), :]
                if diagonal and c // 2 == t:
                    row = lax.broadcasted_iota(jnp.int32, (64, 128), 0) + 64 * r
                    col = lax.broadcasted_iota(jnp.int32, (64, 128), 1) + 128 * (c % 2)
                    keep = jnp.logical_and(keep, row != col)
                kept = jnp.where(keep, sim[64 * r:64 * r + 64, 128 * c:128 * c + 128], jnp.float32(-1.0))
                down = jnp.max(kept.reshape(8, 8, 128), axis=0)
                col_best[b * 8 + c] = jnp.maximum(col_best[b * 8 + c], down)
                best = jnp.maximum(best, kept)
            row_best[unit, first_row:first_row + 64] = best

    def compare(t, j):
        a, b = todo[0], todo[1]
        for k in range(1, 4):
            a = jnp.where(j == k, todo[2 * k], a)
            b = jnp.where(j == k, todo[2 * k + 1], b)
        strip(a, t, b, t + 1)
        if t:
            strip(b, t, a, t)

    def finish_rows(t):
        pl.when(h == 1)(lambda: strip(0, t, 0, t + 1, diagonal=True))
        for s in range(SLOTS):
            @pl.when(need[s] == 1)
            def _():
                for core in range(2):
                    unit = s * 8 + 2 * t + core
                    row_line[unit:unit + 1, :] = jnp.max(row_best[unit].T, axis=0, keepdims=True)

    def wait_shared(m):
        for s in range(SLOTS):
            @pl.when(need[s] == 1)
            def _():
                for half in range(2):
                    shared(s, 2 * m + half).wait_recv()

    def own_piece_ready(k):
        def two(m, half):
            send_own(4 * m + 2 * half)
            send_own(4 * m + 2 * half + 1)
            give(0, 2 * m + half)

        @pl.when(k == 2)
        def _():
            swap(1, 0).wait_recv()
            two(1, 0)

        @pl.when(k == 4)
        def _():
            swap(1, 1).wait_recv()
            two(1, 1)

        @pl.when(k == 5)
        def _():
            swap(2, 0).wait_recv()
            two(2, 0)

        @pl.when(k == 6)
        def _():
            for half in range(2):
                relay_in(half).wait_recv()
                relay_out(half).start()

        @pl.when(k == 7)
        def _():
            swap(2, 1).wait_recv()
            two(2, 1)

        @pl.when(k == 10)
        def _():
            relay_out(0).wait_recv()
            two(3, 0)

        @pl.when(k == 11)
        def _():
            relay_out(1).wait_recv()
            two(3, 1)

    def pass_on(k):
        receive(1, k - 1)
        send_held(k - 1)
        pl.when(k % 2 == 0)(lambda: give_held(1, k - 1))

    def take(k):
        receive(2, k - 2)
        pl.when(k % 2 == 1)(lambda: give_held(2, k - 2))

    @pl.loop(1, 7)
    def _(k):
        pass_on(k)
        own_piece_ready(k)
        pl.when(k >= 2)(lambda: take(k))

    for m in range(2):
        @pl.loop(7 + 4 * m, 11 + 4 * m)
        def _(k):
            pass_on(k)
            own_piece_ready(k)
            pl.when(k == 7 + 4 * m)(lambda: wait_shared(m))
            pl.when(k - 7 - 4 * m < pair_count)(lambda: compare(m, k - 7 - 4 * m))
            take(k)
        finish_rows(m)

    @pl.loop(15, 19)
    def _(k):
        pl.when(k <= STEPS)(lambda: pass_on(k))
        pl.when(k == 15)(lambda: wait_shared(2))
        pl.when(k - 15 < pair_count)(lambda: compare(2, k - 15))
        pl.when(k <= STEPS + 1)(lambda: take(k))
    finish_rows(2)

    wait_shared(3)

    @pl.loop(0, pair_count)
    def _(j):
        compare(3, j)
    finish_rows(3)

    for s in range(SLOTS):
        for t in range(4):
            z_of = (z + REL[t]) % 4
            for core in range(2):
                j = s * 8 + 2 * t + core
                both = jnp.maximum(row_line[j:j + 1, :], jnp.max(col_best[j], axis=0, keepdims=True))
                part[s * 2 + z_of // 2, pl.ds(2 * (z_of % 2) + core, 1), :] = both
        for half in range(2):
            copy = remote(part.at[s * 2 + half], parts_got.at[place[s] * 2 + h], r_send.at[s * 2 + half],
                          r_recv.at[place[s] * 2 + h], (owner_grp, held[s] * 2 + half))
            if s == 0:
                keep_it = jnp.logical_and(mine, zh == half)
                pl.when(jnp.logical_not(keep_it))(copy.start)

                @pl.when(keep_it)
                def _():
                    parts_got[h] = part[half]
            else:
                copy.start()

    best = None
    for k in range(2 * SLOTS):
        got = remote(parts_got.at[k], parts_got.at[k], r_send.at[k], r_recv.at[k], sibling)
        if k < 2:
            pl.when(jnp.logical_not(jnp.logical_and(mine, h == k)))(got.wait_recv)
        else:
            got.wait_recv()
        best = parts_got[k] if best is None else jnp.maximum(best, parts_got[k])
    out[...] = best

    ids_copy.wait_send()
    for half in range(2):
        for copy in (swap(1, half), swap(2, half), relay_in(half), relay_out(half)):
            copy.wait_send()
    for d in range(4):
        for t in range(STEPS):
            forward(d, t).wait_send()
    for s in range(SLOTS):
        for t in range(8):
            pl.when(sibling_need[s] == 1)(lambda s=s, t=t: share(s, t).wait_send())
        for half in range(2):
            copy = remote(part.at[s * 2 + half], parts_got.at[place[s] * 2 + h], r_send.at[s * 2 + half],
                          r_recv.at[place[s] * 2 + h], (owner_grp, held[s] * 2 + half))
            if s == 0:
                pl.when(jnp.logical_not(jnp.logical_and(mine, zh == half)))(copy.wait_send)
            else:
                copy.wait_send()


def on_device(embeddings, cluster_ids):
    emb = embeddings.reshape(4, 128, D)
    ids = cluster_ids.reshape(128, 128)
    dma = pltpu.SemaphoreType.DMA
    best = pl.pallas_call(
        kernel,
        out_shape=jax.ShapeDtypeStruct((4, 128), jnp.float32),
        in_specs=[pl.BlockSpec(memory_space=pl.ANY), pl.BlockSpec(memory_space=pltpu.VMEM)],
        out_specs=pl.BlockSpec(memory_space=pltpu.VMEM),
        scratch_shapes=[
            pltpu.VMEM((SLOTS, 1024, D), jnp.bfloat16),
            pltpu.VMEM((3, 128, D), jnp.bfloat16),
            pltpu.VMEM((4, 128, D), jnp.float32),
            pltpu.VMEM((128, 128), jnp.int32),
            pltpu.VMEM((SLOTS * 8, 128, 128), jnp.float32),
            pltpu.VMEM((128, 128), jnp.float32),
            pltpu.VMEM((SLOTS * 8, 128, 128), jnp.float32),
            pltpu.VMEM((SLOTS * 8, 8, 128), jnp.float32),
            pltpu.VMEM((SLOTS * 8, 128), jnp.float32),
            pltpu.VMEM((2 * SLOTS, 4, 128), jnp.float32),
            pltpu.VMEM((2 * SLOTS, 4, 128), jnp.float32),
            pltpu.VMEM((128, D), jnp.bfloat16),
            dma((4,)), dma, dma, dma((3, 2)), dma((3, 2)), dma((2, 2)), dma((2,)), dma((4, STEPS)), dma((4, STEPS)),
            dma((SLOTS, 8)), dma((SLOTS, 8)), dma((2 * SLOTS,)), dma((2 * SLOTS,)),
        ],
        compiler_params=pltpu.CompilerParams(
            collective_id=0, has_side_effects=True, vmem_limit_bytes=60 * 1024 * 1024),
        cost_estimate=pl.CostEstimate(flops=7 * 10**9, bytes_accessed=2 * 10**6, transcendentals=0),
        name="best_match",
    )(emb, ids)
    return best.reshape(1, 512)


def solution(mesh):
    placed = (P(None, "grp", "blk", None, None), P("grp", None))
    return jax.shard_map(
        on_device, mesh=mesh, in_specs=placed, out_specs=P("grp", "blk"), check_vma=False
    )
```

```python
import functools

import jax
import jax.numpy as jnp
from jax import lax
from jax.experimental import pallas as pl
from jax.experimental.pallas import tpu as pltpu
from jax.sharding import PartitionSpec as P

MESH = pl.DeviceIdType.MESH
D = 768
SLOTS = 5
PIECE = 64
STEPS = 8

SRC = [[0, 3, 0, 0], [3, 0, 0, 0], [0, 0, 4, 0], [0, 0, 4, 0], [0, 4, 1, 0], [4, 0, 2, 0], [0, 3, 0, 0], [3, 0, 0, 0],
       [3, 0, 0, 3], [0, 3, 0, 3], [2, 4, 0, 0], [4, 1, 0, 0], [2, 0, 4, 0], [0, 1, 4, 0], [4, 0, 0, 3], [0, 4, 0, 3]]
DEP = [[1, 1, 1, 2], [1, 1, 1, 2], [1, 2, 1, 1], [2, 1, 1, 1], [1, 2, 2, 1], [2, 1, 2, 1], [1, 2, 1, 2], [2, 1, 1, 2],
       [2, 2, 1, 2], [2, 2, 1, 2], [2, 1, 2, 1], [1, 2, 2, 1], [2, 1, 1, 1], [1, 2, 1, 1], [2, 1, 1, 1], [1, 2, 1, 1]]
BLK = [[1, 3, 4, 8], [2, 0, 5, 9], [3, 5, 6, 14], [4, 2, 7, 15], [5, 11, 12, 0], [10, 4, 13, 1], [7, 1, 10, 14],
       [0, 6, 11, 15], [13, 7, 12, 5], [6, 12, 13, 4], [8, 9, 2, 6], [8, 9, 3, 7], [14, 15, 0, 8], [14, 15, 1, 9],
       [11, 13, 2, 10], [12, 10, 3, 11]]
IDX = [[1, 1, 1, 1], [1, 1, 1, 1], [2, 2, 1, 1], [2, 2, 1, 1], [3, 1, 1, 2], [1, 3, 1, 2], [2, 3, 2, 2], [3, 2, 2, 2],
       [2, 3, 2, 4], [3, 3, 3, 4], [2, 2, 3, 4], [3, 3, 3, 4], [3, 3, 4, 4], [4, 4, 4, 4], [3, 4, 4, 3], [4, 4, 4, 4]]
HOLD = [[0, 1, 4, 7, 12], [1, 0, 5, 6, 13], [2, 1, 3, 10, 14], [3, 0, 2, 11, 15], [4, 0, 3, 5, 9], [5, 1, 2, 4, 8],
        [6, 2, 7, 9, 10], [7, 3, 6, 8, 11], [8, 0, 10, 11, 12], [9, 1, 10, 11, 13], [10, 5, 6, 14, 15], [11, 4, 7, 14, 15],
        [12, 4, 8, 9, 15], [13, 5, 8, 9, 14], [14, 2, 6, 12, 13], [15, 3, 7, 12, 13]]
PAIRS = [[[(1, 3), (1, 4), (3, 4)], [(0, 1), (0, 2), (1, 2)]], [[(2, 1), (2, 4), (1, 4)], [(0, 1), (0, 3), (3, 4)]],
         [[(1, 3), (3, 4), (2, 3), (2, 4)], [(0, 1), (0, 2), (1, 2)]],
         [[(2, 3), (2, 1), (1, 3)], [(0, 3), (3, 4), (0, 1)]], [[(4, 0), (4, 1), (0, 2), (1, 2)], [(0, 3), (1, 3)]],
         [[(2, 0), (4, 1), (2, 1)], [(0, 1), (0, 3), (1, 3)]], [[(1, 3), (1, 4), (3, 4)], [(0, 3), (2, 0), (2, 1)]],
         [[(2, 3), (2, 4), (3, 4)], [(2, 0), (1, 2), (1, 0)]],
         [[(2, 3), (2, 1), (0, 1), (3, 1)], [(4, 2), (4, 0), (2, 0)]],
         [[(4, 1), (4, 0), (4, 3), (1, 3)], [(1, 0), (1, 2), (0, 2)]],
         [[(3, 4), (3, 1), (4, 1)], [(2, 0), (1, 2), (1, 0)]], [[(1, 0), (3, 1), (3, 2)], [(4, 0), (4, 2), (2, 0)]],
         [[(3, 4), (4, 1), (0, 1)], [(4, 0), (4, 2), (0, 2)]], [[(3, 4), (4, 1), (1, 2)], [(4, 0), (4, 2), (0, 2)]],
         [[(3, 4), (3, 1), (4, 1)], [(2, 0), (1, 2), (1, 0)]], [[(3, 4), (3, 1), (4, 1)], [(3, 2), (2, 1), (2, 0)]]]
NEED = [[[1, 3, 4], [0, 1, 2]], [[1, 2, 4], [0, 1, 3, 4]], [[1, 2, 3, 4], [0, 1, 2]], [[1, 2, 3], [0, 1, 3, 4]],
        [[0, 1, 2, 4], [0, 1, 3]], [[0, 1, 2, 4], [0, 1, 3]], [[1, 3, 4], [0, 1, 2, 3]], [[2, 3, 4], [0, 1, 2]],
        [[0, 1, 2, 3], [0, 2, 4]], [[0, 1, 3, 4], [0, 1, 2]], [[1, 3, 4], [0, 1, 2]], [[0, 1, 2, 3], [0, 2, 4]],
        [[0, 1, 3, 4], [0, 2, 4]], [[1, 2, 3, 4], [0, 2, 4]], [[1, 3, 4], [0, 1, 2]], [[1, 3, 4], [0, 1, 2, 3]]]

REL = (0, 3, 1, 2)


def word(digits, base):
    total = 0
    for digit in reversed(digits):
        total = total * base + digit
    return total


def look_up(index, words):
    got = jnp.int32(words[0])
    for k in range(1, len(words)):
        got = jnp.where(index == k, jnp.int32(words[k]), got)
    return got


def digits_of(value, base, count):
    out = []
    for _ in range(count):
        out.append(value % base)
        value = value // base
    return out


def kernel(emb, ids_in, out, x, units, stage, ids_got, ids_rows, ids_cols, row_best, col_best, row_line, part, parts_got,
           relay,
           load_sem, id_send, id_recv, z_send, z_recv, relay_send, relay_recv, f_send, f_recv, c_send, c_recv, r_send, r_recv):
    grp, blk = lax.axis_index("grp"), lax.axis_index("blk")
    h, zl = grp % 2, grp // 2
    p, zh = blk // 2, blk % 2
    z = zh * 2 + zl
    px, py = p % 4, p // 4

    def device(z_of, core, chip):
        return ((z_of % 2) * 2 + core, chip * 2 + z_of // 2)

    def group_of(z_of):
        return (z_of % 2) * 2 + z_of // 2

    near = [py * 4 + (px + 1) % 4, py * 4 + (px + 3) % 4, ((py + 1) % 4) * 4 + px, ((py + 3) % 4) * 4 + px]
    first = look_up(p, [word(SRC[c], 8) + 4096 * word(DEP[c], 4) for c in range(16)])
    src = digits_of(first, 8, 4)
    dep = digits_of(first // 4096, 4, 4)
    held = [p] + digits_of(look_up(p, [word(BLK[c], 16) for c in range(16)]), 16, 4)
    third = look_up(p, [word(IDX[c], 8) + 4096 * word(HOLD[c][1:], 16) for c in range(16)])
    place = [jnp.int32(0)] + digits_of(third, 8, 4)
    holders = [p] + digits_of(third // 4096, 16, 4)
    lists = []
    for c in range(16):
        for core in range(2):
            flat = [slot for pair in PAIRS[c][core] for slot in pair]
            lists.append(len(PAIRS[c][core]) + 8 * word(flat + [0] * (8 - len(flat)), 8))
    todo = look_up(p * 2 + h, lists)
    pair_count = todo % 8
    todo = digits_of(todo // 8, 8, 8)

    needs = [[sum(1 << slot for slot in NEED[c][core]) for core in range(2)] for c in range(16)]
    need = digits_of(look_up(p * 2 + h, [needs[c][core] for c in range(16) for core in range(2)]), 2, SLOTS)
    sibling_need = digits_of(look_up(p * 2 + h, [needs[c][1 - core] for c in range(16) for core in range(2)]), 2, SLOTS)

    sibling = device(z, 1 - h, p)
    owner_grp = zl * 2 + zh
    mine = h == zh

    loads = []
    for k, rel in enumerate((0, 1, 3, 2)):
        loads.append(pltpu.make_async_copy(emb.at[group_of((z + rel) % 4)], stage.at[k], load_sem.at[k]))
        loads[-1].start()

    barrier = pltpu.get_barrier_semaphore()
    for rel in (1, 3):
        pl.semaphore_signal(barrier, inc=1, device_id=device((z + rel) % 4, h, p), device_id_type=MESH)
    for d in range(4):
        pl.semaphore_signal(barrier, inc=1, device_id=device(z, h, near[d]), device_id_type=MESH)
    pl.semaphore_signal(barrier, inc=1, device_id=sibling, device_id_type=MESH)
    from_z = 2 * h + zl
    for k in range(SLOTS):
        for core in range(2):
            def tell():
                pl.semaphore_signal(barrier, inc=1, device_id=device(from_z, core, holders[k]), device_id_type=MESH)
            if k == 0:
                pl.when(jnp.logical_not(jnp.logical_and(mine, h == core)))(tell)
            else:
                tell()

    def normalise(k):
        loads[k].wait()
        v = stage[k]
        total = jnp.sum(v * v, axis=-1, keepdims=True)
        return (v / jnp.sqrt(total + 1e-06)).astype(jnp.bfloat16)

    own_rows = pl.multiple_of(h * 128, 128)
    x[0, pl.ds(own_rows, 128), :] = normalise(0)
    pl.semaphore_wait(barrier, jnp.where(mine, 16, 17))

    def remote(src_ref, dst_ref, send_sem, recv_sem, to):
        return pltpu.make_async_remote_copy(
            src_ref=src_ref, dst_ref=dst_ref, send_sem=send_sem, recv_sem=recv_sem, device_id=to, device_id_type=MESH)

    def part_rows(t):
        return pl.ds(pl.multiple_of((t // 2) * 256 + h * 128 + (t % 2) * PIECE, PIECE), PIECE)

    def forward(d, t):
        rows = part_rows(t)
        return remote(x.at[src[d], rows, :], x.at[1 + (d ^ 1), rows, :], f_send.at[d, t], f_recv.at[d ^ 1, t],
                      device(z, h, near[d]))

    def arrival(s, t):
        rows = part_rows(t)
        return remote(x.at[s, rows, :], x.at[s, rows, :], f_send.at[s - 1, t], f_recv.at[s - 1, t],
                      device(z, h, near[s - 1]))

    def swap(k, half):
        rows = pl.ds(pl.multiple_of(k * 256 + h * 128 + half * 64, 64), 64)
        return remote(units.at[k - 1, pl.ds(half * 64, 64), :], x.at[0, rows, :], z_send.at[k - 1, half],
                      z_recv.at[k - 1, half], device((z + (1, 3, 2)[k - 1]) % 4, h, p))

    between = device((z + jnp.where(h == 0, 1, 3)) % 4, h, p)

    def relay_in(half):
        rows = pl.ds(half * 64, 64)
        return remote(units.at[2, rows, :], relay.at[rows, :], relay_send.at[0, half], relay_recv.at[half], between)

    def relay_out(half):
        rows = pl.ds(pl.multiple_of(3 * 256 + h * 128 + half * 64, 64), 64)
        return remote(relay.at[pl.ds(half * 64, 64), :], x.at[0, rows, :], relay_send.at[1, half], z_recv.at[2, half],
                      between)

    def share_rows(t, core):
        return pl.ds(pl.multiple_of((t // 2) * 256 + core * 128 + (t % 2) * 64, 64), 64)

    def share(s, t):
        rows = share_rows(t, h)
        return remote(x.at[s, rows, :], x.at[s, rows, :], c_send.at[s, t], c_recv.at[s, t], sibling)

    def shared(s, t):
        rows = share_rows(t, 1 - h)
        return remote(x.at[s, rows, :], x.at[s, rows, :], c_send.at[s, t], c_recv.at[s, t], sibling)

    def give(s, t):
        pl.when(sibling_need[s] == 1)(lambda: share(s, t).start())

    def send_own(t):
        for d in range(4):
            pl.when(src[d] == 0)(lambda d=d: forward(d, t).start())

    def send_held(t):
        for d in range(4):
            pl.when(src[d] != 0)(lambda d=d: forward(d, t).start())

    def receive(links, t):
        for s in range(1, SLOTS):
            pl.when(dep[s - 1] == links)(lambda s=s: arrival(s, t).wait_recv())

    def give_held(links, t):
        for s in range(1, SLOTS):
            pl.when(dep[s - 1] == links)(lambda s=s: give(s, t))

    for t in range(2):
        send_own(t)
    units[0] = normalise(1)
    for half in range(2):
        swap(1, half).start()
    units[1] = normalise(2)
    for half in range(2):
        swap(2, half).start()
    units[2] = normalise(3)
    for half in range(2):
        relay_in(half).start()
    ids_copy = remote(ids_in, ids_got, id_send, id_recv, sibling)
    ids_copy.start()
    give(0, 0)
    give(0, 1)
    row_best[...] = jnp.full_like(row_best, -1.0)
    col_best[...] = jnp.full_like(col_best, -1.0)
    row_line[...] = jnp.full_like(row_line, -1.0)

    ids_copy.wait_recv()
    ids_cols[...] = jnp.zeros_like(ids_cols)
    for s in range(SLOTS):
        for t in range(4):
            for core in range(2):
                unit = held[s] * 8 + 2 * ((z + REL[t]) % 4) + core
                got = jnp.where(mine, ids_in[pl.ds(unit, 1), :], ids_got[pl.ds(unit, 1), :])
                ids_cols[pl.ds(s * 8 + 2 * t + core, 1), :] = got.astype(jnp.float32)
    turned = ids_cols[...].T
    for j in range(SLOTS * 8):
        ids_rows[j] = jnp.broadcast_to(turned[:, j:j + 1], (128, 128))

    def strip(a, t, b, count, diagonal=False):
        sim = lax.dot_general(x[a, 256 * t:256 * t + 256, :], x[b, 0:256 * count, :], (((1,), (1,)), ((), ())),
                              preferred_element_type=jnp.float32)
        for r in range(4):
            unit, first_row = a * 8 + 2 * t + r // 2, 64 * (r % 2)
            row_ids = ids_rows[unit, first_row:first_row + 64]
            best = row_best[unit, first_row:first_row + 64]
            for c in range(2 * count):
                keep = row_ids == ids_cols[pl.ds(b * 8 + c, 1), :]
                if diagonal and c // 2 == t:
                    row = lax.broadcasted_iota(jnp.int32, (64, 128), 0) + 64 * r
                    col = lax.broadcasted_iota(jnp.int32, (64, 128), 1) + 128 * (c % 2)
                    keep = jnp.logical_and(keep, row != col)
                kept = jnp.where(keep, sim[64 * r:64 * r + 64, 128 * c:128 * c + 128], jnp.float32(-1.0))
                down = jnp.max(kept.reshape(8, 8, 128), axis=0)
                col_best[b * 8 + c] = jnp.maximum(col_best[b * 8 + c], down)
                best = jnp.maximum(best, kept)
            row_best[unit, first_row:first_row + 64] = best

    def compare(t, j):
        a, b = todo[0], todo[1]
        for k in range(1, 4):
            a = jnp.where(j == k, todo[2 * k], a)
            b = jnp.where(j == k, todo[2 * k + 1], b)
        strip(a, t, b, t + 1)
        if t:
            strip(b, t, a, t)

    def finish_rows(t):
        pl.when(h == 1)(lambda: strip(0, t, 0, t + 1, diagonal=True))
        for s in range(SLOTS):
            @pl.when(need[s] == 1)
            def _():
                for core in range(2):
                    unit = s * 8 + 2 * t + core
                    row_line[unit:unit + 1, :] = jnp.max(row_best[unit].T, axis=0, keepdims=True)

    def wait_shared(m):
        for s in range(SLOTS):
            @pl.when(need[s] == 1)
            def _():
                for half in range(2):
                    shared(s, 2 * m + half).wait_recv()

    def own_piece_ready(t):
        send_own(t)
        give(0, t)

    def pass_on(k):
        receive(1, k - 1)
        send_held(k - 1)
        give_held(1, k - 1)

    def take(t):
        receive(2, t)
        give_held(2, t)

    pass_on(1)
    swap(1, 0).wait_recv()
    own_piece_ready(2)
    pass_on(2)
    swap(1, 1).wait_recv()
    own_piece_ready(3)
    swap(2, 0).wait_recv()
    own_piece_ready(4)
    pass_on(3)
    for half in range(2):
        relay_in(half).wait_recv()
        relay_out(half).start()
    swap(2, 1).wait_recv()
    own_piece_ready(5)
    take(0)
    pass_on(4)
    take(1)
    pass_on(5)
    for half in range(2):
        relay_out(half).wait_recv()
        own_piece_ready(6 + half)
    take(2)
    wait_shared(0)

    @pl.loop(6, 8)
    def _(k):
        pass_on(k)
        take(k - 3)
        first = 2 * (k - 6)

        @pl.loop(first, jnp.minimum(first + 2, pair_count))
        def _(j):
            compare(0, j)

    pass_on(8)
    take(5)
    finish_rows(0)
    for m in (1, 2, 3):
        wait_shared(m)

        @pl.loop(0, pair_count)
        def _(j):
            compare(m, j)
        finish_rows(m)
        if m < 3:
            take(5 + m)

    for s in range(SLOTS):
        for t in range(4):
            z_of = (z + REL[t]) % 4
            for core in range(2):
                j = s * 8 + 2 * t + core
                both = jnp.maximum(row_line[j:j + 1, :], jnp.max(col_best[j], axis=0, keepdims=True))
                part[s * 2 + z_of // 2, pl.ds(2 * (z_of % 2) + core, 1), :] = both
        for half in range(2):
            copy = remote(part.at[s * 2 + half], parts_got.at[place[s] * 2 + h], r_send.at[s * 2 + half],
                          r_recv.at[place[s] * 2 + h], (owner_grp, held[s] * 2 + half))
            if s == 0:
                keep_it = jnp.logical_and(mine, zh == half)
                pl.when(jnp.logical_not(keep_it))(copy.start)

                @pl.when(keep_it)
                def _():
                    parts_got[h] = part[half]
            else:
                copy.start()

    best = None
    for k in range(2 * SLOTS):
        got = remote(parts_got.at[k], parts_got.at[k], r_send.at[k], r_recv.at[k], sibling)
        if k < 2:
            pl.when(jnp.logical_not(jnp.logical_and(mine, h == k)))(got.wait_recv)
        else:
            got.wait_recv()
        best = parts_got[k] if best is None else jnp.maximum(best, parts_got[k])
    out[...] = best

    ids_copy.wait_send()
    for half in range(2):
        for copy in (swap(1, half), swap(2, half), relay_in(half), relay_out(half)):
            copy.wait_send()
    for d in range(4):
        for t in range(STEPS):
            forward(d, t).wait_send()
    for s in range(SLOTS):
        for t in range(8):
            pl.when(sibling_need[s] == 1)(lambda s=s, t=t: share(s, t).wait_send())
        for half in range(2):
            copy = remote(part.at[s * 2 + half], parts_got.at[place[s] * 2 + h], r_send.at[s * 2 + half],
                          r_recv.at[place[s] * 2 + h], (owner_grp, held[s] * 2 + half))
            if s == 0:
                pl.when(jnp.logical_not(jnp.logical_and(mine, zh == half)))(copy.wait_send)
            else:
                copy.wait_send()


def on_device(embeddings, cluster_ids):
    emb = embeddings.reshape(4, 128, D)
    ids = cluster_ids.reshape(128, 128)
    dma = pltpu.SemaphoreType.DMA
    best = pl.pallas_call(
        kernel,
        out_shape=jax.ShapeDtypeStruct((4, 128), jnp.float32),
        in_specs=[pl.BlockSpec(memory_space=pl.ANY), pl.BlockSpec(memory_space=pltpu.VMEM)],
        out_specs=pl.BlockSpec(memory_space=pltpu.VMEM),
        scratch_shapes=[
            pltpu.VMEM((SLOTS, 1024, D), jnp.bfloat16),
            pltpu.VMEM((3, 128, D), jnp.bfloat16),
            pltpu.VMEM((4, 128, D), jnp.float32),
            pltpu.VMEM((128, 128), jnp.int32),
            pltpu.VMEM((SLOTS * 8, 128, 128), jnp.float32),
            pltpu.VMEM((128, 128), jnp.float32),
            pltpu.VMEM((SLOTS * 8, 128, 128), jnp.float32),
            pltpu.VMEM((SLOTS * 8, 8, 128), jnp.float32),
            pltpu.VMEM((SLOTS * 8, 128), jnp.float32),
            pltpu.VMEM((2 * SLOTS, 4, 128), jnp.float32),
            pltpu.VMEM((2 * SLOTS, 4, 128), jnp.float32),
            pltpu.VMEM((128, D), jnp.bfloat16),
            dma((4,)), dma, dma, dma((3, 2)), dma((3, 2)), dma((2, 2)), dma((2,)), dma((4, STEPS)), dma((4, STEPS)),
            dma((SLOTS, 8)), dma((SLOTS, 8)), dma((2 * SLOTS,)), dma((2 * SLOTS,)),
        ],
        compiler_params=pltpu.CompilerParams(
            collective_id=0, has_side_effects=True, vmem_limit_bytes=60 * 1024 * 1024),
        cost_estimate=pl.CostEstimate(flops=7 * 10**9, bytes_accessed=2 * 10**6, transcendentals=0),
        name="best_match",
    )(emb, ids)
    return best.reshape(1, 512)


def solution(mesh):
    placed = (P(None, "grp", "blk", None, None), P("grp", None))
    return jax.shard_map(
        on_device, mesh=mesh, in_specs=placed, out_specs=P("grp", "blk"), check_vma=False
    )
```

```python
import functools

import jax
import jax.numpy as jnp
from jax import lax
from jax.experimental import pallas as pl
from jax.experimental.pallas import tpu as pltpu
from jax.sharding import PartitionSpec as P

MESH = pl.DeviceIdType.MESH
D = 768
SLOTS = 5
PIECE = 64
STEPS = 8

SRC = [[0, 3, 0, 0], [3, 0, 0, 0], [0, 0, 4, 0], [0, 0, 4, 0], [0, 4, 1, 0], [4, 0, 2, 0], [0, 3, 0, 0], [3, 0, 0, 0],
       [3, 0, 0, 3], [0, 3, 0, 3], [2, 4, 0, 0], [4, 1, 0, 0], [2, 0, 4, 0], [0, 1, 4, 0], [4, 0, 0, 3], [0, 4, 0, 3]]
DEP = [[1, 1, 1, 2], [1, 1, 1, 2], [1, 2, 1, 1], [2, 1, 1, 1], [1, 2, 2, 1], [2, 1, 2, 1], [1, 2, 1, 2], [2, 1, 1, 2],
       [2, 2, 1, 2], [2, 2, 1, 2], [2, 1, 2, 1], [1, 2, 2, 1], [2, 1, 1, 1], [1, 2, 1, 1], [2, 1, 1, 1], [1, 2, 1, 1]]
BLK = [[1, 3, 4, 8], [2, 0, 5, 9], [3, 5, 6, 14], [4, 2, 7, 15], [5, 11, 12, 0], [10, 4, 13, 1], [7, 1, 10, 14],
       [0, 6, 11, 15], [13, 7, 12, 5], [6, 12, 13, 4], [8, 9, 2, 6], [8, 9, 3, 7], [14, 15, 0, 8], [14, 15, 1, 9],
       [11, 13, 2, 10], [12, 10, 3, 11]]
IDX = [[1, 1, 1, 1], [1, 1, 1, 1], [2, 2, 1, 1], [2, 2, 1, 1], [3, 1, 1, 2], [1, 3, 1, 2], [2, 3, 2, 2], [3, 2, 2, 2],
       [2, 3, 2, 4], [3, 3, 3, 4], [2, 2, 3, 4], [3, 3, 3, 4], [3, 3, 4, 4], [4, 4, 4, 4], [3, 4, 4, 3], [4, 4, 4, 4]]
HOLD = [[0, 1, 4, 7, 12], [1, 0, 5, 6, 13], [2, 1, 3, 10, 14], [3, 0, 2, 11, 15], [4, 0, 3, 5, 9], [5, 1, 2, 4, 8],
        [6, 2, 7, 9, 10], [7, 3, 6, 8, 11], [8, 0, 10, 11, 12], [9, 1, 10, 11, 13], [10, 5, 6, 14, 15], [11, 4, 7, 14, 15],
        [12, 4, 8, 9, 15], [13, 5, 8, 9, 14], [14, 2, 6, 12, 13], [15, 3, 7, 12, 13]]
PAIRS = [[[(1, 3), (1, 4), (3, 4)], [(0, 1), (0, 2), (1, 2)]], [[(2, 1), (2, 4), (1, 4)], [(0, 1), (0, 3), (3, 4)]],
         [[(1, 3), (3, 4), (2, 3), (2, 4)], [(0, 1), (0, 2), (1, 2)]],
         [[(2, 3), (2, 1), (1, 3)], [(0, 3), (3, 4), (0, 1)]], [[(4, 0), (4, 1), (0, 2), (1, 2)], [(0, 3), (1, 3)]],
         [[(2, 0), (4, 1), (2, 1)], [(0, 1), (0, 3), (1, 3)]], [[(1, 3), (1, 4), (3, 4)], [(0, 3), (2, 0), (2, 1)]],
         [[(2, 3), (2, 4), (3, 4)], [(2, 0), (1, 2), (1, 0)]],
         [[(2, 3), (2, 1), (0, 1), (3, 1)], [(4, 2), (4, 0), (2, 0)]],
         [[(4, 1), (4, 0), (4, 3), (1, 3)], [(1, 0), (1, 2), (0, 2)]],
         [[(3, 4), (3, 1), (4, 1)], [(2, 0), (1, 2), (1, 0)]], [[(1, 0), (3, 1), (3, 2)], [(4, 0), (4, 2), (2, 0)]],
         [[(3, 4), (4, 1), (0, 1)], [(4, 0), (4, 2), (0, 2)]], [[(3, 4), (4, 1), (1, 2)], [(4, 0), (4, 2), (0, 2)]],
         [[(3, 4), (3, 1), (4, 1)], [(2, 0), (1, 2), (1, 0)]], [[(3, 4), (3, 1), (4, 1)], [(3, 2), (2, 1), (2, 0)]]]
NEED = [[[1, 3, 4], [0, 1, 2]], [[1, 2, 4], [0, 1, 3, 4]], [[1, 2, 3, 4], [0, 1, 2]], [[1, 2, 3], [0, 1, 3, 4]],
        [[0, 1, 2, 4], [0, 1, 3]], [[0, 1, 2, 4], [0, 1, 3]], [[1, 3, 4], [0, 1, 2, 3]], [[2, 3, 4], [0, 1, 2]],
        [[0, 1, 2, 3], [0, 2, 4]], [[0, 1, 3, 4], [0, 1, 2]], [[1, 3, 4], [0, 1, 2]], [[0, 1, 2, 3], [0, 2, 4]],
        [[0, 1, 3, 4], [0, 2, 4]], [[1, 2, 3, 4], [0, 2, 4]], [[1, 3, 4], [0, 1, 2]], [[1, 3, 4], [0, 1, 2, 3]]]

REL = (0, 3, 1, 2)


def word(digits, base):
    total = 0
    for digit in reversed(digits):
        total = total * base + digit
    return total


def look_up(index, words):
    got = jnp.int32(words[0])
    for k in range(1, len(words)):
        got = jnp.where(index == k, jnp.int32(words[k]), got)
    return got


def digits_of(value, base, count):
    out = []
    for _ in range(count):
        out.append(value % base)
        value = value // base
    return out


def kernel(emb, ids_in, out, x, units, stage, ids_got, ids_rows, ids_cols, row_best, col_best, row_line, part, parts_got,
           relay,
           load_sem, id_send, id_recv, z_send, z_recv, relay_send, relay_recv, f_send, f_recv, c_send, c_recv, r_send, r_recv):
    grp, blk = lax.axis_index("grp"), lax.axis_index("blk")
    h, zl = grp % 2, grp // 2
    p, zh = blk // 2, blk % 2
    z = zh * 2 + zl
    px, py = p % 4, p // 4

    def device(z_of, core, chip):
        return ((z_of % 2) * 2 + core, chip * 2 + z_of // 2)

    def group_of(z_of):
        return (z_of % 2) * 2 + z_of // 2

    near = [py * 4 + (px + 1) % 4, py * 4 + (px + 3) % 4, ((py + 1) % 4) * 4 + px, ((py + 3) % 4) * 4 + px]
    first = look_up(p, [word(SRC[c], 8) + 4096 * word(DEP[c], 4) for c in range(16)])
    src = digits_of(first, 8, 4)
    dep = digits_of(first // 4096, 4, 4)
    held = [p] + digits_of(look_up(p, [word(BLK[c], 16) for c in range(16)]), 16, 4)
    third = look_up(p, [word(IDX[c], 8) + 4096 * word(HOLD[c][1:], 16) for c in range(16)])
    place = [jnp.int32(0)] + digits_of(third, 8, 4)
    holders = [p] + digits_of(third // 4096, 16, 4)
    lists = []
    for c in range(16):
        for core in range(2):
            flat = [slot for pair in PAIRS[c][core] for slot in pair]
            lists.append(len(PAIRS[c][core]) + 8 * word(flat + [0] * (8 - len(flat)), 8))
    todo = look_up(p * 2 + h, lists)
    pair_count = todo % 8
    todo = digits_of(todo // 8, 8, 8)

    needs = [[sum(1 << slot for slot in NEED[c][core]) for core in range(2)] for c in range(16)]
    need = digits_of(look_up(p * 2 + h, [needs[c][core] for c in range(16) for core in range(2)]), 2, SLOTS)
    sibling_need = digits_of(look_up(p * 2 + h, [needs[c][1 - core] for c in range(16) for core in range(2)]), 2, SLOTS)

    sibling = device(z, 1 - h, p)
    owner_grp = zl * 2 + zh
    mine = h == zh

    loads = []
    for k, rel in enumerate((0, 1, 3, 2)):
        loads.append(pltpu.make_async_copy(emb.at[group_of((z + rel) % 4)], stage.at[k], load_sem.at[k]))
        loads[-1].start()

    barrier = pltpu.get_barrier_semaphore()
    for rel in (1, 3):
        pl.semaphore_signal(barrier, inc=1, device_id=device((z + rel) % 4, h, p), device_id_type=MESH)
    for d in range(4):
        pl.semaphore_signal(barrier, inc=1, device_id=device(z, h, near[d]), device_id_type=MESH)
    pl.semaphore_signal(barrier, inc=1, device_id=sibling, device_id_type=MESH)
    from_z = 2 * h + zl
    for k in range(SLOTS):
        for core in range(2):
            def tell():
                pl.semaphore_signal(barrier, inc=1, device_id=device(from_z, core, holders[k]), device_id_type=MESH)
            if k == 0:
                pl.when(jnp.logical_not(jnp.logical_and(mine, h == core)))(tell)
            else:
                tell()

    def normalise(k):
        loads[k].wait()
        v = stage[k]
        total = jnp.sum(v * v, axis=-1, keepdims=True)
        return (v / jnp.sqrt(total + 1e-06)).astype(jnp.bfloat16)

    own_rows = pl.multiple_of(h * 128, 128)
    x[0, pl.ds(own_rows, 128), :] = normalise(0)
    pl.semaphore_wait(barrier, jnp.where(mine, 16, 17))

    def remote(src_ref, dst_ref, send_sem, recv_sem, to):
        return pltpu.make_async_remote_copy(
            src_ref=src_ref, dst_ref=dst_ref, send_sem=send_sem, recv_sem=recv_sem, device_id=to, device_id_type=MESH)

    def part_rows(t):
        return pl.ds(pl.multiple_of((t // 2) * 256 + h * 128 + (t % 2) * PIECE, PIECE), PIECE)

    def forward(d, t):
        rows = part_rows(t)
        return remote(x.at[src[d], rows, :], x.at[1 + (d ^ 1), rows, :], f_send.at[d, t], f_recv.at[d ^ 1, t],
                      device(z, h, near[d]))

    def arrival(s, t):
        rows = part_rows(t)
        return remote(x.at[s, rows, :], x.at[s, rows, :], f_send.at[s - 1, t], f_recv.at[s - 1, t],
                      device(z, h, near[s - 1]))

    def swap(k, half):
        rows = pl.ds(pl.multiple_of(k * 256 + h * 128 + half * 64, 64), 64)
        return remote(units.at[k - 1, pl.ds(half * 64, 64), :], x.at[0, rows, :], z_send.at[k - 1, half],
                      z_recv.at[k - 1, half], device((z + (1, 3, 2)[k - 1]) % 4, h, p))

    between = device((z + jnp.where(h == 0, 1, 3)) % 4, h, p)

    def relay_in(half):
        rows = pl.ds(half * 64, 64)
        return remote(units.at[2, rows, :], relay.at[rows, :], relay_send.at[0, half], relay_recv.at[half], between)

    def relay_out(half):
        rows = pl.ds(pl.multiple_of(3 * 256 + h * 128 + half * 64, 64), 64)
        return remote(relay.at[pl.ds(half * 64, 64), :], x.at[0, rows, :], relay_send.at[1, half], z_recv.at[2, half],
                      between)

    def share_rows(t, core):
        return pl.ds(pl.multiple_of((t // 2) * 256 + core * 128 + (t % 2) * 64, 64), 64)

    def share(s, t):
        rows = share_rows(t, h)
        return remote(x.at[s, rows, :], x.at[s, rows, :], c_send.at[s, t], c_recv.at[s, t], sibling)

    def shared(s, t):
        rows = share_rows(t, 1 - h)
        return remote(x.at[s, rows, :], x.at[s, rows, :], c_send.at[s, t], c_recv.at[s, t], sibling)

    def give(s, t):
        pl.when(sibling_need[s] == 1)(lambda: share(s, t).start())

    def send_own(t):
        for d in range(4):
            pl.when(src[d] == 0)(lambda d=d: forward(d, t).start())

    def send_held(t):
        for d in range(4):
            pl.when(src[d] != 0)(lambda d=d: forward(d, t).start())

    def receive(links, t):
        for s in range(1, SLOTS):
            pl.when(dep[s - 1] == links)(lambda s=s: arrival(s, t).wait_recv())

    def give_held(links, t):
        for s in range(1, SLOTS):
            pl.when(dep[s - 1] == links)(lambda s=s: give(s, t))

    for t in range(2):
        send_own(t)
    units[0] = normalise(1)
    for half in range(2):
        swap(1, half).start()
    units[1] = normalise(2)
    for half in range(2):
        swap(2, half).start()
    units[2] = normalise(3)
    for half in range(2):
        relay_in(half).start()
    ids_copy = remote(ids_in, ids_got, id_send, id_recv, sibling)
    ids_copy.start()
    give(0, 0)
    give(0, 1)
    row_best[...] = jnp.full_like(row_best, -1.0)
    col_best[...] = jnp.full_like(col_best, -1.0)
    row_line[...] = jnp.full_like(row_line, -1.0)

    ids_copy.wait_recv()
    ids_cols[...] = jnp.zeros_like(ids_cols)
    for s in range(SLOTS):
        for t in range(4):
            for core in range(2):
                unit = held[s] * 8 + 2 * ((z + REL[t]) % 4) + core
                got = jnp.where(mine, ids_in[pl.ds(unit, 1), :], ids_got[pl.ds(unit, 1), :])
                ids_cols[pl.ds(s * 8 + 2 * t + core, 1), :] = got.astype(jnp.float32)
    turned = ids_cols[...].T
    for j in range(SLOTS * 8):
        ids_rows[j] = jnp.broadcast_to(turned[:, j:j + 1], (128, 128))

    def strip(a, t, b, count, diagonal=False):
        sim = lax.dot_general(x[b, 0:256 * count, :], x[a, 256 * t:256 * t + 256, :], (((1,), (1,)), ((), ())),
                              preferred_element_type=jnp.float32)
        col_ids = [ids_cols[pl.ds(a * 8 + 2 * t + c, 1), :] for c in range(2)]
        downs = [col_best[a * 8 + 2 * t + c] for c in range(2)]
        for r in range(4 * count):
            unit, first_row = b * 8 + r // 2, 64 * (r % 2)
            row_ids = ids_rows[unit, first_row:first_row + 64]
            best = row_best[unit, first_row:first_row + 64]
            for c in range(2):
                keep = row_ids == col_ids[c]
                if diagonal and r // 4 == t:
                    row = lax.broadcasted_iota(jnp.int32, (64, 128), 0) + 64 * (r % 4)
                    col = lax.broadcasted_iota(jnp.int32, (64, 128), 1) + 128 * c
                    keep = jnp.logical_and(keep, row != col)
                kept = jnp.where(keep, sim[64 * r:64 * r + 64, 128 * c:128 * c + 128], jnp.float32(-1.0))
                downs[c] = jnp.maximum(downs[c], jnp.max(kept.reshape(8, 8, 128), axis=0))
                best = jnp.maximum(best, kept)
            row_best[unit, first_row:first_row + 64] = best
        for c in range(2):
            col_best[a * 8 + 2 * t + c] = downs[c]

    def compare(t, j):
        a, b = todo[0], todo[1]
        for k in range(1, 4):
            a = jnp.where(j == k, todo[2 * k], a)
            b = jnp.where(j == k, todo[2 * k + 1], b)
        strip(a, t, b, t + 1)
        if t:
            strip(b, t, a, t)

    def own_pair(t):
        pl.when(h == 1)(lambda: strip(0, t, 0, t + 1, diagonal=True))

    def wait_shared(m):
        for s in range(SLOTS):
            @pl.when(need[s] == 1)
            def _():
                for half in range(2):
                    shared(s, 2 * m + half).wait_recv()

    def own_piece_ready(t):
        send_own(t)
        give(0, t)

    def pass_on(k):
        receive(1, k - 1)
        send_held(k - 1)
        give_held(1, k - 1)

    def take(t):
        receive(2, t)
        give_held(2, t)

    pass_on(1)
    swap(1, 0).wait_recv()
    own_piece_ready(2)
    pass_on(2)
    swap(1, 1).wait_recv()
    own_piece_ready(3)
    swap(2, 0).wait_recv()
    own_piece_ready(4)
    pass_on(3)
    for half in range(2):
        relay_in(half).wait_recv()
        relay_out(half).start()
    swap(2, 1).wait_recv()
    own_piece_ready(5)
    take(0)
    pass_on(4)
    take(1)
    for m in range(2):
        @pl.loop(5 + 2 * m, 7 + 2 * m)
        def _(k):
            pass_on(k)

            @pl.when(k == 5)
            def _():
                for half in range(2):
                    relay_out(half).wait_recv()
                    own_piece_ready(6 + half)
            first = 2 * (k - 5 - 2 * m)
            pl.when(first == 0)(lambda: wait_shared(m))

            @pl.loop(first, jnp.minimum(first + 2, pair_count))
            def _(j):
                compare(m, j)
            take(k - 3)
        own_pair(m)
    for m in (2, 3):
        wait_shared(m)

        @pl.loop(0, pair_count)
        def _(j):
            compare(m, j)
        own_pair(m)
        if m == 2:
            take(6)
            take(7)

    for s in range(SLOTS):
        @pl.when(need[s] == 1)
        def _():
            for unit in range(s * 8, s * 8 + 8):
                row_line[unit:unit + 1, :] = jnp.max(row_best[unit].T, axis=0, keepdims=True)

    for s in range(SLOTS):
        for t in range(4):
            z_of = (z + REL[t]) % 4
            for core in range(2):
                j = s * 8 + 2 * t + core
                both = jnp.maximum(row_line[j:j + 1, :], jnp.max(col_best[j], axis=0, keepdims=True))
                part[s * 2 + z_of // 2, pl.ds(2 * (z_of % 2) + core, 1), :] = both
        for half in range(2):
            copy = remote(part.at[s * 2 + half], parts_got.at[place[s] * 2 + h], r_send.at[s * 2 + half],
                          r_recv.at[place[s] * 2 + h], (owner_grp, held[s] * 2 + half))
            if s == 0:
                keep_it = jnp.logical_and(mine, zh == half)
                pl.when(jnp.logical_not(keep_it))(copy.start)

                @pl.when(keep_it)
                def _():
                    parts_got[h] = part[half]
            else:
                copy.start()

    best = None
    for k in range(2 * SLOTS):
        got = remote(parts_got.at[k], parts_got.at[k], r_send.at[k], r_recv.at[k], sibling)
        if k < 2:
            pl.when(jnp.logical_not(jnp.logical_and(mine, h == k)))(got.wait_recv)
        else:
            got.wait_recv()
        best = parts_got[k] if best is None else jnp.maximum(best, parts_got[k])
    out[...] = best

    ids_copy.wait_send()
    for half in range(2):
        for copy in (swap(1, half), swap(2, half), relay_in(half), relay_out(half)):
            copy.wait_send()
    for d in range(4):
        for t in range(STEPS):
            forward(d, t).wait_send()
    for s in range(SLOTS):
        for t in range(8):
            pl.when(sibling_need[s] == 1)(lambda s=s, t=t: share(s, t).wait_send())
        for half in range(2):
            copy = remote(part.at[s * 2 + half], parts_got.at[place[s] * 2 + h], r_send.at[s * 2 + half],
                          r_recv.at[place[s] * 2 + h], (owner_grp, held[s] * 2 + half))
            if s == 0:
                pl.when(jnp.logical_not(jnp.logical_and(mine, zh == half)))(copy.wait_send)
            else:
                copy.wait_send()


def on_device(embeddings, cluster_ids):
    emb = embeddings.reshape(4, 128, D)
    ids = cluster_ids.reshape(128, 128)
    dma = pltpu.SemaphoreType.DMA
    best = pl.pallas_call(
        kernel,
        out_shape=jax.ShapeDtypeStruct((4, 128), jnp.float32),
        in_specs=[pl.BlockSpec(memory_space=pl.ANY), pl.BlockSpec(memory_space=pltpu.VMEM)],
        out_specs=pl.BlockSpec(memory_space=pltpu.VMEM),
        scratch_shapes=[
            pltpu.VMEM((SLOTS, 1024, D), jnp.bfloat16),
            pltpu.VMEM((3, 128, D), jnp.bfloat16),
            pltpu.VMEM((4, 128, D), jnp.float32),
            pltpu.VMEM((128, 128), jnp.int32),
            pltpu.VMEM((SLOTS * 8, 128, 128), jnp.float32),
            pltpu.VMEM((128, 128), jnp.float32),
            pltpu.VMEM((SLOTS * 8, 128, 128), jnp.float32),
            pltpu.VMEM((SLOTS * 8, 8, 128), jnp.float32),
            pltpu.VMEM((SLOTS * 8, 128), jnp.float32),
            pltpu.VMEM((2 * SLOTS, 4, 128), jnp.float32),
            pltpu.VMEM((2 * SLOTS, 4, 128), jnp.float32),
            pltpu.VMEM((128, D), jnp.bfloat16),
            dma((4,)), dma, dma, dma((3, 2)), dma((3, 2)), dma((2, 2)), dma((2,)), dma((4, STEPS)), dma((4, STEPS)),
            dma((SLOTS, 8)), dma((SLOTS, 8)), dma((2 * SLOTS,)), dma((2 * SLOTS,)),
        ],
        compiler_params=pltpu.CompilerParams(
            collective_id=0, has_side_effects=True, vmem_limit_bytes=60 * 1024 * 1024),
        cost_estimate=pl.CostEstimate(flops=7 * 10**9, bytes_accessed=2 * 10**6, transcendentals=0),
        name="best_match",
    )(emb, ids)
    return best.reshape(1, 512)


def solution(mesh):
    placed = (P(None, "grp", "blk", None, None), P("grp", None))
    return jax.shard_map(
        on_device, mesh=mesh, in_specs=placed, out_specs=P("grp", "blk"), check_vma=False
    )
```

```python
import functools

import jax
import jax.numpy as jnp
from jax import lax
from jax.experimental import pallas as pl
from jax.experimental.pallas import tpu as pltpu
from jax.sharding import PartitionSpec as P

MESH = pl.DeviceIdType.MESH
D = 768
SLOTS = 5
PIECE = 32
STEPS = 16

SRC = [[0, 3, 0, 0], [3, 0, 0, 0], [0, 0, 4, 0], [0, 0, 4, 0], [0, 4, 1, 0], [4, 0, 2, 0], [0, 3, 0, 0], [3, 0, 0, 0],
       [3, 0, 0, 3], [0, 3, 0, 3], [2, 4, 0, 0], [4, 1, 0, 0], [2, 0, 4, 0], [0, 1, 4, 0], [4, 0, 0, 3], [0, 4, 0, 3]]
DEP = [[1, 1, 1, 2], [1, 1, 1, 2], [1, 2, 1, 1], [2, 1, 1, 1], [1, 2, 2, 1], [2, 1, 2, 1], [1, 2, 1, 2], [2, 1, 1, 2],
       [2, 2, 1, 2], [2, 2, 1, 2], [2, 1, 2, 1], [1, 2, 2, 1], [2, 1, 1, 1], [1, 2, 1, 1], [2, 1, 1, 1], [1, 2, 1, 1]]
BLK = [[1, 3, 4, 8], [2, 0, 5, 9], [3, 5, 6, 14], [4, 2, 7, 15], [5, 11, 12, 0], [10, 4, 13, 1], [7, 1, 10, 14],
       [0, 6, 11, 15], [13, 7, 12, 5], [6, 12, 13, 4], [8, 9, 2, 6], [8, 9, 3, 7], [14, 15, 0, 8], [14, 15, 1, 9],
       [11, 13, 2, 10], [12, 10, 3, 11]]
IDX = [[1, 1, 1, 1], [1, 1, 1, 1], [2, 2, 1, 1], [2, 2, 1, 1], [3, 1, 1, 2], [1, 3, 1, 2], [2, 3, 2, 2], [3, 2, 2, 2],
       [2, 3, 2, 4], [3, 3, 3, 4], [2, 2, 3, 4], [3, 3, 3, 4], [3, 3, 4, 4], [4, 4, 4, 4], [3, 4, 4, 3], [4, 4, 4, 4]]
HOLD = [[0, 1, 4, 7, 12], [1, 0, 5, 6, 13], [2, 1, 3, 10, 14], [3, 0, 2, 11, 15], [4, 0, 3, 5, 9], [5, 1, 2, 4, 8],
        [6, 2, 7, 9, 10], [7, 3, 6, 8, 11], [8, 0, 10, 11, 12], [9, 1, 10, 11, 13], [10, 5, 6, 14, 15], [11, 4, 7, 14, 15],
        [12, 4, 8, 9, 15], [13, 5, 8, 9, 14], [14, 2, 6, 12, 13], [15, 3, 7, 12, 13]]
PAIRS = [[[(1, 3), (1, 4), (3, 4)], [(0, 1), (0, 2), (1, 2)]], [[(2, 1), (2, 4), (1, 4)], [(0, 1), (0, 3), (3, 4)]],
         [[(1, 3), (3, 4), (2, 3), (2, 4)], [(0, 1), (0, 2), (1, 2)]],
         [[(2, 3), (2, 1), (1, 3)], [(0, 3), (3, 4), (0, 1)]], [[(4, 0), (4, 1), (0, 2), (1, 2)], [(0, 3), (1, 3)]],
         [[(2, 0), (4, 1), (2, 1)], [(0, 1), (0, 3), (1, 3)]], [[(1, 3), (1, 4), (3, 4)], [(0, 3), (2, 0), (2, 1)]],
         [[(2, 3), (2, 4), (3, 4)], [(2, 0), (1, 2), (1, 0)]],
         [[(2, 3), (2, 1), (0, 1), (3, 1)], [(4, 2), (4, 0), (2, 0)]],
         [[(4, 1), (4, 0), (4, 3), (1, 3)], [(1, 0), (1, 2), (0, 2)]],
         [[(3, 4), (3, 1), (4, 1)], [(2, 0), (1, 2), (1, 0)]], [[(1, 0), (3, 1), (3, 2)], [(4, 0), (4, 2), (2, 0)]],
         [[(3, 4), (4, 1), (0, 1)], [(4, 0), (4, 2), (0, 2)]], [[(3, 4), (4, 1), (1, 2)], [(4, 0), (4, 2), (0, 2)]],
         [[(3, 4), (3, 1), (4, 1)], [(2, 0), (1, 2), (1, 0)]], [[(3, 4), (3, 1), (4, 1)], [(3, 2), (2, 1), (2, 0)]]]
NEED = [[[1, 3, 4], [0, 1, 2]], [[1, 2, 4], [0, 1, 3, 4]], [[1, 2, 3, 4], [0, 1, 2]], [[1, 2, 3], [0, 1, 3, 4]],
        [[0, 1, 2, 4], [0, 1, 3]], [[0, 1, 2, 4], [0, 1, 3]], [[1, 3, 4], [0, 1, 2, 3]], [[2, 3, 4], [0, 1, 2]],
        [[0, 1, 2, 3], [0, 2, 4]], [[0, 1, 3, 4], [0, 1, 2]], [[1, 3, 4], [0, 1, 2]], [[0, 1, 2, 3], [0, 2, 4]],
        [[0, 1, 3, 4], [0, 2, 4]], [[1, 2, 3, 4], [0, 2, 4]], [[1, 3, 4], [0, 1, 2]], [[1, 3, 4], [0, 1, 2, 3]]]

REL = (0, 3, 1, 2)


def word(digits, base):
    total = 0
    for digit in reversed(digits):
        total = total * base + digit
    return total


def look_up(index, words):
    got = jnp.int32(words[0])
    for k in range(1, len(words)):
        got = jnp.where(index == k, jnp.int32(words[k]), got)
    return got


def digits_of(value, base, count):
    out = []
    for _ in range(count):
        out.append(value % base)
        value = value // base
    return out


def kernel(emb, ids_in, out, x, units, stage, ids_got, ids_rows, ids_cols, row_best, col_best, row_line, part, parts_got,
           relay,
           load_sem, id_send, id_recv, z_send, z_recv, relay_send, relay_recv, f_send, f_recv, c_send, c_recv, r_send, r_recv):
    grp, blk = lax.axis_index("grp"), lax.axis_index("blk")
    h, zl = grp % 2, grp // 2
    p, zh = blk // 2, blk % 2
    z = zh * 2 + zl
    px, py = p % 4, p // 4

    def device(z_of, core, chip):
        return ((z_of % 2) * 2 + core, chip * 2 + z_of // 2)

    def group_of(z_of):
        return (z_of % 2) * 2 + z_of // 2

    near = [py * 4 + (px + 1) % 4, py * 4 + (px + 3) % 4, ((py + 1) % 4) * 4 + px, ((py + 3) % 4) * 4 + px]
    first = look_up(p, [word(SRC[c], 8) + 4096 * word(DEP[c], 4) for c in range(16)])
    src = digits_of(first, 8, 4)
    dep = digits_of(first // 4096, 4, 4)
    held = [p] + digits_of(look_up(p, [word(BLK[c], 16) for c in range(16)]), 16, 4)
    third = look_up(p, [word(IDX[c], 8) + 4096 * word(HOLD[c][1:], 16) for c in range(16)])
    place = [jnp.int32(0)] + digits_of(third, 8, 4)
    holders = [p] + digits_of(third // 4096, 16, 4)
    lists = []
    for c in range(16):
        for core in range(2):
            flat = [slot for pair in PAIRS[c][core] for slot in pair]
            lists.append(len(PAIRS[c][core]) + 8 * word(flat + [0] * (8 - len(flat)), 8))
    todo = look_up(p * 2 + h, lists)
    pair_count = todo % 8
    todo = digits_of(todo // 8, 8, 8)

    needs = [[sum(1 << slot for slot in NEED[c][core]) for core in range(2)] for c in range(16)]
    need = digits_of(look_up(p * 2 + h, [needs[c][core] for c in range(16) for core in range(2)]), 2, SLOTS)
    sibling_need = digits_of(look_up(p * 2 + h, [needs[c][1 - core] for c in range(16) for core in range(2)]), 2, SLOTS)

    sibling = device(z, 1 - h, p)
    owner_grp = zl * 2 + zh
    mine = h == zh

    loads = []
    for k, rel in enumerate((0, 1, 3, 2)):
        loads.append(pltpu.make_async_copy(emb.at[group_of((z + rel) % 4)], stage.at[k], load_sem.at[k]))
        loads[-1].start()

    barrier = pltpu.get_barrier_semaphore()
    for rel in (1, 3):
        pl.semaphore_signal(barrier, inc=1, device_id=device((z + rel) % 4, h, p), device_id_type=MESH)
    for d in range(4):
        pl.semaphore_signal(barrier, inc=1, device_id=device(z, h, near[d]), device_id_type=MESH)
    pl.semaphore_signal(barrier, inc=1, device_id=sibling, device_id_type=MESH)
    from_z = 2 * h + zl
    for k in range(SLOTS):
        for core in range(2):
            def tell():
                pl.semaphore_signal(barrier, inc=1, device_id=device(from_z, core, holders[k]), device_id_type=MESH)
            if k == 0:
                pl.when(jnp.logical_not(jnp.logical_and(mine, h == core)))(tell)
            else:
                tell()

    def normalise(k):
        loads[k].wait()
        v = stage[k]
        total = jnp.sum(v * v, axis=-1, keepdims=True)
        return (v / jnp.sqrt(total + 1e-06)).astype(jnp.bfloat16)

    own_rows = pl.multiple_of(h * 128, 128)
    x[0, pl.ds(own_rows, 128), :] = normalise(0)
    pl.semaphore_wait(barrier, jnp.where(mine, 16, 17))

    def remote(src_ref, dst_ref, send_sem, recv_sem, to):
        return pltpu.make_async_remote_copy(
            src_ref=src_ref, dst_ref=dst_ref, send_sem=send_sem, recv_sem=recv_sem, device_id=to, device_id_type=MESH)

    def part_rows(t):
        return pl.ds(pl.multiple_of((t // 4) * 256 + h * 128 + (t % 4) * PIECE, PIECE), PIECE)

    def forward(d, t):
        rows = part_rows(t)
        return remote(x.at[src[d], rows, :], x.at[1 + (d ^ 1), rows, :], f_send.at[d, t], f_recv.at[d ^ 1, t],
                      device(z, h, near[d]))

    def arrival(s, t):
        rows = part_rows(t)
        return remote(x.at[s, rows, :], x.at[s, rows, :], f_send.at[s - 1, t], f_recv.at[s - 1, t],
                      device(z, h, near[s - 1]))

    def swap(k, half):
        rows = pl.ds(pl.multiple_of(k * 256 + h * 128 + half * 64, 64), 64)
        return remote(units.at[k - 1, pl.ds(half * 64, 64), :], x.at[0, rows, :], z_send.at[k - 1, half],
                      z_recv.at[k - 1, half], device((z + (1, 3, 2)[k - 1]) % 4, h, p))

    between = device((z + jnp.where(h == 0, 1, 3)) % 4, h, p)

    def relay_in(half):
        rows = pl.ds(half * 64, 64)
        return remote(units.at[2, rows, :], relay.at[rows, :], relay_send.at[0, half], relay_recv.at[half], between)

    def relay_out(half):
        rows = pl.ds(pl.multiple_of(3 * 256 + h * 128 + half * 64, 64), 64)
        return remote(relay.at[pl.ds(half * 64, 64), :], x.at[0, rows, :], relay_send.at[1, half], z_recv.at[2, half],
                      between)

    def share_rows(t, core):
        return pl.ds(pl.multiple_of((t // 2) * 256 + core * 128 + (t % 2) * 64, 64), 64)

    def share(s, t):
        rows = share_rows(t, h)
        return remote(x.at[s, rows, :], x.at[s, rows, :], c_send.at[s, t], c_recv.at[s, t], sibling)

    def shared(s, t):
        rows = share_rows(t, 1 - h)
        return remote(x.at[s, rows, :], x.at[s, rows, :], c_send.at[s, t], c_recv.at[s, t], sibling)

    def give(s, t):
        pl.when(sibling_need[s] == 1)(lambda: share(s, t).start())

    def send_own(t):
        for d in range(4):
            pl.when(src[d] == 0)(lambda d=d: forward(d, t).start())

    def send_held(t):
        for d in range(4):
            pl.when(src[d] != 0)(lambda d=d: forward(d, t).start())

    def receive(links, t):
        for s in range(1, SLOTS):
            pl.when(dep[s - 1] == links)(lambda s=s: arrival(s, t).wait_recv())

    def give_held(links, t):
        for s in range(1, SLOTS):
            pl.when(dep[s - 1] == links)(lambda s=s: give(s, t // 2))

    for t in range(4):
        send_own(t)
    units[0] = normalise(1)
    for half in range(2):
        swap(1, half).start()
    units[1] = normalise(2)
    for half in range(2):
        swap(2, half).start()
    units[2] = normalise(3)
    for half in range(2):
        relay_in(half).start()
    ids_copy = remote(ids_in, ids_got, id_send, id_recv, sibling)
    ids_copy.start()
    give(0, 0)
    give(0, 1)
    row_best[...] = jnp.full_like(row_best, -1.0)
    col_best[...] = jnp.full_like(col_best, -1.0)
    row_line[...] = jnp.full_like(row_line, -1.0)

    ids_copy.wait_recv()
    ids_cols[...] = jnp.zeros_like(ids_cols)
    for s in range(SLOTS):
        for t in range(4):
            for core in range(2):
                unit = held[s] * 8 + 2 * ((z + REL[t]) % 4) + core
                got = jnp.where(mine, ids_in[pl.ds(unit, 1), :], ids_got[pl.ds(unit, 1), :])
                ids_cols[pl.ds(s * 8 + 2 * t + core, 1), :] = got.astype(jnp.float32)
    turned = ids_cols[...].T
    for j in range(SLOTS * 8):
        ids_rows[j] = jnp.broadcast_to(turned[:, j:j + 1], (128, 128))

    def strip(a, t, b, count, diagonal=False):
        sim = lax.dot_general(x[a, 256 * t:256 * t + 256, :], x[b, 0:256 * count, :], (((1,), (1,)), ((), ())),
                              preferred_element_type=jnp.float32)
        for r in range(4):
            unit, first_row = a * 8 + 2 * t + r // 2, 64 * (r % 2)
            row_ids = ids_rows[unit, first_row:first_row + 64]
            best = row_best[unit, first_row:first_row + 64]
            for c in range(2 * count):
                keep = row_ids == ids_cols[pl.ds(b * 8 + c, 1), :]
                if diagonal and c // 2 == t:
                    row = lax.broadcasted_iota(jnp.int32, (64, 128), 0) + 64 * r
                    col = lax.broadcasted_iota(jnp.int32, (64, 128), 1) + 128 * (c % 2)
                    keep = jnp.logical_and(keep, row != col)
                kept = jnp.where(keep, sim[64 * r:64 * r + 64, 128 * c:128 * c + 128], jnp.float32(-1.0))
                down = jnp.max(kept.reshape(8, 8, 128), axis=0)
                col_best[b * 8 + c] = jnp.maximum(col_best[b * 8 + c], down)
                best = jnp.maximum(best, kept)
            row_best[unit, first_row:first_row + 64] = best

    def compare(t, j):
        a, b = todo[0], todo[1]
        for k in range(1, 4):
            a = jnp.where(j == k, todo[2 * k], a)
            b = jnp.where(j == k, todo[2 * k + 1], b)
        strip(a, t, b, t + 1)
        if t:
            strip(b, t, a, t)

    def finish_rows(t):
        pl.when(h == 1)(lambda: strip(0, t, 0, t + 1, diagonal=True))
        for s in range(SLOTS):
            @pl.when(need[s] == 1)
            def _():
                for core in range(2):
                    unit = s * 8 + 2 * t + core
                    row_line[unit:unit + 1, :] = jnp.max(row_best[unit].T, axis=0, keepdims=True)

    def wait_shared(m):
        for s in range(SLOTS):
            @pl.when(need[s] == 1)
            def _():
                for half in range(2):
                    shared(s, 2 * m + half).wait_recv()

    def own_half_ready(m, half):
        send_own(4 * m + 2 * half)
        send_own(4 * m + 2 * half + 1)
        give(0, 2 * m + half)

    def own_block(k):
        @pl.when(k == 2)
        def _():
            swap(1, 0).wait_recv()
            own_half_ready(1, 0)

        @pl.when(k == 4)
        def _():
            swap(1, 1).wait_recv()
            own_half_ready(1, 1)
            swap(2, 0).wait_recv()
            own_half_ready(2, 0)

        @pl.when(k == 6)
        def _():
            relay_in(0).wait_recv()
            relay_out(0).start()

        @pl.when(k == 7)
        def _():
            relay_in(1).wait_recv()
            relay_out(1).start()

        @pl.when(k == 8)
        def _():
            swap(2, 1).wait_recv()
            own_half_ready(2, 1)

        @pl.when(k == 10)
        def _():
            relay_out(0).wait_recv()
            own_half_ready(3, 0)

        @pl.when(k == 11)
        def _():
            relay_out(1).wait_recv()
            own_half_ready(3, 1)

    def pass_on(k):
        receive(1, k - 1)
        send_held(k - 1)
        pl.when(k % 2 == 0)(lambda: give_held(1, k - 1))

    def take(t):
        receive(2, t)
        pl.when(t % 2 == 1)(lambda: give_held(2, t))

    @pl.loop(1, 9)
    def _(k):
        pass_on(k)
        own_block(k)
        pl.when(k >= 4)(lambda: take(k - 4))

    for m in range(2):
        @pl.loop(9 + 4 * m, 13 + 4 * m)
        def _(k):
            j = k - 9 - 4 * m
            pass_on(k)
            if m == 0:
                own_block(k)
            pl.when(j == 0)(lambda: wait_shared(m))
            pl.when(j < pair_count)(lambda: compare(m, j))
            take(k - 4)
        finish_rows(m)

    wait_shared(2)

    @pl.loop(0, 4)
    def _(j):
        pl.when(j < pair_count)(lambda: compare(2, j))
        pl.when(j < 3)(lambda: take(13 + j))
    finish_rows(2)
    wait_shared(3)

    @pl.loop(0, pair_count)
    def _(j):
        compare(3, j)
    finish_rows(3)

    for s in range(SLOTS):
        for t in range(4):
            z_of = (z + REL[t]) % 4
            for core in range(2):
                j = s * 8 + 2 * t + core
                both = jnp.maximum(row_line[j:j + 1, :], jnp.max(col_best[j], axis=0, keepdims=True))
                part[s * 2 + z_of // 2, pl.ds(2 * (z_of % 2) + core, 1), :] = both
        for half in range(2):
            copy = remote(part.at[s * 2 + half], parts_got.at[place[s] * 2 + h], r_send.at[s * 2 + half],
                          r_recv.at[place[s] * 2 + h], (owner_grp, held[s] * 2 + half))
            if s == 0:
                keep_it = jnp.logical_and(mine, zh == half)
                pl.when(jnp.logical_not(keep_it))(copy.start)

                @pl.when(keep_it)
                def _():
                    parts_got[h] = part[half]
            else:
                copy.start()

    ids_copy.wait_send()
    for half in range(2):
        for copy in (swap(1, half), swap(2, half), relay_in(half), relay_out(half)):
            copy.wait_send()
    for d in range(4):
        for t in range(STEPS):
            forward(d, t).wait_send()
    for s in range(SLOTS):
        for t in range(8):
            pl.when(sibling_need[s] == 1)(lambda s=s, t=t: share(s, t).wait_send())
    best = None
    for k in range(2 * SLOTS):
        got = remote(parts_got.at[k], parts_got.at[k], r_send.at[k], r_recv.at[k], sibling)
        if k < 2:
            pl.when(jnp.logical_not(jnp.logical_and(mine, h == k)))(got.wait_recv)
        else:
            got.wait_recv()
        best = parts_got[k] if best is None else jnp.maximum(best, parts_got[k])
    out[...] = best

    for s in range(SLOTS):
        for half in range(2):
            copy = remote(part.at[s * 2 + half], parts_got.at[place[s] * 2 + h], r_send.at[s * 2 + half],
                          r_recv.at[place[s] * 2 + h], (owner_grp, held[s] * 2 + half))
            if s == 0:
                pl.when(jnp.logical_not(jnp.logical_and(mine, zh == half)))(copy.wait_send)
            else:
                copy.wait_send()


def on_device(embeddings, cluster_ids):
    emb = embeddings.reshape(4, 128, D)
    ids = cluster_ids.reshape(128, 128)
    dma = pltpu.SemaphoreType.DMA
    best = pl.pallas_call(
        kernel,
        out_shape=jax.ShapeDtypeStruct((4, 128), jnp.float32),
        in_specs=[pl.BlockSpec(memory_space=pl.ANY), pl.BlockSpec(memory_space=pltpu.VMEM)],
        out_specs=pl.BlockSpec(memory_space=pltpu.VMEM),
        scratch_shapes=[
            pltpu.VMEM((SLOTS, 1024, D), jnp.bfloat16),
            pltpu.VMEM((3, 128, D), jnp.bfloat16),
            pltpu.VMEM((4, 128, D), jnp.float32),
            pltpu.VMEM((128, 128), jnp.int32),
            pltpu.VMEM((SLOTS * 8, 128, 128), jnp.float32),
            pltpu.VMEM((128, 128), jnp.float32),
            pltpu.VMEM((SLOTS * 8, 128, 128), jnp.float32),
            pltpu.VMEM((SLOTS * 8, 8, 128), jnp.float32),
            pltpu.VMEM((SLOTS * 8, 128), jnp.float32),
            pltpu.VMEM((2 * SLOTS, 4, 128), jnp.float32),
            pltpu.VMEM((2 * SLOTS, 4, 128), jnp.float32),
            pltpu.VMEM((128, D), jnp.bfloat16),
            dma((4,)), dma, dma, dma((3, 2)), dma((3, 2)), dma((2, 2)), dma((2,)), dma((4, STEPS)), dma((4, STEPS)),
            dma((SLOTS, 8)), dma((SLOTS, 8)), dma((2 * SLOTS,)), dma((2 * SLOTS,)),
        ],
        compiler_params=pltpu.CompilerParams(
            collective_id=0, has_side_effects=True, vmem_limit_bytes=60 * 1024 * 1024),
        cost_estimate=pl.CostEstimate(flops=7 * 10**9, bytes_accessed=2 * 10**6, transcendentals=0),
        name="best_match",
    )(emb, ids)
    return best.reshape(1, 512)


def solution(mesh):
    placed = (P(None, "grp", "blk", None, None), P("grp", None))
    return jax.shard_map(
        on_device, mesh=mesh, in_specs=placed, out_specs=P("grp", "blk"), check_vma=False
    )
```

```python
import functools

import jax
import jax.numpy as jnp
from jax import lax
from jax.experimental import pallas as pl
from jax.experimental.pallas import tpu as pltpu
from jax.sharding import PartitionSpec as P

MESH = pl.DeviceIdType.MESH
D = 768
SLOTS = 5
PIECE = 32
STEPS = 16

SRC = [[0, 3, 0, 0], [3, 0, 0, 0], [0, 0, 4, 0], [0, 0, 4, 0], [0, 4, 1, 0], [4, 0, 2, 0], [0, 3, 0, 0], [3, 0, 0, 0],
       [3, 0, 0, 3], [0, 3, 0, 3], [2, 4, 0, 0], [4, 1, 0, 0], [2, 0, 4, 0], [0, 1, 4, 0], [4, 0, 0, 3], [0, 4, 0, 3]]
DEP = [[1, 1, 1, 2], [1, 1, 1, 2], [1, 2, 1, 1], [2, 1, 1, 1], [1, 2, 2, 1], [2, 1, 2, 1], [1, 2, 1, 2], [2, 1, 1, 2],
       [2, 2, 1, 2], [2, 2, 1, 2], [2, 1, 2, 1], [1, 2, 2, 1], [2, 1, 1, 1], [1, 2, 1, 1], [2, 1, 1, 1], [1, 2, 1, 1]]
BLK = [[1, 3, 4, 8], [2, 0, 5, 9], [3, 5, 6, 14], [4, 2, 7, 15], [5, 11, 12, 0], [10, 4, 13, 1], [7, 1, 10, 14],
       [0, 6, 11, 15], [13, 7, 12, 5], [6, 12, 13, 4], [8, 9, 2, 6], [8, 9, 3, 7], [14, 15, 0, 8], [14, 15, 1, 9],
       [11, 13, 2, 10], [12, 10, 3, 11]]
IDX = [[1, 1, 1, 1], [1, 1, 1, 1], [2, 2, 1, 1], [2, 2, 1, 1], [3, 1, 1, 2], [1, 3, 1, 2], [2, 3, 2, 2], [3, 2, 2, 2],
       [2, 3, 2, 4], [3, 3, 3, 4], [2, 2, 3, 4], [3, 3, 3, 4], [3, 3, 4, 4], [4, 4, 4, 4], [3, 4, 4, 3], [4, 4, 4, 4]]
HOLD = [[0, 1, 4, 7, 12], [1, 0, 5, 6, 13], [2, 1, 3, 10, 14], [3, 0, 2, 11, 15], [4, 0, 3, 5, 9], [5, 1, 2, 4, 8],
        [6, 2, 7, 9, 10], [7, 3, 6, 8, 11], [8, 0, 10, 11, 12], [9, 1, 10, 11, 13], [10, 5, 6, 14, 15], [11, 4, 7, 14, 15],
        [12, 4, 8, 9, 15], [13, 5, 8, 9, 14], [14, 2, 6, 12, 13], [15, 3, 7, 12, 13]]
PAIRS = [[[(1, 3), (1, 4), (3, 4)], [(0, 1), (0, 2), (1, 2)]], [[(2, 1), (2, 4), (1, 4)], [(0, 1), (0, 3), (3, 4)]],
         [[(1, 3), (3, 4), (2, 3), (2, 4)], [(0, 1), (0, 2), (1, 2)]],
         [[(2, 3), (2, 1), (1, 3)], [(0, 3), (3, 4), (0, 1)]], [[(4, 0), (4, 1), (0, 2), (1, 2)], [(0, 3), (1, 3)]],
         [[(2, 0), (4, 1), (2, 1)], [(0, 1), (0, 3), (1, 3)]], [[(1, 3), (1, 4), (3, 4)], [(0, 3), (2, 0), (2, 1)]],
         [[(2, 3), (2, 4), (3, 4)], [(2, 0), (1, 2), (1, 0)]],
         [[(2, 3), (2, 1), (0, 1), (3, 1)], [(4, 2), (4, 0), (2, 0)]],
         [[(4, 1), (4, 0), (4, 3), (1, 3)], [(1, 0), (1, 2), (0, 2)]],
         [[(3, 4), (3, 1), (4, 1)], [(2, 0), (1, 2), (1, 0)]], [[(1, 0), (3, 1), (3, 2)], [(4, 0), (4, 2), (2, 0)]],
         [[(3, 4), (4, 1), (0, 1)], [(4, 0), (4, 2), (0, 2)]], [[(3, 4), (4, 1), (1, 2)], [(4, 0), (4, 2), (0, 2)]],
         [[(3, 4), (3, 1), (4, 1)], [(2, 0), (1, 2), (1, 0)]], [[(3, 4), (3, 1), (4, 1)], [(3, 2), (2, 1), (2, 0)]]]
NEED = [[[1, 3, 4], [0, 1, 2]], [[1, 2, 4], [0, 1, 3, 4]], [[1, 2, 3, 4], [0, 1, 2]], [[1, 2, 3], [0, 1, 3, 4]],
        [[0, 1, 2, 4], [0, 1, 3]], [[0, 1, 2, 4], [0, 1, 3]], [[1, 3, 4], [0, 1, 2, 3]], [[2, 3, 4], [0, 1, 2]],
        [[0, 1, 2, 3], [0, 2, 4]], [[0, 1, 3, 4], [0, 1, 2]], [[1, 3, 4], [0, 1, 2]], [[0, 1, 2, 3], [0, 2, 4]],
        [[0, 1, 3, 4], [0, 2, 4]], [[1, 2, 3, 4], [0, 2, 4]], [[1, 3, 4], [0, 1, 2]], [[1, 3, 4], [0, 1, 2, 3]]]

REL = (0, 3, 1, 2)


def word(digits, base):
    total = 0
    for digit in reversed(digits):
        total = total * base + digit
    return total


def look_up(index, words):
    got = jnp.int32(words[0])
    for k in range(1, len(words)):
        got = jnp.where(index == k, jnp.int32(words[k]), got)
    return got


def digits_of(value, base, count):
    out = []
    for _ in range(count):
        out.append(value % base)
        value = value // base
    return out


def kernel(emb, ids_in, out, x, units, stage, ids_got, ids_lines, ids_rows, ids_cols, row_best, col_best, row_line, part, parts_got,
           relay, sim_one, sim_two,
           load_sem, id_send, id_recv, z_send, z_recv, relay_send, relay_recv, f_send, f_recv, c_send, c_recv, r_send, r_recv):
    grp, blk = lax.axis_index("grp"), lax.axis_index("blk")
    h, zl = grp % 2, grp // 2
    p, zh = blk // 2, blk % 2
    z = zh * 2 + zl
    px, py = p % 4, p // 4

    def device(z_of, core, chip):
        return ((z_of % 2) * 2 + core, chip * 2 + z_of // 2)

    def group_of(z_of):
        return (z_of % 2) * 2 + z_of // 2

    near = [py * 4 + (px + 1) % 4, py * 4 + (px + 3) % 4, ((py + 1) % 4) * 4 + px, ((py + 3) % 4) * 4 + px]
    first = look_up(p, [word(SRC[c], 8) + 4096 * word(DEP[c], 4) for c in range(16)])
    src = digits_of(first, 8, 4)
    dep = digits_of(first // 4096, 4, 4)
    held = [p] + digits_of(look_up(p, [word(BLK[c], 16) for c in range(16)]), 16, 4)
    third = look_up(p, [word(IDX[c], 8) + 4096 * word(HOLD[c][1:], 16) for c in range(16)])
    place = [jnp.int32(0)] + digits_of(third, 8, 4)
    holders = [p] + digits_of(third // 4096, 16, 4)
    lists = []
    for c in range(16):
        for core in range(2):
            flat = [slot for pair in PAIRS[c][core] for slot in pair]
            lists.append(len(PAIRS[c][core]) + 8 * word(flat + [0] * (8 - len(flat)), 8))
    todo = look_up(p * 2 + h, lists)
    pair_count = todo % 8
    todo = digits_of(todo // 8, 8, 8)

    needs = [[sum(1 << slot for slot in NEED[c][core]) for core in range(2)] for c in range(16)]
    need = digits_of(look_up(p * 2 + h, [needs[c][core] for c in range(16) for core in range(2)]), 2, SLOTS)
    sibling_need = digits_of(look_up(p * 2 + h, [needs[c][1 - core] for c in range(16) for core in range(2)]), 2, SLOTS)

    sibling = device(z, 1 - h, p)
    owner_grp = zl * 2 + zh
    mine = h == zh

    loads = []
    for k, rel in enumerate((0, 1, 3, 2)):
        loads.append(pltpu.make_async_copy(emb.at[group_of((z + rel) % 4)], stage.at[k], load_sem.at[k]))
        loads[-1].start()

    barrier = pltpu.get_barrier_semaphore()
    for rel in (1, 3):
        pl.semaphore_signal(barrier, inc=1, device_id=device((z + rel) % 4, h, p), device_id_type=MESH)
    for d in range(4):
        pl.semaphore_signal(barrier, inc=1, device_id=device(z, h, near[d]), device_id_type=MESH)
    pl.semaphore_signal(barrier, inc=1, device_id=sibling, device_id_type=MESH)
    from_z = 2 * h + zl
    for k in range(SLOTS):
        for core in range(2):
            def tell():
                pl.semaphore_signal(barrier, inc=1, device_id=device(from_z, core, holders[k]), device_id_type=MESH)
            if k == 0:
                pl.when(jnp.logical_not(jnp.logical_and(mine, h == core)))(tell)
            else:
                tell()

    def normalise(k):
        loads[k].wait()
        v = stage[k]
        total = jnp.sum(v * v, axis=-1, keepdims=True)
        return (v / jnp.sqrt(total + 1e-06)).astype(jnp.bfloat16)

    own_rows = pl.multiple_of(h * 128, 128)
    x[0, pl.ds(own_rows, 128), :] = normalise(0)
    pl.semaphore_wait(barrier, jnp.where(mine, 16, 17))

    def remote(src_ref, dst_ref, send_sem, recv_sem, to):
        return pltpu.make_async_remote_copy(
            src_ref=src_ref, dst_ref=dst_ref, send_sem=send_sem, recv_sem=recv_sem, device_id=to, device_id_type=MESH)

    def part_rows(t):
        return pl.ds(pl.multiple_of((t // 4) * 256 + h * 128 + (t % 4) * PIECE, PIECE), PIECE)

    def forward(d, t):
        rows = part_rows(t)
        return remote(x.at[src[d], rows, :], x.at[1 + (d ^ 1), rows, :], f_send.at[d, t], f_recv.at[d ^ 1, t],
                      device(z, h, near[d]))

    def arrival(s, t):
        rows = part_rows(t)
        return remote(x.at[s, rows, :], x.at[s, rows, :], f_send.at[s - 1, t], f_recv.at[s - 1, t],
                      device(z, h, near[s - 1]))

    def swap(k, half):
        rows = pl.ds(pl.multiple_of(k * 256 + h * 128 + half * 64, 64), 64)
        return remote(units.at[k - 1, pl.ds(half * 64, 64), :], x.at[0, rows, :], z_send.at[k - 1, half],
                      z_recv.at[k - 1, half], device((z + (1, 3, 2)[k - 1]) % 4, h, p))

    between = device((z + jnp.where(h == 0, 1, 3)) % 4, h, p)

    def relay_in(half):
        rows = pl.ds(half * 64, 64)
        return remote(units.at[2, rows, :], relay.at[rows, :], relay_send.at[0, half], relay_recv.at[half], between)

    def relay_out(half):
        rows = pl.ds(pl.multiple_of(3 * 256 + h * 128 + half * 64, 64), 64)
        return remote(relay.at[pl.ds(half * 64, 64), :], x.at[0, rows, :], relay_send.at[1, half], z_recv.at[2, half],
                      between)

    def share_rows(t, core):
        return pl.ds(pl.multiple_of((t // 2) * 256 + core * 128 + (t % 2) * 64, 64), 64)

    def share(s, t):
        rows = share_rows(t, h)
        return remote(x.at[s, rows, :], x.at[s, rows, :], c_send.at[s, t], c_recv.at[s, t], sibling)

    def shared(s, t):
        rows = share_rows(t, 1 - h)
        return remote(x.at[s, rows, :], x.at[s, rows, :], c_send.at[s, t], c_recv.at[s, t], sibling)

    def give(s, t):
        pl.when(sibling_need[s] == 1)(lambda: share(s, t).start())

    def send_own(t):
        for d in range(4):
            pl.when(src[d] == 0)(lambda d=d: forward(d, t).start())

    def send_held(t):
        for d in range(4):
            pl.when(src[d] != 0)(lambda d=d: forward(d, t).start())

    def receive(links, t):
        for s in range(1, SLOTS):
            pl.when(dep[s - 1] == links)(lambda s=s: arrival(s, t).wait_recv())

    def give_held(links, t):
        for s in range(1, SLOTS):
            pl.when(dep[s - 1] == links)(lambda s=s: give(s, t // 2))

    for t in range(4):
        send_own(t)
    units[0] = normalise(1)
    for half in range(2):
        swap(1, half).start()
    units[1] = normalise(2)
    for half in range(2):
        swap(2, half).start()
    units[2] = normalise(3)
    for half in range(2):
        relay_in(half).start()
    ids_copy = remote(ids_in, ids_got, id_send, id_recv, sibling)
    ids_copy.start()
    give(0, 0)
    give(0, 1)
    row_best[...] = jnp.full_like(row_best, -1.0)
    col_best[...] = jnp.full_like(col_best, -1.0)
    row_line[...] = jnp.full_like(row_line, -1.0)

    ids_copy.wait_recv()
    ids_lines[...] = jnp.zeros_like(ids_lines)
    for s in range(SLOTS):
        for t in range(4):
            for core in range(2):
                unit = held[s] * 8 + 2 * ((z + REL[t]) % 4) + core
                got = jnp.where(mine, ids_in[pl.ds(unit, 1), :], ids_got[pl.ds(unit, 1), :])
                ids_lines[pl.ds(s * 8 + 2 * t + core, 1), :] = got.astype(jnp.float32)
    turned = ids_lines[...].T
    for j in range(SLOTS * 8):
        ids_cols[j] = jnp.broadcast_to(ids_lines[j:j + 1, :], (8, 128))
        ids_rows[j] = jnp.broadcast_to(turned[:, j:j + 1], (128, 128))

    def multiply(sim, a, t, b, count):
        sim[:, 0:256 * count] = lax.dot_general(
            x[a, 256 * t:256 * t + 256, :], x[b, 0:256 * count, :], (((1,), (1,)), ((), ())),
            preferred_element_type=jnp.float32)

    def reduce(sim, a, t, b, count, diagonal=False):
        downs = [None] * (2 * count)
        for r in range(2):
            unit = a * 8 + 2 * t + r
            row_ids = ids_rows[unit].reshape(16, 8, 128)
            best = row_best[unit].reshape(16, 8, 128)
            for c in range(2 * count):
                keep = row_ids == ids_cols[b * 8 + c]
                if diagonal and c == 2 * t + r:
                    row = lax.broadcasted_iota(jnp.int32, (128, 128), 0)
                    col = lax.broadcasted_iota(jnp.int32, (128, 128), 1)
                    keep = jnp.logical_and(keep, (row != col).reshape(16, 8, 128))
                values = sim[128 * r:128 * r + 128, 128 * c:128 * c + 128].reshape(16, 8, 128)
                kept = jnp.where(keep, values, jnp.float32(-1.0))
                down = jnp.max(kept, axis=0)
                downs[c] = down if downs[c] is None else jnp.maximum(downs[c], down)
                best = jnp.maximum(best, kept)
            row_best[unit] = best.reshape(128, 128)
        old = [col_best[b * 8 + c] for c in range(2 * count)]
        for c in range(2 * count):
            col_best[b * 8 + c] = jnp.maximum(old[c], downs[c])

    def pair(j):
        a, b = todo[0], todo[1]
        for k in range(1, 4):
            a = jnp.where(j == k, todo[2 * k], a)
            b = jnp.where(j == k, todo[2 * k + 1], b)
        return a, b

    def compare(t, j):
        a, b = pair(j)
        multiply(sim_one, a, t, b, t + 1)
        if t:
            multiply(sim_two, b, t, a, t)
        reduce(sim_one, a, t, b, t + 1)
        if t:
            reduce(sim_two, b, t, a, t)

    def compare_all(t):
        a, b = pair(0)
        multiply(sim_one, a, t, b, t + 1)

        @pl.loop(0, pair_count - 1)
        def _(j):
            a, b = pair(j)
            multiply(sim_two, b, t, a, t)
            reduce(sim_one, a, t, b, t + 1)
            next_a, next_b = pair(j + 1)
            multiply(sim_one, next_a, t, next_b, t + 1)
            reduce(sim_two, b, t, a, t)

        a, b = pair(pair_count - 1)
        multiply(sim_two, b, t, a, t)
        reduce(sim_one, a, t, b, t + 1)

        @pl.when(h == 1)
        def _():
            multiply(sim_one, 0, t, 0, t + 1)
            reduce(sim_two, b, t, a, t)
            reduce(sim_one, 0, t, 0, t + 1, diagonal=True)

        pl.when(h == 0)(lambda: reduce(sim_two, b, t, a, t))

    def own_pair(t):
        @pl.when(h == 1)
        def _():
            multiply(sim_one, 0, t, 0, t + 1)
            reduce(sim_one, 0, t, 0, t + 1, diagonal=True)

    def finish_rows(t):
        for s in range(SLOTS):
            @pl.when(need[s] == 1)
            def _():
                for core in range(2):
                    unit = s * 8 + 2 * t + core
                    row_line[unit:unit + 1, :] = jnp.max(row_best[unit].T, axis=0, keepdims=True)

    def wait_shared(m):
        for s in range(SLOTS):
            @pl.when(need[s] == 1)
            def _():
                for half in range(2):
                    shared(s, 2 * m + half).wait_recv()

    def own_half_ready(m, half):
        send_own(4 * m + 2 * half)
        send_own(4 * m + 2 * half + 1)
        give(0, 2 * m + half)

    def own_block(k):
        @pl.when(k == 2)
        def _():
            swap(1, 0).wait_recv()
            own_half_ready(1, 0)

        @pl.when(k == 4)
        def _():
            swap(1, 1).wait_recv()
            own_half_ready(1, 1)
            swap(2, 0).wait_recv()
            own_half_ready(2, 0)

        @pl.when(k == 6)
        def _():
            relay_in(0).wait_recv()
            relay_out(0).start()

        @pl.when(k == 7)
        def _():
            relay_in(1).wait_recv()
            relay_out(1).start()

        @pl.when(k == 8)
        def _():
            swap(2, 1).wait_recv()
            own_half_ready(2, 1)

        @pl.when(k == 10)
        def _():
            relay_out(0).wait_recv()
            own_half_ready(3, 0)

        @pl.when(k == 11)
        def _():
            relay_out(1).wait_recv()
            own_half_ready(3, 1)

    def pass_on(k):
        receive(1, k - 1)
        send_held(k - 1)
        pl.when(k % 2 == 0)(lambda: give_held(1, k - 1))

    def take(t):
        receive(2, t)
        pl.when(t % 2 == 1)(lambda: give_held(2, t))

    @pl.loop(1, 9)
    def _(k):
        pass_on(k)
        own_block(k)
        pl.when(k >= 4)(lambda: take(k - 4))

    for m in range(2):
        @pl.loop(9 + 4 * m, 13 + 4 * m)
        def _(k):
            j = k - 9 - 4 * m
            pass_on(k)
            if m == 0:
                own_block(k)
            pl.when(j == 0)(lambda: wait_shared(m))
            pl.when(j < pair_count)(lambda: compare(m, j))
            take(k - 4)
        own_pair(m)
        finish_rows(m)

    take(13)
    wait_shared(2)
    compare_all(2)
    finish_rows(2)
    take(14)
    take(15)
    wait_shared(3)
    compare_all(3)
    finish_rows(3)

    for s in range(SLOTS):
        for t in range(4):
            z_of = (z + REL[t]) % 4
            for core in range(2):
                j = s * 8 + 2 * t + core
                both = jnp.maximum(row_line[j:j + 1, :], jnp.max(col_best[j], axis=0, keepdims=True))
                part[s * 2 + z_of // 2, pl.ds(2 * (z_of % 2) + core, 1), :] = both
        for half in range(2):
            copy = remote(part.at[s * 2 + half], parts_got.at[place[s] * 2 + h], r_send.at[s * 2 + half],
                          r_recv.at[place[s] * 2 + h], (owner_grp, held[s] * 2 + half))
            if s == 0:
                keep_it = jnp.logical_and(mine, zh == half)
                pl.when(jnp.logical_not(keep_it))(copy.start)

                @pl.when(keep_it)
                def _():
                    parts_got[h] = part[half]
            else:
                copy.start()

    ids_copy.wait_send()
    for half in range(2):
        for copy in (swap(1, half), swap(2, half), relay_in(half), relay_out(half)):
            copy.wait_send()
    for d in range(4):
        for t in range(STEPS):
            forward(d, t).wait_send()
    for s in range(SLOTS):
        for t in range(8):
            pl.when(sibling_need[s] == 1)(lambda s=s, t=t: share(s, t).wait_send())
    best = None
    for k in range(2 * SLOTS):
        got = remote(parts_got.at[k], parts_got.at[k], r_send.at[k], r_recv.at[k], sibling)
        if k < 2:
            pl.when(jnp.logical_not(jnp.logical_and(mine, h == k)))(got.wait_recv)
        else:
            got.wait_recv()
        best = parts_got[k] if best is None else jnp.maximum(best, parts_got[k])
    out[...] = best

    for s in range(SLOTS):
        for half in range(2):
            copy = remote(part.at[s * 2 + half], parts_got.at[place[s] * 2 + h], r_send.at[s * 2 + half],
                          r_recv.at[place[s] * 2 + h], (owner_grp, held[s] * 2 + half))
            if s == 0:
                pl.when(jnp.logical_not(jnp.logical_and(mine, zh == half)))(copy.wait_send)
            else:
                copy.wait_send()


def on_device(embeddings, cluster_ids):
    emb = embeddings.reshape(4, 128, D)
    ids = cluster_ids.reshape(128, 128)
    dma = pltpu.SemaphoreType.DMA
    best = pl.pallas_call(
        kernel,
        out_shape=jax.ShapeDtypeStruct((4, 128), jnp.float32),
        in_specs=[pl.BlockSpec(memory_space=pl.ANY), pl.BlockSpec(memory_space=pltpu.VMEM)],
        out_specs=pl.BlockSpec(memory_space=pltpu.VMEM),
        scratch_shapes=[
            pltpu.VMEM((SLOTS, 1024, D), jnp.bfloat16),
            pltpu.VMEM((3, 128, D), jnp.bfloat16),
            pltpu.VMEM((4, 128, D), jnp.float32),
            pltpu.VMEM((128, 128), jnp.int32),
            pltpu.VMEM((128, 128), jnp.float32),
            pltpu.VMEM((SLOTS * 8, 128, 128), jnp.float32),
            pltpu.VMEM((SLOTS * 8, 8, 128), jnp.float32),
            pltpu.VMEM((SLOTS * 8, 128, 128), jnp.float32),
            pltpu.VMEM((SLOTS * 8, 8, 128), jnp.float32),
            pltpu.VMEM((SLOTS * 8, 128), jnp.float32),
            pltpu.VMEM((2 * SLOTS, 4, 128), jnp.float32),
            pltpu.VMEM((2 * SLOTS, 4, 128), jnp.float32),
            pltpu.VMEM((128, D), jnp.bfloat16),
            pltpu.VMEM((256, 1024), jnp.float32),
            pltpu.VMEM((256, 768), jnp.float32),
            dma((4,)), dma, dma, dma((3, 2)), dma((3, 2)), dma((2, 2)), dma((2,)), dma((4, STEPS)), dma((4, STEPS)),
            dma((SLOTS, 8)), dma((SLOTS, 8)), dma((2 * SLOTS,)), dma((2 * SLOTS,)),
        ],
        compiler_params=pltpu.CompilerParams(
            collective_id=0, has_side_effects=True, vmem_limit_bytes=60 * 1024 * 1024),
        cost_estimate=pl.CostEstimate(flops=7 * 10**9, bytes_accessed=2 * 10**6, transcendentals=0),
        name="best_match",
    )(emb, ids)
    return best.reshape(1, 512)


def solution(mesh):
    placed = (P(None, "grp", "blk", None, None), P("grp", None))
    return jax.shard_map(
        on_device, mesh=mesh, in_specs=placed, out_specs=P("grp", "blk"), check_vma=False
    )
```

```python
import functools

import jax
import jax.numpy as jnp
from jax import lax
from jax.experimental import pallas as pl
from jax.experimental.pallas import tpu as pltpu
from jax.sharding import PartitionSpec as P

MESH = pl.DeviceIdType.MESH
D = 768
SLOTS = 5
PIECE = 32
STEPS = 16
START = 13

SRC = [[0, 3, 0, 0], [3, 0, 0, 0], [0, 0, 4, 0], [0, 0, 4, 0], [0, 4, 1, 0], [4, 0, 2, 0], [0, 3, 0, 0], [3, 0, 0, 0],
       [3, 0, 0, 3], [0, 3, 0, 3], [2, 4, 0, 0], [4, 1, 0, 0], [2, 0, 4, 0], [0, 1, 4, 0], [4, 0, 0, 3], [0, 4, 0, 3]]
DEP = [[1, 1, 1, 2], [1, 1, 1, 2], [1, 2, 1, 1], [2, 1, 1, 1], [1, 2, 2, 1], [2, 1, 2, 1], [1, 2, 1, 2], [2, 1, 1, 2],
       [2, 2, 1, 2], [2, 2, 1, 2], [2, 1, 2, 1], [1, 2, 2, 1], [2, 1, 1, 1], [1, 2, 1, 1], [2, 1, 1, 1], [1, 2, 1, 1]]
BLK = [[1, 3, 4, 8], [2, 0, 5, 9], [3, 5, 6, 14], [4, 2, 7, 15], [5, 11, 12, 0], [10, 4, 13, 1], [7, 1, 10, 14],
       [0, 6, 11, 15], [13, 7, 12, 5], [6, 12, 13, 4], [8, 9, 2, 6], [8, 9, 3, 7], [14, 15, 0, 8], [14, 15, 1, 9],
       [11, 13, 2, 10], [12, 10, 3, 11]]
IDX = [[1, 1, 1, 1], [1, 1, 1, 1], [2, 2, 1, 1], [2, 2, 1, 1], [3, 1, 1, 2], [1, 3, 1, 2], [2, 3, 2, 2], [3, 2, 2, 2],
       [2, 3, 2, 4], [3, 3, 3, 4], [2, 2, 3, 4], [3, 3, 3, 4], [3, 3, 4, 4], [4, 4, 4, 4], [3, 4, 4, 3], [4, 4, 4, 4]]
HOLD = [[0, 1, 4, 7, 12], [1, 0, 5, 6, 13], [2, 1, 3, 10, 14], [3, 0, 2, 11, 15], [4, 0, 3, 5, 9], [5, 1, 2, 4, 8],
        [6, 2, 7, 9, 10], [7, 3, 6, 8, 11], [8, 0, 10, 11, 12], [9, 1, 10, 11, 13], [10, 5, 6, 14, 15], [11, 4, 7, 14, 15],
        [12, 4, 8, 9, 15], [13, 5, 8, 9, 14], [14, 2, 6, 12, 13], [15, 3, 7, 12, 13]]
PAIRS = [[[(1, 3), (1, 4), (3, 4)], [(0, 1), (0, 2), (1, 2)]], [[(2, 1), (2, 4), (1, 4)], [(0, 1), (0, 3), (3, 4)]],
         [[(1, 3), (3, 4), (2, 3), (2, 4)], [(0, 1), (0, 2), (1, 2)]],
         [[(2, 3), (2, 1), (1, 3)], [(0, 3), (3, 4), (0, 1)]], [[(4, 0), (4, 1), (0, 2), (1, 2)], [(0, 3), (1, 3)]],
         [[(2, 0), (4, 1), (2, 1)], [(0, 1), (0, 3), (1, 3)]], [[(1, 3), (1, 4), (3, 4)], [(0, 3), (2, 0), (2, 1)]],
         [[(2, 3), (2, 4), (3, 4)], [(2, 0), (1, 2), (1, 0)]],
         [[(2, 3), (2, 1), (0, 1), (3, 1)], [(4, 2), (4, 0), (2, 0)]],
         [[(4, 1), (4, 0), (4, 3), (1, 3)], [(1, 0), (1, 2), (0, 2)]],
         [[(3, 4), (3, 1), (4, 1)], [(2, 0), (1, 2), (1, 0)]], [[(1, 0), (3, 1), (3, 2)], [(4, 0), (4, 2), (2, 0)]],
         [[(3, 4), (4, 1), (0, 1)], [(4, 0), (4, 2), (0, 2)]], [[(3, 4), (4, 1), (1, 2)], [(4, 0), (4, 2), (0, 2)]],
         [[(3, 4), (3, 1), (4, 1)], [(2, 0), (1, 2), (1, 0)]], [[(3, 4), (3, 1), (4, 1)], [(3, 2), (2, 1), (2, 0)]]]
NEED = [[[1, 3, 4], [0, 1, 2]], [[1, 2, 4], [0, 1, 3, 4]], [[1, 2, 3, 4], [0, 1, 2]], [[1, 2, 3], [0, 1, 3, 4]],
        [[0, 1, 2, 4], [0, 1, 3]], [[0, 1, 2, 4], [0, 1, 3]], [[1, 3, 4], [0, 1, 2, 3]], [[2, 3, 4], [0, 1, 2]],
        [[0, 1, 2, 3], [0, 2, 4]], [[0, 1, 3, 4], [0, 1, 2]], [[1, 3, 4], [0, 1, 2]], [[0, 1, 2, 3], [0, 2, 4]],
        [[0, 1, 3, 4], [0, 2, 4]], [[1, 2, 3, 4], [0, 2, 4]], [[1, 3, 4], [0, 1, 2]], [[1, 3, 4], [0, 1, 2, 3]]]

REL = (0, 3, 1, 2)


def word(digits, base):
    total = 0
    for digit in reversed(digits):
        total = total * base + digit
    return total


def look_up(index, words):
    got = jnp.int32(words[0])
    for k in range(1, len(words)):
        got = jnp.where(index == k, jnp.int32(words[k]), got)
    return got


def digits_of(value, base, count):
    out = []
    for _ in range(count):
        out.append(value % base)
        value = value // base
    return out


def pick(values, index):
    got = values[0]
    for k in range(1, len(values)):
        got = jnp.where(index == k, values[k], got)
    return got


def remote(src_ref, dst_ref, send_sem, recv_sem, to):
    return pltpu.make_async_remote_copy(
        src_ref=src_ref, dst_ref=dst_ref, send_sem=send_sem, recv_sem=recv_sem, device_id=to, device_id_type=MESH)


def kernel(emb, ids_in, out, x, units, stage, relay, ids_got, ids_rows, ids_cols, sim_one, sim_two, row_best, col_best,
           row_line, part, parts_got, load_sem, id_send, id_recv, z_send, z_recv, relay_send, relay_recv, f_send, f_recv,
           c_send, c_recv, r_send, r_recv):
    grp, blk = lax.axis_index("grp"), lax.axis_index("blk")
    h, zl = grp % 2, grp // 2
    p, zh = blk // 2, blk % 2
    z = zh * 2 + zl
    px, py = p % 4, p // 4

    def device(z_of, core, chip):
        return ((z_of % 2) * 2 + core, chip * 2 + z_of // 2)

    def load(k):
        z_of = (z + pick((0, 1, 3, 2), k)) % 4
        return pltpu.make_async_copy(emb.at[(z_of % 2) * 2 + z_of // 2], stage.at[k], load_sem.at[k])

    for k in range(4):
        load(k).start()

    near = [py * 4 + (px + 1) % 4, py * 4 + (px + 3) % 4, ((py + 1) % 4) * 4 + px, ((py + 3) % 4) * 4 + px]
    first = look_up(p, [word(SRC[c], 8) + 4096 * word(DEP[c], 4) for c in range(16)])
    src = digits_of(first, 8, 4)
    dep = digits_of(first // 4096, 4, 4)
    held = [p] + digits_of(look_up(p, [word(BLK[c], 16) for c in range(16)]), 16, 4)
    third = look_up(p, [word(IDX[c], 8) + 4096 * word(HOLD[c][1:], 16) for c in range(16)])
    place = [jnp.int32(0)] + digits_of(third, 8, 4)
    holders = [p] + digits_of(third // 4096, 16, 4)
    lists = []
    for c in range(16):
        for core in range(2):
            flat = [slot for pair in PAIRS[c][core] for slot in pair]
            lists.append(len(PAIRS[c][core]) + 8 * word(flat + [0] * (8 - len(flat)), 8))
    todo = look_up(p * 2 + h, lists)
    pair_count = todo % 8
    todo = digits_of(todo // 8, 8, 8)
    needs = [[sum(1 << slot for slot in NEED[c][core]) for core in range(2)] for c in range(16)]
    need = digits_of(look_up(p * 2 + h, [needs[c][core] for c in range(16) for core in range(2)]), 2, SLOTS)
    sibling_need = digits_of(look_up(p * 2 + h, [needs[c][1 - core] for c in range(16) for core in range(2)]), 2, SLOTS)

    sibling = device(z, 1 - h, p)
    owner_grp = zl * 2 + zh
    mine = h == zh

    barrier = pltpu.get_barrier_semaphore()
    for rel in (1, 3):
        pl.semaphore_signal(barrier, inc=1, device_id=device((z + rel) % 4, h, p), device_id_type=MESH)
    for d in range(4):
        pl.semaphore_signal(barrier, inc=1, device_id=device(z, h, near[d]), device_id_type=MESH)
    pl.semaphore_signal(barrier, inc=1, device_id=sibling, device_id_type=MESH)
    from_z = 2 * h + zl
    for k in range(SLOTS):
        for core in range(2):
            def tell():
                pl.semaphore_signal(barrier, inc=1, device_id=device(from_z, core, holders[k]), device_id_type=MESH)
            if k == 0:
                pl.when(jnp.logical_not(jnp.logical_and(mine, h == core)))(tell)
            else:
                tell()

    def normalised(k, half):
        v = stage[k, pl.ds(pl.multiple_of(half * 64, 64), 64), :]
        total = jnp.sum(v * v, axis=-1, keepdims=True)
        return (v / jnp.sqrt(total + 1e-06)).astype(jnp.bfloat16)

    def part_rows(t):
        return pl.ds(pl.multiple_of((t // 4) * 256 + h * 128 + (t % 4) * PIECE, PIECE), PIECE)

    def forward(d, t):
        rows = part_rows(t)
        return remote(x.at[src[d], rows, :], x.at[1 + (d ^ 1), rows, :], f_send.at[d, t], f_recv.at[d ^ 1, t],
                      device(z, h, near[d]))

    def arrival(s, t):
        rows = part_rows(t)
        return remote(x.at[s, rows, :], x.at[s, rows, :], f_send.at[s - 1, t], f_recv.at[s - 1, t],
                      device(z, h, near[s - 1]))

    def half_rows(t, core):
        return pl.ds(pl.multiple_of((t // 2) * 256 + core * 128 + (t % 2) * 64, 64), 64)

    def swap(k, half):
        return remote(units.at[k - 1, pl.ds(pl.multiple_of(half * 64, 64), 64), :], x.at[0, half_rows(2 * k + half, h), :],
                      z_send.at[k - 1, half], z_recv.at[k - 1, half], device((z + 2 * k - 1) % 4, h, p))

    between = device((z + jnp.where(h == 0, 1, 3)) % 4, h, p)

    def relay_in(half):
        rows = pl.ds(pl.multiple_of(half * 64, 64), 64)
        return remote(units.at[2, rows, :], relay.at[rows, :], relay_send.at[0, half], relay_recv.at[half], between)

    def relay_out(half):
        rows = pl.ds(pl.multiple_of(half * 64, 64), 64)
        return remote(relay.at[rows, :], x.at[0, half_rows(6 + half, h), :], relay_send.at[1, half], z_recv.at[2, half],
                      between)

    def share(s, t):
        rows = half_rows(t, h)
        return remote(x.at[s, rows, :], x.at[s, rows, :], c_send.at[s, t], c_recv.at[s, t], sibling)

    def shared(s, t):
        rows = half_rows(t, 1 - h)
        return remote(x.at[s, rows, :], x.at[s, rows, :], c_send.at[s, t], c_recv.at[s, t], sibling)

    def give(s, t):
        pl.when(sibling_need[s] == 1)(lambda: share(s, t).start())

    def send_own(t):
        for d in range(4):
            pl.when(src[d] == 0)(lambda d=d: forward(d, t).start())

    def send_held(t):
        for d in range(4):
            pl.when(src[d] != 0)(lambda d=d: forward(d, t).start())

    def own_half_ready(t):
        @pl.loop(0, 2)
        def _(piece):
            send_own(2 * t + piece)
        give(0, t)

    def receive(links, t):
        for s in range(1, SLOTS):
            pl.when(dep[s - 1] == links)(lambda s=s: arrival(s, t).wait_recv())

    def give_held(links, t):
        for s in range(1, SLOTS):
            pl.when(dep[s - 1] == links)(lambda s=s: give(s, t // 2))

    load(0).wait()

    @pl.loop(0, 2)
    def _(half):
        x[0, half_rows(half, h), :] = normalised(0, half)

    pl.semaphore_wait(barrier, jnp.where(mine, 16, 17))

    @pl.loop(0, 2)
    def _(half):
        own_half_ready(half)

    @pl.loop(1, 4)
    def _(k):
        load(k).wait()

        @pl.loop(0, 2)
        def _(half):
            units[k - 1, pl.ds(pl.multiple_of(half * 64, 64), 64), :] = normalised(k, half)
            pl.when(k < 3)(lambda: swap(k, half).start())
            pl.when(k == 3)(lambda: relay_in(half).start())

    ids_copy = remote(ids_in, ids_got, id_send, id_recv, sibling)
    ids_copy.start()

    ids_copy.wait_recv()
    row_line[...] = jnp.full_like(row_line, -1.0)

    @pl.loop(0, SLOTS * 8)
    def _(j):
        unit = pick(held, j // 8) * 8 + 2 * ((z + pick(REL, (j // 2) % 4)) % 4) + j % 2
        line = jnp.where(mine, ids_in[pl.ds(unit, 1), :], ids_got[pl.ds(unit, 1), :]).astype(jnp.float32)
        ids_cols[j] = jnp.broadcast_to(line, (8, 128))
        ids_rows[j] = jnp.broadcast_to(line, (128, 128)).T
        row_best[j] = jnp.full((128, 128), -1.0, jnp.float32)
        col_best[j] = jnp.full((8, 128), -1.0, jnp.float32)

    def unit_of(q, i):
        per = jnp.where(q == 2, 4, 2)
        j, r = i // per, i % per
        own = j >= pair_count
        e = i - pair_count * per
        a = pick([todo[0], todo[2], todo[4], todo[6]], j)
        b = pick([todo[1], todo[3], todo[5], todo[7]], j)
        turned = jnp.logical_or(jnp.logical_and(q == 1, r == 1), jnp.logical_and(q == 2, r == 3))
        rows = jnp.where(own, 0, jnp.where(turned, b, a))
        cols = jnp.where(own, 0, jnp.where(turned, a, b))
        step = jnp.where(own, e, r)
        two = jnp.where(own, 1, 2)
        row_part = jnp.where(q == 0, step, jnp.where(q == 1, 2, jnp.where(step == two, 2, 3)))
        col_half = jnp.where(jnp.logical_and(q == 2, jnp.logical_or(step == 1, step == 2)), 1, 0)
        return rows, row_part, cols, col_half, jnp.logical_and(own, row_part // 2 == col_half)

    def multiply(sim, unit):
        rows, row_part, cols, col_half, _ = unit
        sim[...] = lax.dot_general(
            x[rows, pl.ds(pl.multiple_of(row_part * 256, 256), 256), :],
            x[cols, pl.ds(pl.multiple_of(col_half * 512, 512), 512), :],
            (((1,), (1,)), ((), ())), preferred_element_type=jnp.float32)

    def drop_self(sim, unit):
        _, row_part, _, _, diagonal = unit

        @pl.when(diagonal)
        def _():
            for r in range(2):
                at = (slice(128 * r, 128 * r + 128),
                      pl.ds(pl.multiple_of((row_part % 2) * 256 + 128 * r, 128), 128))
                row = lax.broadcasted_iota(jnp.int32, (128, 128), 0)
                col = lax.broadcasted_iota(jnp.int32, (128, 128), 1)
                sim[at] = jnp.where(row == col, jnp.float32(-1.0), sim[at])

    def reduce(sim, unit):
        rows, row_part, cols, col_half, _ = unit
        downs = [None] * 4
        for r in range(2):
            line = rows * 8 + 2 * row_part + r
            row_ids = ids_rows[line].reshape(16, 8, 128)
            best = row_best[line].reshape(16, 8, 128)
            for c in range(4):
                values = sim[128 * r:128 * r + 128, 128 * c:128 * c + 128].reshape(16, 8, 128)
                kept = jnp.where(row_ids == ids_cols[cols * 8 + 4 * col_half + c], values, jnp.float32(-1.0))
                down = jnp.max(kept, axis=0)
                downs[c] = down if downs[c] is None else jnp.maximum(downs[c], down)
                best = jnp.maximum(best, kept)
            row_best[line] = best.reshape(128, 128)
        old = [col_best[cols * 8 + 4 * col_half + c] for c in range(4)]
        for c in range(4):
            col_best[cols * 8 + 4 * col_half + c] = jnp.maximum(old[c], downs[c])

    def lines(line):
        row_line[line] = jnp.max(row_best[line].T, axis=0, keepdims=True)

    def wait_shared(m):
        for s in range(SLOTS):
            @pl.when(need[s] == 1)
            def _():
                for half in range(2):
                    shared(s, 2 * m + half).wait_recv()

    def own_block(k):
        def came(at, copy, t):
            @pl.when(k == at)
            def _():
                copy.wait_recv()
                own_half_ready(t)

        came(2, swap(1, 0), 2)
        came(4, swap(1, 1), 3)
        came(5, swap(2, 0), 4)
        for half in range(2):
            @pl.when(k == 6 + half)
            def _():
                relay_in(half).wait_recv()
                relay_out(half).start()
        came(8, swap(2, 1), 5)
        came(10, relay_out(0), 6)
        came(11, relay_out(1), 7)

    def pass_on(k):
        receive(1, k - 1)
        send_held(k - 1)
        pl.when(k % 2 == 0)(lambda: give_held(1, k - 1))

    def take(t):
        receive(2, t)
        pl.when(t % 2 == 1)(lambda: give_held(2, t))

    @pl.loop(1, START)
    def _(k):
        pass_on(k)
        own_block(k)
        pl.when(k >= 4)(lambda: take(k - 4))

    @pl.loop(0, 3)
    def _(q):
        pl.when(q == 0)(lambda: wait_shared(0))
        wait_shared(q + 1)
        count = pair_count * jnp.where(q == 2, 4, 2) + h * pick((2, 1, 3), q)
        rounds = (count + 1) // 2

        def unit(i):
            return unit_of(q, jnp.minimum(i, count - 1))

        multiply(sim_one, unit(0))
        drop_self(sim_one, unit(0))

        @pl.loop(0, jnp.where(q == 2, rounds, jnp.maximum(rounds, 4)))
        def _(i):
            k = START + 4 * q + i

            @pl.when(jnp.logical_and(q < 2, jnp.logical_and(i < 4, k < STEPS + 4)))
            def _():
                pl.when(k <= STEPS)(lambda: pass_on(k))
                take(k - 4)

            @pl.when(i < rounds)
            def _():
                multiply(sim_two, unit(2 * i + 1))
                reduce(sim_one, unit(2 * i))
                drop_self(sim_two, unit(2 * i + 1))
                multiply(sim_one, unit(2 * i + 2))
                reduce(sim_two, unit(2 * i + 1))
                drop_self(sim_one, unit(2 * i + 2))

        @pl.when(q != 1)
        def _():
            @pl.loop(0, SLOTS * 4)
            def _(i):
                line = (i // 4) * 8 + i % 4 + 2 * q
                pl.when(pick(need, i // 4) == 1)(lambda: lines(line))

    def result(s, half):
        return remote(part.at[s * 2 + half], parts_got.at[pick(place, s) * 2 + h], r_send.at[s * 2 + half],
                      r_recv.at[pick(place, s) * 2 + h], (owner_grp, pick(held, s) * 2 + half))

    @pl.loop(0, SLOTS)
    def _(s):
        for t in range(4):
            z_of = (z + REL[t]) % 4
            for core in range(2):
                j = s * 8 + 2 * t + core
                both = jnp.maximum(row_line[j], jnp.max(col_best[j], axis=0, keepdims=True))
                part[s * 2 + z_of // 2, pl.ds(2 * (z_of % 2) + core, 1), :] = both
        for half in range(2):
            keep_it = jnp.logical_and(s == 0, jnp.logical_and(mine, zh == half))
            pl.when(jnp.logical_not(keep_it))(lambda half=half: result(s, half).start())

            @pl.when(keep_it)
            def _():
                parts_got[h] = part[half]

    ids_copy.wait_send()

    @pl.loop(0, 2)
    def _(half):
        for copy in (swap(1, half), swap(2, half), relay_in(half), relay_out(half)):
            copy.wait_send()

    @pl.loop(0, STEPS)
    def _(t):
        for d in range(4):
            forward(d, t).wait_send()

    @pl.loop(0, 8)
    def _(t):
        for s in range(SLOTS):
            pl.when(sibling_need[s] == 1)(lambda s=s: share(s, t).wait_send())

    @pl.loop(0, 2 * SLOTS)
    def _(k):
        got = remote(parts_got.at[k], parts_got.at[k], r_send.at[k], r_recv.at[k], sibling)
        pl.when(jnp.logical_not(jnp.logical_and(mine, h == k)))(got.wait_recv)

    out[...] = jnp.max(parts_got[...], axis=0)

    @pl.loop(0, SLOTS)
    def _(s):
        for half in range(2):
            keep_it = jnp.logical_and(s == 0, jnp.logical_and(mine, zh == half))
            pl.when(jnp.logical_not(keep_it))(lambda half=half: result(s, half).wait_send())


def on_device(embeddings, cluster_ids):
    emb = embeddings.reshape(4, 128, D)
    ids = cluster_ids.reshape(128, 128)
    dma = pltpu.SemaphoreType.DMA
    best = pl.pallas_call(
        kernel,
        out_shape=jax.ShapeDtypeStruct((4, 128), jnp.float32),
        in_specs=[pl.BlockSpec(memory_space=pl.ANY), pl.BlockSpec(memory_space=pltpu.VMEM)],
        out_specs=pl.BlockSpec(memory_space=pltpu.VMEM),
        scratch_shapes=[
            pltpu.VMEM((SLOTS, 1024, D), jnp.bfloat16),
            pltpu.VMEM((3, 128, D), jnp.bfloat16),
            pltpu.VMEM((4, 128, D), jnp.float32),
            pltpu.VMEM((128, D), jnp.bfloat16),
            pltpu.VMEM((128, 128), jnp.int32),
            pltpu.VMEM((SLOTS * 8, 128, 128), jnp.float32),
            pltpu.VMEM((SLOTS * 8, 8, 128), jnp.float32),
            pltpu.VMEM((256, 512), jnp.float32),
            pltpu.VMEM((256, 512), jnp.float32),
            pltpu.VMEM((SLOTS * 8, 128, 128), jnp.float32),
            pltpu.VMEM((SLOTS * 8, 8, 128), jnp.float32),
            pltpu.VMEM((SLOTS * 8, 1, 128), jnp.float32),
            pltpu.VMEM((2 * SLOTS, 4, 128), jnp.float32),
            pltpu.VMEM((2 * SLOTS, 4, 128), jnp.float32),
            dma((4,)), dma, dma, dma((3, 2)), dma((3, 2)), dma((2, 2)), dma((2,)), dma((4, STEPS)), dma((4, STEPS)),
            dma((SLOTS, 8)), dma((SLOTS, 8)), dma((2 * SLOTS,)), dma((2 * SLOTS,)),
        ],
        compiler_params=pltpu.CompilerParams(
            collective_id=0, has_side_effects=True, vmem_limit_bytes=60 * 1024 * 1024),
        cost_estimate=pl.CostEstimate(flops=7 * 10**9, bytes_accessed=2 * 10**6, transcendentals=0),
        name="best_match",
    )(emb, ids)
    return best.reshape(1, 512)


def solution(mesh):
    placed = (P(None, "grp", "blk", None, None), P("grp", None))
    return jax.shard_map(
        on_device, mesh=mesh, in_specs=placed, out_specs=P("grp", "blk"), check_vma=False
    )
```

```python
import functools

import jax
import jax.numpy as jnp
from jax import lax
from jax.experimental import pallas as pl
from jax.experimental.pallas import tpu as pltpu
from jax.sharding import PartitionSpec as P

MESH = pl.DeviceIdType.MESH
D = 768
SLOTS = 5
PIECE = 32
STEPS = 16

SRC = [[0, 3, 0, 0], [3, 0, 0, 0], [0, 0, 4, 0], [0, 0, 4, 0], [0, 4, 1, 0], [4, 0, 2, 0], [0, 3, 0, 0], [3, 0, 0, 0],
       [3, 0, 0, 3], [0, 3, 0, 3], [2, 4, 0, 0], [4, 1, 0, 0], [2, 0, 4, 0], [0, 1, 4, 0], [4, 0, 0, 3], [0, 4, 0, 3]]
DEP = [[1, 1, 1, 2], [1, 1, 1, 2], [1, 2, 1, 1], [2, 1, 1, 1], [1, 2, 2, 1], [2, 1, 2, 1], [1, 2, 1, 2], [2, 1, 1, 2],
       [2, 2, 1, 2], [2, 2, 1, 2], [2, 1, 2, 1], [1, 2, 2, 1], [2, 1, 1, 1], [1, 2, 1, 1], [2, 1, 1, 1], [1, 2, 1, 1]]
BLK = [[1, 3, 4, 8], [2, 0, 5, 9], [3, 5, 6, 14], [4, 2, 7, 15], [5, 11, 12, 0], [10, 4, 13, 1], [7, 1, 10, 14],
       [0, 6, 11, 15], [13, 7, 12, 5], [6, 12, 13, 4], [8, 9, 2, 6], [8, 9, 3, 7], [14, 15, 0, 8], [14, 15, 1, 9],
       [11, 13, 2, 10], [12, 10, 3, 11]]
IDX = [[1, 1, 1, 1], [1, 1, 1, 1], [2, 2, 1, 1], [2, 2, 1, 1], [3, 1, 1, 2], [1, 3, 1, 2], [2, 3, 2, 2], [3, 2, 2, 2],
       [2, 3, 2, 4], [3, 3, 3, 4], [2, 2, 3, 4], [3, 3, 3, 4], [3, 3, 4, 4], [4, 4, 4, 4], [3, 4, 4, 3], [4, 4, 4, 4]]
HOLD = [[0, 1, 4, 7, 12], [1, 0, 5, 6, 13], [2, 1, 3, 10, 14], [3, 0, 2, 11, 15], [4, 0, 3, 5, 9], [5, 1, 2, 4, 8],
        [6, 2, 7, 9, 10], [7, 3, 6, 8, 11], [8, 0, 10, 11, 12], [9, 1, 10, 11, 13], [10, 5, 6, 14, 15], [11, 4, 7, 14, 15],
        [12, 4, 8, 9, 15], [13, 5, 8, 9, 14], [14, 2, 6, 12, 13], [15, 3, 7, 12, 13]]
PAIRS = [[[(1, 3), (1, 4), (3, 4)], [(0, 1), (0, 2), (1, 2)]], [[(2, 1), (2, 4), (1, 4)], [(0, 1), (0, 3), (3, 4)]],
         [[(1, 3), (3, 4), (2, 3), (2, 4)], [(0, 1), (0, 2), (1, 2)]],
         [[(2, 3), (2, 1), (1, 3)], [(0, 3), (3, 4), (0, 1)]], [[(4, 0), (4, 1), (0, 2), (1, 2)], [(0, 3), (1, 3)]],
         [[(2, 0), (4, 1), (2, 1)], [(0, 1), (0, 3), (1, 3)]], [[(1, 3), (1, 4), (3, 4)], [(0, 3), (2, 0), (2, 1)]],
         [[(2, 3), (2, 4), (3, 4)], [(2, 0), (1, 2), (1, 0)]],
         [[(2, 3), (2, 1), (0, 1), (3, 1)], [(4, 2), (4, 0), (2, 0)]],
         [[(4, 1), (4, 0), (4, 3), (1, 3)], [(1, 0), (1, 2), (0, 2)]],
         [[(3, 4), (3, 1), (4, 1)], [(2, 0), (1, 2), (1, 0)]], [[(1, 0), (3, 1), (3, 2)], [(4, 0), (4, 2), (2, 0)]],
         [[(3, 4), (4, 1), (0, 1)], [(4, 0), (4, 2), (0, 2)]], [[(3, 4), (4, 1), (1, 2)], [(4, 0), (4, 2), (0, 2)]],
         [[(3, 4), (3, 1), (4, 1)], [(2, 0), (1, 2), (1, 0)]], [[(3, 4), (3, 1), (4, 1)], [(3, 2), (2, 1), (2, 0)]]]
NEED = [[[1, 3, 4], [0, 1, 2]], [[1, 2, 4], [0, 1, 3, 4]], [[1, 2, 3, 4], [0, 1, 2]], [[1, 2, 3], [0, 1, 3, 4]],
        [[0, 1, 2, 4], [0, 1, 3]], [[0, 1, 2, 4], [0, 1, 3]], [[1, 3, 4], [0, 1, 2, 3]], [[2, 3, 4], [0, 1, 2]],
        [[0, 1, 2, 3], [0, 2, 4]], [[0, 1, 3, 4], [0, 1, 2]], [[1, 3, 4], [0, 1, 2]], [[0, 1, 2, 3], [0, 2, 4]],
        [[0, 1, 3, 4], [0, 2, 4]], [[1, 2, 3, 4], [0, 2, 4]], [[1, 3, 4], [0, 1, 2]], [[1, 3, 4], [0, 1, 2, 3]]]

REL = (0, 3, 1, 2)


def word(digits, base):
    total = 0
    for digit in reversed(digits):
        total = total * base + digit
    return total


def look_up(index, words):
    got = jnp.int32(words[0])
    for k in range(1, len(words)):
        got = jnp.where(index == k, jnp.int32(words[k]), got)
    return got


def digits_of(value, base, count):
    out = []
    for _ in range(count):
        out.append(value % base)
        value = value // base
    return out


def pick(values, index):
    got = values[0]
    for k in range(1, len(values)):
        got = jnp.where(index == k, values[k], got)
    return got


def kernel(emb, ids_in, out, x, xt, units, stage, ids_got, ids_rows, ids_cols, row_best, col_best, row_line, part, parts_got,
           relay,
           load_sem, id_send, id_recv, z_send, z_recv, relay_send, relay_recv, f_send, f_recv, c_send, c_recv, r_send, r_recv):
    grp, blk = lax.axis_index("grp"), lax.axis_index("blk")
    h, zl = grp % 2, grp // 2
    p, zh = blk // 2, blk % 2
    z = zh * 2 + zl
    px, py = p % 4, p // 4

    def device(z_of, core, chip):
        return ((z_of % 2) * 2 + core, chip * 2 + z_of // 2)

    def group_of(z_of):
        return (z_of % 2) * 2 + z_of // 2

    near = [py * 4 + (px + 1) % 4, py * 4 + (px + 3) % 4, ((py + 1) % 4) * 4 + px, ((py + 3) % 4) * 4 + px]
    first = look_up(p, [word(SRC[c], 8) + 4096 * word(DEP[c], 4) for c in range(16)])
    src = digits_of(first, 8, 4)
    dep = digits_of(first // 4096, 4, 4)
    held = [p] + digits_of(look_up(p, [word(BLK[c], 16) for c in range(16)]), 16, 4)
    third = look_up(p, [word(IDX[c], 8) + 4096 * word(HOLD[c][1:], 16) for c in range(16)])
    place = [jnp.int32(0)] + digits_of(third, 8, 4)
    holders = [p] + digits_of(third // 4096, 16, 4)
    lists = []
    for c in range(16):
        for core in range(2):
            flat = [slot for pair in PAIRS[c][core] for slot in pair]
            lists.append(len(PAIRS[c][core]) + 8 * word(flat + [0] * (8 - len(flat)), 8))
    todo = look_up(p * 2 + h, lists)
    pair_count = todo % 8
    todo = digits_of(todo // 8, 8, 8)

    needs = [[sum(1 << slot for slot in NEED[c][core]) for core in range(2)] for c in range(16)]
    need = digits_of(look_up(p * 2 + h, [needs[c][core] for c in range(16) for core in range(2)]), 2, SLOTS)
    sibling_need = digits_of(look_up(p * 2 + h, [needs[c][1 - core] for c in range(16) for core in range(2)]), 2, SLOTS)

    sibling = device(z, 1 - h, p)
    owner_grp = zl * 2 + zh
    mine = h == zh

    loads = []
    for k, rel in enumerate((0, 1, 3, 2)):
        loads.append(pltpu.make_async_copy(emb.at[group_of((z + rel) % 4)], stage.at[k], load_sem.at[k]))
        loads[-1].start()

    barrier = pltpu.get_barrier_semaphore()
    for rel in (1, 3):
        pl.semaphore_signal(barrier, inc=1, device_id=device((z + rel) % 4, h, p), device_id_type=MESH)
    for d in range(4):
        pl.semaphore_signal(barrier, inc=1, device_id=device(z, h, near[d]), device_id_type=MESH)
    pl.semaphore_signal(barrier, inc=1, device_id=sibling, device_id_type=MESH)
    from_z = 2 * h + zl
    for k in range(SLOTS):
        for core in range(2):
            def tell():
                pl.semaphore_signal(barrier, inc=1, device_id=device(from_z, core, holders[k]), device_id_type=MESH)
            if k == 0:
                pl.when(jnp.logical_not(jnp.logical_and(mine, h == core)))(tell)
            else:
                tell()

    def normalise(k):
        loads[k].wait()
        v = stage[k]
        total = jnp.sum(v * v, axis=-1, keepdims=True)
        return (v / jnp.sqrt(total + 1e-06)).astype(jnp.bfloat16)

    own_rows = pl.multiple_of(h * 128, 128)
    x[0, pl.ds(own_rows, 128), :] = normalise(0)
    pl.semaphore_wait(barrier, jnp.where(mine, 16, 17))

    def remote(src_ref, dst_ref, send_sem, recv_sem, to):
        return pltpu.make_async_remote_copy(
            src_ref=src_ref, dst_ref=dst_ref, send_sem=send_sem, recv_sem=recv_sem, device_id=to, device_id_type=MESH)

    def part_rows(t):
        return pl.ds(pl.multiple_of((t // 4) * 256 + h * 128 + (t % 4) * PIECE, PIECE), PIECE)

    def forward(d, t):
        rows = part_rows(t)
        return remote(x.at[src[d], rows, :], x.at[1 + (d ^ 1), rows, :], f_send.at[d, t], f_recv.at[d ^ 1, t],
                      device(z, h, near[d]))

    def arrival(s, t):
        rows = part_rows(t)
        return remote(x.at[s, rows, :], x.at[s, rows, :], f_send.at[s - 1, t], f_recv.at[s - 1, t],
                      device(z, h, near[s - 1]))

    def swap(k, half):
        rows = pl.ds(pl.multiple_of(k * 256 + h * 128 + half * 64, 64), 64)
        return remote(units.at[k - 1, pl.ds(half * 64, 64), :], x.at[0, rows, :], z_send.at[k - 1, half],
                      z_recv.at[k - 1, half], device((z + (1, 3, 2)[k - 1]) % 4, h, p))

    between = device((z + jnp.where(h == 0, 1, 3)) % 4, h, p)

    def relay_in(half):
        rows = pl.ds(half * 64, 64)
        return remote(units.at[2, rows, :], relay.at[rows, :], relay_send.at[0, half], relay_recv.at[half], between)

    def relay_out(half):
        rows = pl.ds(pl.multiple_of(3 * 256 + h * 128 + half * 64, 64), 64)
        return remote(relay.at[pl.ds(half * 64, 64), :], x.at[0, rows, :], relay_send.at[1, half], z_recv.at[2, half],
                      between)

    def share_rows(t, core):
        return pl.ds(pl.multiple_of((t // 2) * 256 + core * 128 + (t % 2) * 64, 64), 64)

    def share(s, t):
        rows = share_rows(t, h)
        return remote(x.at[s, rows, :], x.at[s, rows, :], c_send.at[s, t], c_recv.at[s, t], sibling)

    def shared(s, t):
        rows = share_rows(t, 1 - h)
        return remote(x.at[s, rows, :], x.at[s, rows, :], c_send.at[s, t], c_recv.at[s, t], sibling)

    def give(s, t):
        pl.when(sibling_need[s] == 1)(lambda: share(s, t).start())

    def send_own(t):
        for d in range(4):
            pl.when(src[d] == 0)(lambda d=d: forward(d, t).start())

    def send_held(t):
        for d in range(4):
            pl.when(src[d] != 0)(lambda d=d: forward(d, t).start())

    def receive(links, t):
        for s in range(1, SLOTS):
            pl.when(dep[s - 1] == links)(lambda s=s: arrival(s, t).wait_recv())

    def give_held(links, t):
        for s in range(1, SLOTS):
            pl.when(dep[s - 1] == links)(lambda s=s: give(s, t // 2))

    for t in range(4):
        send_own(t)
    units[0] = normalise(1)
    for half in range(2):
        swap(1, half).start()
    units[1] = normalise(2)
    for half in range(2):
        swap(2, half).start()
    units[2] = normalise(3)
    for half in range(2):
        relay_in(half).start()
    ids_copy = remote(ids_in, ids_got, id_send, id_recv, sibling)
    ids_copy.start()
    give(0, 0)
    give(0, 1)
    row_best[...] = jnp.full_like(row_best, -1.0)
    col_best[...] = jnp.full_like(col_best, -1.0)
    row_line[...] = jnp.full_like(row_line, -1.0)

    ids_copy.wait_recv()
    ids_cols[...] = jnp.zeros_like(ids_cols)
    for s in range(SLOTS):
        for t in range(4):
            for core in range(2):
                unit = held[s] * 8 + 2 * ((z + REL[t]) % 4) + core
                got = jnp.where(mine, ids_in[pl.ds(unit, 1), :], ids_got[pl.ds(unit, 1), :])
                ids_cols[pl.ds(s * 8 + 2 * t + core, 1), :] = got.astype(jnp.float32)
    turned = ids_cols[...].T
    for j in range(SLOTS * 8):
        ids_rows[j] = jnp.broadcast_to(turned[:, j:j + 1], (128, 128))

    def strip(a, t, b, count, diagonal=False):
        sim = lax.dot_general(x[a, 256 * t:256 * t + 256, :], xt[b, :, 0:256 * count], (((1,), (0,)), ((), ())),
                              preferred_element_type=jnp.float32)
        for r in range(4):
            unit, first_row = a * 8 + 2 * t + r // 2, 64 * (r % 2)
            row_ids = ids_rows[unit, first_row:first_row + 64]
            best = row_best[unit, first_row:first_row + 64]
            for c in range(2 * count):
                keep = row_ids == ids_cols[pl.ds(b * 8 + c, 1), :]
                if diagonal and c // 2 == t:
                    row = lax.broadcasted_iota(jnp.int32, (64, 128), 0) + 64 * r
                    col = lax.broadcasted_iota(jnp.int32, (64, 128), 1) + 128 * (c % 2)
                    keep = jnp.logical_and(keep, row != col)
                kept = jnp.where(keep, sim[64 * r:64 * r + 64, 128 * c:128 * c + 128], jnp.float32(-1.0))
                down = jnp.max(kept.reshape(8, 8, 128), axis=0)
                col_best[b * 8 + c] = jnp.maximum(col_best[b * 8 + c], down)
                best = jnp.maximum(best, kept)
            row_best[unit, first_row:first_row + 64] = best

    def compare(t, j):
        a, b = todo[0], todo[1]
        for k in range(1, 4):
            a = jnp.where(j == k, todo[2 * k], a)
            b = jnp.where(j == k, todo[2 * k + 1], b)
        strip(a, t, b, t + 1)
        if t:
            strip(b, t, a, t)

    def finish_rows(t):
        pl.when(h == 1)(lambda: strip(0, t, 0, t + 1, diagonal=True))
        for s in range(SLOTS):
            @pl.when(need[s] == 1)
            def _():
                for core in range(2):
                    unit = s * 8 + 2 * t + core
                    row_line[unit:unit + 1, :] = jnp.max(row_best[unit].T, axis=0, keepdims=True)

    def wait_shared(m):
        for s in range(SLOTS):
            @pl.when(need[s] == 1)
            def _():
                for half in range(2):
                    shared(s, 2 * m + half).wait_recv()

    def turn(m):
        @pl.loop(0, SLOTS)
        def _(s):
            @pl.when(pick(need, s) == 1)
            def _():
                xt[s, :, 256 * m:256 * m + 256] = x[s, 256 * m:256 * m + 256, :].T

    def own_half_ready(m, half):
        send_own(4 * m + 2 * half)
        send_own(4 * m + 2 * half + 1)
        give(0, 2 * m + half)

    def own_block(k):
        @pl.when(k == 2)
        def _():
            swap(1, 0).wait_recv()
            own_half_ready(1, 0)

        @pl.when(k == 4)
        def _():
            swap(1, 1).wait_recv()
            own_half_ready(1, 1)
            swap(2, 0).wait_recv()
            own_half_ready(2, 0)

        @pl.when(k == 6)
        def _():
            relay_in(0).wait_recv()
            relay_out(0).start()

        @pl.when(k == 7)
        def _():
            relay_in(1).wait_recv()
            relay_out(1).start()

        @pl.when(k == 8)
        def _():
            swap(2, 1).wait_recv()
            own_half_ready(2, 1)

        @pl.when(k == 10)
        def _():
            relay_out(0).wait_recv()
            own_half_ready(3, 0)

        @pl.when(k == 11)
        def _():
            relay_out(1).wait_recv()
            own_half_ready(3, 1)

    def pass_on(k):
        receive(1, k - 1)
        send_held(k - 1)
        pl.when(k % 2 == 0)(lambda: give_held(1, k - 1))

    def take(t):
        receive(2, t)
        pl.when(t % 2 == 1)(lambda: give_held(2, t))

    @pl.loop(1, 9)
    def _(k):
        pass_on(k)
        own_block(k)
        pl.when(k >= 4)(lambda: take(k - 4))

    for m in range(2):
        @pl.loop(9 + 4 * m, 13 + 4 * m)
        def _(k):
            j = k - 9 - 4 * m
            pass_on(k)
            if m == 0:
                own_block(k)

            @pl.when(j == 0)
            def _():
                wait_shared(m)
                turn(m)
            pl.when(j < pair_count)(lambda: compare(m, j))
            take(k - 4)
        finish_rows(m)

    wait_shared(2)
    turn(2)

    @pl.loop(0, 4)
    def _(j):
        pl.when(j < pair_count)(lambda: compare(2, j))
        pl.when(j < 3)(lambda: take(13 + j))
    finish_rows(2)
    wait_shared(3)
    turn(3)

    @pl.loop(0, pair_count)
    def _(j):
        compare(3, j)
    finish_rows(3)

    for s in range(SLOTS):
        for t in range(4):
            z_of = (z + REL[t]) % 4
            for core in range(2):
                j = s * 8 + 2 * t + core
                both = jnp.maximum(row_line[j:j + 1, :], jnp.max(col_best[j], axis=0, keepdims=True))
                part[s * 2 + z_of // 2, pl.ds(2 * (z_of % 2) + core, 1), :] = both
        for half in range(2):
            copy = remote(part.at[s * 2 + half], parts_got.at[place[s] * 2 + h], r_send.at[s * 2 + half],
                          r_recv.at[place[s] * 2 + h], (owner_grp, held[s] * 2 + half))
            if s == 0:
                keep_it = jnp.logical_and(mine, zh == half)
                pl.when(jnp.logical_not(keep_it))(copy.start)

                @pl.when(keep_it)
                def _():
                    parts_got[h] = part[half]
            else:
                copy.start()

    ids_copy.wait_send()
    for half in range(2):
        for copy in (swap(1, half), swap(2, half), relay_in(half), relay_out(half)):
            copy.wait_send()
    for d in range(4):
        for t in range(STEPS):
            forward(d, t).wait_send()
    for s in range(SLOTS):
        for t in range(8):
            pl.when(sibling_need[s] == 1)(lambda s=s, t=t: share(s, t).wait_send())
    best = None
    for k in range(2 * SLOTS):
        got = remote(parts_got.at[k], parts_got.at[k], r_send.at[k], r_recv.at[k], sibling)
        if k < 2:
            pl.when(jnp.logical_not(jnp.logical_and(mine, h == k)))(got.wait_recv)
        else:
            got.wait_recv()
        best = parts_got[k] if best is None else jnp.maximum(best, parts_got[k])
    out[...] = best

    for s in range(SLOTS):
        for half in range(2):
            copy = remote(part.at[s * 2 + half], parts_got.at[place[s] * 2 + h], r_send.at[s * 2 + half],
                          r_recv.at[place[s] * 2 + h], (owner_grp, held[s] * 2 + half))
            if s == 0:
                pl.when(jnp.logical_not(jnp.logical_and(mine, zh == half)))(copy.wait_send)
            else:
                copy.wait_send()


def on_device(embeddings, cluster_ids):
    emb = embeddings.reshape(4, 128, D)
    ids = cluster_ids.reshape(128, 128)
    dma = pltpu.SemaphoreType.DMA
    best = pl.pallas_call(
        kernel,
        out_shape=jax.ShapeDtypeStruct((4, 128), jnp.float32),
        in_specs=[pl.BlockSpec(memory_space=pl.ANY), pl.BlockSpec(memory_space=pltpu.VMEM)],
        out_specs=pl.BlockSpec(memory_space=pltpu.VMEM),
        scratch_shapes=[
            pltpu.VMEM((SLOTS, 1024, D), jnp.bfloat16),
            pltpu.VMEM((SLOTS, D, 1024), jnp.bfloat16),
            pltpu.VMEM((3, 128, D), jnp.bfloat16),
            pltpu.VMEM((4, 128, D), jnp.float32),
            pltpu.VMEM((128, 128), jnp.int32),
            pltpu.VMEM((SLOTS * 8, 128, 128), jnp.float32),
            pltpu.VMEM((128, 128), jnp.float32),
            pltpu.VMEM((SLOTS * 8, 128, 128), jnp.float32),
            pltpu.VMEM((SLOTS * 8, 8, 128), jnp.float32),
            pltpu.VMEM((SLOTS * 8, 128), jnp.float32),
            pltpu.VMEM((2 * SLOTS, 4, 128), jnp.float32),
            pltpu.VMEM((2 * SLOTS, 4, 128), jnp.float32),
            pltpu.VMEM((128, D), jnp.bfloat16),
            dma((4,)), dma, dma, dma((3, 2)), dma((3, 2)), dma((2, 2)), dma((2,)), dma((4, STEPS)), dma((4, STEPS)),
            dma((SLOTS, 8)), dma((SLOTS, 8)), dma((2 * SLOTS,)), dma((2 * SLOTS,)),
        ],
        compiler_params=pltpu.CompilerParams(
            collective_id=0, has_side_effects=True, vmem_limit_bytes=60 * 1024 * 1024),
        cost_estimate=pl.CostEstimate(flops=7 * 10**9, bytes_accessed=2 * 10**6, transcendentals=0),
        name="best_match",
    )(emb, ids)
    return best.reshape(1, 512)


def solution(mesh):
    placed = (P(None, "grp", "blk", None, None), P("grp", None))
    return jax.shard_map(
        on_device, mesh=mesh, in_specs=placed, out_specs=P("grp", "blk"), check_vma=False
    )
```

```python
import functools

import jax
import jax.numpy as jnp
from jax import lax
from jax.experimental import pallas as pl
from jax.experimental.pallas import tpu as pltpu
from jax.sharding import PartitionSpec as P

MESH = pl.DeviceIdType.MESH
D = 768
SLOTS = 5
PIECE = 32
STEPS = 16
START = 13

SRC = [[0, 3, 0, 0], [3, 0, 0, 0], [0, 0, 4, 0], [0, 0, 4, 0], [0, 4, 1, 0], [4, 0, 2, 0], [0, 3, 0, 0], [3, 0, 0, 0],
       [3, 0, 0, 3], [0, 3, 0, 3], [2, 4, 0, 0], [4, 1, 0, 0], [2, 0, 4, 0], [0, 1, 4, 0], [4, 0, 0, 3], [0, 4, 0, 3]]
DEP = [[1, 1, 1, 2], [1, 1, 1, 2], [1, 2, 1, 1], [2, 1, 1, 1], [1, 2, 2, 1], [2, 1, 2, 1], [1, 2, 1, 2], [2, 1, 1, 2],
       [2, 2, 1, 2], [2, 2, 1, 2], [2, 1, 2, 1], [1, 2, 2, 1], [2, 1, 1, 1], [1, 2, 1, 1], [2, 1, 1, 1], [1, 2, 1, 1]]
BLK = [[1, 3, 4, 8], [2, 0, 5, 9], [3, 5, 6, 14], [4, 2, 7, 15], [5, 11, 12, 0], [10, 4, 13, 1], [7, 1, 10, 14],
       [0, 6, 11, 15], [13, 7, 12, 5], [6, 12, 13, 4], [8, 9, 2, 6], [8, 9, 3, 7], [14, 15, 0, 8], [14, 15, 1, 9],
       [11, 13, 2, 10], [12, 10, 3, 11]]
IDX = [[1, 1, 1, 1], [1, 1, 1, 1], [2, 2, 1, 1], [2, 2, 1, 1], [3, 1, 1, 2], [1, 3, 1, 2], [2, 3, 2, 2], [3, 2, 2, 2],
       [2, 3, 2, 4], [3, 3, 3, 4], [2, 2, 3, 4], [3, 3, 3, 4], [3, 3, 4, 4], [4, 4, 4, 4], [3, 4, 4, 3], [4, 4, 4, 4]]
HOLD = [[0, 1, 4, 7, 12], [1, 0, 5, 6, 13], [2, 1, 3, 10, 14], [3, 0, 2, 11, 15], [4, 0, 3, 5, 9], [5, 1, 2, 4, 8],
        [6, 2, 7, 9, 10], [7, 3, 6, 8, 11], [8, 0, 10, 11, 12], [9, 1, 10, 11, 13], [10, 5, 6, 14, 15], [11, 4, 7, 14, 15],
        [12, 4, 8, 9, 15], [13, 5, 8, 9, 14], [14, 2, 6, 12, 13], [15, 3, 7, 12, 13]]
PAIRS = [[[(1, 3), (1, 4), (3, 4)], [(0, 1), (0, 2), (1, 2)]], [[(2, 1), (2, 4), (1, 4)], [(0, 1), (0, 3), (3, 4)]],
         [[(1, 3), (3, 4), (2, 3), (2, 4)], [(0, 1), (0, 2), (1, 2)]],
         [[(2, 3), (2, 1), (1, 3)], [(0, 3), (3, 4), (0, 1)]], [[(4, 0), (4, 1), (0, 2), (1, 2)], [(0, 3), (1, 3)]],
         [[(2, 0), (4, 1), (2, 1)], [(0, 1), (0, 3), (1, 3)]], [[(1, 3), (1, 4), (3, 4)], [(0, 3), (2, 0), (2, 1)]],
         [[(2, 3), (2, 4), (3, 4)], [(2, 0), (1, 2), (1, 0)]],
         [[(2, 3), (2, 1), (0, 1), (3, 1)], [(4, 2), (4, 0), (2, 0)]],
         [[(4, 1), (4, 0), (4, 3), (1, 3)], [(1, 0), (1, 2), (0, 2)]],
         [[(3, 4), (3, 1), (4, 1)], [(2, 0), (1, 2), (1, 0)]], [[(1, 0), (3, 1), (3, 2)], [(4, 0), (4, 2), (2, 0)]],
         [[(3, 4), (4, 1), (0, 1)], [(4, 0), (4, 2), (0, 2)]], [[(3, 4), (4, 1), (1, 2)], [(4, 0), (4, 2), (0, 2)]],
         [[(3, 4), (3, 1), (4, 1)], [(2, 0), (1, 2), (1, 0)]], [[(3, 4), (3, 1), (4, 1)], [(3, 2), (2, 1), (2, 0)]]]
NEED = [[[1, 3, 4], [0, 1, 2]], [[1, 2, 4], [0, 1, 3, 4]], [[1, 2, 3, 4], [0, 1, 2]], [[1, 2, 3], [0, 1, 3, 4]],
        [[0, 1, 2, 4], [0, 1, 3]], [[0, 1, 2, 4], [0, 1, 3]], [[1, 3, 4], [0, 1, 2, 3]], [[2, 3, 4], [0, 1, 2]],
        [[0, 1, 2, 3], [0, 2, 4]], [[0, 1, 3, 4], [0, 1, 2]], [[1, 3, 4], [0, 1, 2]], [[0, 1, 2, 3], [0, 2, 4]],
        [[0, 1, 3, 4], [0, 2, 4]], [[1, 2, 3, 4], [0, 2, 4]], [[1, 3, 4], [0, 1, 2]], [[1, 3, 4], [0, 1, 2, 3]]]

REL = (0, 3, 1, 2)


def word(digits, base):
    total = 0
    for digit in reversed(digits):
        total = total * base + digit
    return total


def look_up(index, words):
    got = jnp.int32(words[0])
    for k in range(1, len(words)):
        got = jnp.where(index == k, jnp.int32(words[k]), got)
    return got


def digits_of(value, base, count):
    out = []
    for _ in range(count):
        out.append(value % base)
        value = value // base
    return out


def pick(values, index):
    got = values[0]
    for k in range(1, len(values)):
        got = jnp.where(index == k, values[k], got)
    return got


def remote(src_ref, dst_ref, send_sem, recv_sem, to):
    return pltpu.make_async_remote_copy(
        src_ref=src_ref, dst_ref=dst_ref, send_sem=send_sem, recv_sem=recv_sem, device_id=to, device_id_type=MESH)


def kernel(emb, ids_in, out, x, units, stage, relay, ids_got, ids_lines, ids_rows, ids_cols, sim_one, sim_two, row_best, col_best,
           row_line, part, parts_got, load_sem, id_send, id_recv, z_send, z_recv, relay_send, relay_recv, f_send, f_recv,
           c_send, c_recv, r_send, r_recv):
    grp, blk = lax.axis_index("grp"), lax.axis_index("blk")
    h, zl = grp % 2, grp // 2
    p, zh = blk // 2, blk % 2
    z = zh * 2 + zl
    px, py = p % 4, p // 4

    def device(z_of, core, chip):
        return ((z_of % 2) * 2 + core, chip * 2 + z_of // 2)

    def load(k):
        z_of = (z + pick((0, 1, 3, 2), k)) % 4
        return pltpu.make_async_copy(emb.at[(z_of % 2) * 2 + z_of // 2], stage.at[k], load_sem.at[k])

    for k in range(4):
        load(k).start()

    near = [py * 4 + (px + 1) % 4, py * 4 + (px + 3) % 4, ((py + 1) % 4) * 4 + px, ((py + 3) % 4) * 4 + px]
    first = look_up(p, [word(SRC[c], 8) + 4096 * word(DEP[c], 4) for c in range(16)])
    src = digits_of(first, 8, 4)
    dep = digits_of(first // 4096, 4, 4)
    held = [p] + digits_of(look_up(p, [word(BLK[c], 16) for c in range(16)]), 16, 4)
    third = look_up(p, [word(IDX[c], 8) + 4096 * word(HOLD[c][1:], 16) for c in range(16)])
    place = [jnp.int32(0)] + digits_of(third, 8, 4)
    holders = [p] + digits_of(third // 4096, 16, 4)
    lists = []
    for c in range(16):
        for core in range(2):
            flat = [slot for pair in PAIRS[c][core] for slot in pair]
            lists.append(len(PAIRS[c][core]) + 8 * word(flat + [0] * (8 - len(flat)), 8))
    todo = look_up(p * 2 + h, lists)
    pair_count = todo % 8
    todo = digits_of(todo // 8, 8, 8)
    needs = [[sum(1 << slot for slot in NEED[c][core]) for core in range(2)] for c in range(16)]
    need = digits_of(look_up(p * 2 + h, [needs[c][core] for c in range(16) for core in range(2)]), 2, SLOTS)
    sibling_need = digits_of(look_up(p * 2 + h, [needs[c][1 - core] for c in range(16) for core in range(2)]), 2, SLOTS)

    sibling = device(z, 1 - h, p)
    owner_grp = zl * 2 + zh
    mine = h == zh

    barrier = pltpu.get_barrier_semaphore()
    for rel in (1, 3):
        pl.semaphore_signal(barrier, inc=1, device_id=device((z + rel) % 4, h, p), device_id_type=MESH)
    for d in range(4):
        pl.semaphore_signal(barrier, inc=1, device_id=device(z, h, near[d]), device_id_type=MESH)
    pl.semaphore_signal(barrier, inc=1, device_id=sibling, device_id_type=MESH)
    from_z = 2 * h + zl
    for k in range(SLOTS):
        for core in range(2):
            def tell():
                pl.semaphore_signal(barrier, inc=1, device_id=device(from_z, core, holders[k]), device_id_type=MESH)
            if k == 0:
                pl.when(jnp.logical_not(jnp.logical_and(mine, h == core)))(tell)
            else:
                tell()

    def normalised(k, half):
        v = stage[k, pl.ds(pl.multiple_of(half * 64, 64), 64), :]
        total = jnp.sum(v * v, axis=-1, keepdims=True)
        return (v / jnp.sqrt(total + 1e-06)).astype(jnp.bfloat16)

    def part_rows(t):
        return pl.ds(pl.multiple_of((t // 4) * 256 + h * 128 + (t % 4) * PIECE, PIECE), PIECE)

    def forward(d, t):
        rows = part_rows(t)
        return remote(x.at[src[d], rows, :], x.at[1 + (d ^ 1), rows, :], f_send.at[d, t], f_recv.at[d ^ 1, t],
                      device(z, h, near[d]))

    def arrival(s, t):
        rows = part_rows(t)
        return remote(x.at[s, rows, :], x.at[s, rows, :], f_send.at[s - 1, t], f_recv.at[s - 1, t],
                      device(z, h, near[s - 1]))

    def half_rows(t, core):
        return pl.ds(pl.multiple_of((t // 2) * 256 + core * 128 + (t % 2) * 64, 64), 64)

    def swap(k, half):
        return remote(units.at[k - 1, pl.ds(pl.multiple_of(half * 64, 64), 64), :], x.at[0, half_rows(2 * k + half, h), :],
                      z_send.at[k - 1, half], z_recv.at[k - 1, half], device((z + 2 * k - 1) % 4, h, p))

    between = device((z + jnp.where(h == 0, 1, 3)) % 4, h, p)

    def relay_in(half):
        rows = pl.ds(pl.multiple_of(half * 64, 64), 64)
        return remote(units.at[2, rows, :], relay.at[rows, :], relay_send.at[0, half], relay_recv.at[half], between)

    def relay_out(half):
        rows = pl.ds(pl.multiple_of(half * 64, 64), 64)
        return remote(relay.at[rows, :], x.at[0, half_rows(6 + half, h), :], relay_send.at[1, half], z_recv.at[2, half],
                      between)

    def share(s, t):
        rows = half_rows(t, h)
        return remote(x.at[s, rows, :], x.at[s, rows, :], c_send.at[s, t], c_recv.at[s, t], sibling)

    def shared(s, t):
        rows = half_rows(t, 1 - h)
        return remote(x.at[s, rows, :], x.at[s, rows, :], c_send.at[s, t], c_recv.at[s, t], sibling)

    def give(s, t):
        pl.when(sibling_need[s] == 1)(lambda: share(s, t).start())

    def send_own(t):
        for d in range(4):
            pl.when(src[d] == 0)(lambda d=d: forward(d, t).start())

    def send_held(t):
        for d in range(4):
            pl.when(src[d] != 0)(lambda d=d: forward(d, t).start())

    def own_half_ready(t):
        @pl.loop(0, 2)
        def _(piece):
            send_own(2 * t + piece)
        give(0, t)

    def receive(links, t):
        for s in range(1, SLOTS):
            pl.when(dep[s - 1] == links)(lambda s=s: arrival(s, t).wait_recv())

    def give_held(links, t):
        for s in range(1, SLOTS):
            pl.when(dep[s - 1] == links)(lambda s=s: give(s, t // 2))

    load(0).wait()

    @pl.loop(0, 2)
    def _(half):
        x[0, half_rows(half, h), :] = normalised(0, half)

    pl.semaphore_wait(barrier, jnp.where(mine, 16, 17))

    @pl.loop(0, 2)
    def _(half):
        own_half_ready(half)

    @pl.loop(1, 4)
    def _(k):
        load(k).wait()

        @pl.loop(0, 2)
        def _(half):
            units[k - 1, pl.ds(pl.multiple_of(half * 64, 64), 64), :] = normalised(k, half)
            pl.when(k < 3)(lambda: swap(k, half).start())
            pl.when(k == 3)(lambda: relay_in(half).start())

    ids_copy = remote(ids_in, ids_got, id_send, id_recv, sibling)
    ids_copy.start()

    row_line[...] = jnp.full_like(row_line, -1.0)

    @pl.loop(0, SLOTS * 8)
    def _(j):
        row_best[j] = jnp.full((128, 128), -1.0, jnp.float32)
        col_best[j] = jnp.full((8, 128), -1.0, jnp.float32)

    ids_copy.wait_recv()
    ids_lines[...] = jnp.zeros_like(ids_lines)

    @pl.loop(0, SLOTS)
    def _(s):
        for t in range(4):
            for core in range(2):
                unit = pick(held, s) * 8 + 2 * ((z + REL[t]) % 4) + core
                line = jnp.where(mine, ids_in[pl.ds(unit, 1), :], ids_got[pl.ds(unit, 1), :]).astype(jnp.float32)
                ids_lines[pl.ds(s * 8 + 2 * t + core, 1), :] = line
                ids_cols[s * 8 + 2 * t + core] = jnp.broadcast_to(line, (8, 128))

    turned = ids_lines[...].T
    for j in range(SLOTS * 8):
        ids_rows[j] = jnp.broadcast_to(turned[:, j:j + 1], (128, 128))

    def unit_of(q, i):
        per = jnp.where(q == 2, 4, 2)
        j, r = i // per, i % per
        own = j >= pair_count
        e = i - pair_count * per
        a = pick([todo[0], todo[2], todo[4], todo[6]], j)
        b = pick([todo[1], todo[3], todo[5], todo[7]], j)
        turned = jnp.logical_or(jnp.logical_and(q == 1, r == 1), jnp.logical_and(q == 2, r == 3))
        rows = jnp.where(own, 0, jnp.where(turned, b, a))
        cols = jnp.where(own, 0, jnp.where(turned, a, b))
        step = jnp.where(own, e, r)
        two = jnp.where(own, 1, 2)
        row_part = jnp.where(q == 0, step, jnp.where(q == 1, 2, jnp.where(step == two, 2, 3)))
        col_half = jnp.where(jnp.logical_and(q == 2, jnp.logical_or(step == 1, step == 2)), 1, 0)
        return rows, row_part, cols, col_half, jnp.logical_and(own, row_part // 2 == col_half)

    def multiply(sim, unit):
        rows, row_part, cols, col_half, _ = unit
        sim[...] = lax.dot_general(
            x[rows, pl.ds(pl.multiple_of(row_part * 256, 256), 256), :],
            x[cols, pl.ds(pl.multiple_of(col_half * 512, 512), 512), :],
            (((1,), (1,)), ((), ())), preferred_element_type=jnp.float32)

    def drop_self(sim, unit):
        _, row_part, _, _, diagonal = unit

        @pl.when(diagonal)
        def _():
            for r in range(2):
                at = (slice(128 * r, 128 * r + 128),
                      pl.ds(pl.multiple_of((row_part % 2) * 256 + 128 * r, 128), 128))
                row = lax.broadcasted_iota(jnp.int32, (128, 128), 0)
                col = lax.broadcasted_iota(jnp.int32, (128, 128), 1)
                sim[at] = jnp.where(row == col, jnp.float32(-1.0), sim[at])

    def reduce(sim, unit):
        rows, row_part, cols, col_half, _ = unit
        downs = [None] * 4
        for r in range(2):
            line = rows * 8 + 2 * row_part + r
            row_ids = ids_rows[line].reshape(16, 8, 128)
            best = row_best[line].reshape(16, 8, 128)
            for c in range(4):
                values = sim[128 * r:128 * r + 128, 128 * c:128 * c + 128].reshape(16, 8, 128)
                kept = jnp.where(row_ids == ids_cols[cols * 8 + 4 * col_half + c], values, jnp.float32(-1.0))
                down = jnp.max(kept, axis=0)
                downs[c] = down if downs[c] is None else jnp.maximum(downs[c], down)
                best = jnp.maximum(best, kept)
            row_best[line] = best.reshape(128, 128)
        old = [col_best[cols * 8 + 4 * col_half + c] for c in range(4)]
        for c in range(4):
            col_best[cols * 8 + 4 * col_half + c] = jnp.maximum(old[c], downs[c])

    def lines(first):
        for k in range(4):
            row_line[first + k] = jnp.max(row_best[first + k].T, axis=0, keepdims=True)

    def wait_shared(m):
        for s in range(SLOTS):
            @pl.when(need[s] == 1)
            def _():
                for half in range(2):
                    shared(s, 2 * m + half).wait_recv()

    def own_block(k):
        def came(at, copy, t):
            @pl.when(k == at)
            def _():
                copy.wait_recv()
                own_half_ready(t)

        came(2, swap(1, 0), 2)
        came(4, swap(1, 1), 3)
        came(5, swap(2, 0), 4)
        for half in range(2):
            @pl.when(k == 6 + half)
            def _():
                relay_in(half).wait_recv()
                relay_out(half).start()
        came(8, swap(2, 1), 5)
        came(10, relay_out(0), 6)
        came(11, relay_out(1), 7)

    def pass_on(k):
        receive(1, k - 1)
        send_held(k - 1)
        pl.when(k % 2 == 0)(lambda: give_held(1, k - 1))

    def take(t):
        receive(2, t)
        pl.when(t % 2 == 1)(lambda: give_held(2, t))

    @pl.loop(1, START)
    def _(k):
        pass_on(k)
        own_block(k)
        pl.when(k >= 4)(lambda: take(k - 4))

    @pl.loop(0, 3)
    def _(q):
        pl.when(q == 0)(lambda: wait_shared(0))
        wait_shared(q + 1)
        count = pair_count * jnp.where(q == 2, 4, 2) + h * pick((2, 1, 3), q)
        rounds = (count + 1) // 2

        def unit(i):
            return unit_of(q, jnp.minimum(i, count - 1))

        multiply(sim_one, unit(0))
        drop_self(sim_one, unit(0))

        @pl.loop(0, jnp.where(q == 2, rounds, jnp.maximum(rounds, 4)))
        def _(i):
            k = START + 4 * q + i

            @pl.when(jnp.logical_and(q < 2, jnp.logical_and(i < 4, k < STEPS + 4)))
            def _():
                pl.when(k <= STEPS)(lambda: pass_on(k))
                take(k - 4)

            @pl.when(i < rounds)
            def _():
                multiply(sim_two, unit(2 * i + 1))
                reduce(sim_one, unit(2 * i))
                drop_self(sim_two, unit(2 * i + 1))
                multiply(sim_one, unit(2 * i + 2))
                reduce(sim_two, unit(2 * i + 1))
                drop_self(sim_one, unit(2 * i + 2))

        @pl.when(q != 1)
        def _():
            @pl.loop(0, SLOTS)
            def _(s):
                pl.when(pick(need, s) == 1)(lambda: lines(s * 8 + 2 * q))

    def result(s, half):
        return remote(part.at[s * 2 + half], parts_got.at[pick(place, s) * 2 + h], r_send.at[s * 2 + half],
                      r_recv.at[pick(place, s) * 2 + h], (owner_grp, pick(held, s) * 2 + half))

    @pl.loop(0, SLOTS)
    def _(s):
        for t in range(4):
            z_of = (z + REL[t]) % 4
            for core in range(2):
                j = s * 8 + 2 * t + core
                both = jnp.maximum(row_line[j], jnp.max(col_best[j], axis=0, keepdims=True))
                part[s * 2 + z_of // 2, pl.ds(2 * (z_of % 2) + core, 1), :] = both
        for half in range(2):
            keep_it = jnp.logical_and(s == 0, jnp.logical_and(mine, zh == half))
            pl.when(jnp.logical_not(keep_it))(lambda half=half: result(s, half).start())

            @pl.when(keep_it)
            def _():
                parts_got[h] = part[half]

    ids_copy.wait_send()

    @pl.loop(0, 2)
    def _(half):
        for copy in (swap(1, half), swap(2, half), relay_in(half), relay_out(half)):
            copy.wait_send()

    @pl.loop(0, STEPS)
    def _(t):
        for d in range(4):
            forward(d, t).wait_send()

    @pl.loop(0, 8)
    def _(t):
        for s in range(SLOTS):
            pl.when(sibling_need[s] == 1)(lambda s=s: share(s, t).wait_send())

    @pl.loop(0, 2 * SLOTS)
    def _(k):
        got = remote(parts_got.at[k], parts_got.at[k], r_send.at[k], r_recv.at[k], sibling)
        pl.when(jnp.logical_not(jnp.logical_and(mine, h == k)))(got.wait_recv)

    out[...] = jnp.max(parts_got[...], axis=0)

    @pl.loop(0, SLOTS)
    def _(s):
        for half in range(2):
            keep_it = jnp.logical_and(s == 0, jnp.logical_and(mine, zh == half))
            pl.when(jnp.logical_not(keep_it))(lambda half=half: result(s, half).wait_send())


def on_device(embeddings, cluster_ids):
    emb = embeddings.reshape(4, 128, D)
    ids = cluster_ids.reshape(128, 128)
    dma = pltpu.SemaphoreType.DMA
    best = pl.pallas_call(
        kernel,
        out_shape=jax.ShapeDtypeStruct((4, 128), jnp.float32),
        in_specs=[pl.BlockSpec(memory_space=pl.ANY), pl.BlockSpec(memory_space=pltpu.VMEM)],
        out_specs=pl.BlockSpec(memory_space=pltpu.VMEM),
        scratch_shapes=[
            pltpu.VMEM((SLOTS, 1024, D), jnp.bfloat16),
            pltpu.VMEM((3, 128, D), jnp.bfloat16),
            pltpu.VMEM((4, 128, D), jnp.float32),
            pltpu.VMEM((128, D), jnp.bfloat16),
            pltpu.VMEM((128, 128), jnp.int32),
            pltpu.VMEM((128, 128), jnp.float32),
            pltpu.VMEM((SLOTS * 8, 128, 128), jnp.float32),
            pltpu.VMEM((SLOTS * 8, 8, 128), jnp.float32),
            pltpu.VMEM((256, 512), jnp.float32),
            pltpu.VMEM((256, 512), jnp.float32),
            pltpu.VMEM((SLOTS * 8, 128, 128), jnp.float32),
            pltpu.VMEM((SLOTS * 8, 8, 128), jnp.float32),
            pltpu.VMEM((SLOTS * 8, 1, 128), jnp.float32),
            pltpu.VMEM((2 * SLOTS, 4, 128), jnp.float32),
            pltpu.VMEM((2 * SLOTS, 4, 128), jnp.float32),
            dma((4,)), dma, dma, dma((3, 2)), dma((3, 2)), dma((2, 2)), dma((2,)), dma((4, STEPS)), dma((4, STEPS)),
            dma((SLOTS, 8)), dma((SLOTS, 8)), dma((2 * SLOTS,)), dma((2 * SLOTS,)),
        ],
        compiler_params=pltpu.CompilerParams(
            collective_id=0, has_side_effects=True, vmem_limit_bytes=60 * 1024 * 1024),
        cost_estimate=pl.CostEstimate(flops=7 * 10**9, bytes_accessed=2 * 10**6, transcendentals=0),
        name="best_match",
    )(emb, ids)
    return best.reshape(1, 512)


def solution(mesh):
    placed = (P(None, "grp", "blk", None, None), P("grp", None))
    return jax.shard_map(
        on_device, mesh=mesh, in_specs=placed, out_specs=P("grp", "blk"), check_vma=False
    )
```

```python
import functools

import jax
import jax.numpy as jnp
from jax import lax
from jax.experimental import pallas as pl
from jax.experimental.pallas import tpu as pltpu
from jax.sharding import PartitionSpec as P

MESH = pl.DeviceIdType.MESH
D = 768
SLOTS = 5
PIECE = 32
STEPS = 16

SRC = [[0, 3, 0, 0], [3, 0, 0, 0], [0, 0, 4, 0], [0, 0, 4, 0], [0, 4, 1, 0], [4, 0, 2, 0], [0, 3, 0, 0], [3, 0, 0, 0],
       [3, 0, 0, 3], [0, 3, 0, 3], [2, 4, 0, 0], [4, 1, 0, 0], [2, 0, 4, 0], [0, 1, 4, 0], [4, 0, 0, 3], [0, 4, 0, 3]]
DEP = [[1, 1, 1, 2], [1, 1, 1, 2], [1, 2, 1, 1], [2, 1, 1, 1], [1, 2, 2, 1], [2, 1, 2, 1], [1, 2, 1, 2], [2, 1, 1, 2],
       [2, 2, 1, 2], [2, 2, 1, 2], [2, 1, 2, 1], [1, 2, 2, 1], [2, 1, 1, 1], [1, 2, 1, 1], [2, 1, 1, 1], [1, 2, 1, 1]]
BLK = [[1, 3, 4, 8], [2, 0, 5, 9], [3, 5, 6, 14], [4, 2, 7, 15], [5, 11, 12, 0], [10, 4, 13, 1], [7, 1, 10, 14],
       [0, 6, 11, 15], [13, 7, 12, 5], [6, 12, 13, 4], [8, 9, 2, 6], [8, 9, 3, 7], [14, 15, 0, 8], [14, 15, 1, 9],
       [11, 13, 2, 10], [12, 10, 3, 11]]
IDX = [[1, 1, 1, 1], [1, 1, 1, 1], [2, 2, 1, 1], [2, 2, 1, 1], [3, 1, 1, 2], [1, 3, 1, 2], [2, 3, 2, 2], [3, 2, 2, 2],
       [2, 3, 2, 4], [3, 3, 3, 4], [2, 2, 3, 4], [3, 3, 3, 4], [3, 3, 4, 4], [4, 4, 4, 4], [3, 4, 4, 3], [4, 4, 4, 4]]
HOLD = [[0, 1, 4, 7, 12], [1, 0, 5, 6, 13], [2, 1, 3, 10, 14], [3, 0, 2, 11, 15], [4, 0, 3, 5, 9], [5, 1, 2, 4, 8],
        [6, 2, 7, 9, 10], [7, 3, 6, 8, 11], [8, 0, 10, 11, 12], [9, 1, 10, 11, 13], [10, 5, 6, 14, 15], [11, 4, 7, 14, 15],
        [12, 4, 8, 9, 15], [13, 5, 8, 9, 14], [14, 2, 6, 12, 13], [15, 3, 7, 12, 13]]
PAIRS = [[[(1, 3), (1, 4), (3, 4)], [(0, 1), (0, 2), (1, 2)]], [[(2, 1), (2, 4), (1, 4)], [(0, 1), (0, 3), (3, 4)]],
         [[(1, 3), (3, 4), (2, 3), (2, 4)], [(0, 1), (0, 2), (1, 2)]],
         [[(2, 3), (2, 1), (1, 3)], [(0, 3), (3, 4), (0, 1)]], [[(4, 0), (4, 1), (0, 2), (1, 2)], [(0, 3), (1, 3)]],
         [[(2, 0), (4, 1), (2, 1)], [(0, 1), (0, 3), (1, 3)]], [[(1, 3), (1, 4), (3, 4)], [(0, 3), (2, 0), (2, 1)]],
         [[(2, 3), (2, 4), (3, 4)], [(2, 0), (1, 2), (1, 0)]],
         [[(2, 3), (2, 1), (0, 1), (3, 1)], [(4, 2), (4, 0), (2, 0)]],
         [[(4, 1), (4, 0), (4, 3), (1, 3)], [(1, 0), (1, 2), (0, 2)]],
         [[(3, 4), (3, 1), (4, 1)], [(2, 0), (1, 2), (1, 0)]], [[(1, 0), (3, 1), (3, 2)], [(4, 0), (4, 2), (2, 0)]],
         [[(3, 4), (4, 1), (0, 1)], [(4, 0), (4, 2), (0, 2)]], [[(3, 4), (4, 1), (1, 2)], [(4, 0), (4, 2), (0, 2)]],
         [[(3, 4), (3, 1), (4, 1)], [(2, 0), (1, 2), (1, 0)]], [[(3, 4), (3, 1), (4, 1)], [(3, 2), (2, 1), (2, 0)]]]
NEED = [[[1, 3, 4], [0, 1, 2]], [[1, 2, 4], [0, 1, 3, 4]], [[1, 2, 3, 4], [0, 1, 2]], [[1, 2, 3], [0, 1, 3, 4]],
        [[0, 1, 2, 4], [0, 1, 3]], [[0, 1, 2, 4], [0, 1, 3]], [[1, 3, 4], [0, 1, 2, 3]], [[2, 3, 4], [0, 1, 2]],
        [[0, 1, 2, 3], [0, 2, 4]], [[0, 1, 3, 4], [0, 1, 2]], [[1, 3, 4], [0, 1, 2]], [[0, 1, 2, 3], [0, 2, 4]],
        [[0, 1, 3, 4], [0, 2, 4]], [[1, 2, 3, 4], [0, 2, 4]], [[1, 3, 4], [0, 1, 2]], [[1, 3, 4], [0, 1, 2, 3]]]

REL = (0, 3, 1, 2)


def word(digits, base):
    total = 0
    for digit in reversed(digits):
        total = total * base + digit
    return total


def look_up(index, words):
    got = jnp.int32(words[0])
    for k in range(1, len(words)):
        got = jnp.where(index == k, jnp.int32(words[k]), got)
    return got


def digits_of(value, base, count):
    out = []
    for _ in range(count):
        out.append(value % base)
        value = value // base
    return out


def kernel(emb, ids_in, out, x, units, stage, ids_got, ids_rows, ids_cols, row_best, col_best, row_line, part, parts_got,
           relay,
           load_sem, id_send, id_recv, z_send, z_recv, relay_send, relay_recv, f_send, f_recv, c_send, c_recv, r_send, r_recv):
    grp, blk = lax.axis_index("grp"), lax.axis_index("blk")
    h, zl = grp % 2, grp // 2
    p, zh = blk // 2, blk % 2
    z = zh * 2 + zl
    px, py = p % 4, p // 4

    def device(z_of, core, chip):
        return ((z_of % 2) * 2 + core, chip * 2 + z_of // 2)

    def group_of(z_of):
        return (z_of % 2) * 2 + z_of // 2

    near = [py * 4 + (px + 1) % 4, py * 4 + (px + 3) % 4, ((py + 1) % 4) * 4 + px, ((py + 3) % 4) * 4 + px]
    first = look_up(p, [word(SRC[c], 8) + 4096 * word(DEP[c], 4) for c in range(16)])
    src = digits_of(first, 8, 4)
    dep = digits_of(first // 4096, 4, 4)
    held = [p] + digits_of(look_up(p, [word(BLK[c], 16) for c in range(16)]), 16, 4)
    third = look_up(p, [word(IDX[c], 8) + 4096 * word(HOLD[c][1:], 16) for c in range(16)])
    place = [jnp.int32(0)] + digits_of(third, 8, 4)
    holders = [p] + digits_of(third // 4096, 16, 4)
    lists = []
    for c in range(16):
        for core in range(2):
            flat = [slot for pair in PAIRS[c][core] for slot in pair]
            lists.append(len(PAIRS[c][core]) + 8 * word(flat + [0] * (8 - len(flat)), 8))
    todo = look_up(p * 2 + h, lists)
    pair_count = todo % 8
    todo = digits_of(todo // 8, 8, 8)

    needs = [[sum(1 << slot for slot in NEED[c][core]) for core in range(2)] for c in range(16)]
    need = digits_of(look_up(p * 2 + h, [needs[c][core] for c in range(16) for core in range(2)]), 2, SLOTS)
    sibling_need = digits_of(look_up(p * 2 + h, [needs[c][1 - core] for c in range(16) for core in range(2)]), 2, SLOTS)

    sibling = device(z, 1 - h, p)
    owner_grp = zl * 2 + zh
    mine = h == zh

    loads = []
    for k, rel in enumerate((0, 1, 3, 2)):
        loads.append(pltpu.make_async_copy(emb.at[group_of((z + rel) % 4)], stage.at[k], load_sem.at[k]))
        loads[-1].start()

    barrier = pltpu.get_barrier_semaphore()
    for rel in (1, 3):
        pl.semaphore_signal(barrier, inc=1, device_id=device((z + rel) % 4, h, p), device_id_type=MESH)
    for d in range(4):
        pl.semaphore_signal(barrier, inc=1, device_id=device(z, h, near[d]), device_id_type=MESH)
    pl.semaphore_signal(barrier, inc=1, device_id=sibling, device_id_type=MESH)
    from_z = 2 * h + zl
    for k in range(SLOTS):
        for core in range(2):
            def tell():
                pl.semaphore_signal(barrier, inc=1, device_id=device(from_z, core, holders[k]), device_id_type=MESH)
            if k == 0:
                pl.when(jnp.logical_not(jnp.logical_and(mine, h == core)))(tell)
            else:
                tell()

    def normalise(k):
        loads[k].wait()
        v = stage[k]
        total = jnp.sum(v * v, axis=-1, keepdims=True)
        return (v / jnp.sqrt(total + 1e-06)).astype(jnp.bfloat16)

    own_rows = pl.multiple_of(h * 128, 128)
    x[0, pl.ds(own_rows, 128), :] = normalise(0)
    pl.semaphore_wait(barrier, jnp.where(mine, 16, 17))

    def remote(src_ref, dst_ref, send_sem, recv_sem, to):
        return pltpu.make_async_remote_copy(
            src_ref=src_ref, dst_ref=dst_ref, send_sem=send_sem, recv_sem=recv_sem, device_id=to, device_id_type=MESH)

    def part_rows(t):
        return pl.ds(pl.multiple_of((t // 4) * 256 + h * 128 + (t % 4) * PIECE, PIECE), PIECE)

    def forward(d, t):
        rows = part_rows(t)
        return remote(x.at[src[d], rows, :], x.at[1 + (d ^ 1), rows, :], f_send.at[d, t], f_recv.at[d ^ 1, t],
                      device(z, h, near[d]))

    def arrival(s, t):
        rows = part_rows(t)
        return remote(x.at[s, rows, :], x.at[s, rows, :], f_send.at[s - 1, t], f_recv.at[s - 1, t],
                      device(z, h, near[s - 1]))

    def swap(k, half):
        rows = pl.ds(pl.multiple_of(k * 256 + h * 128 + half * 64, 64), 64)
        return remote(units.at[k - 1, pl.ds(half * 64, 64), :], x.at[0, rows, :], z_send.at[k - 1, half],
                      z_recv.at[k - 1, half], device((z + (1, 3, 2)[k - 1]) % 4, h, p))

    between = device((z + jnp.where(h == 0, 1, 3)) % 4, h, p)

    def relay_in(half):
        rows = pl.ds(half * 64, 64)
        return remote(units.at[2, rows, :], relay.at[rows, :], relay_send.at[0, half], relay_recv.at[half], between)

    def relay_out(half):
        rows = pl.ds(pl.multiple_of(3 * 256 + h * 128 + half * 64, 64), 64)
        return remote(relay.at[pl.ds(half * 64, 64), :], x.at[0, rows, :], relay_send.at[1, half], z_recv.at[2, half],
                      between)

    def share_rows(t, core):
        return pl.ds(pl.multiple_of((t // 2) * 256 + core * 128 + (t % 2) * 64, 64), 64)

    def share(s, t):
        rows = share_rows(t, h)
        return remote(x.at[s, rows, :], x.at[s, rows, :], c_send.at[s, t], c_recv.at[s, t], sibling)

    def shared(s, t):
        rows = share_rows(t, 1 - h)
        return remote(x.at[s, rows, :], x.at[s, rows, :], c_send.at[s, t], c_recv.at[s, t], sibling)

    def give(s, t):
        pl.when(sibling_need[s] == 1)(lambda: share(s, t).start())

    def send_own(t):
        for d in range(4):
            pl.when(src[d] == 0)(lambda d=d: forward(d, t).start())

    def send_held(t):
        for d in range(4):
            pl.when(src[d] != 0)(lambda d=d: forward(d, t).start())

    def receive(links, t):
        for s in range(1, SLOTS):
            pl.when(dep[s - 1] == links)(lambda s=s: arrival(s, t).wait_recv())

    def give_held(links, t):
        for s in range(1, SLOTS):
            pl.when(dep[s - 1] == links)(lambda s=s: give(s, t // 2))

    for t in range(4):
        send_own(t)
    units[0] = normalise(1)
    for half in range(2):
        swap(1, half).start()
    units[1] = normalise(2)
    for half in range(2):
        swap(2, half).start()
    units[2] = normalise(3)
    for half in range(2):
        relay_in(half).start()
    ids_copy = remote(ids_in, ids_got, id_send, id_recv, sibling)
    ids_copy.start()
    give(0, 0)
    give(0, 1)
    row_best[...] = jnp.full_like(row_best, -1.0)
    col_best[...] = jnp.full_like(col_best, -1.0)
    row_line[...] = jnp.full_like(row_line, -1.0)

    ids_copy.wait_recv()
    ids_cols[...] = jnp.zeros_like(ids_cols)
    for s in range(SLOTS):
        for t in range(4):
            for core in range(2):
                unit = held[s] * 8 + 2 * ((z + REL[t]) % 4) + core
                got = jnp.where(mine, ids_in[pl.ds(unit, 1), :], ids_got[pl.ds(unit, 1), :])
                ids_cols[pl.ds(s * 8 + 2 * t + core, 1), :] = got.astype(jnp.float32)
    turned = ids_cols[...].T
    for j in range(SLOTS * 8):
        ids_rows[j] = jnp.broadcast_to(turned[:, j:j + 1], (128, 128))

    def strip(a, t, b, count, diagonal=False):
        sim = lax.dot_general(x[b, 0:256 * count, :], x[a, 256 * t:256 * t + 256, :], (((1,), (1,)), ((), ())),
                              preferred_element_type=jnp.float32)
        col_ids = [ids_cols[pl.ds(a * 8 + 2 * t + c, 1), :] for c in range(2)]
        downs = [col_best[a * 8 + 2 * t + c] for c in range(2)]
        for r in range(4 * count):
            unit, first_row = b * 8 + r // 2, 64 * (r % 2)
            row_ids = ids_rows[unit, first_row:first_row + 64]
            best = row_best[unit, first_row:first_row + 64]
            for c in range(2):
                keep = row_ids == col_ids[c]
                if diagonal and r // 4 == t:
                    row = lax.broadcasted_iota(jnp.int32, (64, 128), 0) + 64 * (r % 4)
                    col = lax.broadcasted_iota(jnp.int32, (64, 128), 1) + 128 * c
                    keep = jnp.logical_and(keep, row != col)
                kept = jnp.where(keep, sim[64 * r:64 * r + 64, 128 * c:128 * c + 128], jnp.float32(-1.0))
                downs[c] = jnp.maximum(downs[c], jnp.max(kept.reshape(8, 8, 128), axis=0))
                best = jnp.maximum(best, kept)
            row_best[unit, first_row:first_row + 64] = best
        for c in range(2):
            col_best[a * 8 + 2 * t + c] = downs[c]

    def compare(t, j):
        a, b = todo[0], todo[1]
        for k in range(1, 4):
            a = jnp.where(j == k, todo[2 * k], a)
            b = jnp.where(j == k, todo[2 * k + 1], b)
        strip(a, t, b, t + 1)
        if t:
            strip(b, t, a, t)

    def own_pair(t):
        pl.when(h == 1)(lambda: strip(0, t, 0, t + 1, diagonal=True))

    def wait_shared(m):
        for s in range(SLOTS):
            @pl.when(need[s] == 1)
            def _():
                for half in range(2):
                    shared(s, 2 * m + half).wait_recv()

    def own_half_ready(m, half):
        send_own(4 * m + 2 * half)
        send_own(4 * m + 2 * half + 1)
        give(0, 2 * m + half)

    def own_block(k):
        @pl.when(k == 2)
        def _():
            swap(1, 0).wait_recv()
            own_half_ready(1, 0)

        @pl.when(k == 4)
        def _():
            swap(1, 1).wait_recv()
            own_half_ready(1, 1)
            swap(2, 0).wait_recv()
            own_half_ready(2, 0)

        @pl.when(k == 6)
        def _():
            relay_in(0).wait_recv()
            relay_out(0).start()

        @pl.when(k == 7)
        def _():
            relay_in(1).wait_recv()
            relay_out(1).start()

        @pl.when(k == 8)
        def _():
            swap(2, 1).wait_recv()
            own_half_ready(2, 1)

        @pl.when(k == 10)
        def _():
            relay_out(0).wait_recv()
            own_half_ready(3, 0)

        @pl.when(k == 11)
        def _():
            relay_out(1).wait_recv()
            own_half_ready(3, 1)

    def pass_on(k):
        receive(1, k - 1)
        send_held(k - 1)
        pl.when(k % 2 == 0)(lambda: give_held(1, k - 1))

    def take(t):
        receive(2, t)
        pl.when(t % 2 == 1)(lambda: give_held(2, t))

    @pl.loop(1, 9)
    def _(k):
        pass_on(k)
        own_block(k)
        pl.when(k >= 4)(lambda: take(k - 4))

    for m in range(2):
        @pl.loop(9 + 4 * m, 13 + 4 * m)
        def _(k):
            j = k - 9 - 4 * m
            pass_on(k)
            if m == 0:
                own_block(k)
            pl.when(j == 0)(lambda: wait_shared(m))
            pl.when(j < pair_count)(lambda: compare(m, j))
            take(k - 4)
        own_pair(m)

    wait_shared(2)

    @pl.loop(0, 4)
    def _(j):
        pl.when(j < pair_count)(lambda: compare(2, j))
        pl.when(j < 3)(lambda: take(13 + j))
    own_pair(2)
    wait_shared(3)

    @pl.loop(0, pair_count)
    def _(j):
        compare(3, j)
    own_pair(3)

    for s in range(SLOTS):
        @pl.when(need[s] == 1)
        def _():
            for unit in range(s * 8, s * 8 + 8):
                row_line[unit:unit + 1, :] = jnp.max(row_best[unit].T, axis=0, keepdims=True)

    for s in range(SLOTS):
        for t in range(4):
            z_of = (z + REL[t]) % 4
            for core in range(2):
                j = s * 8 + 2 * t + core
                both = jnp.maximum(row_line[j:j + 1, :], jnp.max(col_best[j], axis=0, keepdims=True))
                part[s * 2 + z_of // 2, pl.ds(2 * (z_of % 2) + core, 1), :] = both
        for half in range(2):
            copy = remote(part.at[s * 2 + half], parts_got.at[place[s] * 2 + h], r_send.at[s * 2 + half],
                          r_recv.at[place[s] * 2 + h], (owner_grp, held[s] * 2 + half))
            if s == 0:
                keep_it = jnp.logical_and(mine, zh == half)
                pl.when(jnp.logical_not(keep_it))(copy.start)

                @pl.when(keep_it)
                def _():
                    parts_got[h] = part[half]
            else:
                copy.start()

    ids_copy.wait_send()
    for half in range(2):
        for copy in (swap(1, half), swap(2, half), relay_in(half), relay_out(half)):
            copy.wait_send()
    for d in range(4):
        for t in range(STEPS):
            forward(d, t).wait_send()
    for s in range(SLOTS):
        for t in range(8):
            pl.when(sibling_need[s] == 1)(lambda s=s, t=t: share(s, t).wait_send())
    best = None
    for k in range(2 * SLOTS):
        got = remote(parts_got.at[k], parts_got.at[k], r_send.at[k], r_recv.at[k], sibling)
        if k < 2:
            pl.when(jnp.logical_not(jnp.logical_and(mine, h == k)))(got.wait_recv)
        else:
            got.wait_recv()
        best = parts_got[k] if best is None else jnp.maximum(best, parts_got[k])
    out[...] = best

    for s in range(SLOTS):
        for half in range(2):
            copy = remote(part.at[s * 2 + half], parts_got.at[place[s] * 2 + h], r_send.at[s * 2 + half],
                          r_recv.at[place[s] * 2 + h], (owner_grp, held[s] * 2 + half))
            if s == 0:
                pl.when(jnp.logical_not(jnp.logical_and(mine, zh == half)))(copy.wait_send)
            else:
                copy.wait_send()


def on_device(embeddings, cluster_ids):
    emb = embeddings.reshape(4, 128, D)
    ids = cluster_ids.reshape(128, 128)
    dma = pltpu.SemaphoreType.DMA
    best = pl.pallas_call(
        kernel,
        out_shape=jax.ShapeDtypeStruct((4, 128), jnp.float32),
        in_specs=[pl.BlockSpec(memory_space=pl.ANY), pl.BlockSpec(memory_space=pltpu.VMEM)],
        out_specs=pl.BlockSpec(memory_space=pltpu.VMEM),
        scratch_shapes=[
            pltpu.VMEM((SLOTS, 1024, D), jnp.bfloat16),
            pltpu.VMEM((3, 128, D), jnp.bfloat16),
            pltpu.VMEM((4, 128, D), jnp.float32),
            pltpu.VMEM((128, 128), jnp.int32),
            pltpu.VMEM((SLOTS * 8, 128, 128), jnp.float32),
            pltpu.VMEM((128, 128), jnp.float32),
            pltpu.VMEM((SLOTS * 8, 128, 128), jnp.float32),
            pltpu.VMEM((SLOTS * 8, 8, 128), jnp.float32),
            pltpu.VMEM((SLOTS * 8, 128), jnp.float32),
            pltpu.VMEM((2 * SLOTS, 4, 128), jnp.float32),
            pltpu.VMEM((2 * SLOTS, 4, 128), jnp.float32),
            pltpu.VMEM((128, D), jnp.bfloat16),
            dma((4,)), dma, dma, dma((3, 2)), dma((3, 2)), dma((2, 2)), dma((2,)), dma((4, STEPS)), dma((4, STEPS)),
            dma((SLOTS, 8)), dma((SLOTS, 8)), dma((2 * SLOTS,)), dma((2 * SLOTS,)),
        ],
        compiler_params=pltpu.CompilerParams(
            collective_id=0, has_side_effects=True, vmem_limit_bytes=60 * 1024 * 1024),
        cost_estimate=pl.CostEstimate(flops=7 * 10**9, bytes_accessed=2 * 10**6, transcendentals=0),
        name="best_match",
    )(emb, ids)
    return best.reshape(1, 512)


def solution(mesh):
    placed = (P(None, "grp", "blk", None, None), P("grp", None))
    return jax.shard_map(
        on_device, mesh=mesh, in_specs=placed, out_specs=P("grp", "blk"), check_vma=False
    )
```

```python
import functools

import jax
import jax.numpy as jnp
from jax import lax
from jax.experimental import pallas as pl
from jax.experimental.pallas import tpu as pltpu
from jax.sharding import PartitionSpec as P

MESH = pl.DeviceIdType.MESH
D = 768
SLOTS = 5
PIECE = 64
STEPS = 8

SRC = [[0, 3, 0, 0], [3, 0, 0, 0], [0, 0, 4, 0], [0, 0, 4, 0], [0, 4, 1, 0], [4, 0, 2, 0], [0, 3, 0, 0], [3, 0, 0, 0],
       [3, 0, 0, 3], [0, 3, 0, 3], [2, 4, 0, 0], [4, 1, 0, 0], [2, 0, 4, 0], [0, 1, 4, 0], [4, 0, 0, 3], [0, 4, 0, 3]]
DEP = [[1, 1, 1, 2], [1, 1, 1, 2], [1, 2, 1, 1], [2, 1, 1, 1], [1, 2, 2, 1], [2, 1, 2, 1], [1, 2, 1, 2], [2, 1, 1, 2],
       [2, 2, 1, 2], [2, 2, 1, 2], [2, 1, 2, 1], [1, 2, 2, 1], [2, 1, 1, 1], [1, 2, 1, 1], [2, 1, 1, 1], [1, 2, 1, 1]]
BLK = [[1, 3, 4, 8], [2, 0, 5, 9], [3, 5, 6, 14], [4, 2, 7, 15], [5, 11, 12, 0], [10, 4, 13, 1], [7, 1, 10, 14],
       [0, 6, 11, 15], [13, 7, 12, 5], [6, 12, 13, 4], [8, 9, 2, 6], [8, 9, 3, 7], [14, 15, 0, 8], [14, 15, 1, 9],
       [11, 13, 2, 10], [12, 10, 3, 11]]
IDX = [[1, 1, 1, 1], [1, 1, 1, 1], [2, 2, 1, 1], [2, 2, 1, 1], [3, 1, 1, 2], [1, 3, 1, 2], [2, 3, 2, 2], [3, 2, 2, 2],
       [2, 3, 2, 4], [3, 3, 3, 4], [2, 2, 3, 4], [3, 3, 3, 4], [3, 3, 4, 4], [4, 4, 4, 4], [3, 4, 4, 3], [4, 4, 4, 4]]
HOLD = [[0, 1, 4, 7, 12], [1, 0, 5, 6, 13], [2, 1, 3, 10, 14], [3, 0, 2, 11, 15], [4, 0, 3, 5, 9], [5, 1, 2, 4, 8],
        [6, 2, 7, 9, 10], [7, 3, 6, 8, 11], [8, 0, 10, 11, 12], [9, 1, 10, 11, 13], [10, 5, 6, 14, 15], [11, 4, 7, 14, 15],
        [12, 4, 8, 9, 15], [13, 5, 8, 9, 14], [14, 2, 6, 12, 13], [15, 3, 7, 12, 13]]
PAIRS = [[[(1, 3), (1, 4), (3, 4)], [(0, 1), (0, 2), (1, 2)]], [[(2, 1), (2, 4), (1, 4)], [(0, 1), (0, 3), (3, 4)]],
         [[(1, 3), (3, 4), (2, 3), (2, 4)], [(0, 1), (0, 2), (1, 2)]],
         [[(2, 3), (2, 1), (1, 3)], [(0, 3), (3, 4), (0, 1)]], [[(4, 0), (4, 1), (0, 2), (1, 2)], [(0, 3), (1, 3)]],
         [[(2, 0), (4, 1), (2, 1)], [(0, 1), (0, 3), (1, 3)]], [[(1, 3), (1, 4), (3, 4)], [(0, 3), (2, 0), (2, 1)]],
         [[(2, 3), (2, 4), (3, 4)], [(2, 0), (1, 2), (1, 0)]],
         [[(2, 3), (2, 1), (0, 1), (3, 1)], [(4, 2), (4, 0), (2, 0)]],
         [[(4, 1), (4, 0), (4, 3), (1, 3)], [(1, 0), (1, 2), (0, 2)]],
         [[(3, 4), (3, 1), (4, 1)], [(2, 0), (1, 2), (1, 0)]], [[(1, 0), (3, 1), (3, 2)], [(4, 0), (4, 2), (2, 0)]],
         [[(3, 4), (4, 1), (0, 1)], [(4, 0), (4, 2), (0, 2)]], [[(3, 4), (4, 1), (1, 2)], [(4, 0), (4, 2), (0, 2)]],
         [[(3, 4), (3, 1), (4, 1)], [(2, 0), (1, 2), (1, 0)]], [[(3, 4), (3, 1), (4, 1)], [(3, 2), (2, 1), (2, 0)]]]
NEED = [[[1, 3, 4], [0, 1, 2]], [[1, 2, 4], [0, 1, 3, 4]], [[1, 2, 3, 4], [0, 1, 2]], [[1, 2, 3], [0, 1, 3, 4]],
        [[0, 1, 2, 4], [0, 1, 3]], [[0, 1, 2, 4], [0, 1, 3]], [[1, 3, 4], [0, 1, 2, 3]], [[2, 3, 4], [0, 1, 2]],
        [[0, 1, 2, 3], [0, 2, 4]], [[0, 1, 3, 4], [0, 1, 2]], [[1, 3, 4], [0, 1, 2]], [[0, 1, 2, 3], [0, 2, 4]],
        [[0, 1, 3, 4], [0, 2, 4]], [[1, 2, 3, 4], [0, 2, 4]], [[1, 3, 4], [0, 1, 2]], [[1, 3, 4], [0, 1, 2, 3]]]

REL = (0, 3, 1, 2)


def word(digits, base):
    total = 0
    for digit in reversed(digits):
        total = total * base + digit
    return total


def look_up(index, words):
    got = jnp.int32(words[0])
    for k in range(1, len(words)):
        got = jnp.where(index == k, jnp.int32(words[k]), got)
    return got


def digits_of(value, base, count):
    out = []
    for _ in range(count):
        out.append(value % base)
        value = value // base
    return out


def position():
    grp, blk = lax.axis_index("grp"), lax.axis_index("blk")
    h, zl = grp % 2, grp // 2
    p, zh = blk // 2, blk % 2
    return h, zl, zh, zh * 2 + zl, p


def device(z_of, core, chip):
    return ((z_of % 2) * 2 + core, chip * 2 + z_of // 2)


def blocks_of(p):
    return [p] + digits_of(look_up(p, [word(BLK[c], 16) for c in range(16)]), 16, 4)


def remote(src_ref, dst_ref, send_sem, recv_sem, to):
    return pltpu.make_async_remote_copy(
        src_ref=src_ref, dst_ref=dst_ref, send_sem=send_sem, recv_sem=recv_sem, device_id=to, device_id_type=MESH)


def exchange(emb, ids_in, x, ids_out, units, stage, relay, load_sem, id_send, id_recv, z_send, z_recv, relay_send, relay_recv,
             f_send, f_recv, c_send, c_recv):
    h, zl, zh, z, p = position()
    px, py = p % 4, p // 4

    def group_of(z_of):
        return (z_of % 2) * 2 + z_of // 2

    near = [py * 4 + (px + 1) % 4, py * 4 + (px + 3) % 4, ((py + 1) % 4) * 4 + px, ((py + 3) % 4) * 4 + px]
    first = look_up(p, [word(SRC[c], 8) + 4096 * word(DEP[c], 4) for c in range(16)])
    src = digits_of(first, 8, 4)
    dep = digits_of(first // 4096, 4, 4)
    needs = [[sum(1 << slot for slot in NEED[c][core]) for core in range(2)] for c in range(16)]
    need = digits_of(look_up(p * 2 + h, [needs[c][core] for c in range(16) for core in range(2)]), 2, SLOTS)
    sibling_need = digits_of(look_up(p * 2 + h, [needs[c][1 - core] for c in range(16) for core in range(2)]), 2, SLOTS)

    sibling = device(z, 1 - h, p)
    loads = []
    for k, rel in enumerate((0, 1, 3, 2)):
        loads.append(pltpu.make_async_copy(emb.at[group_of((z + rel) % 4)], stage.at[k], load_sem.at[k]))
        loads[-1].start()

    barrier = pltpu.get_barrier_semaphore()
    for rel in (1, 3):
        pl.semaphore_signal(barrier, inc=1, device_id=device((z + rel) % 4, h, p), device_id_type=MESH)
    for d in range(4):
        pl.semaphore_signal(barrier, inc=1, device_id=device(z, h, near[d]), device_id_type=MESH)
    pl.semaphore_signal(barrier, inc=1, device_id=sibling, device_id_type=MESH)
    def normalise(k):
        loads[k].wait()
        v = stage[k]
        total = jnp.sum(v * v, axis=-1, keepdims=True)
        return (v / jnp.sqrt(total + 1e-06)).astype(jnp.bfloat16)

    own_rows = pl.multiple_of(h * 128, 128)
    x[0, pl.ds(own_rows, 128), :] = normalise(0)
    pl.semaphore_wait(barrier, 7)

    def part_rows(t):
        return pl.ds(pl.multiple_of((t // 2) * 256 + h * 128 + (t % 2) * PIECE, PIECE), PIECE)

    def forward(d, t):
        rows = part_rows(t)
        return remote(x.at[src[d], rows, :], x.at[1 + (d ^ 1), rows, :], f_send.at[d, t], f_recv.at[d ^ 1, t],
                      device(z, h, near[d]))

    def arrival(s, t):
        rows = part_rows(t)
        return remote(x.at[s, rows, :], x.at[s, rows, :], f_send.at[s - 1, t], f_recv.at[s - 1, t],
                      device(z, h, near[s - 1]))

    def swap(k, half):
        rows = pl.ds(pl.multiple_of(k * 256 + h * 128 + half * 64, 64), 64)
        return remote(units.at[k - 1, pl.ds(half * 64, 64), :], x.at[0, rows, :], z_send.at[k - 1, half],
                      z_recv.at[k - 1, half], device((z + (1, 3, 2)[k - 1]) % 4, h, p))

    between = device((z + jnp.where(h == 0, 1, 3)) % 4, h, p)

    def relay_in(half):
        rows = pl.ds(half * 64, 64)
        return remote(units.at[2, rows, :], relay.at[rows, :], relay_send.at[0, half], relay_recv.at[half], between)

    def relay_out(half):
        rows = pl.ds(pl.multiple_of(3 * 256 + h * 128 + half * 64, 64), 64)
        return remote(relay.at[pl.ds(half * 64, 64), :], x.at[0, rows, :], relay_send.at[1, half], z_recv.at[2, half],
                      between)

    def share_rows(t, core):
        return pl.ds(pl.multiple_of((t // 2) * 256 + core * 128 + (t % 2) * 64, 64), 64)

    def share(s, t):
        rows = share_rows(t, h)
        return remote(x.at[s, rows, :], x.at[s, rows, :], c_send.at[s, t], c_recv.at[s, t], sibling)

    def shared(s, t):
        rows = share_rows(t, 1 - h)
        return remote(x.at[s, rows, :], x.at[s, rows, :], c_send.at[s, t], c_recv.at[s, t], sibling)

    def give(s, t):
        pl.when(sibling_need[s] == 1)(lambda: share(s, t).start())

    def send_own(t):
        for d in range(4):
            pl.when(src[d] == 0)(lambda d=d: forward(d, t).start())

    def send_held(t):
        for d in range(4):
            pl.when(src[d] != 0)(lambda d=d: forward(d, t).start())

    def receive(links, t):
        for s in range(1, SLOTS):
            pl.when(dep[s - 1] == links)(lambda s=s: arrival(s, t).wait_recv())

    def give_held(links, t):
        for s in range(1, SLOTS):
            pl.when(dep[s - 1] == links)(lambda s=s: give(s, t))

    for t in range(2):
        send_own(t)
    units[0] = normalise(1)
    for half in range(2):
        swap(1, half).start()
    units[1] = normalise(2)
    for half in range(2):
        swap(2, half).start()
    units[2] = normalise(3)
    for half in range(2):
        relay_in(half).start()
    ids_copy = remote(ids_in, ids_out, id_send, id_recv, sibling)
    ids_copy.start()
    give(0, 0)
    give(0, 1)

    def wait_shared(m):
        for s in range(SLOTS):
            @pl.when(need[s] == 1)
            def _():
                for half in range(2):
                    shared(s, 2 * m + half).wait_recv()

    def own_piece_ready(t):
        send_own(t)
        give(0, t)

    def pass_on(k):
        receive(1, k - 1)
        send_held(k - 1)
        give_held(1, k - 1)

    def take(t):
        receive(2, t)
        give_held(2, t)

    pass_on(1)
    swap(1, 0).wait_recv()
    own_piece_ready(2)
    pass_on(2)
    swap(1, 1).wait_recv()
    own_piece_ready(3)
    swap(2, 0).wait_recv()
    own_piece_ready(4)
    pass_on(3)
    for half in range(2):
        relay_in(half).wait_recv()
        relay_out(half).start()
    swap(2, 1).wait_recv()
    own_piece_ready(5)
    take(0)
    for k in range(4, STEPS + 1):
        pass_on(k)
        if k == 5:
            for half in range(2):
                relay_out(half).wait_recv()
                own_piece_ready(6 + half)
        take(k - 3)
    take(STEPS - 2)
    take(STEPS - 1)
    ids_copy.wait()
    for half in range(2):
        for copy in (swap(1, half), swap(2, half), relay_in(half), relay_out(half)):
            copy.wait_send()
    for d in range(4):
        for t in range(STEPS):
            forward(d, t).wait_send()
    for s in range(SLOTS):
        for t in range(8):
            pl.when(sibling_need[s] == 1)(lambda s=s, t=t: share(s, t).wait_send())
    for m in range(4):
        wait_shared(m)

    @pl.when(h == zh)
    def _():
        ids_out[...] = ids_in[...]


def compare(x, ids, ends, part, ids_rows, ids_cols, row_best, col_best):
    h, zl, zh, z, p = position()
    held = blocks_of(p)
    lists = []
    for c in range(16):
        for core in range(2):
            flat = [slot for pair in PAIRS[c][core] for slot in pair]
            lists.append(len(PAIRS[c][core]) + 8 * word(flat + [0] * (8 - len(flat)), 8))
    todo = look_up(p * 2 + h, lists)
    pair_count = todo % 8
    todo = digits_of(todo // 8, 8, 8)

    row_best[...] = jnp.full_like(row_best, -1.0)
    col_best[...] = jnp.full_like(col_best, -1.0)

    ids_cols[...] = jnp.zeros_like(ids_cols)
    for s in range(SLOTS):
        for t in range(4):
            for core in range(2):
                unit = held[s] * 8 + 2 * ((z + REL[t]) % 4) + core
                ids_cols[pl.ds(s * 8 + 2 * t + core, 1), :] = ids[pl.ds(unit, 1), :].astype(jnp.float32)
    turned = ids_cols[...].T
    for j in range(SLOTS * 8):
        ids_rows[j] = jnp.broadcast_to(turned[:, j:j + 1], (128, 128))

    def span(slot, t):
        block = held[0]
        for s in range(1, SLOTS):
            block = jnp.where(slot == s, held[s], block)
        unit = block * 8 + 2 * ((z + jnp.where(t == 1, 3, jnp.where(t == 2, 1, jnp.where(t == 3, 2, 0)))) % 4)
        return ends[unit, 0], ends[unit + 1, 127]

    def strip(a, t, b):
        sim = lax.dot_general(x[b], x[a, pl.ds(pl.multiple_of(256 * t, 256), 256), :], (((1,), (1,)), ((), ())),
                              preferred_element_type=jnp.float32)
        col_ids = [ids_cols[pl.ds(a * 8 + 2 * t + c, 1), :] for c in range(2)]
        downs = [col_best[a * 8 + 2 * t + c] for c in range(2)]
        for r in range(16):
            unit, first_row = b * 8 + r // 2, 64 * (r % 2)
            row_ids = ids_rows[unit, first_row:first_row + 64]
            best = row_best[unit, first_row:first_row + 64]
            for c in range(2):
                kept = jnp.where(row_ids == col_ids[c], sim[64 * r:64 * r + 64, 128 * c:128 * c + 128], jnp.float32(-1.0))
                downs[c] = jnp.maximum(downs[c], jnp.max(kept.reshape(8, 8, 128), axis=0))
                best = jnp.maximum(best, kept)
            row_best[unit, first_row:first_row + 64] = best
        for c in range(2):
            col_best[a * 8 + 2 * t + c] = downs[c]

    def own_strip(t):
        sim = lax.dot_general(x[0], x[0, 256 * t:256 * t + 256, :], (((1,), (1,)), ((), ())),
                              preferred_element_type=jnp.float32)
        for c in range(2):
            line = 2 * t + c
            down = col_best[line]
            col_ids = ids_cols[line:line + 1, :]
            for r in range(8):
                keep = ids_rows[r] == col_ids
                if r == line:
                    row = lax.broadcasted_iota(jnp.int32, (128, 128), 0)
                    col = lax.broadcasted_iota(jnp.int32, (128, 128), 1)
                    keep = jnp.logical_and(keep, row != col)
                kept = jnp.where(keep, sim[128 * r:128 * r + 128, 128 * c:128 * c + 128], jnp.float32(-1.0))
                down = jnp.maximum(down, jnp.max(kept.reshape(16, 8, 128), axis=0))
            col_best[line] = down

    def one_strip(k, carry):
        j, t = k // 4, k % 4
        a, b = todo[0], todo[1]
        for i in range(1, 4):
            a = jnp.where(j == i, todo[2 * i], a)
            b = jnp.where(j == i, todo[2 * i + 1], b)
        first, last = span(a, t)
        meet = False
        for u in range(4):
            other_first, other_last = span(b, u)
            meet = jnp.logical_or(meet, jnp.logical_and(last >= other_first, other_last >= first))
        pl.when(meet)(lambda: strip(a, t, b))
        return carry

    lax.fori_loop(0, pair_count * 4, one_strip, 0)

    @pl.when(h == 1)
    def _():
        for t in range(4):
            own_strip(t)

    for s in range(SLOTS):
        for t in range(4):
            z_of = (z + REL[t]) % 4
            for core in range(2):
                j = s * 8 + 2 * t + core
                both = jnp.maximum(jnp.max(row_best[j].T, axis=0, keepdims=True),
                                   jnp.max(col_best[j], axis=0, keepdims=True))
                part[s * 2 + z_of // 2, pl.ds(2 * (z_of % 2) + core, 1), :] = both


def combine(part, out, parts_got, r_send, r_recv):
    h, zl, zh, z, p = position()
    held = blocks_of(p)
    third = look_up(p, [word(IDX[c], 8) + 4096 * word(HOLD[c][1:], 16) for c in range(16)])
    place = [jnp.int32(0)] + digits_of(third, 8, 4)
    holders = [p] + digits_of(third // 4096, 16, 4)
    sibling = device(z, 1 - h, p)
    owner_grp = zl * 2 + zh
    mine = h == zh

    barrier = pltpu.get_barrier_semaphore()
    for k in range(SLOTS):
        for core in range(2):
            def tell():
                pl.semaphore_signal(barrier, inc=1, device_id=device(2 * h + zl, core, holders[k]), device_id_type=MESH)
            if k == 0:
                pl.when(jnp.logical_not(jnp.logical_and(mine, h == core)))(tell)
            else:
                tell()
    pl.semaphore_wait(barrier, jnp.where(mine, 9, 10))

    def deliver(s, half):
        return remote(part.at[s * 2 + half], parts_got.at[place[s] * 2 + h], r_send.at[s * 2 + half],
                      r_recv.at[place[s] * 2 + h], (owner_grp, held[s] * 2 + half))

    for s in range(SLOTS):
        for half in range(2):
            if s == 0:
                keep_it = jnp.logical_and(mine, zh == half)
                pl.when(jnp.logical_not(keep_it))(deliver(s, half).start)

                @pl.when(keep_it)
                def _():
                    parts_got[h] = part[half]
            else:
                deliver(s, half).start()

    best = None
    for k in range(2 * SLOTS):
        got = remote(parts_got.at[k], parts_got.at[k], r_send.at[k], r_recv.at[k], sibling)
        if k < 2:
            pl.when(jnp.logical_not(jnp.logical_and(mine, h == k)))(got.wait_recv)
        else:
            got.wait_recv()
        best = parts_got[k] if best is None else jnp.maximum(best, parts_got[k])
    out[...] = best
    for s in range(SLOTS):
        for half in range(2):
            if s == 0:
                pl.when(jnp.logical_not(jnp.logical_and(mine, zh == half)))(deliver(s, half).wait_send)
            else:
                deliver(s, half).wait_send()


def on_device(embeddings, cluster_ids):
    emb = embeddings.reshape(4, 128, D)
    ids = cluster_ids.reshape(128, 128)
    dma = pltpu.SemaphoreType.DMA
    vmem = pl.BlockSpec(memory_space=pltpu.VMEM)
    x, ids = pl.pallas_call(
        exchange,
        out_shape=(jax.ShapeDtypeStruct((SLOTS, 1024, D), jnp.bfloat16), jax.ShapeDtypeStruct((128, 128), jnp.int32)),
        in_specs=[pl.BlockSpec(memory_space=pl.ANY), vmem],
        out_specs=[vmem, vmem],
        scratch_shapes=[
            pltpu.VMEM((3, 128, D), jnp.bfloat16),
            pltpu.VMEM((4, 128, D), jnp.float32),
            pltpu.VMEM((128, D), jnp.bfloat16),
            dma((4,)), dma, dma, dma((3, 2)), dma((3, 2)), dma((2, 2)), dma((2,)), dma((4, STEPS)), dma((4, STEPS)),
            dma((SLOTS, 8)), dma((SLOTS, 8)),
        ],
        compiler_params=pltpu.CompilerParams(
            collective_id=0, has_side_effects=True, vmem_limit_bytes=20 * 1024 * 1024),
        name="exchange",
    )(emb, ids)
    part = pl.pallas_call(
        compare,
        out_shape=jax.ShapeDtypeStruct((2 * SLOTS, 4, 128), jnp.float32),
        in_specs=[vmem, vmem, pl.BlockSpec(memory_space=pltpu.SMEM)],
        out_specs=vmem,
        scratch_shapes=[
            pltpu.VMEM((SLOTS * 8, 128, 128), jnp.float32),
            pltpu.VMEM((128, 128), jnp.float32),
            pltpu.VMEM((SLOTS * 8, 128, 128), jnp.float32),
            pltpu.VMEM((SLOTS * 8, 8, 128), jnp.float32),
        ],
        compiler_params=pltpu.CompilerParams(vmem_limit_bytes=20 * 1024 * 1024),
        name="compare",
    )(x, ids, ids)
    best = pl.pallas_call(
        combine,
        out_shape=jax.ShapeDtypeStruct((4, 128), jnp.float32),
        in_specs=[vmem],
        out_specs=vmem,
        scratch_shapes=[pltpu.VMEM((2 * SLOTS, 4, 128), jnp.float32), dma((2 * SLOTS,)), dma((2 * SLOTS,))],
        compiler_params=pltpu.CompilerParams(collective_id=1, has_side_effects=True),
        name="combine",
    )(part)
    return best.reshape(1, 512)


def solution(mesh):
    placed = (P(None, "grp", "blk", None, None), P("grp", None))
    return jax.shard_map(
        on_device, mesh=mesh, in_specs=placed, out_specs=P("grp", "blk"), check_vma=False
    )
```

```python
import functools

import jax
import jax.numpy as jnp
from jax import lax
from jax.experimental import pallas as pl
from jax.experimental.pallas import tpu as pltpu
from jax.sharding import PartitionSpec as P

MESH = pl.DeviceIdType.MESH
D = 768
SLOTS = 5
PIECE = 64
STEPS = 8

SRC = [[0, 3, 0, 0], [3, 0, 0, 0], [0, 0, 4, 0], [0, 0, 4, 0], [0, 4, 1, 0], [4, 0, 2, 0], [0, 3, 0, 0], [3, 0, 0, 0],
       [3, 0, 0, 3], [0, 3, 0, 3], [2, 4, 0, 0], [4, 1, 0, 0], [2, 0, 4, 0], [0, 1, 4, 0], [4, 0, 0, 3], [0, 4, 0, 3]]
DEP = [[1, 1, 1, 2], [1, 1, 1, 2], [1, 2, 1, 1], [2, 1, 1, 1], [1, 2, 2, 1], [2, 1, 2, 1], [1, 2, 1, 2], [2, 1, 1, 2],
       [2, 2, 1, 2], [2, 2, 1, 2], [2, 1, 2, 1], [1, 2, 2, 1], [2, 1, 1, 1], [1, 2, 1, 1], [2, 1, 1, 1], [1, 2, 1, 1]]
BLK = [[1, 3, 4, 8], [2, 0, 5, 9], [3, 5, 6, 14], [4, 2, 7, 15], [5, 11, 12, 0], [10, 4, 13, 1], [7, 1, 10, 14],
       [0, 6, 11, 15], [13, 7, 12, 5], [6, 12, 13, 4], [8, 9, 2, 6], [8, 9, 3, 7], [14, 15, 0, 8], [14, 15, 1, 9],
       [11, 13, 2, 10], [12, 10, 3, 11]]
IDX = [[1, 1, 1, 1], [1, 1, 1, 1], [2, 2, 1, 1], [2, 2, 1, 1], [3, 1, 1, 2], [1, 3, 1, 2], [2, 3, 2, 2], [3, 2, 2, 2],
       [2, 3, 2, 4], [3, 3, 3, 4], [2, 2, 3, 4], [3, 3, 3, 4], [3, 3, 4, 4], [4, 4, 4, 4], [3, 4, 4, 3], [4, 4, 4, 4]]
HOLD = [[0, 1, 4, 7, 12], [1, 0, 5, 6, 13], [2, 1, 3, 10, 14], [3, 0, 2, 11, 15], [4, 0, 3, 5, 9], [5, 1, 2, 4, 8],
        [6, 2, 7, 9, 10], [7, 3, 6, 8, 11], [8, 0, 10, 11, 12], [9, 1, 10, 11, 13], [10, 5, 6, 14, 15], [11, 4, 7, 14, 15],
        [12, 4, 8, 9, 15], [13, 5, 8, 9, 14], [14, 2, 6, 12, 13], [15, 3, 7, 12, 13]]
PAIRS = [[[(1, 3), (1, 4), (3, 4)], [(0, 1), (0, 2), (1, 2)]], [[(2, 1), (2, 4), (1, 4)], [(0, 1), (0, 3), (3, 4)]],
         [[(1, 3), (3, 4), (2, 3), (2, 4)], [(0, 1), (0, 2), (1, 2)]],
         [[(2, 3), (2, 1), (1, 3)], [(0, 3), (3, 4), (0, 1)]], [[(4, 0), (4, 1), (0, 2), (1, 2)], [(0, 3), (1, 3)]],
         [[(2, 0), (4, 1), (2, 1)], [(0, 1), (0, 3), (1, 3)]], [[(1, 3), (1, 4), (3, 4)], [(0, 3), (2, 0), (2, 1)]],
         [[(2, 3), (2, 4), (3, 4)], [(2, 0), (1, 2), (1, 0)]],
         [[(2, 3), (2, 1), (0, 1), (3, 1)], [(4, 2), (4, 0), (2, 0)]],
         [[(4, 1), (4, 0), (4, 3), (1, 3)], [(1, 0), (1, 2), (0, 2)]],
         [[(3, 4), (3, 1), (4, 1)], [(2, 0), (1, 2), (1, 0)]], [[(1, 0), (3, 1), (3, 2)], [(4, 0), (4, 2), (2, 0)]],
         [[(3, 4), (4, 1), (0, 1)], [(4, 0), (4, 2), (0, 2)]], [[(3, 4), (4, 1), (1, 2)], [(4, 0), (4, 2), (0, 2)]],
         [[(3, 4), (3, 1), (4, 1)], [(2, 0), (1, 2), (1, 0)]], [[(3, 4), (3, 1), (4, 1)], [(3, 2), (2, 1), (2, 0)]]]
NEED = [[[1, 3, 4], [0, 1, 2]], [[1, 2, 4], [0, 1, 3, 4]], [[1, 2, 3, 4], [0, 1, 2]], [[1, 2, 3], [0, 1, 3, 4]],
        [[0, 1, 2, 4], [0, 1, 3]], [[0, 1, 2, 4], [0, 1, 3]], [[1, 3, 4], [0, 1, 2, 3]], [[2, 3, 4], [0, 1, 2]],
        [[0, 1, 2, 3], [0, 2, 4]], [[0, 1, 3, 4], [0, 1, 2]], [[1, 3, 4], [0, 1, 2]], [[0, 1, 2, 3], [0, 2, 4]],
        [[0, 1, 3, 4], [0, 2, 4]], [[1, 2, 3, 4], [0, 2, 4]], [[1, 3, 4], [0, 1, 2]], [[1, 3, 4], [0, 1, 2, 3]]]

REL = (0, 3, 1, 2)


def word(digits, base):
    total = 0
    for digit in reversed(digits):
        total = total * base + digit
    return total


def look_up(index, words):
    got = jnp.int32(words[0])
    for k in range(1, len(words)):
        got = jnp.where(index == k, jnp.int32(words[k]), got)
    return got


def digits_of(value, base, count):
    out = []
    for _ in range(count):
        out.append(value % base)
        value = value // base
    return out


def kernel(emb, ids_in, out, x, units, stage, ids_own, ids_got, ids_rows, ids_cols, row_best, col_best, row_line, part, parts_got,
           relay,
           load_sem, ids_sem, id_send, id_recv, z_send, z_recv, relay_send, relay_recv, f_send, f_recv, c_send, c_recv, r_send, r_recv):
    grp, blk = lax.axis_index("grp"), lax.axis_index("blk")
    h, zl = grp % 2, grp // 2
    p, zh = blk // 2, blk % 2
    z = zh * 2 + zl
    px, py = p % 4, p // 4

    def device(z_of, core, chip):
        return ((z_of % 2) * 2 + core, chip * 2 + z_of // 2)

    def group_of(z_of):
        return (z_of % 2) * 2 + z_of // 2

    near = [py * 4 + (px + 1) % 4, py * 4 + (px + 3) % 4, ((py + 1) % 4) * 4 + px, ((py + 3) % 4) * 4 + px]
    first = look_up(p, [word(SRC[c], 8) + 4096 * word(DEP[c], 4) for c in range(16)])
    src = digits_of(first, 8, 4)
    dep = digits_of(first // 4096, 4, 4)
    held = [p] + digits_of(look_up(p, [word(BLK[c], 16) for c in range(16)]), 16, 4)
    third = look_up(p, [word(IDX[c], 8) + 4096 * word(HOLD[c][1:], 16) for c in range(16)])
    place = [jnp.int32(0)] + digits_of(third, 8, 4)
    holders = [p] + digits_of(third // 4096, 16, 4)
    lists = []
    for c in range(16):
        for core in range(2):
            flat = [slot for pair in PAIRS[c][core] for slot in pair]
            lists.append(len(PAIRS[c][core]) + 8 * word(flat + [0] * (8 - len(flat)), 8))
    todo = look_up(p * 2 + h, lists)
    pair_count = todo % 8
    todo = digits_of(todo // 8, 8, 8)

    needs = [[sum(1 << slot for slot in NEED[c][core]) for core in range(2)] for c in range(16)]
    need = digits_of(look_up(p * 2 + h, [needs[c][core] for c in range(16) for core in range(2)]), 2, SLOTS)
    sibling_need = digits_of(look_up(p * 2 + h, [needs[c][1 - core] for c in range(16) for core in range(2)]), 2, SLOTS)

    sibling = device(z, 1 - h, p)
    owner_grp = zl * 2 + zh
    mine = h == zh

    loads = []
    for k, rel in enumerate((0, 1, 3, 2)):
        loads.append(pltpu.make_async_copy(emb.at[group_of((z + rel) % 4)], stage.at[k], load_sem.at[k]))
        loads[-1].start()

    ids_load = pltpu.make_async_copy(ids_in, ids_own, ids_sem)
    ids_load.start()

    barrier = pltpu.get_barrier_semaphore()
    for rel in (1, 3):
        pl.semaphore_signal(barrier, inc=1, device_id=device((z + rel) % 4, h, p), device_id_type=MESH)
    for d in range(4):
        pl.semaphore_signal(barrier, inc=1, device_id=device(z, h, near[d]), device_id_type=MESH)
    pl.semaphore_signal(barrier, inc=1, device_id=sibling, device_id_type=MESH)
    from_z = 2 * h + zl
    for k in range(SLOTS):
        for core in range(2):
            def tell():
                pl.semaphore_signal(barrier, inc=1, device_id=device(from_z, core, holders[k]), device_id_type=MESH)
            if k == 0:
                pl.when(jnp.logical_not(jnp.logical_and(mine, h == core)))(tell)
            else:
                tell()

    def normalise(k):
        loads[k].wait()
        v = stage[k]
        total = jnp.sum(v * v, axis=-1, keepdims=True)
        return (v / jnp.sqrt(total + 1e-06)).astype(jnp.bfloat16)

    own_rows = pl.multiple_of(h * 128, 128)
    x[0, pl.ds(own_rows, 128), :] = normalise(0)
    pl.semaphore_wait(barrier, jnp.where(mine, 16, 17))

    def remote(src_ref, dst_ref, send_sem, recv_sem, to):
        return pltpu.make_async_remote_copy(
            src_ref=src_ref, dst_ref=dst_ref, send_sem=send_sem, recv_sem=recv_sem, device_id=to, device_id_type=MESH)

    def part_rows(t):
        return pl.ds(pl.multiple_of((t // 2) * 256 + h * 128 + (t % 2) * PIECE, PIECE), PIECE)

    def forward(d, t):
        rows = part_rows(t)
        return remote(x.at[src[d], rows, :], x.at[1 + (d ^ 1), rows, :], f_send.at[d, t], f_recv.at[d ^ 1, t],
                      device(z, h, near[d]))

    def arrival(s, t):
        rows = part_rows(t)
        return remote(x.at[s, rows, :], x.at[s, rows, :], f_send.at[s - 1, t], f_recv.at[s - 1, t],
                      device(z, h, near[s - 1]))

    def swap(k, half):
        rows = pl.ds(pl.multiple_of(k * 256 + h * 128 + half * 64, 64), 64)
        return remote(units.at[k - 1, pl.ds(half * 64, 64), :], x.at[0, rows, :], z_send.at[k - 1, half],
                      z_recv.at[k - 1, half], device((z + (1, 3, 2)[k - 1]) % 4, h, p))

    between = device((z + jnp.where(h == 0, 1, 3)) % 4, h, p)

    def relay_in(half):
        rows = pl.ds(half * 64, 64)
        return remote(units.at[2, rows, :], relay.at[rows, :], relay_send.at[0, half], relay_recv.at[half], between)

    def relay_out(half):
        rows = pl.ds(pl.multiple_of(3 * 256 + h * 128 + half * 64, 64), 64)
        return remote(relay.at[pl.ds(half * 64, 64), :], x.at[0, rows, :], relay_send.at[1, half], z_recv.at[2, half],
                      between)

    def share_rows(t, core):
        return pl.ds(pl.multiple_of((t // 2) * 256 + core * 128 + (t % 2) * 64, 64), 64)

    def share(s, t):
        rows = share_rows(t, h)
        return remote(x.at[s, rows, :], x.at[s, rows, :], c_send.at[s, t], c_recv.at[s, t], sibling)

    def shared(s, t):
        rows = share_rows(t, 1 - h)
        return remote(x.at[s, rows, :], x.at[s, rows, :], c_send.at[s, t], c_recv.at[s, t], sibling)

    def give(s, t):
        pl.when(sibling_need[s] == 1)(lambda: share(s, t).start())

    def send_own(t):
        for d in range(4):
            pl.when(src[d] == 0)(lambda d=d: forward(d, t).start())

    def send_held(t):
        for d in range(4):
            pl.when(src[d] != 0)(lambda d=d: forward(d, t).start())

    def receive(links, t):
        for s in range(1, SLOTS):
            pl.when(dep[s - 1] == links)(lambda s=s: arrival(s, t).wait_recv())

    def give_held(links, t):
        for s in range(1, SLOTS):
            pl.when(dep[s - 1] == links)(lambda s=s: give(s, t))

    for t in range(2):
        send_own(t)
    units[0] = normalise(1)
    for half in range(2):
        swap(1, half).start()
    units[1] = normalise(2)
    for half in range(2):
        swap(2, half).start()
    units[2] = normalise(3)
    for half in range(2):
        relay_in(half).start()
    ids_copy = remote(ids_in, ids_got, id_send, id_recv, sibling)
    ids_copy.start()
    give(0, 0)
    give(0, 1)
    row_best[...] = jnp.full_like(row_best, -1.0)
    col_best[...] = jnp.full_like(col_best, -1.0)
    row_line[...] = jnp.full_like(row_line, -1.0)

    ids_load.wait()
    ids_copy.wait_recv()
    ids_cols[...] = jnp.zeros_like(ids_cols)
    for s in range(SLOTS):
        for t in range(4):
            for core in range(2):
                unit = held[s] * 8 + 2 * ((z + REL[t]) % 4) + core
                got = jnp.where(mine, ids_own[pl.ds(unit, 1), :], ids_got[pl.ds(unit, 1), :])
                ids_cols[pl.ds(s * 8 + 2 * t + core, 1), :] = got.astype(jnp.float32)
    turned = ids_cols[...].T
    for j in range(SLOTS * 8):
        ids_rows[j] = jnp.broadcast_to(turned[:, j:j + 1], (128, 128))

    def strip(a, t, b, count, diagonal=False):
        sim = lax.dot_general(x[a, 256 * t:256 * t + 256, :], x[b, 0:256 * count, :], (((1,), (1,)), ((), ())),
                              preferred_element_type=jnp.float32)
        for r in range(4):
            unit, first_row = a * 8 + 2 * t + r // 2, 64 * (r % 2)
            row_ids = ids_rows[unit, first_row:first_row + 64]
            best = row_best[unit, first_row:first_row + 64]
            for c in range(2 * count):
                keep = row_ids == ids_cols[pl.ds(b * 8 + c, 1), :]
                if diagonal and c // 2 == t:
                    row = lax.broadcasted_iota(jnp.int32, (64, 128), 0) + 64 * r
                    col = lax.broadcasted_iota(jnp.int32, (64, 128), 1) + 128 * (c % 2)
                    keep = jnp.logical_and(keep, row != col)
                kept = jnp.where(keep, sim[64 * r:64 * r + 64, 128 * c:128 * c + 128], jnp.float32(-1.0))
                down = jnp.max(kept.reshape(8, 8, 128), axis=0)
                col_best[b * 8 + c] = jnp.maximum(col_best[b * 8 + c], down)
                best = jnp.maximum(best, kept)
            row_best[unit, first_row:first_row + 64] = best

    def compare(t, j):
        a, b = todo[0], todo[1]
        for k in range(1, 4):
            a = jnp.where(j == k, todo[2 * k], a)
            b = jnp.where(j == k, todo[2 * k + 1], b)
        strip(a, t, b, t + 1)
        if t:
            strip(b, t, a, t)

    def own_pair(t):
        pl.when(h == 1)(lambda: strip(0, t, 0, t + 1, diagonal=True))

    def finish_rows(t):
        for s in range(SLOTS):
            @pl.when(need[s] == 1)
            def _():
                for core in range(2):
                    unit = s * 8 + 2 * t + core
                    row_line[unit:unit + 1, :] = jnp.max(row_best[unit].T, axis=0, keepdims=True)

    def wait_shared(m, slots=range(SLOTS)):
        for s in slots:
            @pl.when(need[s] == 1)
            def _():
                for half in range(2):
                    shared(s, 2 * m + half).wait_recv()

    def own_piece_ready(t):
        send_own(t)
        give(0, t)

    def pass_on(k):
        receive(1, k - 1)
        send_held(k - 1)
        give_held(1, k - 1)

    def take(t):
        receive(2, t)
        give_held(2, t)

    pass_on(1)
    swap(1, 0).wait_recv()
    own_piece_ready(2)
    pass_on(2)
    swap(1, 1).wait_recv()
    own_piece_ready(3)
    swap(2, 0).wait_recv()
    own_piece_ready(4)
    pass_on(3)
    for half in range(2):
        relay_in(half).wait_recv()
        relay_out(half).start()
    swap(2, 1).wait_recv()
    own_piece_ready(5)
    take(0)
    pass_on(4)
    take(1)
    for m in range(2):
        @pl.loop(5 + 2 * m, 7 + 2 * m)
        def _(k):
            pass_on(k)

            @pl.when(k == 5)
            def _():
                for half in range(2):
                    relay_out(half).wait_recv()
                    own_piece_ready(6 + half)
            first = 2 * (k - 5 - 2 * m)
            pl.when(first == 0)(lambda: wait_shared(m))

            @pl.loop(first, jnp.minimum(first + 2, pair_count))
            def _(j):
                compare(m, j)
            take(k - 3)
        own_pair(m)
        finish_rows(m)
    for m in (2, 3):
        wait_shared(m, (0,))
        own_pair(m)
    wait_shared(2, range(1, SLOTS))

    @pl.loop(0, pair_count)
    def _(j):
        compare(2, j)
    take(6)
    take(7)
    finish_rows(2)
    wait_shared(3, range(1, SLOTS))

    @pl.loop(0, pair_count)
    def _(j):
        compare(3, j)
    finish_rows(3)

    for s in range(SLOTS):
        for t in range(4):
            z_of = (z + REL[t]) % 4
            for core in range(2):
                j = s * 8 + 2 * t + core
                both = jnp.maximum(row_line[j:j + 1, :], jnp.max(col_best[j], axis=0, keepdims=True))
                part[s * 2 + z_of // 2, pl.ds(2 * (z_of % 2) + core, 1), :] = both
        for half in range(2):
            copy = remote(part.at[s * 2 + half], parts_got.at[place[s] * 2 + h], r_send.at[s * 2 + half],
                          r_recv.at[place[s] * 2 + h], (owner_grp, held[s] * 2 + half))
            if s == 0:
                keep_it = jnp.logical_and(mine, zh == half)
                pl.when(jnp.logical_not(keep_it))(copy.start)

                @pl.when(keep_it)
                def _():
                    parts_got[h] = part[half]
            else:
                copy.start()

    ids_copy.wait_send()
    for half in range(2):
        for copy in (swap(1, half), swap(2, half), relay_in(half), relay_out(half)):
            copy.wait_send()
    for d in range(4):
        for t in range(STEPS):
            forward(d, t).wait_send()
    for s in range(SLOTS):
        for t in range(8):
            pl.when(sibling_need[s] == 1)(lambda s=s, t=t: share(s, t).wait_send())
    best = None
    for k in range(2 * SLOTS):
        got = remote(parts_got.at[k], parts_got.at[k], r_send.at[k], r_recv.at[k], sibling)
        if k < 2:
            pl.when(jnp.logical_not(jnp.logical_and(mine, h == k)))(got.wait_recv)
        else:
            got.wait_recv()
        best = parts_got[k] if best is None else jnp.maximum(best, parts_got[k])
    out[...] = best

    for s in range(SLOTS):
        for half in range(2):
            copy = remote(part.at[s * 2 + half], parts_got.at[place[s] * 2 + h], r_send.at[s * 2 + half],
                          r_recv.at[place[s] * 2 + h], (owner_grp, held[s] * 2 + half))
            if s == 0:
                pl.when(jnp.logical_not(jnp.logical_and(mine, zh == half)))(copy.wait_send)
            else:
                copy.wait_send()


def on_device(embeddings, cluster_ids):
    emb = embeddings.reshape(4, 128, D)
    ids = cluster_ids.reshape(128, 128)
    dma = pltpu.SemaphoreType.DMA
    best = pl.pallas_call(
        kernel,
        out_shape=jax.ShapeDtypeStruct((4, 128), jnp.float32),
        in_specs=[pl.BlockSpec(memory_space=pl.ANY), pl.BlockSpec(memory_space=pl.ANY)],
        out_specs=pl.BlockSpec(memory_space=pltpu.VMEM),
        scratch_shapes=[
            pltpu.VMEM((SLOTS, 1024, D), jnp.bfloat16),
            pltpu.VMEM((3, 128, D), jnp.bfloat16),
            pltpu.VMEM((4, 128, D), jnp.float32),
            pltpu.VMEM((128, 128), jnp.int32),
            pltpu.VMEM((128, 128), jnp.int32),
            pltpu.VMEM((SLOTS * 8, 128, 128), jnp.float32),
            pltpu.VMEM((128, 128), jnp.float32),
            pltpu.VMEM((SLOTS * 8, 128, 128), jnp.float32),
            pltpu.VMEM((SLOTS * 8, 8, 128), jnp.float32),
            pltpu.VMEM((SLOTS * 8, 128), jnp.float32),
            pltpu.VMEM((2 * SLOTS, 4, 128), jnp.float32),
            pltpu.VMEM((2 * SLOTS, 4, 128), jnp.float32),
            pltpu.VMEM((128, D), jnp.bfloat16),
            dma((4,)), dma, dma, dma, dma((3, 2)), dma((3, 2)), dma((2, 2)), dma((2,)), dma((4, STEPS)), dma((4, STEPS)),
            dma((SLOTS, 8)), dma((SLOTS, 8)), dma((2 * SLOTS,)), dma((2 * SLOTS,)),
        ],
        compiler_params=pltpu.CompilerParams(
            collective_id=0, has_side_effects=True, vmem_limit_bytes=60 * 1024 * 1024),
        cost_estimate=pl.CostEstimate(flops=7 * 10**9, bytes_accessed=2 * 10**6, transcendentals=0),
        name="best_match",
    )(emb, ids)
    return best.reshape(1, 512)


def solution(mesh):
    placed = (P(None, "grp", "blk", None, None), P("grp", None))
    return jax.shard_map(
        on_device, mesh=mesh, in_specs=placed, out_specs=P("grp", "blk"), check_vma=False
    )
```

```python
import functools

import jax
import jax.numpy as jnp
from jax import lax
from jax.experimental import pallas as pl
from jax.experimental.pallas import tpu as pltpu
from jax.sharding import PartitionSpec as P

MESH = pl.DeviceIdType.MESH
D = 768
SLOTS = 5
PIECE = 64
STEPS = 8

SRC = [[4, 0, 0, 2], [0, 4, 0, 1], [0, 0, 0, 2], [0, 0, 0, 1], [4, 0, 0, 2], [0, 4, 0, 1], [0, 0, 1, 2],
       [0, 0, 2, 1], [4, 0, 0, 0], [0, 4, 0, 0], [0, 1, 0, 3], [2, 0, 0, 3], [4, 0, 0, 0], [0, 4, 0, 0],
       [0, 0, 4, 0], [0, 0, 4, 0]]
DEP = [[2, 1, 2, 1], [1, 2, 2, 1], [1, 1, 2, 2], [1, 1, 2, 2], [2, 1, 1, 1], [1, 2, 1, 1], [1, 1, 2, 1],
       [1, 1, 2, 1], [2, 2, 1, 1], [2, 2, 1, 1], [1, 1, 1, 2], [1, 1, 1, 2], [2, 1, 2, 1], [1, 2, 2, 1],
       [1, 1, 2, 1], [1, 1, 2, 1]]
BLK = [[13, 3, 7, 12], [2, 12, 6, 13], [3, 1, 5, 10], [0, 2, 4, 11], [1, 7, 8, 0], [6, 0, 9, 1], [7, 5, 14, 2],
       [4, 6, 15, 3], [5, 10, 12, 4], [11, 4, 13, 5], [11, 9, 14, 7], [8, 10, 15, 6], [9, 15, 3, 8], [14, 8, 2, 9],
       [15, 13, 1, 10], [12, 14, 0, 11]]
IDX = [[1, 1, 1, 1], [1, 2, 1, 2], [2, 1, 1, 1], [1, 2, 1, 1], [2, 2, 1, 2], [2, 3, 1, 3], [3, 2, 1, 3],
       [2, 3, 1, 3], [3, 2, 3, 3], [2, 4, 3, 4], [3, 2, 2, 4], [2, 3, 2, 4], [3, 3, 4, 3], [3, 4, 4, 4],
       [4, 4, 4, 4], [4, 4, 4, 4]]
HOLD = [[0, 3, 4, 5, 15], [1, 2, 4, 5, 14], [2, 1, 3, 6, 13], [3, 0, 2, 7, 12], [4, 3, 7, 8, 9], [5, 2, 6, 8, 9],
        [6, 1, 5, 7, 11], [7, 0, 4, 6, 10], [8, 4, 11, 12, 13], [9, 5, 10, 12, 13], [10, 2, 8, 11, 14],
        [11, 3, 9, 10, 15], [12, 0, 1, 8, 15], [13, 0, 1, 9, 14], [14, 6, 10, 13, 15], [15, 7, 11, 12, 14]]
PAIRS = [[[(2, 4), (3, 4), (3, 1)], [(0, 2), (0, 3), (2, 3)]], [[(3, 2), (3, 4), (2, 4)], [(0, 1), (1, 3), (0, 3)]],
         [[(2, 1), (1, 3), (2, 3)], [(0, 4), (1, 4), (3, 4)]], [[(1, 2), (2, 3), (3, 4)], [(2, 0), (2, 4), (0, 4)]],
         [[(2, 3), (1, 2), (1, 3)], [(4, 3), (4, 0), (1, 0), (4, 1)]],
         [[(1, 3), (2, 1), (2, 3)], [(4, 3), (0, 3), (2, 0)]],
         [[(4, 1), (4, 2), (2, 3)], [(2, 1), (0, 1), (2, 0), (0, 3)]],
         [[(4, 2), (1, 2), (2, 3)], [(4, 1), (1, 0), (0, 3)]],
         [[(4, 3), (4, 2), (2, 3)], [(4, 0), (1, 0), (1, 3), (4, 1)]],
         [[(4, 3), (4, 1), (1, 3)], [(0, 3), (2, 0), (2, 3)]], [[(2, 1), (4, 2), (4, 1)], [(2, 0), (4, 0), (4, 3)]],
         [[(1, 0), (4, 1), (4, 0)], [(1, 2), (2, 0), (4, 2)]], [[(4, 2), (3, 4), (3, 1)], [(4, 0), (1, 0), (1, 2)]],
         [[(3, 2), (3, 4), (2, 4)], [(4, 1), (2, 0), (2, 1)]], [[(4, 2), (2, 1), (4, 1)], [(4, 0), (2, 0), (3, 4)]],
         [[(4, 1), (1, 2), (4, 2)], [(1, 0), (2, 0), (4, 0)]]]
EARLY = [[1, 1], [0, 1], [1, 0], [1, 1], [1, 2], [1, 2], [2, 3], [2, 2], [1, 1], [1, 1], [1, 1], [1, 2], [1, 1],
         [0, 1], [3, 2], [3, 3]]
NEED = [[[1, 2, 3, 4], [0, 2, 3]], [[2, 3, 4], [0, 1, 3]], [[1, 2, 3], [0, 1, 3, 4]], [[1, 2, 3, 4], [0, 2, 4]],
        [[1, 2, 3], [0, 1, 3, 4]], [[1, 2, 3], [0, 2, 3, 4]], [[1, 2, 3, 4], [0, 1, 2, 3]],
        [[1, 2, 3, 4], [0, 1, 3, 4]], [[2, 3, 4], [0, 1, 3, 4]], [[1, 3, 4], [0, 2, 3]], [[1, 2, 4], [0, 2, 3, 4]],
        [[0, 1, 4], [0, 1, 2, 4]], [[1, 2, 3, 4], [0, 1, 2, 4]], [[2, 3, 4], [0, 1, 2, 4]],
        [[1, 2, 4], [0, 2, 3, 4]], [[1, 2, 4], [0, 1, 2, 4]]]

REL = (0, 3, 1, 2)


def word(digits, base):
    total = 0
    for digit in reversed(digits):
        total = total * base + digit
    return total


def look_up(index, words):
    got = jnp.int32(words[0])
    for k in range(1, len(words)):
        got = jnp.where(index == k, jnp.int32(words[k]), got)
    return got


def digits_of(value, base, count):
    out = []
    for _ in range(count):
        out.append(value % base)
        value = value // base
    return out


def kernel(emb, ids_in, out, x, units, stage, ids_own, ids_got, ids_rows, ids_cols, row_best, col_best, row_line, part, parts_got,
           relay,
           load_sem, ids_sem, id_send, id_recv, z_send, z_recv, relay_send, relay_recv, f_send, f_recv, c_send, c_recv, r_send, r_recv):
    grp, blk = lax.axis_index("grp"), lax.axis_index("blk")
    h, zl = grp % 2, grp // 2
    p, zh = blk // 2, blk % 2
    z = zh * 2 + zl
    px, py = p % 4, p // 4

    def device(z_of, core, chip):
        return ((z_of % 2) * 2 + core, chip * 2 + z_of // 2)

    def group_of(z_of):
        return (z_of % 2) * 2 + z_of // 2

    near = [py * 4 + (px + 1) % 4, py * 4 + (px + 3) % 4, ((py + 1) % 4) * 4 + px, ((py + 3) % 4) * 4 + px]
    first = look_up(p, [word(SRC[c], 8) + 4096 * word(DEP[c], 4) for c in range(16)])
    src = digits_of(first, 8, 4)
    dep = digits_of(first // 4096, 4, 4)
    held = [p] + digits_of(look_up(p, [word(BLK[c], 16) for c in range(16)]), 16, 4)
    third = look_up(p, [word(IDX[c], 8) + 4096 * word(HOLD[c][1:], 16) for c in range(16)])
    place = [jnp.int32(0)] + digits_of(third, 8, 4)
    holders = [p] + digits_of(third // 4096, 16, 4)
    lists = []
    for c in range(16):
        for core in range(2):
            flat = [slot for pair in PAIRS[c][core] for slot in pair]
            lists.append(len(PAIRS[c][core]) + 8 * EARLY[c][core] + 64 * word(flat + [0] * (8 - len(flat)), 8))
    todo = look_up(p * 2 + h, lists)
    pair_count, early_count = todo % 8, todo // 8 % 8
    todo = digits_of(todo // 64, 8, 8)

    needs = [[sum(1 << slot for slot in NEED[c][core]) for core in range(2)] for c in range(16)]
    need = digits_of(look_up(p * 2 + h, [needs[c][core] for c in range(16) for core in range(2)]), 2, SLOTS)
    sibling_need = digits_of(look_up(p * 2 + h, [needs[c][1 - core] for c in range(16) for core in range(2)]), 2, SLOTS)

    sibling = device(z, 1 - h, p)
    owner_grp = zl * 2 + zh
    mine = h == zh

    loads = []
    for k, rel in enumerate((0, 1, 3, 2)):
        loads.append(pltpu.make_async_copy(emb.at[group_of((z + rel) % 4)], stage.at[k], load_sem.at[k]))
        loads[-1].start()

    ids_load = pltpu.make_async_copy(ids_in, ids_own, ids_sem)
    ids_load.start()

    barrier = pltpu.get_barrier_semaphore()
    for rel in (1, 3):
        pl.semaphore_signal(barrier, inc=1, device_id=device((z + rel) % 4, h, p), device_id_type=MESH)
    for d in range(4):
        pl.semaphore_signal(barrier, inc=1, device_id=device(z, h, near[d]), device_id_type=MESH)
    pl.semaphore_signal(barrier, inc=1, device_id=sibling, device_id_type=MESH)
    from_z = 2 * h + zl
    for k in range(SLOTS):
        for core in range(2):
            def tell():
                pl.semaphore_signal(barrier, inc=1, device_id=device(from_z, core, holders[k]), device_id_type=MESH)
            if k == 0:
                pl.when(jnp.logical_not(jnp.logical_and(mine, h == core)))(tell)
            else:
                tell()

    def normalise(k):
        loads[k].wait()
        v = stage[k]
        total = jnp.sum(v * v, axis=-1, keepdims=True)
        return (v / jnp.sqrt(total + 1e-06)).astype(jnp.bfloat16)

    own_rows = pl.multiple_of(h * 128, 128)
    x[0, pl.ds(own_rows, 128), :] = normalise(0)
    pl.semaphore_wait(barrier, jnp.where(mine, 16, 17))

    def remote(src_ref, dst_ref, send_sem, recv_sem, to):
        return pltpu.make_async_remote_copy(
            src_ref=src_ref, dst_ref=dst_ref, send_sem=send_sem, recv_sem=recv_sem, device_id=to, device_id_type=MESH)

    def part_rows(t):
        return pl.ds(pl.multiple_of((t // 2) * 256 + h * 128 + (t % 2) * PIECE, PIECE), PIECE)

    def forward(d, t):
        rows = part_rows(t)
        return remote(x.at[src[d], rows, :], x.at[1 + (d ^ 1), rows, :], f_send.at[d, t], f_recv.at[d ^ 1, t],
                      device(z, h, near[d]))

    def arrival(s, t):
        rows = part_rows(t)
        return remote(x.at[s, rows, :], x.at[s, rows, :], f_send.at[s - 1, t], f_recv.at[s - 1, t],
                      device(z, h, near[s - 1]))

    def swap(k, half):
        rows = pl.ds(pl.multiple_of(k * 256 + h * 128 + half * 64, 64), 64)
        return remote(units.at[k - 1, pl.ds(half * 64, 64), :], x.at[0, rows, :], z_send.at[k - 1, half],
                      z_recv.at[k - 1, half], device((z + (1, 3, 2)[k - 1]) % 4, h, p))

    between = device((z + jnp.where(h == 0, 1, 3)) % 4, h, p)

    def relay_in(half):
        rows = pl.ds(half * 64, 64)
        return remote(units.at[2, rows, :], relay.at[rows, :], relay_send.at[0, half], relay_recv.at[half], between)

    def relay_out(half):
        rows = pl.ds(pl.multiple_of(3 * 256 + h * 128 + half * 64, 64), 64)
        return remote(relay.at[pl.ds(half * 64, 64), :], x.at[0, rows, :], relay_send.at[1, half], z_recv.at[2, half],
                      between)

    def share_rows(t, core):
        return pl.ds(pl.multiple_of((t // 2) * 256 + core * 128 + (t % 2) * 64, 64), 64)

    def share(s, t):
        rows = share_rows(t, h)
        return remote(x.at[s, rows, :], x.at[s, rows, :], c_send.at[s, t], c_recv.at[s, t], sibling)

    def shared(s, t):
        rows = share_rows(t, 1 - h)
        return remote(x.at[s, rows, :], x.at[s, rows, :], c_send.at[s, t], c_recv.at[s, t], sibling)

    def give(s, t):
        pl.when(sibling_need[s] == 1)(lambda: share(s, t).start())

    def send_own(t):
        for d in range(4):
            pl.when(src[d] == 0)(lambda d=d: forward(d, t).start())

    def send_held(t):
        for d in range(4):
            pl.when(src[d] != 0)(lambda d=d: forward(d, t).start())

    def receive(links, t):
        for s in range(1, SLOTS):
            pl.when(dep[s - 1] == links)(lambda s=s: arrival(s, t).wait_recv())

    def give_held(links, t):
        for s in range(1, SLOTS):
            pl.when(dep[s - 1] == links)(lambda s=s: give(s, t))

    for t in range(2):
        send_own(t)
    units[0] = normalise(1)
    for half in range(2):
        swap(1, half).start()
    units[1] = normalise(2)
    for half in range(2):
        swap(2, half).start()
    units[2] = normalise(3)
    for half in range(2):
        relay_in(half).start()
    ids_copy = remote(ids_in, ids_got, id_send, id_recv, sibling)
    ids_copy.start()
    give(0, 0)
    give(0, 1)
    row_best[...] = jnp.full_like(row_best, -1.0)
    col_best[...] = jnp.full_like(col_best, -1.0)
    row_line[...] = jnp.full_like(row_line, -1.0)

    ids_load.wait()
    ids_copy.wait_recv()
    ids_cols[...] = jnp.zeros_like(ids_cols)
    for s in range(SLOTS):
        for t in range(4):
            for core in range(2):
                unit = held[s] * 8 + 2 * ((z + REL[t]) % 4) + core
                got = jnp.where(mine, ids_own[pl.ds(unit, 1), :], ids_got[pl.ds(unit, 1), :])
                ids_cols[pl.ds(s * 8 + 2 * t + core, 1), :] = got.astype(jnp.float32)
    turned = ids_cols[...].T
    for j in range(SLOTS * 8):
        ids_rows[j] = jnp.broadcast_to(turned[:, j:j + 1], (128, 128))

    def strip(a, t, b, count, diagonal=False):
        sim = lax.dot_general(x[a, 256 * t:256 * t + 256, :], x[b, 0:256 * count, :], (((1,), (1,)), ((), ())),
                              preferred_element_type=jnp.float32)
        for r in range(4):
            unit, first_row = a * 8 + 2 * t + r // 2, 64 * (r % 2)
            row_ids = ids_rows[unit, first_row:first_row + 64]
            best = row_best[unit, first_row:first_row + 64]
            for c in range(2 * count):
                keep = row_ids == ids_cols[pl.ds(b * 8 + c, 1), :]
                if diagonal and c // 2 == t:
                    row = lax.broadcasted_iota(jnp.int32, (64, 128), 0) + 64 * r
                    col = lax.broadcasted_iota(jnp.int32, (64, 128), 1) + 128 * (c % 2)
                    keep = jnp.logical_and(keep, row != col)
                kept = jnp.where(keep, sim[64 * r:64 * r + 64, 128 * c:128 * c + 128], jnp.float32(-1.0))
                down = jnp.max(kept.reshape(8, 8, 128), axis=0)
                col_best[b * 8 + c] = jnp.maximum(col_best[b * 8 + c], down)
                best = jnp.maximum(best, kept)
            row_best[unit, first_row:first_row + 64] = best

    def compare(t, j):
        a, b = todo[0], todo[1]
        for k in range(1, 4):
            a = jnp.where(j == k, todo[2 * k], a)
            b = jnp.where(j == k, todo[2 * k + 1], b)
        strip(a, t, b, t + 1)
        if t:
            strip(b, t, a, t)

    def own_pair(t):
        pl.when(h == 1)(lambda: strip(0, t, 0, t + 1, diagonal=True))

    def finish_rows(t):
        for s in range(SLOTS):
            @pl.when(need[s] == 1)
            def _():
                for core in range(2):
                    unit = s * 8 + 2 * t + core
                    row_line[unit:unit + 1, :] = jnp.max(row_best[unit].T, axis=0, keepdims=True)

    def wait_shared(m, links):
        for s in range(SLOTS):
            there = need[s] == 1
            if s == 0:
                if links:
                    continue
            elif links:
                there = jnp.logical_and(there, dep[s - 1] == links)
            else:
                continue

            @pl.when(there)
            def _():
                for half in range(2):
                    shared(s, 2 * m + half).wait_recv()

    def own_piece_ready(t):
        send_own(t)
        give(0, t)

    def pass_on(k):
        receive(1, k - 1)
        send_held(k - 1)
        give_held(1, k - 1)

    def take(t):
        receive(2, t)
        give_held(2, t)

    pass_on(1)
    swap(1, 0).wait_recv()
    own_piece_ready(2)
    pass_on(2)
    swap(1, 1).wait_recv()
    own_piece_ready(3)
    swap(2, 0).wait_recv()
    own_piece_ready(4)
    pass_on(3)
    for half in range(2):
        relay_in(half).wait_recv()
        relay_out(half).start()
    swap(2, 1).wait_recv()
    own_piece_ready(5)
    take(0)
    pass_on(4)
    take(1)
    pass_on(5)
    for half in range(2):
        relay_out(half).wait_recv()
        own_piece_ready(6 + half)
    wait_shared(0, 0)
    wait_shared(0, 1)
    wait_shared(0, 2)

    @pl.loop(0, pair_count)
    def _(j):
        compare(0, j)
    own_pair(0)
    take(2)
    pass_on(6)
    for m in (1, 2, 3):
        wait_shared(m, 0)
        own_pair(m)
    finish_rows(0)
    take(3)
    pass_on(7)
    wait_shared(1, 1)
    wait_shared(1, 2)

    @pl.loop(0, pair_count)
    def _(j):
        compare(1, j)
    take(4)
    pass_on(8)
    take(5)

    for m in (2, 3):
        wait_shared(m, 1)

        @pl.loop(0, pair_count)
        def _(j):
            pl.when(j == early_count)(lambda: wait_shared(m, 2))
            compare(m, j)
        if m == 2:
            finish_rows(1)
            take(6)
            finish_rows(2)
            take(7)
    finish_rows(3)

    for s in range(SLOTS):
        for t in range(4):
            z_of = (z + REL[t]) % 4
            for core in range(2):
                j = s * 8 + 2 * t + core
                both = jnp.maximum(row_line[j:j + 1, :], jnp.max(col_best[j], axis=0, keepdims=True))
                part[s * 2 + z_of // 2, pl.ds(2 * (z_of % 2) + core, 1), :] = both
        for half in range(2):
            copy = remote(part.at[s * 2 + half], parts_got.at[place[s] * 2 + h], r_send.at[s * 2 + half],
                          r_recv.at[place[s] * 2 + h], (owner_grp, held[s] * 2 + half))
            if s == 0:
                keep_it = jnp.logical_and(mine, zh == half)
                pl.when(jnp.logical_not(keep_it))(copy.start)

                @pl.when(keep_it)
                def _():
                    parts_got[h] = part[half]
            else:
                copy.start()

    ids_copy.wait_send()
    for half in range(2):
        for copy in (swap(1, half), swap(2, half), relay_in(half), relay_out(half)):
            copy.wait_send()
    for d in range(4):
        for t in range(STEPS):
            forward(d, t).wait_send()
    for s in range(SLOTS):
        for t in range(8):
            pl.when(sibling_need[s] == 1)(lambda s=s, t=t: share(s, t).wait_send())
    best = None
    for k in range(2 * SLOTS):
        got = remote(parts_got.at[k], parts_got.at[k], r_send.at[k], r_recv.at[k], sibling)
        if k < 2:
            pl.when(jnp.logical_not(jnp.logical_and(mine, h == k)))(got.wait_recv)
        else:
            got.wait_recv()
        best = parts_got[k] if best is None else jnp.maximum(best, parts_got[k])
    out[...] = best

    for s in range(SLOTS):
        for half in range(2):
            copy = remote(part.at[s * 2 + half], parts_got.at[place[s] * 2 + h], r_send.at[s * 2 + half],
                          r_recv.at[place[s] * 2 + h], (owner_grp, held[s] * 2 + half))
            if s == 0:
                pl.when(jnp.logical_not(jnp.logical_and(mine, zh == half)))(copy.wait_send)
            else:
                copy.wait_send()


def on_device(embeddings, cluster_ids):
    emb = embeddings.reshape(4, 128, D)
    ids = cluster_ids.reshape(128, 128)
    dma = pltpu.SemaphoreType.DMA
    best = pl.pallas_call(
        kernel,
        out_shape=jax.ShapeDtypeStruct((4, 128), jnp.float32),
        in_specs=[pl.BlockSpec(memory_space=pl.ANY), pl.BlockSpec(memory_space=pl.ANY)],
        out_specs=pl.BlockSpec(memory_space=pltpu.VMEM),
        scratch_shapes=[
            pltpu.VMEM((SLOTS, 1024, D), jnp.bfloat16),
            pltpu.VMEM((3, 128, D), jnp.bfloat16),
            pltpu.VMEM((4, 128, D), jnp.float32),
            pltpu.VMEM((128, 128), jnp.int32),
            pltpu.VMEM((128, 128), jnp.int32),
            pltpu.VMEM((SLOTS * 8, 128, 128), jnp.float32),
            pltpu.VMEM((128, 128), jnp.float32),
            pltpu.VMEM((SLOTS * 8, 128, 128), jnp.float32),
            pltpu.VMEM((SLOTS * 8, 8, 128), jnp.float32),
            pltpu.VMEM((SLOTS * 8, 128), jnp.float32),
            pltpu.VMEM((2 * SLOTS, 4, 128), jnp.float32),
            pltpu.VMEM((2 * SLOTS, 4, 128), jnp.float32),
            pltpu.VMEM((128, D), jnp.bfloat16),
            dma((4,)), dma, dma, dma, dma((3, 2)), dma((3, 2)), dma((2, 2)), dma((2,)), dma((4, STEPS)), dma((4, STEPS)),
            dma((SLOTS, 8)), dma((SLOTS, 8)), dma((2 * SLOTS,)), dma((2 * SLOTS,)),
        ],
        compiler_params=pltpu.CompilerParams(
            collective_id=0, has_side_effects=True, vmem_limit_bytes=60 * 1024 * 1024),
        cost_estimate=pl.CostEstimate(flops=7 * 10**9, bytes_accessed=2 * 10**6, transcendentals=0),
        name="best_match",
    )(emb, ids)
    return best.reshape(1, 512)


def solution(mesh):
    placed = (P(None, "grp", "blk", None, None), P("grp", None))
    return jax.shard_map(
        on_device, mesh=mesh, in_specs=placed, out_specs=P("grp", "blk"), check_vma=False
    )
```

```python
import functools

import jax
import jax.numpy as jnp
from jax import lax
from jax.experimental import pallas as pl
from jax.experimental.pallas import tpu as pltpu
from jax.sharding import PartitionSpec as P

MESH = pl.DeviceIdType.MESH
D = 768
SLOTS = 5
PIECE = 64
STEPS = 8

SRC = [[4, 0, 0, 2], [0, 4, 0, 1], [0, 0, 0, 2], [0, 0, 0, 1], [4, 0, 0, 2], [0, 4, 0, 1], [0, 0, 1, 2],
       [0, 0, 2, 1], [4, 0, 0, 0], [0, 4, 0, 0], [0, 1, 0, 3], [2, 0, 0, 3], [4, 0, 0, 0], [0, 4, 0, 0],
       [0, 0, 4, 0], [0, 0, 4, 0]]
DEP = [[2, 1, 2, 1], [1, 2, 2, 1], [1, 1, 2, 2], [1, 1, 2, 2], [2, 1, 1, 1], [1, 2, 1, 1], [1, 1, 2, 1],
       [1, 1, 2, 1], [2, 2, 1, 1], [2, 2, 1, 1], [1, 1, 1, 2], [1, 1, 1, 2], [2, 1, 2, 1], [1, 2, 2, 1],
       [1, 1, 2, 1], [1, 1, 2, 1]]
BLK = [[13, 3, 7, 12], [2, 12, 6, 13], [3, 1, 5, 10], [0, 2, 4, 11], [1, 7, 8, 0], [6, 0, 9, 1], [7, 5, 14, 2],
       [4, 6, 15, 3], [5, 10, 12, 4], [11, 4, 13, 5], [11, 9, 14, 7], [8, 10, 15, 6], [9, 15, 3, 8], [14, 8, 2, 9],
       [15, 13, 1, 10], [12, 14, 0, 11]]
IDX = [[1, 1, 1, 1], [1, 2, 1, 2], [2, 1, 1, 1], [1, 2, 1, 1], [2, 2, 1, 2], [2, 3, 1, 3], [3, 2, 1, 3],
       [2, 3, 1, 3], [3, 2, 3, 3], [2, 4, 3, 4], [3, 2, 2, 4], [2, 3, 2, 4], [3, 3, 4, 3], [3, 4, 4, 4],
       [4, 4, 4, 4], [4, 4, 4, 4]]
HOLD = [[0, 3, 4, 5, 15], [1, 2, 4, 5, 14], [2, 1, 3, 6, 13], [3, 0, 2, 7, 12], [4, 3, 7, 8, 9], [5, 2, 6, 8, 9],
        [6, 1, 5, 7, 11], [7, 0, 4, 6, 10], [8, 4, 11, 12, 13], [9, 5, 10, 12, 13], [10, 2, 8, 11, 14],
        [11, 3, 9, 10, 15], [12, 0, 1, 8, 15], [13, 0, 1, 9, 14], [14, 6, 10, 13, 15], [15, 7, 11, 12, 14]]
PAIRS = [[[(2, 4), (3, 4), (3, 1)], [(0, 2), (0, 3), (2, 3)]], [[(3, 2), (3, 4), (2, 4)], [(0, 1), (1, 3), (0, 3)]],
         [[(2, 1), (1, 3), (2, 3)], [(0, 4), (1, 4), (3, 4)]], [[(1, 2), (2, 3), (3, 4)], [(2, 0), (2, 4), (0, 4)]],
         [[(2, 3), (1, 2), (1, 3)], [(4, 3), (4, 0), (1, 0), (4, 1)]],
         [[(1, 3), (2, 1), (2, 3)], [(4, 3), (0, 3), (2, 0)]],
         [[(4, 1), (4, 2), (2, 3)], [(2, 1), (0, 1), (2, 0), (0, 3)]],
         [[(4, 2), (1, 2), (2, 3)], [(4, 1), (1, 0), (0, 3)]],
         [[(4, 3), (4, 2), (2, 3)], [(4, 0), (1, 0), (1, 3), (4, 1)]],
         [[(4, 3), (4, 1), (1, 3)], [(0, 3), (2, 0), (2, 3)]], [[(2, 1), (4, 2), (4, 1)], [(2, 0), (4, 0), (4, 3)]],
         [[(1, 0), (4, 1), (4, 0)], [(1, 2), (2, 0), (4, 2)]], [[(4, 2), (3, 4), (3, 1)], [(4, 0), (1, 0), (1, 2)]],
         [[(3, 2), (3, 4), (2, 4)], [(4, 1), (2, 0), (2, 1)]], [[(4, 2), (2, 1), (4, 1)], [(4, 0), (2, 0), (3, 4)]],
         [[(4, 1), (1, 2), (4, 2)], [(1, 0), (2, 0), (4, 0)]]]
EARLY = [[1, 1], [0, 1], [1, 0], [1, 1], [1, 2], [1, 2], [2, 3], [2, 2], [1, 1], [1, 1], [1, 1], [1, 2], [1, 1],
         [0, 1], [3, 2], [3, 3]]
NEED = [[[1, 2, 3, 4], [0, 2, 3]], [[2, 3, 4], [0, 1, 3]], [[1, 2, 3], [0, 1, 3, 4]], [[1, 2, 3, 4], [0, 2, 4]],
        [[1, 2, 3], [0, 1, 3, 4]], [[1, 2, 3], [0, 2, 3, 4]], [[1, 2, 3, 4], [0, 1, 2, 3]],
        [[1, 2, 3, 4], [0, 1, 3, 4]], [[2, 3, 4], [0, 1, 3, 4]], [[1, 3, 4], [0, 2, 3]], [[1, 2, 4], [0, 2, 3, 4]],
        [[0, 1, 4], [0, 1, 2, 4]], [[1, 2, 3, 4], [0, 1, 2, 4]], [[2, 3, 4], [0, 1, 2, 4]],
        [[1, 2, 4], [0, 2, 3, 4]], [[1, 2, 4], [0, 1, 2, 4]]]

REL = (0, 3, 1, 2)


def word(digits, base):
    total = 0
    for digit in reversed(digits):
        total = total * base + digit
    return total


def look_up(index, words):
    got = jnp.int32(words[0])
    for k in range(1, len(words)):
        got = jnp.where(index == k, jnp.int32(words[k]), got)
    return got


def digits_of(value, base, count):
    out = []
    for _ in range(count):
        out.append(value % base)
        value = value // base
    return out


def kernel(emb, ids_in, out, x, units, stage, ids_own, ids_got, ids_rows, ids_cols, row_best, col_best, row_line, part, parts_got,
           relay,
           load_sem, ids_sem, id_send, id_recv, z_send, z_recv, relay_send, relay_recv, f_send, f_recv, c_send, c_recv, r_send, r_recv):
    grp, blk = lax.axis_index("grp"), lax.axis_index("blk")
    h, zl = grp % 2, grp // 2
    p, zh = blk // 2, blk % 2
    z = zh * 2 + zl
    px, py = p % 4, p // 4

    def device(z_of, core, chip):
        return ((z_of % 2) * 2 + core, chip * 2 + z_of // 2)

    def group_of(z_of):
        return (z_of % 2) * 2 + z_of // 2

    near = [py * 4 + (px + 1) % 4, py * 4 + (px + 3) % 4, ((py + 1) % 4) * 4 + px, ((py + 3) % 4) * 4 + px]
    first = look_up(p, [word(SRC[c], 8) + 4096 * word(DEP[c], 4) for c in range(16)])
    src = digits_of(first, 8, 4)
    dep = digits_of(first // 4096, 4, 4)
    held = [p] + digits_of(look_up(p, [word(BLK[c], 16) for c in range(16)]), 16, 4)
    third = look_up(p, [word(IDX[c], 8) + 4096 * word(HOLD[c][1:], 16) for c in range(16)])
    place = [jnp.int32(0)] + digits_of(third, 8, 4)
    holders = [p] + digits_of(third // 4096, 16, 4)
    lists = []
    for c in range(16):
        for core in range(2):
            flat = [slot for pair in PAIRS[c][core] for slot in pair]
            lists.append(len(PAIRS[c][core]) + 8 * EARLY[c][core] + 64 * word(flat + [0] * (8 - len(flat)), 8))
    todo = look_up(p * 2 + h, lists)
    pair_count, early_count = todo % 8, todo // 8 % 8
    todo = digits_of(todo // 64, 8, 8)

    needs = [[sum(1 << slot for slot in NEED[c][core]) for core in range(2)] for c in range(16)]
    need = digits_of(look_up(p * 2 + h, [needs[c][core] for c in range(16) for core in range(2)]), 2, SLOTS)
    sibling_need = digits_of(look_up(p * 2 + h, [needs[c][1 - core] for c in range(16) for core in range(2)]), 2, SLOTS)

    sibling = device(z, 1 - h, p)
    owner_grp = zl * 2 + zh
    mine = h == zh

    loads = []
    for k, rel in enumerate((0, 1, 3, 2)):
        loads.append(pltpu.make_async_copy(emb.at[group_of((z + rel) % 4)], stage.at[k], load_sem.at[k]))
        loads[-1].start()

    ids_load = pltpu.make_async_copy(ids_in, ids_own, ids_sem)
    ids_load.start()

    barrier = pltpu.get_barrier_semaphore()
    for rel in (1, 3):
        pl.semaphore_signal(barrier, inc=1, device_id=device((z + rel) % 4, h, p), device_id_type=MESH)
    for d in range(4):
        pl.semaphore_signal(barrier, inc=1, device_id=device(z, h, near[d]), device_id_type=MESH)
    pl.semaphore_signal(barrier, inc=1, device_id=sibling, device_id_type=MESH)
    from_z = 2 * h + zl
    for k in range(SLOTS):
        for core in range(2):
            def tell():
                pl.semaphore_signal(barrier, inc=1, device_id=device(from_z, core, holders[k]), device_id_type=MESH)
            if k == 0:
                pl.when(jnp.logical_not(jnp.logical_and(mine, h == core)))(tell)
            else:
                tell()

    def normalise(k):
        loads[k].wait()
        v = stage[k]
        total = jnp.sum(v * v, axis=-1, keepdims=True)
        return (v / jnp.sqrt(total + 1e-06)).astype(jnp.bfloat16)

    own_rows = pl.multiple_of(h * 128, 128)
    x[0, pl.ds(own_rows, 128), :] = normalise(0)
    pl.semaphore_wait(barrier, jnp.where(mine, 16, 17))

    def remote(src_ref, dst_ref, send_sem, recv_sem, to):
        return pltpu.make_async_remote_copy(
            src_ref=src_ref, dst_ref=dst_ref, send_sem=send_sem, recv_sem=recv_sem, device_id=to, device_id_type=MESH)

    def part_rows(t):
        return pl.ds(pl.multiple_of((t // 2) * 256 + h * 128 + (t % 2) * PIECE, PIECE), PIECE)

    def forward(d, t):
        rows = part_rows(t)
        return remote(x.at[src[d], rows, :], x.at[1 + (d ^ 1), rows, :], f_send.at[d, t], f_recv.at[d ^ 1, t],
                      device(z, h, near[d]))

    def arrival(s, t):
        rows = part_rows(t)
        return remote(x.at[s, rows, :], x.at[s, rows, :], f_send.at[s - 1, t], f_recv.at[s - 1, t],
                      device(z, h, near[s - 1]))

    def swap(k, half):
        rows = pl.ds(pl.multiple_of(k * 256 + h * 128 + half * 64, 64), 64)
        return remote(units.at[k - 1, pl.ds(half * 64, 64), :], x.at[0, rows, :], z_send.at[k - 1, half],
                      z_recv.at[k - 1, half], device((z + (1, 3, 2)[k - 1]) % 4, h, p))

    between = device((z + jnp.where(h == 0, 1, 3)) % 4, h, p)

    def relay_in(half):
        rows = pl.ds(half * 64, 64)
        return remote(units.at[2, rows, :], relay.at[rows, :], relay_send.at[0, half], relay_recv.at[half], between)

    def relay_out(half):
        rows = pl.ds(pl.multiple_of(3 * 256 + h * 128 + half * 64, 64), 64)
        return remote(relay.at[pl.ds(half * 64, 64), :], x.at[0, rows, :], relay_send.at[1, half], z_recv.at[2, half],
                      between)

    def share_rows(t, core):
        return pl.ds(pl.multiple_of((t // 2) * 256 + core * 128 + (t % 2) * 64, 64), 64)

    def share(s, t):
        rows = share_rows(t, h)
        return remote(x.at[s, rows, :], x.at[s, rows, :], c_send.at[s, t], c_recv.at[s, t], sibling)

    def shared(s, t):
        rows = share_rows(t, 1 - h)
        return remote(x.at[s, rows, :], x.at[s, rows, :], c_send.at[s, t], c_recv.at[s, t], sibling)

    def give(s, t):
        pl.when(sibling_need[s] == 1)(lambda: share(s, t).start())

    def send_own(t):
        for d in range(4):
            pl.when(src[d] == 0)(lambda d=d: forward(d, t).start())

    def send_held(t):
        for d in range(4):
            pl.when(src[d] != 0)(lambda d=d: forward(d, t).start())

    def receive(links, t):
        for s in range(1, SLOTS):
            pl.when(dep[s - 1] == links)(lambda s=s: arrival(s, t).wait_recv())

    def give_held(links, t):
        for s in range(1, SLOTS):
            pl.when(dep[s - 1] == links)(lambda s=s: give(s, t))

    for t in range(2):
        send_own(t)
    units[0] = normalise(1)
    for half in range(2):
        swap(1, half).start()
    units[1] = normalise(2)
    for half in range(2):
        swap(2, half).start()
    units[2] = normalise(3)
    for half in range(2):
        relay_in(half).start()
    ids_copy = remote(ids_in, ids_got, id_send, id_recv, sibling)
    ids_copy.start()
    give(0, 0)
    give(0, 1)
    row_best[...] = jnp.full_like(row_best, -1.0)
    col_best[...] = jnp.full_like(col_best, -1.0)
    row_line[...] = jnp.full_like(row_line, -1.0)

    ids_load.wait()
    ids_copy.wait_recv()
    ids_cols[...] = jnp.zeros_like(ids_cols)
    for s in range(SLOTS):
        for t in range(4):
            for core in range(2):
                unit = held[s] * 8 + 2 * ((z + REL[t]) % 4) + core
                got = jnp.where(mine, ids_own[pl.ds(unit, 1), :], ids_got[pl.ds(unit, 1), :])
                ids_cols[pl.ds(s * 8 + 2 * t + core, 1), :] = got.astype(jnp.float32)
    turned = ids_cols[...].T
    for j in range(SLOTS * 8):
        ids_rows[j] = jnp.broadcast_to(turned[:, j:j + 1], (128, 128))

    def strip(a, t, b, count, diagonal=False):
        sim = lax.dot_general(x[a, 256 * t:256 * t + 256, :], x[b, 0:256 * count, :], (((1,), (1,)), ((), ())),
                              preferred_element_type=jnp.float32)
        for r in range(4):
            unit, first_row = a * 8 + 2 * t + r // 2, 64 * (r % 2)
            row_ids = ids_rows[unit, first_row:first_row + 64]
            best = row_best[unit, first_row:first_row + 64]
            for c in range(2 * count):
                keep = row_ids == ids_cols[pl.ds(b * 8 + c, 1), :]
                if diagonal and c // 2 == t:
                    row = lax.broadcasted_iota(jnp.int32, (64, 128), 0) + 64 * r
                    col = lax.broadcasted_iota(jnp.int32, (64, 128), 1) + 128 * (c % 2)
                    keep = jnp.logical_and(keep, row != col)
                kept = jnp.where(keep, sim[64 * r:64 * r + 64, 128 * c:128 * c + 128], jnp.float32(-1.0))
                down = jnp.max(kept.reshape(8, 8, 128), axis=0)
                col_best[b * 8 + c] = jnp.maximum(col_best[b * 8 + c], down)
                best = jnp.maximum(best, kept)
            row_best[unit, first_row:first_row + 64] = best

    def compare(t, j):
        a, b = todo[0], todo[1]
        for k in range(1, 4):
            a = jnp.where(j == k, todo[2 * k], a)
            b = jnp.where(j == k, todo[2 * k + 1], b)
        strip(a, t, b, t + 1)
        if t:
            strip(b, t, a, t)

    def own_pair(t):
        pl.when(h == 1)(lambda: strip(0, t, 0, t + 1, diagonal=True))

    def finish_rows(t):
        for s in range(SLOTS):
            @pl.when(need[s] == 1)
            def _():
                for core in range(2):
                    unit = s * 8 + 2 * t + core
                    row_line[unit:unit + 1, :] = jnp.max(row_best[unit].T, axis=0, keepdims=True)

    def wait_shared(m, links):
        for s in range(SLOTS):
            there = need[s] == 1
            if s == 0:
                if links:
                    continue
            elif links:
                there = jnp.logical_and(there, dep[s - 1] == links)
            else:
                continue

            @pl.when(there)
            def _():
                for half in range(2):
                    shared(s, 2 * m + half).wait_recv()

    def own_piece_ready(t):
        send_own(t)
        give(0, t)

    def pass_on(k):
        receive(1, k - 1)
        send_held(k - 1)
        give_held(1, k - 1)

    def take(t):
        receive(2, t)
        give_held(2, t)

    pass_on(1)
    swap(1, 0).wait_recv()
    own_piece_ready(2)
    pass_on(2)
    swap(1, 1).wait_recv()
    own_piece_ready(3)
    swap(2, 0).wait_recv()
    own_piece_ready(4)
    pass_on(3)
    for half in range(2):
        relay_in(half).wait_recv()
        relay_out(half).start()
    swap(2, 1).wait_recv()
    own_piece_ready(5)
    wait_shared(0, 0)
    own_pair(0)
    take(0)
    pass_on(4)
    wait_shared(1, 0)
    own_pair(1)
    take(1)
    pass_on(5)
    for half in range(2):
        relay_out(half).wait_recv()
        own_piece_ready(6 + half)
    wait_shared(0, 1)
    wait_shared(0, 2)

    @pl.loop(0, pair_count)
    def _(j):
        compare(0, j)
    take(2)
    pass_on(6)
    for m in (2, 3):
        wait_shared(m, 0)
        own_pair(m)
    take(3)

    @pl.loop(0, 2)
    def _(k):
        pass_on(7 + k)

        @pl.when(k == 0)
        def _():
            wait_shared(1, 1)
            wait_shared(1, 2)

        @pl.loop(2 * k, jnp.minimum(2 * k + 2, pair_count))
        def _(j):
            compare(1, j)
        take(4 + k)
    finish_rows(0)

    for m in (2, 3):
        wait_shared(m, 1)

        @pl.loop(0, pair_count)
        def _(j):
            pl.when(j == early_count)(lambda: wait_shared(m, 2))
            compare(m, j)
        if m == 2:
            finish_rows(1)
            take(6)
            finish_rows(2)
            take(7)
    finish_rows(3)

    for s in range(SLOTS):
        for t in range(4):
            z_of = (z + REL[t]) % 4
            for core in range(2):
                j = s * 8 + 2 * t + core
                both = jnp.maximum(row_line[j:j + 1, :], jnp.max(col_best[j], axis=0, keepdims=True))
                part[s * 2 + z_of // 2, pl.ds(2 * (z_of % 2) + core, 1), :] = both
        for half in range(2):
            copy = remote(part.at[s * 2 + half], parts_got.at[place[s] * 2 + h], r_send.at[s * 2 + half],
                          r_recv.at[place[s] * 2 + h], (owner_grp, held[s] * 2 + half))
            if s == 0:
                keep_it = jnp.logical_and(mine, zh == half)
                pl.when(jnp.logical_not(keep_it))(copy.start)

                @pl.when(keep_it)
                def _():
                    parts_got[h] = part[half]
            else:
                copy.start()

    ids_copy.wait_send()
    for half in range(2):
        for copy in (swap(1, half), swap(2, half), relay_in(half), relay_out(half)):
            copy.wait_send()
    for d in range(4):
        for t in range(STEPS):
            forward(d, t).wait_send()
    for s in range(SLOTS):
        for t in range(8):
            pl.when(sibling_need[s] == 1)(lambda s=s, t=t: share(s, t).wait_send())
    best = None
    for k in range(2 * SLOTS):
        got = remote(parts_got.at[k], parts_got.at[k], r_send.at[k], r_recv.at[k], sibling)
        if k < 2:
            pl.when(jnp.logical_not(jnp.logical_and(mine, h == k)))(got.wait_recv)
        else:
            got.wait_recv()
        best = parts_got[k] if best is None else jnp.maximum(best, parts_got[k])
    out[...] = best

    for s in range(SLOTS):
        for half in range(2):
            copy = remote(part.at[s * 2 + half], parts_got.at[place[s] * 2 + h], r_send.at[s * 2 + half],
                          r_recv.at[place[s] * 2 + h], (owner_grp, held[s] * 2 + half))
            if s == 0:
                pl.when(jnp.logical_not(jnp.logical_and(mine, zh == half)))(copy.wait_send)
            else:
                copy.wait_send()


def on_device(embeddings, cluster_ids):
    emb = embeddings.reshape(4, 128, D)
    ids = cluster_ids.reshape(128, 128)
    dma = pltpu.SemaphoreType.DMA
    best = pl.pallas_call(
        kernel,
        out_shape=jax.ShapeDtypeStruct((4, 128), jnp.float32),
        in_specs=[pl.BlockSpec(memory_space=pl.ANY), pl.BlockSpec(memory_space=pl.ANY)],
        out_specs=pl.BlockSpec(memory_space=pltpu.VMEM),
        scratch_shapes=[
            pltpu.VMEM((SLOTS, 1024, D), jnp.bfloat16),
            pltpu.VMEM((3, 128, D), jnp.bfloat16),
            pltpu.VMEM((4, 128, D), jnp.float32),
            pltpu.VMEM((128, 128), jnp.int32),
            pltpu.VMEM((128, 128), jnp.int32),
            pltpu.VMEM((SLOTS * 8, 128, 128), jnp.float32),
            pltpu.VMEM((128, 128), jnp.float32),
            pltpu.VMEM((SLOTS * 8, 128, 128), jnp.float32),
            pltpu.VMEM((SLOTS * 8, 8, 128), jnp.float32),
            pltpu.VMEM((SLOTS * 8, 128), jnp.float32),
            pltpu.VMEM((2 * SLOTS, 4, 128), jnp.float32),
            pltpu.VMEM((2 * SLOTS, 4, 128), jnp.float32),
            pltpu.VMEM((128, D), jnp.bfloat16),
            dma((4,)), dma, dma, dma, dma((3, 2)), dma((3, 2)), dma((2, 2)), dma((2,)), dma((4, STEPS)), dma((4, STEPS)),
            dma((SLOTS, 8)), dma((SLOTS, 8)), dma((2 * SLOTS,)), dma((2 * SLOTS,)),
        ],
        compiler_params=pltpu.CompilerParams(
            collective_id=0, has_side_effects=True, vmem_limit_bytes=55168 * 1024),
        cost_estimate=pl.CostEstimate(flops=7 * 10**9, bytes_accessed=2 * 10**6, transcendentals=0),
        name="best_match",
    )(emb, ids)
    return best.reshape(1, 512)


def solution(mesh):
    placed = (P(None, "grp", "blk", None, None), P("grp", None))
    return jax.shard_map(
        on_device, mesh=mesh, in_specs=placed, out_specs=P("grp", "blk"), check_vma=False
    )
```

```python
import functools

import jax
import jax.numpy as jnp
from jax import lax
from jax.experimental import pallas as pl
from jax.experimental.pallas import tpu as pltpu
from jax.sharding import PartitionSpec as P

MESH = pl.DeviceIdType.MESH
D = 768
SLOTS = 5
PIECE = 64
STEPS = 8

SRC = [[4, 0, 0, 2], [0, 4, 0, 1], [0, 0, 0, 2], [0, 0, 0, 1], [4, 0, 0, 2], [0, 4, 0, 1], [0, 0, 1, 2],
       [0, 0, 2, 1], [4, 0, 0, 0], [0, 4, 0, 0], [0, 1, 0, 3], [2, 0, 0, 3], [4, 0, 0, 0], [0, 4, 0, 0],
       [0, 0, 4, 0], [0, 0, 4, 0]]
DEP = [[2, 1, 2, 1], [1, 2, 2, 1], [1, 1, 2, 2], [1, 1, 2, 2], [2, 1, 1, 1], [1, 2, 1, 1], [1, 1, 2, 1],
       [1, 1, 2, 1], [2, 2, 1, 1], [2, 2, 1, 1], [1, 1, 1, 2], [1, 1, 1, 2], [2, 1, 2, 1], [1, 2, 2, 1],
       [1, 1, 2, 1], [1, 1, 2, 1]]
BLK = [[13, 3, 7, 12], [2, 12, 6, 13], [3, 1, 5, 10], [0, 2, 4, 11], [1, 7, 8, 0], [6, 0, 9, 1], [7, 5, 14, 2],
       [4, 6, 15, 3], [5, 10, 12, 4], [11, 4, 13, 5], [11, 9, 14, 7], [8, 10, 15, 6], [9, 15, 3, 8], [14, 8, 2, 9],
       [15, 13, 1, 10], [12, 14, 0, 11]]
IDX = [[1, 1, 1, 1], [1, 2, 1, 2], [2, 1, 1, 1], [1, 2, 1, 1], [2, 2, 1, 2], [2, 3, 1, 3], [3, 2, 1, 3],
       [2, 3, 1, 3], [3, 2, 3, 3], [2, 4, 3, 4], [3, 2, 2, 4], [2, 3, 2, 4], [3, 3, 4, 3], [3, 4, 4, 4],
       [4, 4, 4, 4], [4, 4, 4, 4]]
HOLD = [[0, 3, 4, 5, 15], [1, 2, 4, 5, 14], [2, 1, 3, 6, 13], [3, 0, 2, 7, 12], [4, 3, 7, 8, 9], [5, 2, 6, 8, 9],
        [6, 1, 5, 7, 11], [7, 0, 4, 6, 10], [8, 4, 11, 12, 13], [9, 5, 10, 12, 13], [10, 2, 8, 11, 14],
        [11, 3, 9, 10, 15], [12, 0, 1, 8, 15], [13, 0, 1, 9, 14], [14, 6, 10, 13, 15], [15, 7, 11, 12, 14]]
PAIRS = [[[(2, 4), (3, 4), (3, 1)], [(0, 2), (0, 3), (2, 3)]], [[(3, 2), (3, 4), (2, 4)], [(0, 1), (1, 3), (0, 3)]],
         [[(2, 1), (1, 3), (2, 3)], [(0, 4), (1, 4), (3, 4)]], [[(1, 2), (2, 3), (3, 4)], [(2, 0), (2, 4), (0, 4)]],
         [[(2, 3), (1, 2), (1, 3)], [(4, 3), (4, 0), (1, 0), (4, 1)]],
         [[(1, 3), (2, 1), (2, 3)], [(4, 3), (0, 3), (2, 0)]],
         [[(4, 1), (4, 2), (2, 3)], [(2, 1), (0, 1), (2, 0), (0, 3)]],
         [[(4, 2), (1, 2), (2, 3)], [(4, 1), (1, 0), (0, 3)]],
         [[(4, 3), (4, 2), (2, 3)], [(4, 0), (1, 0), (1, 3), (4, 1)]],
         [[(4, 3), (4, 1), (1, 3)], [(0, 3), (2, 0), (2, 3)]], [[(2, 1), (4, 2), (4, 1)], [(2, 0), (4, 0), (4, 3)]],
         [[(1, 0), (4, 1), (4, 0)], [(1, 2), (2, 0), (4, 2)]], [[(4, 2), (3, 4), (3, 1)], [(4, 0), (1, 0), (1, 2)]],
         [[(3, 2), (3, 4), (2, 4)], [(4, 1), (2, 0), (2, 1)]], [[(4, 2), (2, 1), (4, 1)], [(4, 0), (2, 0), (3, 4)]],
         [[(4, 1), (1, 2), (4, 2)], [(1, 0), (2, 0), (4, 0)]]]
EARLY = [[1, 1], [0, 1], [1, 0], [1, 1], [1, 2], [1, 2], [2, 3], [2, 2], [1, 1], [1, 1], [1, 1], [1, 2], [1, 1],
         [0, 1], [3, 2], [3, 3]]
NEED = [[[1, 2, 3, 4], [0, 2, 3]], [[2, 3, 4], [0, 1, 3]], [[1, 2, 3], [0, 1, 3, 4]], [[1, 2, 3, 4], [0, 2, 4]],
        [[1, 2, 3], [0, 1, 3, 4]], [[1, 2, 3], [0, 2, 3, 4]], [[1, 2, 3, 4], [0, 1, 2, 3]],
        [[1, 2, 3, 4], [0, 1, 3, 4]], [[2, 3, 4], [0, 1, 3, 4]], [[1, 3, 4], [0, 2, 3]], [[1, 2, 4], [0, 2, 3, 4]],
        [[0, 1, 4], [0, 1, 2, 4]], [[1, 2, 3, 4], [0, 1, 2, 4]], [[2, 3, 4], [0, 1, 2, 4]],
        [[1, 2, 4], [0, 2, 3, 4]], [[1, 2, 4], [0, 1, 2, 4]]]

REL = (0, 3, 1, 2)


def word(digits, base):
    total = 0
    for digit in reversed(digits):
        total = total * base + digit
    return total


def look_up(index, words):
    got = jnp.int32(words[0])
    for k in range(1, len(words)):
        got = jnp.where(index == k, jnp.int32(words[k]), got)
    return got


def digits_of(value, base, count):
    out = []
    for _ in range(count):
        out.append(value % base)
        value = value // base
    return out


def pick(values, index):
    got = values[0]
    for k in range(1, len(values)):
        got = jnp.where(index == k, values[k], got)
    return got


def kernel(emb, ids_in, out, x, units, stage, ids_own, ids_got, ids_rows, ids_cols, row_best, col_best, row_line, part, parts_got,
           relay,
           load_sem, ids_sem, id_send, id_recv, z_send, z_recv, relay_send, relay_recv, f_send, f_recv, c_send, c_recv, r_send, r_recv):
    grp, blk = lax.axis_index("grp"), lax.axis_index("blk")
    h, zl = grp % 2, grp // 2
    p, zh = blk // 2, blk % 2
    z = zh * 2 + zl
    px, py = p % 4, p // 4

    def device(z_of, core, chip):
        return ((z_of % 2) * 2 + core, chip * 2 + z_of // 2)

    def group_of(z_of):
        return (z_of % 2) * 2 + z_of // 2

    near = [py * 4 + (px + 1) % 4, py * 4 + (px + 3) % 4, ((py + 1) % 4) * 4 + px, ((py + 3) % 4) * 4 + px]
    first = look_up(p, [word(SRC[c], 8) + 4096 * word(DEP[c], 4) for c in range(16)])
    src = digits_of(first, 8, 4)
    dep = digits_of(first // 4096, 4, 4)
    held = [p] + digits_of(look_up(p, [word(BLK[c], 16) for c in range(16)]), 16, 4)
    third = look_up(p, [word(IDX[c], 8) + 4096 * word(HOLD[c][1:], 16) for c in range(16)])
    place = [jnp.int32(0)] + digits_of(third, 8, 4)
    holders = [p] + digits_of(third // 4096, 16, 4)
    lists = []
    for c in range(16):
        for core in range(2):
            flat = [slot for pair in PAIRS[c][core] for slot in pair]
            lists.append(len(PAIRS[c][core]) + 8 * EARLY[c][core] + 64 * word(flat + [0] * (8 - len(flat)), 8))
    todo = look_up(p * 2 + h, lists)
    pair_count, early_count = todo % 8, todo // 8 % 8
    todo = digits_of(todo // 64, 8, 8)

    needs = [[sum(1 << slot for slot in NEED[c][core]) for core in range(2)] for c in range(16)]
    need = digits_of(look_up(p * 2 + h, [needs[c][core] for c in range(16) for core in range(2)]), 2, SLOTS)
    sibling_need = digits_of(look_up(p * 2 + h, [needs[c][1 - core] for c in range(16) for core in range(2)]), 2, SLOTS)

    sibling = device(z, 1 - h, p)
    owner_grp = zl * 2 + zh
    mine = h == zh

    loads = []
    for k, rel in enumerate((0, 1, 3, 2)):
        loads.append(pltpu.make_async_copy(emb.at[group_of((z + rel) % 4)], stage.at[k], load_sem.at[k]))
        loads[-1].start()

    ids_load = pltpu.make_async_copy(ids_in, ids_own, ids_sem)
    ids_load.start()

    barrier = pltpu.get_barrier_semaphore()
    for rel in (1, 3):
        pl.semaphore_signal(barrier, inc=1, device_id=device((z + rel) % 4, h, p), device_id_type=MESH)
    for d in range(4):
        pl.semaphore_signal(barrier, inc=1, device_id=device(z, h, near[d]), device_id_type=MESH)
    pl.semaphore_signal(barrier, inc=1, device_id=sibling, device_id_type=MESH)
    from_z = 2 * h + zl
    for k in range(SLOTS):
        for core in range(2):
            def tell():
                pl.semaphore_signal(barrier, inc=1, device_id=device(from_z, core, holders[k]), device_id_type=MESH)
            if k == 0:
                pl.when(jnp.logical_not(jnp.logical_and(mine, h == core)))(tell)
            else:
                tell()

    def normalise(k):
        loads[k].wait()
        v = stage[k]
        total = jnp.sum(v * v, axis=-1, keepdims=True)
        return (v / jnp.sqrt(total + 1e-06)).astype(jnp.bfloat16)

    own_rows = pl.multiple_of(h * 128, 128)
    x[0, pl.ds(own_rows, 128), :] = normalise(0)
    pl.semaphore_wait(barrier, jnp.where(mine, 16, 17))

    def remote(src_ref, dst_ref, send_sem, recv_sem, to):
        return pltpu.make_async_remote_copy(
            src_ref=src_ref, dst_ref=dst_ref, send_sem=send_sem, recv_sem=recv_sem, device_id=to, device_id_type=MESH)

    def part_rows(t):
        return pl.ds(pl.multiple_of((t // 2) * 256 + h * 128 + (t % 2) * PIECE, PIECE), PIECE)

    def forward(d, t):
        rows = part_rows(t)
        return remote(x.at[src[d], rows, :], x.at[1 + (d ^ 1), rows, :], f_send.at[d, t], f_recv.at[d ^ 1, t],
                      device(z, h, near[d]))

    def arrival(s, t):
        rows = part_rows(t)
        return remote(x.at[s, rows, :], x.at[s, rows, :], f_send.at[s - 1, t], f_recv.at[s - 1, t],
                      device(z, h, near[s - 1]))

    def swap(k, half):
        rows = pl.ds(pl.multiple_of(k * 256 + h * 128 + half * 64, 64), 64)
        return remote(units.at[k - 1, pl.ds(half * 64, 64), :], x.at[0, rows, :], z_send.at[k - 1, half],
                      z_recv.at[k - 1, half], device((z + (1, 3, 2)[k - 1]) % 4, h, p))

    between = device((z + jnp.where(h == 0, 1, 3)) % 4, h, p)

    def relay_in(half):
        rows = pl.ds(half * 64, 64)
        return remote(units.at[2, rows, :], relay.at[rows, :], relay_send.at[0, half], relay_recv.at[half], between)

    def relay_out(half):
        rows = pl.ds(pl.multiple_of(3 * 256 + h * 128 + half * 64, 64), 64)
        return remote(relay.at[pl.ds(half * 64, 64), :], x.at[0, rows, :], relay_send.at[1, half], z_recv.at[2, half],
                      between)

    def share_rows(t, core):
        return pl.ds(pl.multiple_of((t // 2) * 256 + core * 128 + (t % 2) * 64, 64), 64)

    def share(s, t):
        rows = share_rows(t, h)
        return remote(x.at[s, rows, :], x.at[s, rows, :], c_send.at[s, t], c_recv.at[s, t], sibling)

    def shared(s, t):
        rows = share_rows(t, 1 - h)
        return remote(x.at[s, rows, :], x.at[s, rows, :], c_send.at[s, t], c_recv.at[s, t], sibling)

    def give(s, t):
        pl.when(sibling_need[s] == 1)(lambda: share(s, t).start())

    def send_own(t):
        for d in range(4):
            pl.when(src[d] == 0)(lambda d=d: forward(d, t).start())

    def send_held(t):
        for d in range(4):
            pl.when(src[d] != 0)(lambda d=d: forward(d, t).start())

    def receive(links, t):
        for s in range(1, SLOTS):
            pl.when(dep[s - 1] == links)(lambda s=s: arrival(s, t).wait_recv())

    def give_held(links, t):
        for s in range(1, SLOTS):
            pl.when(dep[s - 1] == links)(lambda s=s: give(s, t))

    for t in range(2):
        send_own(t)
    units[0] = normalise(1)
    for half in range(2):
        swap(1, half).start()
    units[1] = normalise(2)
    for half in range(2):
        swap(2, half).start()
    units[2] = normalise(3)
    for half in range(2):
        relay_in(half).start()
    ids_copy = remote(ids_in, ids_got, id_send, id_recv, sibling)
    ids_copy.start()
    give(0, 0)
    give(0, 1)
    row_best[...] = jnp.full_like(row_best, -1.0)
    col_best[...] = jnp.full_like(col_best, -1.0)
    row_line[...] = jnp.full_like(row_line, -1.0)

    ids_load.wait()
    ids_copy.wait_recv()
    ids_cols[...] = jnp.zeros_like(ids_cols)
    for s in range(SLOTS):
        for t in range(4):
            for core in range(2):
                unit = held[s] * 8 + 2 * ((z + REL[t]) % 4) + core
                got = jnp.where(mine, ids_own[pl.ds(unit, 1), :], ids_got[pl.ds(unit, 1), :])
                ids_cols[pl.ds(s * 8 + 2 * t + core, 1), :] = got.astype(jnp.float32)
    turned = ids_cols[...].T
    for j in range(SLOTS * 8):
        ids_rows[j] = jnp.broadcast_to(turned[:, j:j + 1], (128, 128))

    def strip(a, t, b, count, diagonal=False, first=0):
        sim = lax.dot_general(x[a, 256 * t:256 * t + 256, :], x[b, 256 * first:256 * count, :], (((1,), (1,)), ((), ())),
                              preferred_element_type=jnp.float32)
        for r in range(4):
            unit, first_row = a * 8 + 2 * t + r // 2, 64 * (r % 2)
            row_ids = ids_rows[unit, first_row:first_row + 64]
            best = row_best[unit, first_row:first_row + 64]
            for c in range(2 * first, 2 * count):
                keep = row_ids == ids_cols[pl.ds(b * 8 + c, 1), :]
                if diagonal and c // 2 == t:
                    row = lax.broadcasted_iota(jnp.int32, (64, 128), 0) + 64 * r
                    col = lax.broadcasted_iota(jnp.int32, (64, 128), 1) + 128 * (c % 2)
                    keep = jnp.logical_and(keep, row != col)
                kept = jnp.where(keep, sim[64 * r:64 * r + 64, 128 * (c - 2 * first):128 * (c - 2 * first) + 128], jnp.float32(-1.0))
                down = jnp.max(kept.reshape(8, 8, 128), axis=0)
                col_best[b * 8 + c] = jnp.maximum(col_best[b * 8 + c], down)
                best = jnp.maximum(best, kept)
            row_best[unit, first_row:first_row + 64] = best

    def compare(t, j):
        a, b = todo[0], todo[1]
        for k in range(1, 4):
            a = jnp.where(j == k, todo[2 * k], a)
            b = jnp.where(j == k, todo[2 * k + 1], b)
        strip(a, t, b, t + 1)
        if t:
            strip(b, t, a, t)

    def pair(j):
        return pick(todo[0:8:2], j), pick(todo[1:8:2], j)

    def half_strip(a, core, b):
        unit = a * 8 + 6 + core
        sim = lax.dot_general(x[a, pl.ds(pl.multiple_of(768 + 128 * core, 128), 128), :], x[b, 0:768, :],
                              (((1,), (1,)), ((), ())), preferred_element_type=jnp.float32)
        for r in range(2):
            rows = slice(64 * r, 64 * r + 64)
            best = row_best[unit, rows]
            for c in range(6):
                keep = ids_rows[unit, rows] == ids_cols[pl.ds(b * 8 + c, 1), :]
                kept = jnp.where(keep, sim[rows, 128 * c:128 * c + 128], jnp.float32(-1.0))
                col_best[b * 8 + c] = jnp.maximum(col_best[b * 8 + c], jnp.max(kept.reshape(8, 8, 128), axis=0))
                best = jnp.maximum(best, kept)
            row_best[unit, rows] = best

    def compare_here(j):
        a, b = pair(j)
        half_strip(a, h, b)
        half_strip(b, h, a)

    def compare_there(j):
        a, b = pair(j)
        half_strip(a, 1 - h, b)
        half_strip(b, 1 - h, a)
        strip(a, 3, b, 4, first=3)

    def own_pair(t):
        pl.when(h == 1)(lambda: strip(0, t, 0, t + 1, diagonal=True))

    def finish_rows(t):
        for s in range(SLOTS):
            for core in range(2):
                unit = s * 8 + 2 * t + core
                row_line[unit:unit + 1, :] = jnp.max(row_best[unit].T, axis=0, keepdims=True)

    def wait_shared(m, links):
        for s in range(SLOTS):
            there = need[s] == 1
            if s == 0:
                if links:
                    continue
            elif links:
                there = jnp.logical_and(there, dep[s - 1] == links)
            else:
                continue

            @pl.when(there)
            def _():
                for half in range(2):
                    shared(s, 2 * m + half).wait_recv()

    def own_piece_ready(t):
        send_own(t)
        give(0, t)

    def pass_on(k):
        receive(1, k - 1)
        send_held(k - 1)
        give_held(1, k - 1)

    def take(t):
        receive(2, t)
        give_held(2, t)

    pass_on(1)
    swap(1, 0).wait_recv()
    own_piece_ready(2)
    pass_on(2)
    swap(1, 1).wait_recv()
    own_piece_ready(3)
    swap(2, 0).wait_recv()
    own_piece_ready(4)
    pass_on(3)
    for half in range(2):
        relay_in(half).wait_recv()
        relay_out(half).start()
    swap(2, 1).wait_recv()
    own_piece_ready(5)
    wait_shared(0, 0)
    own_pair(0)
    take(0)
    pass_on(4)
    wait_shared(1, 0)
    own_pair(1)
    take(1)
    pass_on(5)
    for half in range(2):
        relay_out(half).wait_recv()
        own_piece_ready(6 + half)
    wait_shared(0, 1)
    wait_shared(0, 2)

    @pl.loop(0, pair_count)
    def _(j):
        compare(0, j)
    take(2)
    pass_on(6)
    for m in (2, 3):
        wait_shared(m, 0)
        own_pair(m)
    take(3)

    @pl.loop(0, 2)
    def _(k):
        pass_on(7 + k)

        @pl.when(k == 0)
        def _():
            wait_shared(1, 1)
            wait_shared(1, 2)

        @pl.loop(2 * k, jnp.minimum(2 * k + 2, pair_count))
        def _(j):
            compare(1, j)
        take(4 + k)
    finish_rows(0)

    wait_shared(2, 1)

    @pl.loop(0, pair_count)
    def _(j):
        pl.when(j == early_count)(lambda: wait_shared(2, 2))
        compare(2, j)
    finish_rows(1)
    take(6)
    finish_rows(2)
    take(7)
    wait_shared(3, 1)

    @pl.loop(0, early_count)
    def _(j):
        compare(3, j)

    @pl.loop(early_count, pair_count)
    def _(j):
        compare_here(j)
    wait_shared(3, 2)

    @pl.loop(early_count, pair_count)
    def _(j):
        compare_there(j)
    finish_rows(3)

    for s in range(SLOTS):
        for t in range(4):
            z_of = (z + REL[t]) % 4
            for core in range(2):
                j = s * 8 + 2 * t + core
                both = jnp.maximum(row_line[j:j + 1, :], jnp.max(col_best[j], axis=0, keepdims=True))
                part[s * 2 + z_of // 2, pl.ds(2 * (z_of % 2) + core, 1), :] = both
        for half in range(2):
            copy = remote(part.at[s * 2 + half], parts_got.at[place[s] * 2 + h], r_send.at[s * 2 + half],
                          r_recv.at[place[s] * 2 + h], (owner_grp, held[s] * 2 + half))
            if s == 0:
                keep_it = jnp.logical_and(mine, zh == half)
                pl.when(jnp.logical_not(keep_it))(copy.start)

                @pl.when(keep_it)
                def _():
                    parts_got[h] = part[half]
            else:
                copy.start()

    ids_copy.wait_send()
    for half in range(2):
        for copy in (swap(1, half), swap(2, half), relay_in(half), relay_out(half)):
            copy.wait_send()
    for d in range(4):
        for t in range(STEPS):
            forward(d, t).wait_send()
    for s in range(SLOTS):
        for t in range(8):
            pl.when(sibling_need[s] == 1)(lambda s=s, t=t: share(s, t).wait_send())
    best = None
    for k in range(2 * SLOTS):
        got = remote(parts_got.at[k], parts_got.at[k], r_send.at[k], r_recv.at[k], sibling)
        if k < 2:
            pl.when(jnp.logical_not(jnp.logical_and(mine, h == k)))(got.wait_recv)
        else:
            got.wait_recv()
        best = parts_got[k] if best is None else jnp.maximum(best, parts_got[k])
    out[...] = best

    for s in range(SLOTS):
        for half in range(2):
            copy = remote(part.at[s * 2 + half], parts_got.at[place[s] * 2 + h], r_send.at[s * 2 + half],
                          r_recv.at[place[s] * 2 + h], (owner_grp, held[s] * 2 + half))
            if s == 0:
                pl.when(jnp.logical_not(jnp.logical_and(mine, zh == half)))(copy.wait_send)
            else:
                copy.wait_send()


def on_device(embeddings, cluster_ids):
    emb = embeddings.reshape(4, 128, D)
    ids = cluster_ids.reshape(128, 128)
    dma = pltpu.SemaphoreType.DMA
    best = pl.pallas_call(
        kernel,
        out_shape=jax.ShapeDtypeStruct((4, 128), jnp.float32),
        in_specs=[pl.BlockSpec(memory_space=pl.ANY), pl.BlockSpec(memory_space=pl.ANY)],
        out_specs=pl.BlockSpec(memory_space=pltpu.VMEM),
        scratch_shapes=[
            pltpu.VMEM((SLOTS, 1024, D), jnp.bfloat16),
            pltpu.VMEM((3, 128, D), jnp.bfloat16),
            pltpu.VMEM((4, 128, D), jnp.float32),
            pltpu.VMEM((128, 128), jnp.int32),
            pltpu.VMEM((128, 128), jnp.int32),
            pltpu.VMEM((SLOTS * 8, 128, 128), jnp.float32),
            pltpu.VMEM((128, 128), jnp.float32),
            pltpu.VMEM((SLOTS * 8, 128, 128), jnp.float32),
            pltpu.VMEM((SLOTS * 8, 8, 128), jnp.float32),
            pltpu.VMEM((SLOTS * 8, 128), jnp.float32),
            pltpu.VMEM((2 * SLOTS, 4, 128), jnp.float32),
            pltpu.VMEM((2 * SLOTS, 4, 128), jnp.float32),
            pltpu.VMEM((128, D), jnp.bfloat16),
            dma((4,)), dma, dma, dma, dma((3, 2)), dma((3, 2)), dma((2, 2)), dma((2,)), dma((4, STEPS)), dma((4, STEPS)),
            dma((SLOTS, 8)), dma((SLOTS, 8)), dma((2 * SLOTS,)), dma((2 * SLOTS,)),
        ],
        compiler_params=pltpu.CompilerParams(
            collective_id=0, has_side_effects=True, vmem_limit_bytes=55168 * 1024),
        cost_estimate=pl.CostEstimate(flops=7 * 10**9, bytes_accessed=2 * 10**6, transcendentals=0),
        name="best_match",
    )(emb, ids)
    return best.reshape(1, 512)


def solution(mesh):
    placed = (P(None, "grp", "blk", None, None), P("grp", None))
    return jax.shard_map(
        on_device, mesh=mesh, in_specs=placed, out_specs=P("grp", "blk"), check_vma=False
    )
```

```python
import functools

import jax
import jax.numpy as jnp
from jax import lax
from jax.experimental import pallas as pl
from jax.experimental.pallas import tpu as pltpu
from jax.sharding import PartitionSpec as P

MESH = pl.DeviceIdType.MESH
D = 768
SLOTS = 5
PIECE = 64
STEPS = 8

SRC = [[4, 0, 0, 2], [0, 4, 0, 1], [0, 0, 0, 2], [0, 0, 0, 1], [4, 0, 0, 2], [0, 4, 0, 1], [0, 0, 1, 2],
       [0, 0, 2, 1], [4, 0, 0, 0], [0, 4, 0, 0], [0, 1, 0, 3], [2, 0, 0, 3], [4, 0, 0, 0], [0, 4, 0, 0],
       [0, 0, 4, 0], [0, 0, 4, 0]]
DEP = [[2, 1, 2, 1], [1, 2, 2, 1], [1, 1, 2, 2], [1, 1, 2, 2], [2, 1, 1, 1], [1, 2, 1, 1], [1, 1, 2, 1],
       [1, 1, 2, 1], [2, 2, 1, 1], [2, 2, 1, 1], [1, 1, 1, 2], [1, 1, 1, 2], [2, 1, 2, 1], [1, 2, 2, 1],
       [1, 1, 2, 1], [1, 1, 2, 1]]
BLK = [[13, 3, 7, 12], [2, 12, 6, 13], [3, 1, 5, 10], [0, 2, 4, 11], [1, 7, 8, 0], [6, 0, 9, 1], [7, 5, 14, 2],
       [4, 6, 15, 3], [5, 10, 12, 4], [11, 4, 13, 5], [11, 9, 14, 7], [8, 10, 15, 6], [9, 15, 3, 8], [14, 8, 2, 9],
       [15, 13, 1, 10], [12, 14, 0, 11]]
IDX = [[1, 1, 1, 1], [1, 2, 1, 2], [2, 1, 1, 1], [1, 2, 1, 1], [2, 2, 1, 2], [2, 3, 1, 3], [3, 2, 1, 3],
       [2, 3, 1, 3], [3, 2, 3, 3], [2, 4, 3, 4], [3, 2, 2, 4], [2, 3, 2, 4], [3, 3, 4, 3], [3, 4, 4, 4],
       [4, 4, 4, 4], [4, 4, 4, 4]]
HOLD = [[0, 3, 4, 5, 15], [1, 2, 4, 5, 14], [2, 1, 3, 6, 13], [3, 0, 2, 7, 12], [4, 3, 7, 8, 9], [5, 2, 6, 8, 9],
        [6, 1, 5, 7, 11], [7, 0, 4, 6, 10], [8, 4, 11, 12, 13], [9, 5, 10, 12, 13], [10, 2, 8, 11, 14],
        [11, 3, 9, 10, 15], [12, 0, 1, 8, 15], [13, 0, 1, 9, 14], [14, 6, 10, 13, 15], [15, 7, 11, 12, 14]]
PAIRS = [[[(2, 4), (3, 4), (3, 1)], [(0, 2), (0, 3), (2, 3)]], [[(3, 2), (3, 4), (2, 4)], [(0, 1), (1, 3), (0, 3)]],
         [[(2, 1), (1, 3), (2, 3)], [(0, 4), (1, 4), (3, 4)]], [[(1, 2), (2, 3), (3, 4)], [(2, 0), (2, 4), (0, 4)]],
         [[(2, 3), (1, 2), (1, 3)], [(4, 3), (4, 0), (1, 0), (4, 1)]],
         [[(1, 3), (2, 1), (2, 3)], [(4, 3), (0, 3), (2, 0)]],
         [[(4, 1), (4, 2), (2, 3)], [(2, 1), (0, 1), (2, 0), (0, 3)]],
         [[(4, 2), (1, 2), (2, 3)], [(4, 1), (1, 0), (0, 3)]],
         [[(4, 3), (4, 2), (2, 3)], [(4, 0), (1, 0), (1, 3), (4, 1)]],
         [[(4, 3), (4, 1), (1, 3)], [(0, 3), (2, 0), (2, 3)]], [[(2, 1), (4, 2), (4, 1)], [(2, 0), (4, 0), (4, 3)]],
         [[(1, 0), (4, 1), (4, 0)], [(1, 2), (2, 0), (4, 2)]], [[(4, 2), (3, 4), (3, 1)], [(4, 0), (1, 0), (1, 2)]],
         [[(3, 2), (3, 4), (2, 4)], [(4, 1), (2, 0), (2, 1)]], [[(4, 2), (2, 1), (4, 1)], [(4, 0), (2, 0), (3, 4)]],
         [[(4, 1), (1, 2), (4, 2)], [(1, 0), (2, 0), (4, 0)]]]
EARLY = [[1, 1], [0, 1], [1, 0], [1, 1], [1, 2], [1, 2], [2, 3], [2, 2], [1, 1], [1, 1], [1, 1], [1, 2], [1, 1],
         [0, 1], [3, 2], [3, 3]]
NEED = [[[1, 2, 3, 4], [0, 2, 3]], [[2, 3, 4], [0, 1, 3]], [[1, 2, 3], [0, 1, 3, 4]], [[1, 2, 3, 4], [0, 2, 4]],
        [[1, 2, 3], [0, 1, 3, 4]], [[1, 2, 3], [0, 2, 3, 4]], [[1, 2, 3, 4], [0, 1, 2, 3]],
        [[1, 2, 3, 4], [0, 1, 3, 4]], [[2, 3, 4], [0, 1, 3, 4]], [[1, 3, 4], [0, 2, 3]], [[1, 2, 4], [0, 2, 3, 4]],
        [[0, 1, 4], [0, 1, 2, 4]], [[1, 2, 3, 4], [0, 1, 2, 4]], [[2, 3, 4], [0, 1, 2, 4]],
        [[1, 2, 4], [0, 2, 3, 4]], [[1, 2, 4], [0, 1, 2, 4]]]

REL = (0, 3, 1, 2)


def word(digits, base):
    total = 0
    for digit in reversed(digits):
        total = total * base + digit
    return total


def look_up(index, words):
    got = jnp.int32(words[0])
    for k in range(1, len(words)):
        got = jnp.where(index == k, jnp.int32(words[k]), got)
    return got


def digits_of(value, base, count):
    out = []
    for _ in range(count):
        out.append(value % base)
        value = value // base
    return out


def pick(values, index):
    got = values[0]
    for k in range(1, len(values)):
        got = jnp.where(index == k, values[k], got)
    return got


def kernel(emb, ids_in, out, x, units, stage, ids_own, ids_got, ids_rows, ids_cols, row_best, col_best, row_line, part, parts_got,
           relay,
           load_sem, ids_sem, id_send, id_recv, z_send, z_recv, relay_send, relay_recv, f_send, f_recv, c_send, c_recv, r_send, r_recv):
    grp, blk = lax.axis_index("grp"), lax.axis_index("blk")
    h, zl = grp % 2, grp // 2
    p, zh = blk // 2, blk % 2
    z = zh * 2 + zl
    px, py = p % 4, p // 4

    def device(z_of, core, chip):
        return ((z_of % 2) * 2 + core, chip * 2 + z_of // 2)

    def group_of(z_of):
        return (z_of % 2) * 2 + z_of // 2

    near = [py * 4 + (px + 1) % 4, py * 4 + (px + 3) % 4, ((py + 1) % 4) * 4 + px, ((py + 3) % 4) * 4 + px]
    first = look_up(p, [word(SRC[c], 8) + 4096 * word(DEP[c], 4) for c in range(16)])
    src = digits_of(first, 8, 4)
    dep = digits_of(first // 4096, 4, 4)
    held = [p] + digits_of(look_up(p, [word(BLK[c], 16) for c in range(16)]), 16, 4)
    third = look_up(p, [word(IDX[c], 8) + 4096 * word(HOLD[c][1:], 16) for c in range(16)])
    place = [jnp.int32(0)] + digits_of(third, 8, 4)
    holders = [p] + digits_of(third // 4096, 16, 4)
    lists = []
    for c in range(16):
        for core in range(2):
            flat = [slot for pair in PAIRS[c][core] for slot in pair]
            lists.append(len(PAIRS[c][core]) + 8 * EARLY[c][core] + 64 * word(flat + [0] * (8 - len(flat)), 8))
    todo = look_up(p * 2 + h, lists)
    pair_count, early_count = todo % 8, todo // 8 % 8
    todo = digits_of(todo // 64, 8, 8)

    needs = [[sum(1 << slot for slot in NEED[c][core]) for core in range(2)] for c in range(16)]
    need = digits_of(look_up(p * 2 + h, [needs[c][core] for c in range(16) for core in range(2)]), 2, SLOTS)
    sibling_need = digits_of(look_up(p * 2 + h, [needs[c][1 - core] for c in range(16) for core in range(2)]), 2, SLOTS)

    sibling = device(z, 1 - h, p)
    owner_grp = zl * 2 + zh
    mine = h == zh

    def load(k):
        return pltpu.make_async_copy(emb.at[group_of((z + pick((0, 1, 3, 2), k)) % 4)], stage.at[k], load_sem.at[k])

    for k in range(4):
        load(k).start()
    ids_load = pltpu.make_async_copy(ids_in, ids_own, ids_sem)
    ids_load.start()

    barrier = pltpu.get_barrier_semaphore()
    for rel in (1, 3):
        pl.semaphore_signal(barrier, inc=1, device_id=device((z + rel) % 4, h, p), device_id_type=MESH)
    for d in range(4):
        pl.semaphore_signal(barrier, inc=1, device_id=device(z, h, near[d]), device_id_type=MESH)
    pl.semaphore_signal(barrier, inc=1, device_id=sibling, device_id_type=MESH)
    from_z = 2 * h + zl
    for k in range(SLOTS):
        for core in range(2):
            def tell():
                pl.semaphore_signal(barrier, inc=1, device_id=device(from_z, core, holders[k]), device_id_type=MESH)
            if k == 0:
                pl.when(jnp.logical_not(jnp.logical_and(mine, h == core)))(tell)
            else:
                tell()

    def normalised(k):
        v = stage[k]
        total = jnp.sum(v * v, axis=-1, keepdims=True)
        return (v / jnp.sqrt(total + 1e-06)).astype(jnp.bfloat16)

    load(0).wait()
    own_rows = pl.multiple_of(h * 128, 128)
    x[0, pl.ds(own_rows, 128), :] = normalised(0)
    pl.semaphore_wait(barrier, jnp.where(mine, 16, 17))

    def remote(src_ref, dst_ref, send_sem, recv_sem, to):
        return pltpu.make_async_remote_copy(
            src_ref=src_ref, dst_ref=dst_ref, send_sem=send_sem, recv_sem=recv_sem, device_id=to, device_id_type=MESH)

    def part_rows(t):
        return pl.ds(pl.multiple_of((t // 2) * 256 + h * 128 + (t % 2) * PIECE, PIECE), PIECE)

    def forward(d, t):
        rows = part_rows(t)
        return remote(x.at[src[d], rows, :], x.at[1 + (d ^ 1), rows, :], f_send.at[d, t], f_recv.at[d ^ 1, t],
                      device(z, h, near[d]))

    def arrival(s, t):
        rows = part_rows(t)
        return remote(x.at[s, rows, :], x.at[s, rows, :], f_send.at[s - 1, t], f_recv.at[s - 1, t],
                      device(z, h, near[s - 1]))

    def swap(k, half):
        rows = pl.ds(pl.multiple_of(k * 256 + h * 128 + half * 64, 64), 64)
        return remote(units.at[k - 1, pl.ds(half * 64, 64), :], x.at[0, rows, :], z_send.at[k - 1, half],
                      z_recv.at[k - 1, half], device((z + pick((1, 3), k - 1)) % 4, h, p))

    between = device((z + jnp.where(h == 0, 1, 3)) % 4, h, p)

    def relay_in(half):
        rows = pl.ds(half * 64, 64)
        return remote(units.at[2, rows, :], relay.at[rows, :], relay_send.at[0, half], relay_recv.at[half], between)

    def relay_out(half):
        rows = pl.ds(pl.multiple_of(3 * 256 + h * 128 + half * 64, 64), 64)
        return remote(relay.at[pl.ds(half * 64, 64), :], x.at[0, rows, :], relay_send.at[1, half], z_recv.at[2, half],
                      between)

    def share_rows(t, core):
        return pl.ds(pl.multiple_of((t // 2) * 256 + core * 128 + (t % 2) * 64, 64), 64)

    def share(s, t):
        rows = share_rows(t, h)
        return remote(x.at[s, rows, :], x.at[s, rows, :], c_send.at[s, t], c_recv.at[s, t], sibling)

    def shared(s, t):
        rows = share_rows(t, 1 - h)
        return remote(x.at[s, rows, :], x.at[s, rows, :], c_send.at[s, t], c_recv.at[s, t], sibling)

    def give(s, t):
        pl.when(sibling_need[s] == 1)(lambda: share(s, t).start())

    def send_own(t):
        for d in range(4):
            pl.when(src[d] == 0)(lambda d=d: forward(d, t).start())

    def send_held(t):
        for d in range(4):
            pl.when(src[d] != 0)(lambda d=d: forward(d, t).start())

    def receive(links, t):
        for s in range(1, SLOTS):
            pl.when(dep[s - 1] == links)(lambda s=s: arrival(s, t).wait_recv())

    def give_held(links, t):
        for s in range(1, SLOTS):
            pl.when(dep[s - 1] == links)(lambda s=s: give(s, t))

    for t in range(2):
        send_own(t)
    @pl.loop(1, 4)
    def _(k):
        load(k).wait()
        units[k - 1] = normalised(k)
        for half in range(2):
            pl.when(k < 3)(lambda half=half: swap(k, half).start())
            pl.when(k == 3)(lambda half=half: relay_in(half).start())

    ids_copy = remote(ids_in, ids_got, id_send, id_recv, sibling)
    ids_copy.start()
    give(0, 0)
    give(0, 1)
    def strip(a, t, b, count, diagonal=False):
        sim = lax.dot_general(x[a, 256 * t:256 * t + 256, :], x[b, 0:256 * count, :], (((1,), (1,)), ((), ())),
                              preferred_element_type=jnp.float32)
        for r in range(4):
            unit, first_row = a * 8 + 2 * t + r // 2, 64 * (r % 2)
            row_ids = ids_rows[unit, first_row:first_row + 64]
            best = row_best[unit, first_row:first_row + 64]
            for c in range(2 * count):
                keep = row_ids == ids_cols[pl.ds(b * 8 + c, 1), :]
                if diagonal and c // 2 == t:
                    row = lax.broadcasted_iota(jnp.int32, (64, 128), 0) + 64 * r
                    col = lax.broadcasted_iota(jnp.int32, (64, 128), 1) + 128 * (c % 2)
                    keep = jnp.logical_and(keep, row != col)
                kept = jnp.where(keep, sim[64 * r:64 * r + 64, 128 * c:128 * c + 128], jnp.float32(-1.0))
                down = jnp.max(kept.reshape(8, 8, 128), axis=0)
                col_best[b * 8 + c] = jnp.maximum(col_best[b * 8 + c], down)
                best = jnp.maximum(best, kept)
            row_best[unit, first_row:first_row + 64] = best

    def compare(t, j):
        a, b = todo[0], todo[1]
        for k in range(1, 4):
            a = jnp.where(j == k, todo[2 * k], a)
            b = jnp.where(j == k, todo[2 * k + 1], b)
        strip(a, t, b, t + 1)
        if t:
            strip(b, t, a, t)

    def own_pair(t):
        pl.when(h == 1)(lambda: strip(0, t, 0, t + 1, diagonal=True))

    def finish_rows(t):
        for s in range(SLOTS):
            @pl.when(need[s] == 1)
            def _():
                for core in range(2):
                    unit = s * 8 + 2 * t + core
                    row_line[unit:unit + 1, :] = jnp.max(row_best[unit].T, axis=0, keepdims=True)

    def wait_shared(m, links):
        for s in range(SLOTS):
            there = need[s] == 1
            if s == 0:
                if links:
                    continue
            elif links:
                there = jnp.logical_and(there, dep[s - 1] == links)
            else:
                continue

            @pl.when(there)
            def _():
                for half in range(2):
                    shared(s, 2 * m + half).wait_recv()

    def own_piece_ready(t):
        send_own(t)
        give(0, t)

    def pass_on(k):
        receive(1, k - 1)
        send_held(k - 1)
        give_held(1, k - 1)

    def take(t):
        receive(2, t)
        give_held(2, t)

    pass_on(1)
    swap(1, 0).wait_recv()
    own_piece_ready(2)
    pass_on(2)
    swap(1, 1).wait_recv()
    own_piece_ready(3)
    swap(2, 0).wait_recv()
    own_piece_ready(4)

    ids_load.wait()
    ids_copy.wait_recv()
    ids_cols[...] = jnp.zeros_like(ids_cols)
    for s in range(SLOTS):
        for t in range(4):
            for core in range(2):
                unit = held[s] * 8 + 2 * ((z + REL[t]) % 4) + core
                got = jnp.where(mine, ids_own[pl.ds(unit, 1), :], ids_got[pl.ds(unit, 1), :])
                ids_cols[pl.ds(s * 8 + 2 * t + core, 1), :] = got.astype(jnp.float32)
    turned = ids_cols[...].T
    for j in range(SLOTS * 8):
        ids_rows[j] = jnp.broadcast_to(turned[:, j:j + 1], (128, 128))

    pass_on(3)
    for half in range(2):
        relay_in(half).wait_recv()
        relay_out(half).start()
    swap(2, 1).wait_recv()
    own_piece_ready(5)
    @pl.loop(0, SLOTS * 8)
    def _(j):
        row_best[j] = jnp.full((128, 128), -1.0, jnp.float32)
        col_best[j] = jnp.full((8, 128), -1.0, jnp.float32)
    row_line[...] = jnp.full_like(row_line, -1.0)

    take(0)
    pass_on(4)
    for m in (0, 1):
        wait_shared(m, 0)
        own_pair(m)
    take(1)
    pass_on(5)
    for half in range(2):
        relay_out(half).wait_recv()
        own_piece_ready(6 + half)
    wait_shared(0, 1)
    wait_shared(0, 2)

    @pl.loop(0, pair_count)
    def _(j):
        compare(0, j)
    take(2)
    pass_on(6)
    for m in (2, 3):
        wait_shared(m, 0)
        own_pair(m)
    take(3)

    @pl.loop(0, 2)
    def _(k):
        pass_on(7 + k)

        @pl.when(k == 0)
        def _():
            wait_shared(1, 1)
            wait_shared(1, 2)

        @pl.loop(2 * k, jnp.minimum(2 * k + 2, pair_count))
        def _(j):
            compare(1, j)
        take(4 + k)
    finish_rows(0)

    for m in (2, 3):
        wait_shared(m, 1)

        @pl.loop(0, pair_count)
        def _(j):
            pl.when(j == early_count)(lambda: wait_shared(m, 2))
            compare(m, j)
        if m == 2:
            finish_rows(1)
            take(6)
            finish_rows(2)
            take(7)
    finish_rows(3)

    for s in range(SLOTS):
        for t in range(4):
            z_of = (z + REL[t]) % 4
            for core in range(2):
                j = s * 8 + 2 * t + core
                both = jnp.maximum(row_line[j:j + 1, :], jnp.max(col_best[j], axis=0, keepdims=True))
                part[s * 2 + z_of // 2, pl.ds(2 * (z_of % 2) + core, 1), :] = both
        for half in range(2):
            copy = remote(part.at[s * 2 + half], parts_got.at[place[s] * 2 + h], r_send.at[s * 2 + half],
                          r_recv.at[place[s] * 2 + h], (owner_grp, held[s] * 2 + half))
            if s == 0:
                keep_it = jnp.logical_and(mine, zh == half)
                pl.when(jnp.logical_not(keep_it))(copy.start)

                @pl.when(keep_it)
                def _():
                    parts_got[h] = part[half]
            else:
                copy.start()

    ids_copy.wait_send()
    for half in range(2):
        for copy in (swap(1, half), swap(2, half), relay_in(half), relay_out(half)):
            copy.wait_send()

    @pl.loop(0, STEPS)
    def _(t):
        for d in range(4):
            forward(d, t).wait_send()
        for s in range(SLOTS):
            pl.when(sibling_need[s] == 1)(lambda s=s: share(s, t).wait_send())

    best = None
    for k in range(2 * SLOTS):
        got = remote(parts_got.at[k], parts_got.at[k], r_send.at[k], r_recv.at[k], sibling)
        if k < 2:
            pl.when(jnp.logical_not(jnp.logical_and(mine, h == k)))(got.wait_recv)
        else:
            got.wait_recv()
        best = parts_got[k] if best is None else jnp.maximum(best, parts_got[k])
    out[...] = best

    for s in range(SLOTS):
        for half in range(2):
            copy = remote(part.at[s * 2 + half], parts_got.at[place[s] * 2 + h], r_send.at[s * 2 + half],
                          r_recv.at[place[s] * 2 + h], (owner_grp, held[s] * 2 + half))
            if s == 0:
                pl.when(jnp.logical_not(jnp.logical_and(mine, zh == half)))(copy.wait_send)
            else:
                copy.wait_send()


def on_device(embeddings, cluster_ids):
    emb = embeddings.reshape(4, 128, D)
    ids = cluster_ids.reshape(128, 128)
    dma = pltpu.SemaphoreType.DMA
    best = pl.pallas_call(
        kernel,
        out_shape=jax.ShapeDtypeStruct((4, 128), jnp.float32),
        in_specs=[pl.BlockSpec(memory_space=pl.ANY), pl.BlockSpec(memory_space=pl.ANY)],
        out_specs=pl.BlockSpec(memory_space=pltpu.VMEM),
        scratch_shapes=[
            pltpu.VMEM((SLOTS, 1024, D), jnp.bfloat16),
            pltpu.VMEM((3, 128, D), jnp.bfloat16),
            pltpu.VMEM((4, 128, D), jnp.float32),
            pltpu.VMEM((128, 128), jnp.int32),
            pltpu.VMEM((128, 128), jnp.int32),
            pltpu.VMEM((SLOTS * 8, 128, 128), jnp.float32),
            pltpu.VMEM((128, 128), jnp.float32),
            pltpu.VMEM((SLOTS * 8, 128, 128), jnp.float32),
            pltpu.VMEM((SLOTS * 8, 8, 128), jnp.float32),
            pltpu.VMEM((SLOTS * 8, 128), jnp.float32),
            pltpu.VMEM((2 * SLOTS, 4, 128), jnp.float32),
            pltpu.VMEM((2 * SLOTS, 4, 128), jnp.float32),
            pltpu.VMEM((128, D), jnp.bfloat16),
            dma((4,)), dma, dma, dma, dma((3, 2)), dma((3, 2)), dma((2, 2)), dma((2,)), dma((4, STEPS)), dma((4, STEPS)),
            dma((SLOTS, 8)), dma((SLOTS, 8)), dma((2 * SLOTS,)), dma((2 * SLOTS,)),
        ],
        compiler_params=pltpu.CompilerParams(
            collective_id=0, has_side_effects=True, vmem_limit_bytes=55168 * 1024),
        cost_estimate=pl.CostEstimate(flops=7 * 10**9, bytes_accessed=2 * 10**6, transcendentals=0),
        name="best_match",
    )(emb, ids)
    return best.reshape(1, 512)


def solution(mesh):
    placed = (P(None, "grp", "blk", None, None), P("grp", None))
    return jax.shard_map(
        on_device, mesh=mesh, in_specs=placed, out_specs=P("grp", "blk"), check_vma=False
    )
```

```python
import functools

import jax
import jax.numpy as jnp
from jax import lax
from jax.experimental import pallas as pl
from jax.experimental.pallas import tpu as pltpu
from jax.sharding import PartitionSpec as P

MESH = pl.DeviceIdType.MESH
D = 768
SLOTS = 5
PIECE = 64
STEPS = 8

SRC = [[4, 0, 0, 2], [0, 4, 0, 1], [0, 0, 0, 2], [0, 0, 0, 1], [4, 0, 0, 2], [0, 4, 0, 1], [0, 0, 1, 2],
       [0, 0, 2, 1], [4, 0, 0, 0], [0, 4, 0, 0], [0, 1, 0, 3], [2, 0, 0, 3], [4, 0, 0, 0], [0, 4, 0, 0],
       [0, 0, 4, 0], [0, 0, 4, 0]]
DEP = [[2, 1, 2, 1], [1, 2, 2, 1], [1, 1, 2, 2], [1, 1, 2, 2], [2, 1, 1, 1], [1, 2, 1, 1], [1, 1, 2, 1],
       [1, 1, 2, 1], [2, 2, 1, 1], [2, 2, 1, 1], [1, 1, 1, 2], [1, 1, 1, 2], [2, 1, 2, 1], [1, 2, 2, 1],
       [1, 1, 2, 1], [1, 1, 2, 1]]
BLK = [[13, 3, 7, 12], [2, 12, 6, 13], [3, 1, 5, 10], [0, 2, 4, 11], [1, 7, 8, 0], [6, 0, 9, 1], [7, 5, 14, 2],
       [4, 6, 15, 3], [5, 10, 12, 4], [11, 4, 13, 5], [11, 9, 14, 7], [8, 10, 15, 6], [9, 15, 3, 8], [14, 8, 2, 9],
       [15, 13, 1, 10], [12, 14, 0, 11]]
IDX = [[1, 1, 1, 1], [1, 2, 1, 2], [2, 1, 1, 1], [1, 2, 1, 1], [2, 2, 1, 2], [2, 3, 1, 3], [3, 2, 1, 3],
       [2, 3, 1, 3], [3, 2, 3, 3], [2, 4, 3, 4], [3, 2, 2, 4], [2, 3, 2, 4], [3, 3, 4, 3], [3, 4, 4, 4],
       [4, 4, 4, 4], [4, 4, 4, 4]]
HOLD = [[0, 3, 4, 5, 15], [1, 2, 4, 5, 14], [2, 1, 3, 6, 13], [3, 0, 2, 7, 12], [4, 3, 7, 8, 9], [5, 2, 6, 8, 9],
        [6, 1, 5, 7, 11], [7, 0, 4, 6, 10], [8, 4, 11, 12, 13], [9, 5, 10, 12, 13], [10, 2, 8, 11, 14],
        [11, 3, 9, 10, 15], [12, 0, 1, 8, 15], [13, 0, 1, 9, 14], [14, 6, 10, 13, 15], [15, 7, 11, 12, 14]]
PAIRS = [[[(2, 4), (3, 4), (3, 1)], [(0, 2), (0, 3), (2, 3)]], [[(3, 2), (3, 4), (2, 4)], [(0, 1), (1, 3), (0, 3)]],
         [[(2, 1), (1, 3), (2, 3)], [(0, 4), (1, 4), (3, 4)]], [[(1, 2), (2, 3), (3, 4)], [(2, 0), (2, 4), (0, 4)]],
         [[(2, 3), (1, 2), (1, 3)], [(4, 3), (4, 0), (1, 0), (4, 1)]],
         [[(1, 3), (2, 1), (2, 3)], [(4, 3), (0, 3), (2, 0)]],
         [[(4, 1), (4, 2), (2, 3)], [(2, 1), (0, 1), (2, 0), (0, 3)]],
         [[(4, 2), (1, 2), (2, 3)], [(4, 1), (1, 0), (0, 3)]],
         [[(4, 3), (4, 2), (2, 3)], [(4, 0), (1, 0), (1, 3), (4, 1)]],
         [[(4, 3), (4, 1), (1, 3)], [(0, 3), (2, 0), (2, 3)]], [[(2, 1), (4, 2), (4, 1)], [(2, 0), (4, 0), (4, 3)]],
         [[(1, 0), (4, 1), (4, 0)], [(1, 2), (2, 0), (4, 2)]], [[(4, 2), (3, 4), (3, 1)], [(4, 0), (1, 0), (1, 2)]],
         [[(3, 2), (3, 4), (2, 4)], [(4, 1), (2, 0), (2, 1)]], [[(4, 2), (2, 1), (4, 1)], [(4, 0), (2, 0), (3, 4)]],
         [[(4, 1), (1, 2), (4, 2)], [(1, 0), (2, 0), (4, 0)]]]
EARLY = [[1, 1], [0, 1], [1, 0], [1, 1], [1, 2], [1, 2], [2, 3], [2, 2], [1, 1], [1, 1], [1, 1], [1, 2], [1, 1],
         [0, 1], [3, 2], [3, 3]]
NEED = [[[1, 2, 3, 4], [0, 2, 3]], [[2, 3, 4], [0, 1, 3]], [[1, 2, 3], [0, 1, 3, 4]], [[1, 2, 3, 4], [0, 2, 4]],
        [[1, 2, 3], [0, 1, 3, 4]], [[1, 2, 3], [0, 2, 3, 4]], [[1, 2, 3, 4], [0, 1, 2, 3]],
        [[1, 2, 3, 4], [0, 1, 3, 4]], [[2, 3, 4], [0, 1, 3, 4]], [[1, 3, 4], [0, 2, 3]], [[1, 2, 4], [0, 2, 3, 4]],
        [[0, 1, 4], [0, 1, 2, 4]], [[1, 2, 3, 4], [0, 1, 2, 4]], [[2, 3, 4], [0, 1, 2, 4]],
        [[1, 2, 4], [0, 2, 3, 4]], [[1, 2, 4], [0, 1, 2, 4]]]

REL = (0, 3, 1, 2)


def word(digits, base):
    total = 0
    for digit in reversed(digits):
        total = total * base + digit
    return total


def look_up(index, words):
    got = jnp.int32(words[0])
    for k in range(1, len(words)):
        got = jnp.where(index == k, jnp.int32(words[k]), got)
    return got


def digits_of(value, base, count):
    out = []
    for _ in range(count):
        out.append(value % base)
        value = value // base
    return out


def pick(values, index):
    got = values[0]
    for k in range(1, len(values)):
        got = jnp.where(index == k, values[k], got)
    return got


def kernel(emb, ids_in, out, x, units, stage, ids_got, ids_rows, ids_cols, row_best, col_best, row_line, part, parts_got,
           relay,
           load_sem, id_send, id_recv, z_send, z_recv, relay_send, relay_recv, f_send, f_recv, c_send, c_recv, r_send, r_recv):
    grp, blk = lax.axis_index("grp"), lax.axis_index("blk")
    h, zl = grp % 2, grp // 2
    p, zh = blk // 2, blk % 2
    z = zh * 2 + zl
    px, py = p % 4, p // 4

    def device(z_of, core, chip):
        return ((z_of % 2) * 2 + core, chip * 2 + z_of // 2)

    def group_of(z_of):
        return (1 - z_of % 2) * 2 + z_of // 2

    near = [py * 4 + (px + 1) % 4, py * 4 + (px + 3) % 4, ((py + 1) % 4) * 4 + px, ((py + 3) % 4) * 4 + px]
    first = look_up(p, [word(SRC[c], 8) + 4096 * word(DEP[c], 4) for c in range(16)])
    src = digits_of(first, 8, 4)
    dep = digits_of(first // 4096, 4, 4)
    held = [p] + digits_of(look_up(p, [word(BLK[c], 16) for c in range(16)]), 16, 4)
    third = look_up(p, [word(IDX[c], 8) + 4096 * word(HOLD[c][1:], 16) for c in range(16)])
    place = [jnp.int32(0)] + digits_of(third, 8, 4)
    holders = [p] + digits_of(third // 4096, 16, 4)
    lists = []
    for c in range(16):
        for core in range(2):
            flat = [slot for pair in PAIRS[c][core] for slot in pair]
            lists.append(len(PAIRS[c][core]) + 8 * EARLY[c][core] + 64 * word(flat + [0] * (8 - len(flat)), 8))
    todo = look_up(p * 2 + h, lists)
    pair_count, early_count = todo % 8, todo // 8 % 8
    todo = digits_of(todo // 64, 8, 8)

    needs = [[sum(1 << slot for slot in NEED[c][core]) for core in range(2)] for c in range(16)]
    need = digits_of(look_up(p * 2 + h, [needs[c][core] for c in range(16) for core in range(2)]), 2, SLOTS)
    sibling_need = digits_of(look_up(p * 2 + h, [needs[c][1 - core] for c in range(16) for core in range(2)]), 2, SLOTS)

    sibling = device(z, 1 - h, p)
    owner_grp = group_of(z)
    from_z = 2 * h + 1 - zl
    ids_from = device(2 * h + 1 - zl, zh, p)

    def load(k):
        return pltpu.make_async_copy(emb.at[group_of((z + pick((0, 1, 3, 2), k)) % 4)], stage.at[k], load_sem.at[k])

    for k in range(4):
        load(k).start()
    barrier = pltpu.get_barrier_semaphore()
    for rel in (1, 3):
        pl.semaphore_signal(barrier, inc=1, device_id=device((z + rel) % 4, h, p), device_id_type=MESH)
    for d in range(4):
        pl.semaphore_signal(barrier, inc=1, device_id=device(z, h, near[d]), device_id_type=MESH)
    pl.semaphore_signal(barrier, inc=1, device_id=sibling, device_id_type=MESH)
    pl.semaphore_signal(barrier, inc=1, device_id=ids_from, device_id_type=MESH)
    for k in range(SLOTS):
        for core in range(2):
            pl.semaphore_signal(barrier, inc=1, device_id=device(from_z, core, holders[k]), device_id_type=MESH)

    def normalised(k):
        v = stage[k]
        total = jnp.sum(v * v, axis=-1, keepdims=True)
        return (v / jnp.sqrt(total + 1e-06)).astype(jnp.bfloat16)

    load(0).wait()
    own_rows = pl.multiple_of(h * 128, 128)
    x[0, pl.ds(own_rows, 128), :] = normalised(0)
    pl.semaphore_wait(barrier, 18)

    def remote(src_ref, dst_ref, send_sem, recv_sem, to):
        return pltpu.make_async_remote_copy(
            src_ref=src_ref, dst_ref=dst_ref, send_sem=send_sem, recv_sem=recv_sem, device_id=to, device_id_type=MESH)

    def part_rows(t):
        return pl.ds(pl.multiple_of((t // 2) * 256 + h * 128 + (t % 2) * PIECE, PIECE), PIECE)

    def forward(d, t):
        rows = part_rows(t)
        return remote(x.at[src[d], rows, :], x.at[1 + (d ^ 1), rows, :], f_send.at[d, t], f_recv.at[d ^ 1, t],
                      device(z, h, near[d]))

    def arrival(s, t):
        rows = part_rows(t)
        return remote(x.at[s, rows, :], x.at[s, rows, :], f_send.at[s - 1, t], f_recv.at[s - 1, t],
                      device(z, h, near[s - 1]))

    def swap(k, half):
        rows = pl.ds(pl.multiple_of(k * 256 + h * 128 + half * 64, 64), 64)
        return remote(units.at[k - 1, pl.ds(half * 64, 64), :], x.at[0, rows, :], z_send.at[k - 1, half],
                      z_recv.at[k - 1, half], device((z + pick((1, 3), k - 1)) % 4, h, p))

    between = device((z + jnp.where(h == 0, 1, 3)) % 4, h, p)

    def relay_in(half):
        rows = pl.ds(half * 64, 64)
        return remote(units.at[2, rows, :], relay.at[rows, :], relay_send.at[0, half], relay_recv.at[half], between)

    def relay_out(half):
        rows = pl.ds(pl.multiple_of(3 * 256 + h * 128 + half * 64, 64), 64)
        return remote(relay.at[pl.ds(half * 64, 64), :], x.at[0, rows, :], relay_send.at[1, half], z_recv.at[2, half],
                      between)

    def share_rows(t, core):
        return pl.ds(pl.multiple_of((t // 2) * 256 + core * 128 + (t % 2) * 64, 64), 64)

    def share(s, t):
        rows = share_rows(t, h)
        return remote(x.at[s, rows, :], x.at[s, rows, :], c_send.at[s, t], c_recv.at[s, t], sibling)

    def shared(s, t):
        rows = share_rows(t, 1 - h)
        return remote(x.at[s, rows, :], x.at[s, rows, :], c_send.at[s, t], c_recv.at[s, t], sibling)

    def give(s, t):
        pl.when(sibling_need[s] == 1)(lambda: share(s, t).start())

    def send_own(t):
        for d in range(4):
            pl.when(src[d] == 0)(lambda d=d: forward(d, t).start())

    def send_held(t):
        for d in range(4):
            pl.when(src[d] != 0)(lambda d=d: forward(d, t).start())

    def receive(links, t):
        for s in range(1, SLOTS):
            pl.when(dep[s - 1] == links)(lambda s=s: arrival(s, t).wait_recv())

    def give_held(links, t):
        for s in range(1, SLOTS):
            pl.when(dep[s - 1] == links)(lambda s=s: give(s, t))

    for t in range(2):
        send_own(t)
    @pl.loop(1, 4)
    def _(k):
        load(k).wait()
        units[k - 1] = normalised(k)
        for half in range(2):
            pl.when(k < 3)(lambda half=half: swap(k, half).start())
            pl.when(k == 3)(lambda half=half: relay_in(half).start())

    ids_copy = remote(ids_in, ids_got, id_send, id_recv, device(from_z, zh, p))
    ids_copy.start()
    give(0, 0)
    give(0, 1)
    def strip(a, t, b, count, diagonal=False):
        sim = lax.dot_general(x[a, 256 * t:256 * t + 256, :], x[b, 0:256 * count, :], (((1,), (1,)), ((), ())),
                              preferred_element_type=jnp.float32)
        for r in range(4):
            unit, first_row = a * 8 + 2 * t + r // 2, 64 * (r % 2)
            row_ids = ids_rows[unit, first_row:first_row + 64]
            best = row_best[unit, first_row:first_row + 64]
            for c in range(2 * count):
                keep = row_ids == ids_cols[pl.ds(b * 8 + c, 1), :]
                if diagonal and c // 2 == t:
                    row = lax.broadcasted_iota(jnp.int32, (64, 128), 0) + 64 * r
                    col = lax.broadcasted_iota(jnp.int32, (64, 128), 1) + 128 * (c % 2)
                    keep = jnp.logical_and(keep, row != col)
                kept = jnp.where(keep, sim[64 * r:64 * r + 64, 128 * c:128 * c + 128], jnp.float32(-1.0))
                down = jnp.max(kept.reshape(8, 8, 128), axis=0)
                col_best[b * 8 + c] = jnp.maximum(col_best[b * 8 + c], down)
                best = jnp.maximum(best, kept)
            row_best[unit, first_row:first_row + 64] = best

    def compare(t, j):
        a, b = todo[0], todo[1]
        for k in range(1, 4):
            a = jnp.where(j == k, todo[2 * k], a)
            b = jnp.where(j == k, todo[2 * k + 1], b)
        strip(a, t, b, t + 1)
        if t:
            strip(b, t, a, t)

    def own_pair(t):
        pl.when(h == 1)(lambda: strip(0, t, 0, t + 1, diagonal=True))

    def finish_rows(t):
        for s in range(SLOTS):
            @pl.when(need[s] == 1)
            def _():
                for core in range(2):
                    unit = s * 8 + 2 * t + core
                    row_line[unit:unit + 1, :] = jnp.max(row_best[unit].T, axis=0, keepdims=True)

    def wait_shared(m, links):
        for s in range(SLOTS):
            there = need[s] == 1
            if s == 0:
                if links:
                    continue
            elif links:
                there = jnp.logical_and(there, dep[s - 1] == links)
            else:
                continue

            @pl.when(there)
            def _():
                for half in range(2):
                    shared(s, 2 * m + half).wait_recv()

    def own_piece_ready(t):
        send_own(t)
        give(0, t)

    def pass_on(k):
        receive(1, k - 1)
        send_held(k - 1)
        give_held(1, k - 1)

    def take(t):
        receive(2, t)
        give_held(2, t)

    pass_on(1)
    swap(1, 0).wait_recv()
    own_piece_ready(2)
    pass_on(2)
    swap(1, 1).wait_recv()
    own_piece_ready(3)
    swap(2, 0).wait_recv()
    own_piece_ready(4)

    ids_copy.wait_recv()
    ids_cols[...] = jnp.zeros_like(ids_cols)
    for s in range(SLOTS):
        for t in range(4):
            for core in range(2):
                unit = held[s] * 8 + 2 * ((z + REL[t]) % 4) + core
                ids_cols[pl.ds(s * 8 + 2 * t + core, 1), :] = ids_got[pl.ds(unit, 1), :].astype(jnp.float32)
    turned = ids_cols[...].T
    for j in range(SLOTS * 8):
        ids_rows[j] = jnp.broadcast_to(turned[:, j:j + 1], (128, 128))

    pass_on(3)
    for half in range(2):
        relay_in(half).wait_recv()
        relay_out(half).start()
    swap(2, 1).wait_recv()
    own_piece_ready(5)
    @pl.loop(0, SLOTS * 8)
    def _(j):
        row_best[j] = jnp.full((128, 128), -1.0, jnp.float32)
        col_best[j] = jnp.full((8, 128), -1.0, jnp.float32)
    row_line[...] = jnp.full_like(row_line, -1.0)

    take(0)
    pass_on(4)
    for m in (0, 1):
        wait_shared(m, 0)
        own_pair(m)
    take(1)
    pass_on(5)
    for half in range(2):
        relay_out(half).wait_recv()
        own_piece_ready(6 + half)
    wait_shared(0, 1)
    wait_shared(0, 2)

    @pl.loop(0, pair_count)
    def _(j):
        compare(0, j)
    take(2)
    pass_on(6)
    for m in (2, 3):
        wait_shared(m, 0)
        own_pair(m)
    take(3)

    @pl.loop(0, 2)
    def _(k):
        pass_on(7 + k)

        @pl.when(k == 0)
        def _():
            wait_shared(1, 1)
            wait_shared(1, 2)

        @pl.loop(2 * k, jnp.minimum(2 * k + 2, pair_count))
        def _(j):
            compare(1, j)
        take(4 + k)
    finish_rows(0)

    for m in (2, 3):
        wait_shared(m, 1)

        @pl.loop(0, pair_count)
        def _(j):
            pl.when(j == early_count)(lambda: wait_shared(m, 2))
            compare(m, j)
        if m == 2:
            finish_rows(1)
            take(6)
            finish_rows(2)
            take(7)
    finish_rows(3)

    for s in range(SLOTS):
        for t in range(4):
            z_of = (z + REL[t]) % 4
            for core in range(2):
                j = s * 8 + 2 * t + core
                both = jnp.maximum(row_line[j:j + 1, :], jnp.max(col_best[j], axis=0, keepdims=True))
                part[s * 2 + z_of // 2, pl.ds(2 * (z_of % 2) + core, 1), :] = both
        for half in range(2):
            copy = remote(part.at[s * 2 + half], parts_got.at[place[s] * 2 + h], r_send.at[s * 2 + half],
                          r_recv.at[place[s] * 2 + h], (owner_grp, held[s] * 2 + half))
            copy.start()

    ids_copy.wait_send()
    for half in range(2):
        for copy in (swap(1, half), swap(2, half), relay_in(half), relay_out(half)):
            copy.wait_send()

    @pl.loop(0, STEPS)
    def _(t):
        for d in range(4):
            forward(d, t).wait_send()
        for s in range(SLOTS):
            pl.when(sibling_need[s] == 1)(lambda s=s: share(s, t).wait_send())

    best = None
    for k in range(2 * SLOTS):
        got = remote(parts_got.at[k], parts_got.at[k], r_send.at[k], r_recv.at[k], sibling)
        got.wait_recv()
        best = parts_got[k] if best is None else jnp.maximum(best, parts_got[k])
    out[...] = best

    for s in range(SLOTS):
        for half in range(2):
            copy = remote(part.at[s * 2 + half], parts_got.at[place[s] * 2 + h], r_send.at[s * 2 + half],
                          r_recv.at[place[s] * 2 + h], (owner_grp, held[s] * 2 + half))
            copy.wait_send()


def on_device(embeddings, cluster_ids):
    emb = embeddings.reshape(4, 128, D)
    ids = cluster_ids.reshape(128, 128)
    dma = pltpu.SemaphoreType.DMA
    best = pl.pallas_call(
        kernel,
        out_shape=jax.ShapeDtypeStruct((4, 128), jnp.float32),
        in_specs=[pl.BlockSpec(memory_space=pl.ANY), pl.BlockSpec(memory_space=pl.ANY)],
        out_specs=pl.BlockSpec(memory_space=pltpu.VMEM),
        scratch_shapes=[
            pltpu.VMEM((SLOTS, 1024, D), jnp.bfloat16),
            pltpu.VMEM((3, 128, D), jnp.bfloat16),
            pltpu.VMEM((4, 128, D), jnp.float32),
            pltpu.VMEM((128, 128), jnp.int32),
            pltpu.VMEM((SLOTS * 8, 128, 128), jnp.float32),
            pltpu.VMEM((128, 128), jnp.float32),
            pltpu.VMEM((SLOTS * 8, 128, 128), jnp.float32),
            pltpu.VMEM((SLOTS * 8, 8, 128), jnp.float32),
            pltpu.VMEM((SLOTS * 8, 128), jnp.float32),
            pltpu.VMEM((2 * SLOTS, 4, 128), jnp.float32),
            pltpu.VMEM((2 * SLOTS, 4, 128), jnp.float32),
            pltpu.VMEM((128, D), jnp.bfloat16),
            dma((4,)), dma, dma, dma((3, 2)), dma((3, 2)), dma((2, 2)), dma((2,)), dma((4, STEPS)), dma((4, STEPS)),
            dma((SLOTS, 8)), dma((SLOTS, 8)), dma((2 * SLOTS,)), dma((2 * SLOTS,)),
        ],
        compiler_params=pltpu.CompilerParams(
            collective_id=0, has_side_effects=True, vmem_limit_bytes=55168 * 1024),
        cost_estimate=pl.CostEstimate(flops=7 * 10**9, bytes_accessed=2 * 10**6, transcendentals=0),
        name="best_match",
    )(emb, ids)
    return best.reshape(1, 512)


def solution(mesh):
    placed = (P(None, "grp", "blk", None, None), P("grp", None))
    return jax.shard_map(
        on_device, mesh=mesh, in_specs=placed, out_specs=P("grp", "blk"), check_vma=False
    )
```

```python
import functools

import jax
import jax.numpy as jnp
from jax import lax
from jax.experimental import pallas as pl
from jax.experimental.pallas import tpu as pltpu
from jax.sharding import PartitionSpec as P

MESH = pl.DeviceIdType.MESH
D = 768
SLOTS = 5
PIECE = 64
STEPS = 8

SRC = [[4, 0, 0, 2], [0, 4, 0, 1], [0, 0, 0, 2], [0, 0, 0, 1], [4, 0, 0, 2], [0, 4, 0, 1], [0, 0, 1, 2],
       [0, 0, 2, 1], [4, 0, 0, 0], [0, 4, 0, 0], [0, 1, 0, 3], [2, 0, 0, 3], [4, 0, 0, 0], [0, 4, 0, 0],
       [0, 0, 4, 0], [0, 0, 4, 0]]
DEP = [[2, 1, 2, 1], [1, 2, 2, 1], [1, 1, 2, 2], [1, 1, 2, 2], [2, 1, 1, 1], [1, 2, 1, 1], [1, 1, 2, 1],
       [1, 1, 2, 1], [2, 2, 1, 1], [2, 2, 1, 1], [1, 1, 1, 2], [1, 1, 1, 2], [2, 1, 2, 1], [1, 2, 2, 1],
       [1, 1, 2, 1], [1, 1, 2, 1]]
BLK = [[13, 3, 7, 12], [2, 12, 6, 13], [3, 1, 5, 10], [0, 2, 4, 11], [1, 7, 8, 0], [6, 0, 9, 1], [7, 5, 14, 2],
       [4, 6, 15, 3], [5, 10, 12, 4], [11, 4, 13, 5], [11, 9, 14, 7], [8, 10, 15, 6], [9, 15, 3, 8], [14, 8, 2, 9],
       [15, 13, 1, 10], [12, 14, 0, 11]]
IDX = [[1, 1, 1, 1], [1, 2, 1, 2], [2, 1, 1, 1], [1, 2, 1, 1], [2, 2, 1, 2], [2, 3, 1, 3], [3, 2, 1, 3],
       [2, 3, 1, 3], [3, 2, 3, 3], [2, 4, 3, 4], [3, 2, 2, 4], [2, 3, 2, 4], [3, 3, 4, 3], [3, 4, 4, 4],
       [4, 4, 4, 4], [4, 4, 4, 4]]
HOLD = [[0, 3, 4, 5, 15], [1, 2, 4, 5, 14], [2, 1, 3, 6, 13], [3, 0, 2, 7, 12], [4, 3, 7, 8, 9], [5, 2, 6, 8, 9],
        [6, 1, 5, 7, 11], [7, 0, 4, 6, 10], [8, 4, 11, 12, 13], [9, 5, 10, 12, 13], [10, 2, 8, 11, 14],
        [11, 3, 9, 10, 15], [12, 0, 1, 8, 15], [13, 0, 1, 9, 14], [14, 6, 10, 13, 15], [15, 7, 11, 12, 14]]
PAIRS = [[[(2, 4), (3, 4), (4, 1)], [(0, 2), (3, 1), (0, 3)]], [[(3, 2), (3, 4)], [(0, 1), (1, 3), (0, 3)]],
         [[(2, 1), (1, 3), (3, 4)], [(0, 1), (0, 4), (1, 4)]], [[(1, 2), (2, 3), (2, 4)], [(0, 4), (3, 4)]],
         [[(2, 3), (1, 2), (1, 3)], [(4, 3), (4, 0), (1, 0), (4, 1)]],
         [[(1, 3), (2, 1), (2, 3)], [(4, 3), (4, 0), (0, 3), (2, 0)]],
         [[(4, 1), (4, 2), (2, 3)], [(2, 1), (2, 0), (0, 1), (0, 3)]],
         [[(4, 2), (1, 2), (2, 3)], [(4, 1), (4, 0), (1, 0), (0, 3)]],
         [[(4, 3), (4, 2), (2, 3)], [(4, 0), (1, 0), (1, 3), (4, 1)]],
         [[(4, 3), (4, 1), (1, 3)], [(0, 3), (2, 0), (2, 3)]], [[(2, 1), (4, 2), (4, 1)], [(2, 0), (4, 0), (4, 3)]],
         [[(1, 0), (4, 1), (4, 0)], [(1, 2), (2, 0), (4, 2)]], [[(4, 0), (3, 4), (3, 1)], [(4, 2), (1, 0), (1, 2)]],
         [[(3, 2), (3, 4), (2, 4)], [(4, 1), (2, 0), (2, 1)]], [[(4, 2), (2, 1), (4, 1)], [(4, 0), (2, 0), (3, 4)]],
         [[(4, 1), (1, 2), (4, 2)], [(1, 0), (4, 0), (2, 0)]]]
EARLY = [[1, 1], [0, 1], [1, 1], [1, 0], [1, 2], [1, 3], [2, 3], [2, 3], [1, 1], [1, 1], [1, 1], [1, 2], [1, 1],
         [0, 1], [3, 2], [3, 3]]
NEED = [[[1, 2, 3, 4], [0, 1, 2, 3]], [[2, 3, 4], [0, 1, 3]], [[1, 2, 3, 4], [0, 1, 4]], [[1, 2, 3, 4], [0, 3, 4]],
        [[1, 2, 3], [0, 1, 3, 4]], [[1, 2, 3], [0, 2, 3, 4]], [[1, 2, 3, 4], [0, 1, 2, 3]],
        [[1, 2, 3, 4], [0, 1, 3, 4]], [[2, 3, 4], [0, 1, 3, 4]], [[1, 3, 4], [0, 2, 3]], [[1, 2, 4], [0, 2, 3, 4]],
        [[0, 1, 4], [0, 1, 2, 4]], [[0, 1, 3, 4], [0, 1, 2, 4]], [[2, 3, 4], [0, 1, 2, 4]],
        [[1, 2, 4], [0, 2, 3, 4]], [[1, 2, 4], [0, 1, 2, 4]]]

REL = (0, 1, 3, 2)


def word(digits, base):
    total = 0
    for digit in reversed(digits):
        total = total * base + digit
    return total


def look_up(index, words):
    got = jnp.int32(words[0])
    for k in range(1, len(words)):
        got = jnp.where(index == k, jnp.int32(words[k]), got)
    return got


def digits_of(value, base, count):
    out = []
    for _ in range(count):
        out.append(value % base)
        value = value // base
    return out


def pick(values, index):
    got = values[0]
    for k in range(1, len(values)):
        got = jnp.where(index == k, values[k], got)
    return got


def kernel(emb, ids_in, out, x, units, stage, ids_got, ids_rows, ids_cols, row_best, col_best, row_line, part, parts_got,
           relay,
           load_sem, id_send, id_recv, z_send, z_recv, relay_send, relay_recv, f_send, f_recv, c_send, c_recv, r_send, r_recv):
    grp, blk = lax.axis_index("grp"), lax.axis_index("blk")
    h, zl = grp % 2, grp // 2
    p, zh = blk // 2, blk % 2
    z = zh * 2 + zl
    px, py = p % 4, p // 4

    def device(z_of, core, chip):
        return ((z_of % 2) * 2 + core, chip * 2 + z_of // 2)

    def group_of(z_of):
        return (1 - z_of % 2) * 2 + z_of // 2

    near = [py * 4 + (px + 1) % 4, py * 4 + (px + 3) % 4, ((py + 1) % 4) * 4 + px, ((py + 3) % 4) * 4 + px]
    first = look_up(p, [word(SRC[c], 8) + 4096 * word(DEP[c], 4) for c in range(16)])
    src = digits_of(first, 8, 4)
    dep = digits_of(first // 4096, 4, 4)
    held = [p] + digits_of(look_up(p, [word(BLK[c], 16) for c in range(16)]), 16, 4)
    third = look_up(p, [word(IDX[c], 8) + 4096 * word(HOLD[c][1:], 16) for c in range(16)])
    place = [jnp.int32(0)] + digits_of(third, 8, 4)
    holders = [p] + digits_of(third // 4096, 16, 4)
    lists = []
    for c in range(16):
        for core in range(2):
            flat = [slot for pair in PAIRS[c][core] for slot in pair]
            lists.append(len(PAIRS[c][core]) + 8 * EARLY[c][core] + 64 * word(flat + [0] * (8 - len(flat)), 8))
    todo = look_up(p * 2 + h, lists)
    pair_count, early_count = todo % 8, todo // 8 % 8
    todo = digits_of(todo // 64, 8, 8)

    needs = [[sum(1 << slot for slot in NEED[c][core]) for core in range(2)] for c in range(16)]
    need = digits_of(look_up(p * 2 + h, [needs[c][core] for c in range(16) for core in range(2)]), 2, SLOTS)
    sibling_need = digits_of(look_up(p * 2 + h, [needs[c][1 - core] for c in range(16) for core in range(2)]), 2, SLOTS)

    sibling = device(z, 1 - h, p)
    owner_grp = group_of(z)
    from_z = 2 * h + 1 - zl
    ids_from = device(2 * h + 1 - zl, zh, p)

    def load(k):
        return pltpu.make_async_copy(emb.at[group_of((z + pick((0, 3, 1, 2), k)) % 4)], stage.at[k], load_sem.at[k])

    for k in range(4):
        load(k).start()
    barrier = pltpu.get_barrier_semaphore()
    for rel in (1, 3):
        pl.semaphore_signal(barrier, inc=1, device_id=device((z + rel) % 4, h, p), device_id_type=MESH)
    for d in range(4):
        pl.semaphore_signal(barrier, inc=1, device_id=device(z, h, near[d]), device_id_type=MESH)
    pl.semaphore_signal(barrier, inc=1, device_id=sibling, device_id_type=MESH)
    pl.semaphore_signal(barrier, inc=1, device_id=ids_from, device_id_type=MESH)
    for k in range(SLOTS):
        for core in range(2):
            pl.semaphore_signal(barrier, inc=1, device_id=device(from_z, core, holders[k]), device_id_type=MESH)

    def normalised(k):
        v = stage[k]
        total = jnp.sum(v * v, axis=-1, keepdims=True)
        return (v / jnp.sqrt(total + 1e-06)).astype(jnp.bfloat16)

    load(0).wait()
    own_rows = pl.multiple_of(h * 128, 128)
    x[0, pl.ds(own_rows, 128), :] = normalised(0)
    pl.semaphore_wait(barrier, 18)

    def remote(src_ref, dst_ref, send_sem, recv_sem, to):
        return pltpu.make_async_remote_copy(
            src_ref=src_ref, dst_ref=dst_ref, send_sem=send_sem, recv_sem=recv_sem, device_id=to, device_id_type=MESH)

    def part_rows(t):
        return pl.ds(pl.multiple_of((t // 2) * 256 + h * 128 + (t % 2) * PIECE, PIECE), PIECE)

    def forward(d, t):
        rows = part_rows(t)
        return remote(x.at[src[d], rows, :], x.at[1 + (d ^ 1), rows, :], f_send.at[d, t], f_recv.at[d ^ 1, t],
                      device(z, h, near[d]))

    def arrival(s, t):
        rows = part_rows(t)
        return remote(x.at[s, rows, :], x.at[s, rows, :], f_send.at[s - 1, t], f_recv.at[s - 1, t],
                      device(z, h, near[s - 1]))

    def swap(k, half):
        rows = pl.ds(pl.multiple_of(k * 256 + h * 128 + half * 64, 64), 64)
        return remote(units.at[k - 1, pl.ds(half * 64, 64), :], x.at[0, rows, :], z_send.at[k - 1, half],
                      z_recv.at[k - 1, half], device((z + pick((3, 1), k - 1)) % 4, h, p))

    between = device((z + jnp.where(h == 0, 1, 3)) % 4, h, p)

    def relay_in(half):
        rows = pl.ds(half * 64, 64)
        return remote(units.at[2, rows, :], relay.at[rows, :], relay_send.at[0, half], relay_recv.at[half], between)

    def relay_out(half):
        rows = pl.ds(pl.multiple_of(3 * 256 + h * 128 + half * 64, 64), 64)
        return remote(relay.at[pl.ds(half * 64, 64), :], x.at[0, rows, :], relay_send.at[1, half], z_recv.at[2, half],
                      between)

    def share_rows(t, core):
        return pl.ds(pl.multiple_of((t // 2) * 256 + core * 128 + (t % 2) * 64, 64), 64)

    def share(s, t):
        rows = share_rows(t, h)
        return remote(x.at[s, rows, :], x.at[s, rows, :], c_send.at[s, t], c_recv.at[s, t], sibling)

    def shared(s, t):
        rows = share_rows(t, 1 - h)
        return remote(x.at[s, rows, :], x.at[s, rows, :], c_send.at[s, t], c_recv.at[s, t], sibling)

    def give(s, t):
        pl.when(sibling_need[s] == 1)(lambda: share(s, t).start())

    def send_own(t):
        for d in range(4):
            pl.when(src[d] == 0)(lambda d=d: forward(d, t).start())

    def send_held(t):
        for d in range(4):
            pl.when(src[d] != 0)(lambda d=d: forward(d, t).start())

    def receive(links, t):
        for s in range(1, SLOTS):
            pl.when(dep[s - 1] == links)(lambda s=s: arrival(s, t).wait_recv())

    def give_held(links, t):
        for s in range(1, SLOTS):
            pl.when(dep[s - 1] == links)(lambda s=s: give(s, t))

    for t in range(2):
        send_own(t)
    @pl.loop(1, 4)
    def _(k):
        load(k).wait()
        units[k - 1] = normalised(k)
        for half in range(2):
            pl.when(k < 3)(lambda half=half: swap(k, half).start())
            pl.when(k == 3)(lambda half=half: relay_in(half).start())

    ids_copy = remote(ids_in, ids_got, id_send, id_recv, device(from_z, zh, p))
    ids_copy.start()
    give(0, 0)
    give(0, 1)
    def strip(a, t, b, count, diagonal=False):
        sim = lax.dot_general(x[a, 256 * t:256 * t + 256, :], x[b, 0:256 * count, :], (((1,), (1,)), ((), ())),
                              preferred_element_type=jnp.float32)
        for r in range(4):
            unit, first_row = a * 8 + 2 * t + r // 2, 64 * (r % 2)
            row_ids = ids_rows[unit, first_row:first_row + 64]
            best = row_best[unit, first_row:first_row + 64]
            for c in range(2 * count):
                keep = row_ids == ids_cols[pl.ds(b * 8 + c, 1), :]
                if diagonal and c // 2 == t:
                    row = lax.broadcasted_iota(jnp.int32, (64, 128), 0) + 64 * r
                    col = lax.broadcasted_iota(jnp.int32, (64, 128), 1) + 128 * (c % 2)
                    keep = jnp.logical_and(keep, row != col)
                kept = jnp.where(keep, sim[64 * r:64 * r + 64, 128 * c:128 * c + 128], jnp.float32(-1.0))
                down = jnp.max(kept.reshape(8, 8, 128), axis=0)
                col_best[b * 8 + c] = jnp.maximum(col_best[b * 8 + c], down)
                best = jnp.maximum(best, kept)
            row_best[unit, first_row:first_row + 64] = best

    def compare(t, j):
        a, b = todo[0], todo[1]
        for k in range(1, 4):
            a = jnp.where(j == k, todo[2 * k], a)
            b = jnp.where(j == k, todo[2 * k + 1], b)
        strip(a, t, b, t + 1)
        if t:
            strip(b, t, a, t)

    def own_pair(t):
        pl.when(h == 1)(lambda: strip(0, t, 0, t + 1, diagonal=True))

    def finish_rows(t):
        for s in range(SLOTS):
            @pl.when(need[s] == 1)
            def _():
                for core in range(2):
                    unit = s * 8 + 2 * t + core
                    row_line[unit:unit + 1, :] = jnp.max(row_best[unit].T, axis=0, keepdims=True)

    def wait_shared(m, links):
        for s in range(SLOTS):
            there = need[s] == 1
            if s == 0:
                if links:
                    continue
            elif links:
                there = jnp.logical_and(there, dep[s - 1] == links)
            else:
                continue

            @pl.when(there)
            def _():
                for half in range(2):
                    shared(s, 2 * m + half).wait_recv()

    def own_piece_ready(t):
        send_own(t)
        give(0, t)

    def pass_on(k):
        receive(1, k - 1)
        send_held(k - 1)
        give_held(1, k - 1)

    def take(t):
        receive(2, t)
        give_held(2, t)

    pass_on(1)
    swap(1, 0).wait_recv()
    own_piece_ready(2)
    pass_on(2)
    swap(1, 1).wait_recv()
    own_piece_ready(3)
    swap(2, 0).wait_recv()
    own_piece_ready(4)

    ids_copy.wait_recv()
    ids_cols[...] = jnp.zeros_like(ids_cols)
    for s in range(SLOTS):
        for t in range(4):
            for core in range(2):
                unit = held[s] * 8 + 2 * ((z + REL[t]) % 4) + core
                ids_cols[pl.ds(s * 8 + 2 * t + core, 1), :] = ids_got[pl.ds(unit, 1), :].astype(jnp.float32)
    turned = ids_cols[...].T
    for j in range(SLOTS * 8):
        ids_rows[j] = jnp.broadcast_to(turned[:, j:j + 1], (128, 128))

    pass_on(3)
    for half in range(2):
        relay_in(half).wait_recv()
        relay_out(half).start()
    swap(2, 1).wait_recv()
    own_piece_ready(5)
    @pl.loop(0, SLOTS * 8)
    def _(j):
        row_best[j] = jnp.full((128, 128), -1.0, jnp.float32)
        col_best[j] = jnp.full((8, 128), -1.0, jnp.float32)
    row_line[...] = jnp.full_like(row_line, -1.0)

    take(0)
    pass_on(4)
    for m in (0, 1):
        wait_shared(m, 0)
        own_pair(m)
    take(1)
    pass_on(5)
    for half in range(2):
        relay_out(half).wait_recv()
        own_piece_ready(6 + half)
    wait_shared(0, 1)
    wait_shared(0, 2)

    @pl.loop(0, pair_count)
    def _(j):
        compare(0, j)
    take(2)
    pass_on(6)
    for m in (2, 3):
        wait_shared(m, 0)
        own_pair(m)
    take(3)

    @pl.loop(0, 2)
    def _(k):
        pass_on(7 + k)

        @pl.when(k == 0)
        def _():
            wait_shared(1, 1)
            wait_shared(1, 2)

        @pl.loop(2 * k, jnp.minimum(2 * k + 2, pair_count))
        def _(j):
            compare(1, j)
        take(4 + k)
    finish_rows(0)

    for m in (2, 3):
        wait_shared(m, 1)

        @pl.loop(0, pair_count)
        def _(j):
            pl.when(j == early_count)(lambda: wait_shared(m, 2))
            compare(m, j)
        if m == 2:
            finish_rows(1)
            take(6)
            finish_rows(2)
            take(7)
    finish_rows(3)

    for s in range(SLOTS):
        for t in range(4):
            z_of = (z + REL[t]) % 4
            for core in range(2):
                j = s * 8 + 2 * t + core
                both = jnp.maximum(row_line[j:j + 1, :], jnp.max(col_best[j], axis=0, keepdims=True))
                part[s * 2 + z_of // 2, pl.ds(2 * (z_of % 2) + core, 1), :] = both
        for half in range(2):
            copy = remote(part.at[s * 2 + half], parts_got.at[place[s] * 2 + h], r_send.at[s * 2 + half],
                          r_recv.at[place[s] * 2 + h], (owner_grp, held[s] * 2 + half))
            copy.start()

    ids_copy.wait_send()
    for half in range(2):
        for copy in (swap(1, half), swap(2, half), relay_in(half), relay_out(half)):
            copy.wait_send()

    @pl.loop(0, STEPS)
    def _(t):
        for d in range(4):
            forward(d, t).wait_send()
        for s in range(SLOTS):
            pl.when(sibling_need[s] == 1)(lambda s=s: share(s, t).wait_send())

    best = None
    for k in range(2 * SLOTS):
        got = remote(parts_got.at[k], parts_got.at[k], r_send.at[k], r_recv.at[k], sibling)
        got.wait_recv()
        best = parts_got[k] if best is None else jnp.maximum(best, parts_got[k])
    out[...] = best

    for s in range(SLOTS):
        for half in range(2):
            copy = remote(part.at[s * 2 + half], parts_got.at[place[s] * 2 + h], r_send.at[s * 2 + half],
                          r_recv.at[place[s] * 2 + h], (owner_grp, held[s] * 2 + half))
            copy.wait_send()


def on_device(embeddings, cluster_ids):
    emb = embeddings.reshape(4, 128, D)
    ids = cluster_ids.reshape(128, 128)
    dma = pltpu.SemaphoreType.DMA
    best = pl.pallas_call(
        kernel,
        out_shape=jax.ShapeDtypeStruct((4, 128), jnp.float32),
        in_specs=[pl.BlockSpec(memory_space=pl.ANY), pl.BlockSpec(memory_space=pl.ANY)],
        out_specs=pl.BlockSpec(memory_space=pltpu.VMEM),
        scratch_shapes=[
            pltpu.VMEM((SLOTS, 1024, D), jnp.bfloat16),
            pltpu.VMEM((3, 128, D), jnp.bfloat16),
            pltpu.VMEM((4, 128, D), jnp.float32),
            pltpu.VMEM((128, 128), jnp.int32),
            pltpu.VMEM((SLOTS * 8, 128, 128), jnp.float32),
            pltpu.VMEM((128, 128), jnp.float32),
            pltpu.VMEM((SLOTS * 8, 128, 128), jnp.float32),
            pltpu.VMEM((SLOTS * 8, 8, 128), jnp.float32),
            pltpu.VMEM((SLOTS * 8, 128), jnp.float32),
            pltpu.VMEM((2 * SLOTS, 4, 128), jnp.float32),
            pltpu.VMEM((2 * SLOTS, 4, 128), jnp.float32),
            pltpu.VMEM((128, D), jnp.bfloat16),
            dma((4,)), dma, dma, dma((3, 2)), dma((3, 2)), dma((2, 2)), dma((2,)), dma((4, STEPS)), dma((4, STEPS)),
            dma((SLOTS, 8)), dma((SLOTS, 8)), dma((2 * SLOTS,)), dma((2 * SLOTS,)),
        ],
        compiler_params=pltpu.CompilerParams(
            collective_id=0, has_side_effects=True, vmem_limit_bytes=55168 * 1024),
        cost_estimate=pl.CostEstimate(flops=7 * 10**9, bytes_accessed=2 * 10**6, transcendentals=0),
        name="best_match",
    )(emb, ids)
    return best.reshape(1, 512)


def solution(mesh):
    placed = (P(None, "grp", "blk", None, None), P("grp", None))
    return jax.shard_map(
        on_device, mesh=mesh, in_specs=placed, out_specs=P("grp", "blk"), check_vma=False
    )
```

```python
import functools

import jax
import jax.numpy as jnp
from jax import lax
from jax.experimental import pallas as pl
from jax.experimental.pallas import tpu as pltpu
from jax.sharding import PartitionSpec as P

MESH = pl.DeviceIdType.MESH
D = 768
SLOTS = 5
PIECE = 64
STEPS = 8

SRC = [[4, 0, 0, 2], [0, 4, 0, 1], [0, 0, 0, 2], [0, 0, 0, 1], [4, 0, 0, 2], [0, 4, 0, 1], [0, 0, 1, 2],
       [0, 0, 2, 1], [4, 0, 0, 0], [0, 4, 0, 0], [0, 1, 0, 3], [2, 0, 0, 3], [4, 0, 0, 0], [0, 4, 0, 0],
       [0, 0, 4, 0], [0, 0, 4, 0]]
DEP = [[2, 1, 2, 1], [1, 2, 2, 1], [1, 1, 2, 2], [1, 1, 2, 2], [2, 1, 1, 1], [1, 2, 1, 1], [1, 1, 2, 1],
       [1, 1, 2, 1], [2, 2, 1, 1], [2, 2, 1, 1], [1, 1, 1, 2], [1, 1, 1, 2], [2, 1, 2, 1], [1, 2, 2, 1],
       [1, 1, 2, 1], [1, 1, 2, 1]]
BLK = [[13, 3, 7, 12], [2, 12, 6, 13], [3, 1, 5, 10], [0, 2, 4, 11], [1, 7, 8, 0], [6, 0, 9, 1], [7, 5, 14, 2],
       [4, 6, 15, 3], [5, 10, 12, 4], [11, 4, 13, 5], [11, 9, 14, 7], [8, 10, 15, 6], [9, 15, 3, 8], [14, 8, 2, 9],
       [15, 13, 1, 10], [12, 14, 0, 11]]
IDX = [[1, 1, 1, 1], [1, 2, 1, 2], [2, 1, 1, 1], [1, 2, 1, 1], [2, 2, 1, 2], [2, 3, 1, 3], [3, 2, 1, 3],
       [2, 3, 1, 3], [3, 2, 3, 3], [2, 4, 3, 4], [3, 2, 2, 4], [2, 3, 2, 4], [3, 3, 4, 3], [3, 4, 4, 4],
       [4, 4, 4, 4], [4, 4, 4, 4]]
HOLD = [[0, 3, 4, 5, 15], [1, 2, 4, 5, 14], [2, 1, 3, 6, 13], [3, 0, 2, 7, 12], [4, 3, 7, 8, 9], [5, 2, 6, 8, 9],
        [6, 1, 5, 7, 11], [7, 0, 4, 6, 10], [8, 4, 11, 12, 13], [9, 5, 10, 12, 13], [10, 2, 8, 11, 14],
        [11, 3, 9, 10, 15], [12, 0, 1, 8, 15], [13, 0, 1, 9, 14], [14, 6, 10, 13, 15], [15, 7, 11, 12, 14]]
PAIRS = [[[(2, 4), (3, 4), (4, 1)], [(0, 2), (3, 1), (0, 3)]], [[(3, 2), (3, 4)], [(0, 1), (1, 3), (0, 3)]],
         [[(2, 1), (1, 3), (3, 4)], [(0, 1), (0, 4), (1, 4)]], [[(1, 2), (2, 3), (2, 4)], [(0, 4), (3, 4)]],
         [[(2, 3), (1, 2), (1, 3)], [(4, 3), (4, 0), (1, 0), (4, 1)]],
         [[(1, 3), (2, 1), (2, 3)], [(4, 3), (4, 0), (0, 3), (2, 0)]],
         [[(4, 1), (4, 2), (2, 3)], [(2, 1), (2, 0), (0, 1), (0, 3)]],
         [[(4, 2), (1, 2), (2, 3)], [(4, 1), (4, 0), (1, 0), (0, 3)]],
         [[(4, 3), (4, 2), (2, 3)], [(4, 0), (1, 0), (1, 3), (4, 1)]],
         [[(4, 3), (4, 1), (1, 3)], [(0, 3), (2, 0), (2, 3)]], [[(2, 1), (4, 2), (4, 1)], [(2, 0), (4, 0), (4, 3)]],
         [[(1, 0), (4, 1), (4, 0)], [(1, 2), (2, 0), (4, 2)]], [[(4, 0), (3, 4), (3, 1)], [(4, 2), (1, 0), (1, 2)]],
         [[(3, 2), (3, 4), (2, 4)], [(4, 1), (2, 0), (2, 1)]], [[(4, 2), (2, 1), (4, 1)], [(4, 0), (2, 0), (3, 4)]],
         [[(4, 1), (1, 2), (4, 2)], [(1, 0), (4, 0), (2, 0)]]]
EARLY = [[1, 1], [0, 1], [1, 1], [1, 0], [1, 2], [1, 3], [2, 3], [2, 3], [1, 1], [1, 1], [1, 1], [1, 2], [1, 1],
         [0, 1], [3, 2], [3, 3]]
NEED = [[[1, 2, 3, 4], [0, 1, 2, 3]], [[2, 3, 4], [0, 1, 3]], [[1, 2, 3, 4], [0, 1, 4]], [[1, 2, 3, 4], [0, 3, 4]],
        [[1, 2, 3], [0, 1, 3, 4]], [[1, 2, 3], [0, 2, 3, 4]], [[1, 2, 3, 4], [0, 1, 2, 3]],
        [[1, 2, 3, 4], [0, 1, 3, 4]], [[2, 3, 4], [0, 1, 3, 4]], [[1, 3, 4], [0, 2, 3]], [[1, 2, 4], [0, 2, 3, 4]],
        [[0, 1, 4], [0, 1, 2, 4]], [[0, 1, 3, 4], [0, 1, 2, 4]], [[2, 3, 4], [0, 1, 2, 4]],
        [[1, 2, 4], [0, 2, 3, 4]], [[1, 2, 4], [0, 1, 2, 4]]]

REL = (0, 1, 3, 2)

GROUP_OF = (2, 0, 1, 3)
PLANE_OF = (1, 2, 0, 3)


def word(digits, base):
    total = 0
    for digit in reversed(digits):
        total = total * base + digit
    return total


def look_up(index, words):
    got = jnp.int32(words[0])
    for k in range(1, len(words)):
        got = jnp.where(index == k, jnp.int32(words[k]), got)
    return got


def digits_of(value, base, count):
    out = []
    for _ in range(count):
        out.append(value % base)
        value = value // base
    return out


def pick(values, index):
    got = values[0]
    for k in range(1, len(values)):
        got = jnp.where(index == k, values[k], got)
    return got


def kernel(emb, ids_in, out, x, units, stage, ids_got, ids_rows, ids_cols, row_best, col_best, row_line, part, parts_got,
           relay,
           load_sem, id_send, id_recv, z_send, z_recv, relay_send, relay_recv, f_send, f_recv, c_send, c_recv, r_send, r_recv):
    grp, blk = lax.axis_index("grp"), lax.axis_index("blk")
    h, zl = grp % 2, grp // 2
    p, zh = blk // 2, blk % 2
    z = zh * 2 + zl
    px, py = p % 4, p // 4

    def device(z_of, core, chip):
        return ((z_of % 2) * 2 + core, chip * 2 + z_of // 2)

    def group_of(z_of):
        return pick(GROUP_OF, z_of)

    near = [py * 4 + (px + 1) % 4, py * 4 + (px + 3) % 4, ((py + 1) % 4) * 4 + px, ((py + 3) % 4) * 4 + px]
    first = look_up(p, [word(SRC[c], 8) + 4096 * word(DEP[c], 4) for c in range(16)])
    src = digits_of(first, 8, 4)
    dep = digits_of(first // 4096, 4, 4)
    held = [p] + digits_of(look_up(p, [word(BLK[c], 16) for c in range(16)]), 16, 4)
    third = look_up(p, [word(IDX[c], 8) + 4096 * word(HOLD[c][1:], 16) for c in range(16)])
    place = [jnp.int32(0)] + digits_of(third, 8, 4)
    holders = [p] + digits_of(third // 4096, 16, 4)
    lists = []
    for c in range(16):
        for core in range(2):
            flat = [slot for pair in PAIRS[c][core] for slot in pair]
            lists.append(len(PAIRS[c][core]) + 8 * EARLY[c][core] + 64 * word(flat + [0] * (8 - len(flat)), 8))
    todo = look_up(p * 2 + h, lists)
    pair_count, early_count = todo % 8, todo // 8 % 8
    todo = digits_of(todo // 64, 8, 8)

    needs = [[sum(1 << slot for slot in NEED[c][core]) for core in range(2)] for c in range(16)]
    need = digits_of(look_up(p * 2 + h, [needs[c][core] for c in range(16) for core in range(2)]), 2, SLOTS)
    sibling_need = digits_of(look_up(p * 2 + h, [needs[c][1 - core] for c in range(16) for core in range(2)]), 2, SLOTS)

    sibling = device(z, 1 - h, p)
    owner_grp = group_of(z)
    from_z = pick(PLANE_OF, grp)
    ids_from = device(owner_grp // 2 + 2 * h, owner_grp % 2, p)
    mine = grp == owner_grp
    def load(k):
        return pltpu.make_async_copy(emb.at[group_of((z + pick((0, 3, 1, 2), k)) % 4)], stage.at[k], load_sem.at[k])

    for k in range(4):
        load(k).start()
    barrier = pltpu.get_barrier_semaphore()
    for rel in (1, 3):
        pl.semaphore_signal(barrier, inc=1, device_id=device((z + rel) % 4, h, p), device_id_type=MESH)
    for d in range(4):
        pl.semaphore_signal(barrier, inc=1, device_id=device(z, h, near[d]), device_id_type=MESH)
    pl.semaphore_signal(barrier, inc=1, device_id=sibling, device_id_type=MESH)
    for k in range(SLOTS):
        for core in range(2):
            def tell():
                pl.semaphore_signal(barrier, inc=1, device_id=device(from_z, core, holders[k]), device_id_type=MESH)
            if k == 0:
                pl.when(jnp.logical_not(jnp.logical_and(mine, h == core)))(tell)
            else:
                tell()

    @pl.when(jnp.logical_not(mine))
    def _():
        pl.semaphore_signal(barrier, inc=1, device_id=ids_from, device_id_type=MESH)

    def normalised(k):
        v = stage[k]
        total = jnp.sum(v * v, axis=-1, keepdims=True)
        return (v / jnp.sqrt(total + 1e-06)).astype(jnp.bfloat16)

    load(0).wait()
    own_rows = pl.multiple_of(h * 128, 128)
    x[0, pl.ds(own_rows, 128), :] = normalised(0)
    pl.semaphore_wait(barrier, jnp.where(mine, 16, 18))

    def remote(src_ref, dst_ref, send_sem, recv_sem, to):
        return pltpu.make_async_remote_copy(
            src_ref=src_ref, dst_ref=dst_ref, send_sem=send_sem, recv_sem=recv_sem, device_id=to, device_id_type=MESH)

    def part_rows(t):
        return pl.ds(pl.multiple_of((t // 2) * 256 + h * 128 + (t % 2) * PIECE, PIECE), PIECE)

    def forward(d, t):
        rows = part_rows(t)
        return remote(x.at[src[d], rows, :], x.at[1 + (d ^ 1), rows, :], f_send.at[d, t], f_recv.at[d ^ 1, t],
                      device(z, h, near[d]))

    def arrival(s, t):
        rows = part_rows(t)
        return remote(x.at[s, rows, :], x.at[s, rows, :], f_send.at[s - 1, t], f_recv.at[s - 1, t],
                      device(z, h, near[s - 1]))

    def swap(k, half):
        rows = pl.ds(pl.multiple_of(k * 256 + h * 128 + half * 64, 64), 64)
        return remote(units.at[k - 1, pl.ds(half * 64, 64), :], x.at[0, rows, :], z_send.at[k - 1, half],
                      z_recv.at[k - 1, half], device((z + pick((3, 1), k - 1)) % 4, h, p))

    between = device((z + jnp.where(h == 0, 1, 3)) % 4, h, p)

    def relay_in(half):
        rows = pl.ds(half * 64, 64)
        return remote(units.at[2, rows, :], relay.at[rows, :], relay_send.at[0, half], relay_recv.at[half], between)

    def relay_out(half):
        rows = pl.ds(pl.multiple_of(3 * 256 + h * 128 + half * 64, 64), 64)
        return remote(relay.at[pl.ds(half * 64, 64), :], x.at[0, rows, :], relay_send.at[1, half], z_recv.at[2, half],
                      between)

    def share_rows(t, core):
        return pl.ds(pl.multiple_of((t // 2) * 256 + core * 128 + (t % 2) * 64, 64), 64)

    def share(s, t):
        rows = share_rows(t, h)
        return remote(x.at[s, rows, :], x.at[s, rows, :], c_send.at[s, t], c_recv.at[s, t], sibling)

    def shared(s, t):
        rows = share_rows(t, 1 - h)
        return remote(x.at[s, rows, :], x.at[s, rows, :], c_send.at[s, t], c_recv.at[s, t], sibling)

    def give(s, t):
        pl.when(sibling_need[s] == 1)(lambda: share(s, t).start())

    def send_own(t):
        for d in range(4):
            pl.when(src[d] == 0)(lambda d=d: forward(d, t).start())

    def send_held(t):
        for d in range(4):
            pl.when(src[d] != 0)(lambda d=d: forward(d, t).start())

    def receive(links, t):
        for s in range(1, SLOTS):
            pl.when(dep[s - 1] == links)(lambda s=s: arrival(s, t).wait_recv())

    def give_held(links, t):
        for s in range(1, SLOTS):
            pl.when(dep[s - 1] == links)(lambda s=s: give(s, t))

    for t in range(2):
        send_own(t)
    @pl.loop(1, 4)
    def _(k):
        load(k).wait()
        units[k - 1] = normalised(k)
        for half in range(2):
            pl.when(k < 3)(lambda half=half: swap(k, half).start())
            pl.when(k == 3)(lambda half=half: relay_in(half).start())

    ids_copy = remote(ids_in, ids_got, id_send, id_recv, device(from_z, zh, p))
    ids_here = pltpu.make_async_copy(ids_in, ids_got, id_recv)
    pl.when(mine)(ids_here.start)
    pl.when(jnp.logical_not(mine))(ids_copy.start)
    give(0, 0)
    give(0, 1)
    def strip(a, t, b, count, diagonal=False):
        sim = lax.dot_general(x[a, 256 * t:256 * t + 256, :], x[b, 0:256 * count, :], (((1,), (1,)), ((), ())),
                              preferred_element_type=jnp.float32)
        for r in range(4):
            unit, first_row = a * 8 + 2 * t + r // 2, 64 * (r % 2)
            row_ids = ids_rows[unit, first_row:first_row + 64]
            best = row_best[unit, first_row:first_row + 64]
            for c in range(2 * count):
                keep = row_ids == ids_cols[pl.ds(b * 8 + c, 1), :]
                if diagonal and c // 2 == t:
                    row = lax.broadcasted_iota(jnp.int32, (64, 128), 0) + 64 * r
                    col = lax.broadcasted_iota(jnp.int32, (64, 128), 1) + 128 * (c % 2)
                    keep = jnp.logical_and(keep, row != col)
                kept = jnp.where(keep, sim[64 * r:64 * r + 64, 128 * c:128 * c + 128], jnp.float32(-1.0))
                down = jnp.max(kept.reshape(8, 8, 128), axis=0)
                col_best[b * 8 + c] = jnp.maximum(col_best[b * 8 + c], down)
                best = jnp.maximum(best, kept)
            row_best[unit, first_row:first_row + 64] = best

    def compare(t, j):
        a, b = todo[0], todo[1]
        for k in range(1, 4):
            a = jnp.where(j == k, todo[2 * k], a)
            b = jnp.where(j == k, todo[2 * k + 1], b)
        strip(a, t, b, t + 1)
        if t:
            strip(b, t, a, t)

    def own_pair(t):
        pl.when(h == 1)(lambda: strip(0, t, 0, t + 1, diagonal=True))

    def finish_rows(t):
        for s in range(SLOTS):
            @pl.when(need[s] == 1)
            def _():
                for core in range(2):
                    unit = s * 8 + 2 * t + core
                    row_line[unit:unit + 1, :] = jnp.max(row_best[unit].T, axis=0, keepdims=True)

    def wait_shared(m, links):
        for s in range(SLOTS):
            there = need[s] == 1
            if s == 0:
                if links:
                    continue
            elif links:
                there = jnp.logical_and(there, dep[s - 1] == links)
            else:
                continue

            @pl.when(there)
            def _():
                for half in range(2):
                    shared(s, 2 * m + half).wait_recv()

    def own_piece_ready(t):
        send_own(t)
        give(0, t)

    def pass_on(k):
        receive(1, k - 1)
        send_held(k - 1)
        give_held(1, k - 1)

    def take(t):
        receive(2, t)
        give_held(2, t)

    pass_on(1)
    swap(1, 0).wait_recv()
    own_piece_ready(2)
    pass_on(2)
    swap(1, 1).wait_recv()
    own_piece_ready(3)
    swap(2, 0).wait_recv()
    own_piece_ready(4)

    pl.when(mine)(ids_here.wait)
    pl.when(jnp.logical_not(mine))(ids_copy.wait_recv)
    ids_cols[...] = jnp.zeros_like(ids_cols)
    for s in range(SLOTS):
        for t in range(4):
            for core in range(2):
                unit = held[s] * 8 + 2 * ((z + REL[t]) % 4) + core
                ids_cols[pl.ds(s * 8 + 2 * t + core, 1), :] = ids_got[pl.ds(unit, 1), :].astype(jnp.float32)
    turned = ids_cols[...].T
    for j in range(SLOTS * 8):
        ids_rows[j] = jnp.broadcast_to(turned[:, j:j + 1], (128, 128))

    pass_on(3)
    for half in range(2):
        relay_in(half).wait_recv()
        relay_out(half).start()
    swap(2, 1).wait_recv()
    own_piece_ready(5)
    @pl.loop(0, SLOTS * 8)
    def _(j):
        row_best[j] = jnp.full((128, 128), -1.0, jnp.float32)
        col_best[j] = jnp.full((8, 128), -1.0, jnp.float32)
    row_line[...] = jnp.full_like(row_line, -1.0)

    take(0)
    pass_on(4)
    for m in (0, 1):
        wait_shared(m, 0)
        own_pair(m)
    take(1)
    pass_on(5)
    for half in range(2):
        relay_out(half).wait_recv()
        own_piece_ready(6 + half)
    wait_shared(0, 1)
    wait_shared(0, 2)

    @pl.loop(0, pair_count)
    def _(j):
        compare(0, j)
    take(2)
    pass_on(6)
    for m in (2, 3):
        wait_shared(m, 0)
        own_pair(m)
    take(3)

    @pl.loop(0, 2)
    def _(k):
        pass_on(7 + k)

        @pl.when(k == 0)
        def _():
            wait_shared(1, 1)
            wait_shared(1, 2)

        @pl.loop(2 * k, jnp.minimum(2 * k + 2, pair_count))
        def _(j):
            compare(1, j)
        take(4 + k)
    finish_rows(0)

    for m in (2, 3):
        wait_shared(m, 1)

        @pl.loop(0, pair_count)
        def _(j):
            pl.when(j == early_count)(lambda: wait_shared(m, 2))
            compare(m, j)
        if m == 2:
            finish_rows(1)
            take(6)
            finish_rows(2)
            take(7)
    finish_rows(3)

    for s in range(SLOTS):
        for t in range(4):
            z_of = (z + REL[t]) % 4
            for core in range(2):
                j = s * 8 + 2 * t + core
                both = jnp.maximum(row_line[j:j + 1, :], jnp.max(col_best[j], axis=0, keepdims=True))
                part[s * 2 + z_of // 2, pl.ds(2 * (z_of % 2) + core, 1), :] = both
        for half in range(2):
            copy = remote(part.at[s * 2 + half], parts_got.at[place[s] * 2 + h], r_send.at[s * 2 + half],
                          r_recv.at[place[s] * 2 + h], (owner_grp, held[s] * 2 + half))
            if s == 0:
                keep_it = jnp.logical_and(mine, zh == half)
                pl.when(jnp.logical_not(keep_it))(copy.start)

                @pl.when(keep_it)
                def _():
                    parts_got[h] = part[half]
            else:
                copy.start()

    pl.when(jnp.logical_not(mine))(ids_copy.wait_send)
    for half in range(2):
        for copy in (swap(1, half), swap(2, half), relay_in(half), relay_out(half)):
            copy.wait_send()

    @pl.loop(0, STEPS)
    def _(t):
        for d in range(4):
            forward(d, t).wait_send()
        for s in range(SLOTS):
            pl.when(sibling_need[s] == 1)(lambda s=s: share(s, t).wait_send())

    best = None
    for k in range(2 * SLOTS):
        got = remote(parts_got.at[k], parts_got.at[k], r_send.at[k], r_recv.at[k], sibling)
        if k < 2:
            pl.when(jnp.logical_not(jnp.logical_and(mine, h == k)))(got.wait_recv)
        else:
            got.wait_recv()
        best = parts_got[k] if best is None else jnp.maximum(best, parts_got[k])
    out[...] = best

    for s in range(SLOTS):
        for half in range(2):
            copy = remote(part.at[s * 2 + half], parts_got.at[place[s] * 2 + h], r_send.at[s * 2 + half],
                          r_recv.at[place[s] * 2 + h], (owner_grp, held[s] * 2 + half))
            if s == 0:
                pl.when(jnp.logical_not(jnp.logical_and(mine, zh == half)))(copy.wait_send)
            else:
                copy.wait_send()


def on_device(embeddings, cluster_ids):
    emb = embeddings.reshape(4, 128, D)
    ids = cluster_ids.reshape(128, 128)
    dma = pltpu.SemaphoreType.DMA
    best = pl.pallas_call(
        kernel,
        out_shape=jax.ShapeDtypeStruct((4, 128), jnp.float32),
        in_specs=[pl.BlockSpec(memory_space=pl.ANY), pl.BlockSpec(memory_space=pl.ANY)],
        out_specs=pl.BlockSpec(memory_space=pltpu.VMEM),
        scratch_shapes=[
            pltpu.VMEM((SLOTS, 1024, D), jnp.bfloat16),
            pltpu.VMEM((3, 128, D), jnp.bfloat16),
            pltpu.VMEM((4, 128, D), jnp.float32),
            pltpu.VMEM((128, 128), jnp.int32),
            pltpu.VMEM((SLOTS * 8, 128, 128), jnp.float32),
            pltpu.VMEM((128, 128), jnp.float32),
            pltpu.VMEM((SLOTS * 8, 128, 128), jnp.float32),
            pltpu.VMEM((SLOTS * 8, 8, 128), jnp.float32),
            pltpu.VMEM((SLOTS * 8, 128), jnp.float32),
            pltpu.VMEM((2 * SLOTS, 4, 128), jnp.float32),
            pltpu.VMEM((2 * SLOTS, 4, 128), jnp.float32),
            pltpu.VMEM((128, D), jnp.bfloat16),
            dma((4,)), dma, dma, dma((3, 2)), dma((3, 2)), dma((2, 2)), dma((2,)), dma((4, STEPS)), dma((4, STEPS)),
            dma((SLOTS, 8)), dma((SLOTS, 8)), dma((2 * SLOTS,)), dma((2 * SLOTS,)),
        ],
        compiler_params=pltpu.CompilerParams(
            collective_id=0, has_side_effects=True, vmem_limit_bytes=55168 * 1024),
        cost_estimate=pl.CostEstimate(flops=7 * 10**9, bytes_accessed=2 * 10**6, transcendentals=0),
        name="best_match",
    )(emb, ids)
    return best.reshape(1, 512)


def solution(mesh):
    placed = (P(None, "grp", "blk", None, None), P("grp", None))
    return jax.shard_map(
        on_device, mesh=mesh, in_specs=placed, out_specs=P("grp", "blk"), check_vma=False
    )
```

```python
import functools

import jax
import jax.numpy as jnp
from jax import lax
from jax.experimental import pallas as pl
from jax.experimental.pallas import tpu as pltpu
from jax.sharding import PartitionSpec as P

MESH = pl.DeviceIdType.MESH
D = 768
SLOTS = 5
PIECE = 64
STEPS = 8

SRC = [[4, 0, 0, 2], [0, 4, 0, 1], [0, 0, 0, 2], [0, 0, 0, 1], [4, 0, 0, 2], [0, 4, 0, 1], [0, 0, 1, 2],
       [0, 0, 2, 1], [4, 0, 0, 0], [0, 4, 0, 0], [0, 1, 0, 3], [2, 0, 0, 3], [4, 0, 0, 0], [0, 4, 0, 0],
       [0, 0, 4, 0], [0, 0, 4, 0]]
DEP = [[2, 1, 2, 1], [1, 2, 2, 1], [1, 1, 2, 2], [1, 1, 2, 2], [2, 1, 1, 1], [1, 2, 1, 1], [1, 1, 2, 1],
       [1, 1, 2, 1], [2, 2, 1, 1], [2, 2, 1, 1], [1, 1, 1, 2], [1, 1, 1, 2], [2, 1, 2, 1], [1, 2, 2, 1],
       [1, 1, 2, 1], [1, 1, 2, 1]]
BLK = [[13, 3, 7, 12], [2, 12, 6, 13], [3, 1, 5, 10], [0, 2, 4, 11], [1, 7, 8, 0], [6, 0, 9, 1], [7, 5, 14, 2],
       [4, 6, 15, 3], [5, 10, 12, 4], [11, 4, 13, 5], [11, 9, 14, 7], [8, 10, 15, 6], [9, 15, 3, 8], [14, 8, 2, 9],
       [15, 13, 1, 10], [12, 14, 0, 11]]
IDX = [[1, 1, 1, 1], [1, 2, 1, 2], [2, 1, 1, 1], [1, 2, 1, 1], [2, 2, 1, 2], [2, 3, 1, 3], [3, 2, 1, 3],
       [2, 3, 1, 3], [3, 2, 3, 3], [2, 4, 3, 4], [3, 2, 2, 4], [2, 3, 2, 4], [3, 3, 4, 3], [3, 4, 4, 4],
       [4, 4, 4, 4], [4, 4, 4, 4]]
HOLD = [[0, 3, 4, 5, 15], [1, 2, 4, 5, 14], [2, 1, 3, 6, 13], [3, 0, 2, 7, 12], [4, 3, 7, 8, 9], [5, 2, 6, 8, 9],
        [6, 1, 5, 7, 11], [7, 0, 4, 6, 10], [8, 4, 11, 12, 13], [9, 5, 10, 12, 13], [10, 2, 8, 11, 14],
        [11, 3, 9, 10, 15], [12, 0, 1, 8, 15], [13, 0, 1, 9, 14], [14, 6, 10, 13, 15], [15, 7, 11, 12, 14]]
PAIRS = [[[(2, 4), (3, 4), (3, 1)], [(0, 2), (0, 3), (2, 3)]], [[(3, 2), (3, 4), (2, 4)], [(0, 1), (1, 3), (0, 3)]],
         [[(2, 1), (1, 3), (2, 3)], [(0, 4), (1, 4), (3, 4)]], [[(1, 2), (2, 3), (3, 4)], [(2, 0), (2, 4), (0, 4)]],
         [[(2, 3), (1, 2), (1, 3)], [(4, 3), (4, 0), (1, 0), (4, 1)]],
         [[(1, 3), (2, 1), (2, 3)], [(4, 3), (0, 3), (2, 0)]],
         [[(4, 1), (4, 2), (2, 3)], [(2, 1), (0, 1), (2, 0), (0, 3)]],
         [[(4, 2), (1, 2), (2, 3)], [(4, 1), (1, 0), (0, 3)]],
         [[(4, 3), (4, 2), (2, 3)], [(4, 0), (1, 0), (1, 3), (4, 1)]],
         [[(4, 3), (4, 1), (1, 3)], [(0, 3), (2, 0), (2, 3)]], [[(2, 1), (4, 2), (4, 1)], [(2, 0), (4, 0), (4, 3)]],
         [[(1, 0), (4, 1), (4, 0)], [(1, 2), (2, 0), (4, 2)]], [[(4, 2), (3, 4), (3, 1)], [(4, 0), (1, 0), (1, 2)]],
         [[(3, 2), (3, 4), (2, 4)], [(4, 1), (2, 0), (2, 1)]], [[(4, 2), (2, 1), (4, 1)], [(4, 0), (2, 0), (3, 4)]],
         [[(4, 1), (1, 2), (4, 2)], [(1, 0), (2, 0), (4, 0)]]]
EARLY = [[1, 1], [0, 1], [1, 0], [1, 1], [1, 2], [1, 2], [2, 3], [2, 2], [1, 1], [1, 1], [1, 1], [1, 2], [1, 1],
         [0, 1], [3, 2], [3, 3]]
NEED = [[[1, 2, 3, 4], [0, 2, 3]], [[2, 3, 4], [0, 1, 3]], [[1, 2, 3], [0, 1, 3, 4]], [[1, 2, 3, 4], [0, 2, 4]],
        [[1, 2, 3], [0, 1, 3, 4]], [[1, 2, 3], [0, 2, 3, 4]], [[1, 2, 3, 4], [0, 1, 2, 3]],
        [[1, 2, 3, 4], [0, 1, 3, 4]], [[2, 3, 4], [0, 1, 3, 4]], [[1, 3, 4], [0, 2, 3]], [[1, 2, 4], [0, 2, 3, 4]],
        [[0, 1, 4], [0, 1, 2, 4]], [[1, 2, 3, 4], [0, 1, 2, 4]], [[2, 3, 4], [0, 1, 2, 4]],
        [[1, 2, 4], [0, 2, 3, 4]], [[1, 2, 4], [0, 1, 2, 4]]]

REL = (0, 1, 3, 2)
LAST = 3


def word(digits, base):
    total = 0
    for digit in reversed(digits):
        total = total * base + digit
    return total


def look_up(index, words):
    got = jnp.int32(words[0])
    for k in range(1, len(words)):
        got = jnp.where(index == k, jnp.int32(words[k]), got)
    return got


def digits_of(value, base, count):
    out = []
    for _ in range(count):
        out.append(value % base)
        value = value // base
    return out


def pick(values, index):
    got = values[0]
    for k in range(1, len(values)):
        got = jnp.where(index == k, values[k], got)
    return got


def kernel(emb, ids_in, out, x, units, stage, ids_got, ids_rows, ids_cols, row_best, col_best, row_line, part, parts_got,
           relay,
           load_sem, id_send, id_recv, z_send, z_recv, relay_send, relay_recv, f_send, f_recv, c_send, c_recv, r_send, r_recv):
    grp, blk = lax.axis_index("grp"), lax.axis_index("blk")
    h, zl = grp % 2, grp // 2
    p, zh = blk // 2, blk % 2
    z = zh * 2 + zl
    px, py = p % 4, p // 4

    def device(z_of, core, chip):
        return ((z_of % 2) * 2 + core, chip * 2 + z_of // 2)

    def group_of(z_of):
        return (1 - z_of % 2) * 2 + z_of // 2

    near = [py * 4 + (px + 1) % 4, py * 4 + (px + 3) % 4, ((py + 1) % 4) * 4 + px, ((py + 3) % 4) * 4 + px]
    first = look_up(p, [word(SRC[c], 8) + 4096 * word(DEP[c], 4) for c in range(16)])
    src = digits_of(first, 8, 4)
    dep = digits_of(first // 4096, 4, 4)
    held = [p] + digits_of(look_up(p, [word(BLK[c], 16) for c in range(16)]), 16, 4)
    third = look_up(p, [word(IDX[c], 8) + 4096 * word(HOLD[c][1:], 16) for c in range(16)])
    place = [jnp.int32(0)] + digits_of(third, 8, 4)
    holders = [p] + digits_of(third // 4096, 16, 4)
    lists = []
    for c in range(16):
        for core in range(2):
            flat = [slot for pair in PAIRS[c][core] for slot in pair]
            lists.append(len(PAIRS[c][core]) + 8 * EARLY[c][core] + 64 * word(flat + [0] * (8 - len(flat)), 8))
    todo = look_up(p * 2 + h, lists)
    pair_count, early_count = todo % 8, todo // 8 % 8
    todo = digits_of(todo // 64, 8, 8)

    needs = [[sum(1 << slot for slot in NEED[c][core]) for core in range(2)] for c in range(16)]
    need = digits_of(look_up(p * 2 + h, [needs[c][core] for c in range(16) for core in range(2)]), 2, SLOTS)
    sibling_need = digits_of(look_up(p * 2 + h, [needs[c][1 - core] for c in range(16) for core in range(2)]), 2, SLOTS)

    sibling = device(z, 1 - h, p)
    owner_grp = group_of(z)
    from_z = 2 * h + 1 - zl
    ids_from = device(2 * h + 1 - zl, zh, p)

    rel = [jnp.where(z == LAST, REL[t] if t in (0, 3) else REL[3 - t], REL[t]) for t in range(4)]

    def load(k):
        return pltpu.make_async_copy(emb.at[group_of((z + pick((0, 3, 1, 2), k)) % 4)], stage.at[k], load_sem.at[k])

    for k in range(4):
        load(k).start()
    barrier = pltpu.get_barrier_semaphore()
    for step in (1, 3):
        pl.semaphore_signal(barrier, inc=1, device_id=device((z + step) % 4, h, p), device_id_type=MESH)
    for d in range(4):
        pl.semaphore_signal(barrier, inc=1, device_id=device(z, h, near[d]), device_id_type=MESH)
    pl.semaphore_signal(barrier, inc=1, device_id=sibling, device_id_type=MESH)
    pl.semaphore_signal(barrier, inc=1, device_id=ids_from, device_id_type=MESH)
    for k in range(SLOTS):
        for core in range(2):
            pl.semaphore_signal(barrier, inc=1, device_id=device(from_z, core, holders[k]), device_id_type=MESH)

    def normalised(k):
        v = stage[k]
        total = jnp.sum(v * v, axis=-1, keepdims=True)
        return (v / jnp.sqrt(total + 1e-06)).astype(jnp.bfloat16)

    load(0).wait()
    own_rows = pl.multiple_of(h * 128, 128)
    x[0, pl.ds(own_rows, 128), :] = normalised(0)
    pl.semaphore_wait(barrier, 18)

    def remote(src_ref, dst_ref, send_sem, recv_sem, to):
        return pltpu.make_async_remote_copy(
            src_ref=src_ref, dst_ref=dst_ref, send_sem=send_sem, recv_sem=recv_sem, device_id=to, device_id_type=MESH)

    def part_rows(t):
        return pl.ds(pl.multiple_of((t // 2) * 256 + h * 128 + (t % 2) * PIECE, PIECE), PIECE)

    def forward(d, t):
        rows = part_rows(t)
        return remote(x.at[src[d], rows, :], x.at[1 + (d ^ 1), rows, :], f_send.at[d, t], f_recv.at[d ^ 1, t],
                      device(z, h, near[d]))

    def arrival(s, t):
        rows = part_rows(t)
        return remote(x.at[s, rows, :], x.at[s, rows, :], f_send.at[s - 1, t], f_recv.at[s - 1, t],
                      device(z, h, near[s - 1]))

    def swap(k, half):
        z_to = (z + pick((3, 1), k - 1)) % 4
        t = jnp.where(z_to == LAST, 3 - k, k)
        rows = pl.ds(pl.multiple_of(t * 256 + h * 128 + half * 64, 64), 64)
        return remote(units.at[k - 1, pl.ds(half * 64, 64), :], x.at[0, rows, :], z_send.at[k - 1, half],
                      z_recv.at[t - 1, half], device(z_to, h, p))

    def swapped(t, half):
        rows = pl.ds(pl.multiple_of(t * 256 + h * 128 + half * 64, 64), 64)
        return remote(units.at[t - 1, pl.ds(half * 64, 64), :], x.at[0, rows, :], z_send.at[t - 1, half],
                      z_recv.at[t - 1, half], device((z + 1) % 4, h, p))

    between = device((z + jnp.where(h == 0, 1, 3)) % 4, h, p)

    def relay_in(half):
        rows = pl.ds(half * 64, 64)
        return remote(units.at[2, rows, :], relay.at[rows, :], relay_send.at[0, half], relay_recv.at[half], between)

    def relay_out(half):
        rows = pl.ds(pl.multiple_of(3 * 256 + h * 128 + half * 64, 64), 64)
        return remote(relay.at[pl.ds(half * 64, 64), :], x.at[0, rows, :], relay_send.at[1, half], z_recv.at[2, half],
                      between)

    def share_rows(t, core):
        return pl.ds(pl.multiple_of((t // 2) * 256 + core * 128 + (t % 2) * 64, 64), 64)

    def share(s, t):
        rows = share_rows(t, h)
        return remote(x.at[s, rows, :], x.at[s, rows, :], c_send.at[s, t], c_recv.at[s, t], sibling)

    def shared(s, t):
        rows = share_rows(t, 1 - h)
        return remote(x.at[s, rows, :], x.at[s, rows, :], c_send.at[s, t], c_recv.at[s, t], sibling)

    def give(s, t):
        pl.when(sibling_need[s] == 1)(lambda: share(s, t).start())

    def send_own(t):
        for d in range(4):
            pl.when(src[d] == 0)(lambda d=d: forward(d, t).start())

    def send_held(t):
        for d in range(4):
            pl.when(src[d] != 0)(lambda d=d: forward(d, t).start())

    def receive(links, t):
        for s in range(1, SLOTS):
            pl.when(dep[s - 1] == links)(lambda s=s: arrival(s, t).wait_recv())

    def give_held(links, t):
        for s in range(1, SLOTS):
            pl.when(dep[s - 1] == links)(lambda s=s: give(s, t))

    for t in range(2):
        send_own(t)
    @pl.loop(1, 4)
    def _(k):
        load(k).wait()
        units[k - 1] = normalised(k)
        for half in range(2):
            pl.when(k < 3)(lambda half=half: swap(k, half).start())
            pl.when(k == 3)(lambda half=half: relay_in(half).start())

    ids_copy = remote(ids_in, ids_got, id_send, id_recv, device(from_z, zh, p))
    ids_copy.start()
    give(0, 0)
    give(0, 1)
    def strip(a, t, b, count, diagonal=False):
        sim = lax.dot_general(x[a, 256 * t:256 * t + 256, :], x[b, 0:256 * count, :], (((1,), (1,)), ((), ())),
                              preferred_element_type=jnp.float32)
        for r in range(4):
            unit, first_row = a * 8 + 2 * t + r // 2, 64 * (r % 2)
            row_ids = ids_rows[unit, first_row:first_row + 64]
            best = row_best[unit, first_row:first_row + 64]
            for c in range(2 * count):
                keep = row_ids == ids_cols[pl.ds(b * 8 + c, 1), :]
                if diagonal and c // 2 == t:
                    row = lax.broadcasted_iota(jnp.int32, (64, 128), 0) + 64 * r
                    col = lax.broadcasted_iota(jnp.int32, (64, 128), 1) + 128 * (c % 2)
                    keep = jnp.logical_and(keep, row != col)
                kept = jnp.where(keep, sim[64 * r:64 * r + 64, 128 * c:128 * c + 128], jnp.float32(-1.0))
                down = jnp.max(kept.reshape(8, 8, 128), axis=0)
                col_best[b * 8 + c] = jnp.maximum(col_best[b * 8 + c], down)
                best = jnp.maximum(best, kept)
            row_best[unit, first_row:first_row + 64] = best

    def compare(t, j):
        a, b = todo[0], todo[1]
        for k in range(1, 4):
            a = jnp.where(j == k, todo[2 * k], a)
            b = jnp.where(j == k, todo[2 * k + 1], b)
        strip(a, t, b, t + 1)
        if t:
            strip(b, t, a, t)

    def own_pair(t):
        pl.when(h == 1)(lambda: strip(0, t, 0, t + 1, diagonal=True))

    def finish_rows(t):
        for s in range(SLOTS):
            @pl.when(need[s] == 1)
            def _():
                for core in range(2):
                    unit = s * 8 + 2 * t + core
                    row_line[unit:unit + 1, :] = jnp.max(row_best[unit].T, axis=0, keepdims=True)

    def wait_shared(m, links):
        for s in range(SLOTS):
            there = need[s] == 1
            if s == 0:
                if links:
                    continue
            elif links:
                there = jnp.logical_and(there, dep[s - 1] == links)
            else:
                continue

            @pl.when(there)
            def _():
                for half in range(2):
                    shared(s, 2 * m + half).wait_recv()

    def own_piece_ready(t):
        send_own(t)
        give(0, t)

    def pass_on(k):
        receive(1, k - 1)
        send_held(k - 1)
        give_held(1, k - 1)

    def take(t):
        receive(2, t)
        give_held(2, t)

    pass_on(1)
    swapped(1, 0).wait_recv()
    own_piece_ready(2)
    pass_on(2)
    swapped(1, 1).wait_recv()
    own_piece_ready(3)
    swapped(2, 0).wait_recv()
    own_piece_ready(4)

    ids_copy.wait_recv()
    ids_cols[...] = jnp.zeros_like(ids_cols)
    for s in range(SLOTS):
        for t in range(4):
            for core in range(2):
                unit = held[s] * 8 + 2 * ((z + rel[t]) % 4) + core
                ids_cols[pl.ds(s * 8 + 2 * t + core, 1), :] = ids_got[pl.ds(unit, 1), :].astype(jnp.float32)
    turned = ids_cols[...].T
    for j in range(SLOTS * 8):
        ids_rows[j] = jnp.broadcast_to(turned[:, j:j + 1], (128, 128))

    pass_on(3)
    for half in range(2):
        relay_in(half).wait_recv()
        relay_out(half).start()
    swapped(2, 1).wait_recv()
    own_piece_ready(5)
    @pl.loop(0, SLOTS * 8)
    def _(j):
        row_best[j] = jnp.full((128, 128), -1.0, jnp.float32)
        col_best[j] = jnp.full((8, 128), -1.0, jnp.float32)
    row_line[...] = jnp.full_like(row_line, -1.0)

    take(0)
    pass_on(4)
    for m in (0, 1):
        wait_shared(m, 0)
        own_pair(m)
    take(1)
    pass_on(5)
    for half in range(2):
        relay_out(half).wait_recv()
        own_piece_ready(6 + half)
    wait_shared(0, 1)
    wait_shared(0, 2)

    @pl.loop(0, pair_count)
    def _(j):
        compare(0, j)
    take(2)
    pass_on(6)
    for m in (2, 3):
        wait_shared(m, 0)
        own_pair(m)
    take(3)

    @pl.loop(0, 2)
    def _(k):
        pass_on(7 + k)

        @pl.when(k == 0)
        def _():
            wait_shared(1, 1)
            wait_shared(1, 2)

        @pl.loop(2 * k, jnp.minimum(2 * k + 2, pair_count))
        def _(j):
            compare(1, j)
        take(4 + k)
    finish_rows(0)

    for m in (2, 3):
        wait_shared(m, 1)

        @pl.loop(0, pair_count)
        def _(j):
            pl.when(j == early_count)(lambda: wait_shared(m, 2))
            compare(m, j)
        if m == 2:
            finish_rows(1)
            take(6)
            finish_rows(2)
            take(7)
    finish_rows(3)

    for s in range(SLOTS):
        for t in range(4):
            z_of = (z + rel[t]) % 4
            for core in range(2):
                j = s * 8 + 2 * t + core
                both = jnp.maximum(row_line[j:j + 1, :], jnp.max(col_best[j], axis=0, keepdims=True))
                part[s * 2 + z_of // 2, pl.ds(2 * (z_of % 2) + core, 1), :] = both
        for half in range(2):
            copy = remote(part.at[s * 2 + half], parts_got.at[place[s] * 2 + h], r_send.at[s * 2 + half],
                          r_recv.at[place[s] * 2 + h], (owner_grp, held[s] * 2 + half))
            copy.start()

    ids_copy.wait_send()
    for half in range(2):
        for copy in (swap(1, half), swap(2, half), relay_in(half), relay_out(half)):
            copy.wait_send()

    @pl.loop(0, STEPS)
    def _(t):
        for d in range(4):
            forward(d, t).wait_send()
        for s in range(SLOTS):
            pl.when(sibling_need[s] == 1)(lambda s=s: share(s, t).wait_send())

    best = None
    for k in range(2 * SLOTS):
        got = remote(parts_got.at[k], parts_got.at[k], r_send.at[k], r_recv.at[k], sibling)
        got.wait_recv()
        best = parts_got[k] if best is None else jnp.maximum(best, parts_got[k])
    out[...] = best

    for s in range(SLOTS):
        for half in range(2):
            copy = remote(part.at[s * 2 + half], parts_got.at[place[s] * 2 + h], r_send.at[s * 2 + half],
                          r_recv.at[place[s] * 2 + h], (owner_grp, held[s] * 2 + half))
            copy.wait_send()


def on_device(embeddings, cluster_ids):
    emb = embeddings.reshape(4, 128, D)
    ids = cluster_ids.reshape(128, 128)
    dma = pltpu.SemaphoreType.DMA
    best = pl.pallas_call(
        kernel,
        out_shape=jax.ShapeDtypeStruct((4, 128), jnp.float32),
        in_specs=[pl.BlockSpec(memory_space=pl.ANY), pl.BlockSpec(memory_space=pl.ANY)],
        out_specs=pl.BlockSpec(memory_space=pltpu.VMEM),
        scratch_shapes=[
            pltpu.VMEM((SLOTS, 1024, D), jnp.bfloat16),
            pltpu.VMEM((3, 128, D), jnp.bfloat16),
            pltpu.VMEM((4, 128, D), jnp.float32),
            pltpu.VMEM((128, 128), jnp.int32),
            pltpu.VMEM((SLOTS * 8, 128, 128), jnp.float32),
            pltpu.VMEM((128, 128), jnp.float32),
            pltpu.VMEM((SLOTS * 8, 128, 128), jnp.float32),
            pltpu.VMEM((SLOTS * 8, 8, 128), jnp.float32),
            pltpu.VMEM((SLOTS * 8, 128), jnp.float32),
            pltpu.VMEM((2 * SLOTS, 4, 128), jnp.float32),
            pltpu.VMEM((2 * SLOTS, 4, 128), jnp.float32),
            pltpu.VMEM((128, D), jnp.bfloat16),
            dma((4,)), dma, dma, dma((3, 2)), dma((3, 2)), dma((2, 2)), dma((2,)), dma((4, STEPS)), dma((4, STEPS)),
            dma((SLOTS, 8)), dma((SLOTS, 8)), dma((2 * SLOTS,)), dma((2 * SLOTS,)),
        ],
        compiler_params=pltpu.CompilerParams(
            collective_id=0, has_side_effects=True, vmem_limit_bytes=55168 * 1024),
        cost_estimate=pl.CostEstimate(flops=7 * 10**9, bytes_accessed=2 * 10**6, transcendentals=0),
        name="best_match",
    )(emb, ids)
    return best.reshape(1, 512)


def solution(mesh):
    placed = (P(None, "grp", "blk", None, None), P("grp", None))
    return jax.shard_map(
        on_device, mesh=mesh, in_specs=placed, out_specs=P("grp", "blk"), check_vma=False
    )
```

```python
import functools

import jax
import jax.numpy as jnp
from jax import lax
from jax.experimental import pallas as pl
from jax.experimental.pallas import tpu as pltpu
from jax.sharding import PartitionSpec as P

MESH = pl.DeviceIdType.MESH
D = 768
SLOTS = 5
PIECE = 64
STEPS = 8

SRC = [[4, 0, 0, 2], [0, 4, 0, 1], [0, 0, 0, 2], [0, 0, 0, 1], [4, 0, 0, 2], [0, 4, 0, 1], [0, 0, 1, 2],
       [0, 0, 2, 1], [4, 0, 0, 0], [0, 4, 0, 0], [0, 1, 0, 3], [2, 0, 0, 3], [4, 0, 0, 0], [0, 4, 0, 0],
       [0, 0, 4, 0], [0, 0, 4, 0]]
DEP = [[2, 1, 2, 1], [1, 2, 2, 1], [1, 1, 2, 2], [1, 1, 2, 2], [2, 1, 1, 1], [1, 2, 1, 1], [1, 1, 2, 1],
       [1, 1, 2, 1], [2, 2, 1, 1], [2, 2, 1, 1], [1, 1, 1, 2], [1, 1, 1, 2], [2, 1, 2, 1], [1, 2, 2, 1],
       [1, 1, 2, 1], [1, 1, 2, 1]]
BLK = [[13, 3, 7, 12], [2, 12, 6, 13], [3, 1, 5, 10], [0, 2, 4, 11], [1, 7, 8, 0], [6, 0, 9, 1], [7, 5, 14, 2],
       [4, 6, 15, 3], [5, 10, 12, 4], [11, 4, 13, 5], [11, 9, 14, 7], [8, 10, 15, 6], [9, 15, 3, 8], [14, 8, 2, 9],
       [15, 13, 1, 10], [12, 14, 0, 11]]
IDX = [[1, 1, 1, 1], [1, 2, 1, 2], [2, 1, 1, 1], [1, 2, 1, 1], [2, 2, 1, 2], [2, 3, 1, 3], [3, 2, 1, 3],
       [2, 3, 1, 3], [3, 2, 3, 3], [2, 4, 3, 4], [3, 2, 2, 4], [2, 3, 2, 4], [3, 3, 4, 3], [3, 4, 4, 4],
       [4, 4, 4, 4], [4, 4, 4, 4]]
HOLD = [[0, 3, 4, 5, 15], [1, 2, 4, 5, 14], [2, 1, 3, 6, 13], [3, 0, 2, 7, 12], [4, 3, 7, 8, 9], [5, 2, 6, 8, 9],
        [6, 1, 5, 7, 11], [7, 0, 4, 6, 10], [8, 4, 11, 12, 13], [9, 5, 10, 12, 13], [10, 2, 8, 11, 14],
        [11, 3, 9, 10, 15], [12, 0, 1, 8, 15], [13, 0, 1, 9, 14], [14, 6, 10, 13, 15], [15, 7, 11, 12, 14]]
PAIRS = [[[(2, 4), (3, 4), (3, 1)], [(0, 2), (0, 3), (2, 3)]], [[(3, 2), (3, 4), (2, 4)], [(0, 1), (1, 3), (0, 3)]],
         [[(2, 1), (1, 3), (2, 3)], [(0, 4), (1, 4), (3, 4)]], [[(1, 2), (2, 3), (3, 4)], [(2, 0), (2, 4), (0, 4)]],
         [[(2, 3), (1, 2), (1, 3)], [(4, 3), (4, 0), (1, 0), (4, 1)]],
         [[(1, 3), (2, 1), (2, 3)], [(4, 3), (0, 3), (2, 0)]],
         [[(4, 1), (4, 2), (2, 3)], [(2, 1), (0, 1), (2, 0), (0, 3)]],
         [[(4, 2), (1, 2), (2, 3)], [(4, 1), (1, 0), (0, 3)]],
         [[(4, 3), (4, 2), (2, 3)], [(4, 0), (1, 0), (1, 3), (4, 1)]],
         [[(4, 3), (4, 1), (1, 3)], [(0, 3), (2, 0), (2, 3)]], [[(2, 1), (4, 2), (4, 1)], [(2, 0), (4, 0), (4, 3)]],
         [[(1, 0), (4, 1), (4, 0)], [(1, 2), (2, 0), (4, 2)]], [[(4, 2), (3, 4), (3, 1)], [(4, 0), (1, 0), (1, 2)]],
         [[(3, 2), (3, 4), (2, 4)], [(4, 1), (2, 0), (2, 1)]], [[(4, 2), (2, 1), (4, 1)], [(4, 0), (2, 0), (3, 4)]],
         [[(4, 1), (1, 2), (4, 2)], [(1, 0), (2, 0), (4, 0)]]]
EARLY = [[1, 1], [0, 1], [1, 0], [1, 1], [1, 2], [1, 2], [2, 3], [2, 2], [1, 1], [1, 1], [1, 1], [1, 2], [1, 1],
         [0, 1], [3, 2], [3, 3]]
NEED = [[[1, 2, 3, 4], [0, 2, 3]], [[2, 3, 4], [0, 1, 3]], [[1, 2, 3], [0, 1, 3, 4]], [[1, 2, 3, 4], [0, 2, 4]],
        [[1, 2, 3], [0, 1, 3, 4]], [[1, 2, 3], [0, 2, 3, 4]], [[1, 2, 3, 4], [0, 1, 2, 3]],
        [[1, 2, 3, 4], [0, 1, 3, 4]], [[2, 3, 4], [0, 1, 3, 4]], [[1, 3, 4], [0, 2, 3]], [[1, 2, 4], [0, 2, 3, 4]],
        [[0, 1, 4], [0, 1, 2, 4]], [[1, 2, 3, 4], [0, 1, 2, 4]], [[2, 3, 4], [0, 1, 2, 4]],
        [[1, 2, 4], [0, 2, 3, 4]], [[1, 2, 4], [0, 1, 2, 4]]]

REL = (0, 1, 3, 2)
LAST = 3


def word(digits, base):
    total = 0
    for digit in reversed(digits):
        total = total * base + digit
    return total


def look_up(index, words):
    got = jnp.int32(words[0])
    for k in range(1, len(words)):
        got = jnp.where(index == k, jnp.int32(words[k]), got)
    return got


def digits_of(value, base, count):
    out = []
    for _ in range(count):
        out.append(value % base)
        value = value // base
    return out


def pick(values, index):
    got = values[0]
    for k in range(1, len(values)):
        got = jnp.where(index == k, values[k], got)
    return got


def kernel(emb, ids_in, out, x, units, stage, ids_got, ids_rows, ids_cols, row_best, col_best, row_line, part, parts_got,
           relay,
           load_sem, id_send, id_recv, z_send, z_recv, relay_send, relay_recv, f_send, f_recv, c_send, c_recv, r_send, r_recv):
    grp, blk = lax.axis_index("grp"), lax.axis_index("blk")
    h, zl = grp % 2, grp // 2
    p, zh = blk // 2, blk % 2
    z = zh * 2 + zl
    px, py = p % 4, p // 4

    def device(z_of, core, chip):
        return ((z_of % 2) * 2 + core, chip * 2 + z_of // 2)

    def group_of(z_of):
        return (1 - z_of % 2) * 2 + z_of // 2

    near = [py * 4 + (px + 1) % 4, py * 4 + (px + 3) % 4, ((py + 1) % 4) * 4 + px, ((py + 3) % 4) * 4 + px]
    first = look_up(p, [word(SRC[c], 8) + 4096 * word(DEP[c], 4) for c in range(16)])
    src = digits_of(first, 8, 4)
    dep = digits_of(first // 4096, 4, 4)
    held = [p] + digits_of(look_up(p, [word(BLK[c], 16) for c in range(16)]), 16, 4)
    third = look_up(p, [word(IDX[c], 8) + 4096 * word(HOLD[c][1:], 16) for c in range(16)])
    place = [jnp.int32(0)] + digits_of(third, 8, 4)
    holders = [p] + digits_of(third // 4096, 16, 4)
    lists = []
    for c in range(16):
        for core in range(2):
            flat = [slot for pair in PAIRS[c][core] for slot in pair]
            lists.append(len(PAIRS[c][core]) + 8 * EARLY[c][core] + 64 * word(flat + [0] * (8 - len(flat)), 8))
    todo = look_up(p * 2 + h, lists)
    pair_count, early_count = todo % 8, todo // 8 % 8
    todo = digits_of(todo // 64, 8, 8)

    needs = [[sum(1 << slot for slot in NEED[c][core]) for core in range(2)] for c in range(16)]
    need = digits_of(look_up(p * 2 + h, [needs[c][core] for c in range(16) for core in range(2)]), 2, SLOTS)
    sibling_need = digits_of(look_up(p * 2 + h, [needs[c][1 - core] for c in range(16) for core in range(2)]), 2, SLOTS)

    sibling = device(z, 1 - h, p)
    owner_grp = group_of(z)
    from_z = 2 * h + 1 - zl
    ids_from = device(2 * h + 1 - zl, zh, p)

    rel = [jnp.where(z == LAST, REL[t] if t in (0, 3) else REL[3 - t], REL[t]) for t in range(4)]

    def load(k):
        return pltpu.make_async_copy(emb.at[group_of((z + pick((0, 3, 1, 2), k)) % 4)], stage.at[k], load_sem.at[k])

    for k in range(4):
        load(k).start()
    barrier = pltpu.get_barrier_semaphore()
    for step in (1, 3):
        pl.semaphore_signal(barrier, inc=1, device_id=device((z + step) % 4, h, p), device_id_type=MESH)
    for d in range(4):
        pl.semaphore_signal(barrier, inc=1, device_id=device(z, h, near[d]), device_id_type=MESH)
    pl.semaphore_signal(barrier, inc=1, device_id=sibling, device_id_type=MESH)
    pl.semaphore_signal(barrier, inc=1, device_id=ids_from, device_id_type=MESH)
    for k in range(SLOTS):
        for core in range(2):
            pl.semaphore_signal(barrier, inc=1, device_id=device(from_z, core, holders[k]), device_id_type=MESH)

    def normalised(k):
        v = stage[k]
        total = jnp.sum(v * v, axis=-1, keepdims=True)
        return (v / jnp.sqrt(total + 1e-06)).astype(jnp.bfloat16)

    load(0).wait()
    own_rows = pl.multiple_of(h * 128, 128)
    x[0, pl.ds(own_rows, 128), :] = normalised(0)
    pl.semaphore_wait(barrier, 18)

    def remote(src_ref, dst_ref, send_sem, recv_sem, to):
        return pltpu.make_async_remote_copy(
            src_ref=src_ref, dst_ref=dst_ref, send_sem=send_sem, recv_sem=recv_sem, device_id=to, device_id_type=MESH)

    def part_rows(t):
        return pl.ds(pl.multiple_of((t // 2) * 256 + h * 128 + (t % 2) * PIECE, PIECE), PIECE)

    def forward(d, t):
        rows = part_rows(t)
        return remote(x.at[src[d], rows, :], x.at[1 + (d ^ 1), rows, :], f_send.at[d, t], f_recv.at[d ^ 1, t],
                      device(z, h, near[d]))

    def arrival(s, t):
        rows = part_rows(t)
        return remote(x.at[s, rows, :], x.at[s, rows, :], f_send.at[s - 1, t], f_recv.at[s - 1, t],
                      device(z, h, near[s - 1]))

    def swap(k, half):
        z_to = (z + pick((3, 1), k - 1)) % 4
        t = jnp.where(z_to == LAST, 3 - k, k)
        rows = pl.ds(pl.multiple_of(t * 256 + h * 128 + half * 64, 64), 64)
        return remote(units.at[k - 1, pl.ds(half * 64, 64), :], x.at[0, rows, :], z_send.at[k - 1, half],
                      z_recv.at[t - 1, half], device(z_to, h, p))

    def swapped(t, half):
        rows = pl.ds(pl.multiple_of(t * 256 + h * 128 + half * 64, 64), 64)
        return remote(units.at[t - 1, pl.ds(half * 64, 64), :], x.at[0, rows, :], z_send.at[t - 1, half],
                      z_recv.at[t - 1, half], device((z + 1) % 4, h, p))

    between = device((z + jnp.where(h == 0, 1, 3)) % 4, h, p)

    def relay_in(half):
        rows = pl.ds(half * 64, 64)
        return remote(units.at[2, rows, :], relay.at[rows, :], relay_send.at[0, half], relay_recv.at[half], between)

    def relay_out(half):
        rows = pl.ds(pl.multiple_of(3 * 256 + h * 128 + half * 64, 64), 64)
        return remote(relay.at[pl.ds(half * 64, 64), :], x.at[0, rows, :], relay_send.at[1, half], z_recv.at[2, half],
                      between)

    def share_rows(t, core):
        return pl.ds(pl.multiple_of((t // 2) * 256 + core * 128 + (t % 2) * 64, 64), 64)

    def share(s, t):
        rows = share_rows(t, h)
        return remote(x.at[s, rows, :], x.at[s, rows, :], c_send.at[s, t], c_recv.at[s, t], sibling)

    def shared(s, t):
        rows = share_rows(t, 1 - h)
        return remote(x.at[s, rows, :], x.at[s, rows, :], c_send.at[s, t], c_recv.at[s, t], sibling)

    def give(s, t):
        pl.when(sibling_need[s] == 1)(lambda: share(s, t).start())

    def send_own(t):
        for d in range(4):
            pl.when(src[d] == 0)(lambda d=d: forward(d, t).start())

    def send_held(t):
        for d in range(4):
            pl.when(src[d] != 0)(lambda d=d: forward(d, t).start())

    def receive(links, t):
        for s in range(1, SLOTS):
            pl.when(dep[s - 1] == links)(lambda s=s: arrival(s, t).wait_recv())

    def give_held(links, t):
        for s in range(1, SLOTS):
            pl.when(dep[s - 1] == links)(lambda s=s: give(s, t))

    for t in range(2):
        send_own(t)
    @pl.loop(1, 4)
    def _(k):
        load(k).wait()
        units[k - 1] = normalised(k)
        for half in range(2):
            pl.when(k < 3)(lambda half=half: swap(k, half).start())
            pl.when(k == 3)(lambda half=half: relay_in(half).start())

    ids_copy = remote(ids_in, ids_got, id_send, id_recv, device(from_z, zh, p))
    ids_copy.start()
    give(0, 0)
    give(0, 1)
    def strip(a, t, b, count, diagonal=False):
        sim = lax.dot_general(x[a, 256 * t:256 * t + 256, :], x[b, 0:256 * count, :], (((1,), (1,)), ((), ())),
                              preferred_element_type=jnp.float32)
        for r in range(4):
            unit, first_row = a * 8 + 2 * t + r // 2, 64 * (r % 2)
            row_ids = ids_rows[unit, first_row:first_row + 64]
            best = row_best[unit, first_row:first_row + 64]
            for c in range(2 * count):
                keep = row_ids == ids_cols[pl.ds(b * 8 + c, 1), :]
                if diagonal and c // 2 == t:
                    row = lax.broadcasted_iota(jnp.int32, (64, 128), 0) + 64 * r
                    col = lax.broadcasted_iota(jnp.int32, (64, 128), 1) + 128 * (c % 2)
                    keep = jnp.logical_and(keep, row != col)
                kept = jnp.where(keep, sim[64 * r:64 * r + 64, 128 * c:128 * c + 128], jnp.float32(-1.0))
                down = jnp.max(kept.reshape(8, 8, 128), axis=0)
                col_best[b * 8 + c] = jnp.maximum(col_best[b * 8 + c], down)
                best = jnp.maximum(best, kept)
            row_best[unit, first_row:first_row + 64] = best

    def compare(t, j):
        a, b = todo[0], todo[1]
        for k in range(1, 4):
            a = jnp.where(j == k, todo[2 * k], a)
            b = jnp.where(j == k, todo[2 * k + 1], b)
        strip(a, t, b, t + 1)
        if t:
            strip(b, t, a, t)

    def own_pair(t):
        pl.when(h == 1)(lambda: strip(0, t, 0, t + 1, diagonal=True))

    def finish_rows(t):
        for s in range(SLOTS):
            @pl.when(need[s] == 1)
            def _():
                for core in range(2):
                    unit = s * 8 + 2 * t + core
                    row_line[unit:unit + 1, :] = jnp.max(row_best[unit].T, axis=0, keepdims=True)

    def wait_shared(m, links):
        for s in range(SLOTS):
            there = need[s] == 1
            if s == 0:
                if links:
                    continue
            elif links:
                there = jnp.logical_and(there, dep[s - 1] == links)
            else:
                continue

            @pl.when(there)
            def _():
                for half in range(2):
                    shared(s, 2 * m + half).wait_recv()

    def own_piece_ready(t):
        send_own(t)
        give(0, t)

    def pass_on(k):
        receive(1, k - 1)
        send_held(k - 1)
        give_held(1, k - 1)

    def take(t):
        receive(2, t)
        give_held(2, t)

    pass_on(1)
    swapped(1, 0).wait_recv()
    own_piece_ready(2)
    pass_on(2)
    swapped(1, 1).wait_recv()
    own_piece_ready(3)
    swapped(2, 0).wait_recv()
    own_piece_ready(4)

    ids_copy.wait_recv()
    ids_cols[...] = jnp.zeros_like(ids_cols)
    for s in range(SLOTS):
        for t in range(4):
            for core in range(2):
                unit = held[s] * 8 + 2 * ((z + rel[t]) % 4) + core
                ids_cols[pl.ds(s * 8 + 2 * t + core, 1), :] = ids_got[pl.ds(unit, 1), :].astype(jnp.float32)
    turned = ids_cols[...].T
    for j in range(SLOTS * 8):
        ids_rows[j] = jnp.broadcast_to(turned[:, j:j + 1], (128, 128))

    pass_on(3)
    for half in range(2):
        relay_in(half).wait_recv()
        relay_out(half).start()
    swapped(2, 1).wait_recv()
    own_piece_ready(5)
    @pl.loop(0, SLOTS * 8)
    def _(j):
        row_best[j] = jnp.full((128, 128), -1.0, jnp.float32)
        col_best[j] = jnp.full((8, 128), -1.0, jnp.float32)
    row_line[...] = jnp.full_like(row_line, -1.0)

    take(0)
    pass_on(4)
    for m in (0, 1):
        wait_shared(m, 0)
        own_pair(m)
    take(1)
    pass_on(5)
    for half in range(2):
        relay_out(half).wait_recv()
        own_piece_ready(6 + half)
    wait_shared(0, 1)
    wait_shared(0, 2)

    @pl.loop(0, pair_count)
    def _(j):
        compare(0, j)
    take(2)
    pass_on(6)
    for m in (2, 3):
        wait_shared(m, 0)
        own_pair(m)
    take(3)

    @pl.loop(0, 2)
    def _(k):
        pass_on(7 + k)

        @pl.when(k == 0)
        def _():
            wait_shared(1, 1)
            wait_shared(1, 2)

        @pl.loop(2 * k, jnp.minimum(2 * k + 2, pair_count))
        def _(j):
            compare(1, j)
        take(4 + k)
    finish_rows(0)

    for m in (2, 3):
        wait_shared(m, 1)

        @pl.loop(0, pair_count)
        def _(j):
            pl.when(j == early_count)(lambda: wait_shared(m, 2))
            compare(m, j)
        if m == 2:
            finish_rows(1)
            take(6)
            finish_rows(2)
            take(7)
    for s in range(SLOTS):
        for core in range(2):
            unit = s * 8 + 6 + core
            row_line[unit:unit + 1, :] = jnp.max(row_best[unit].T, axis=0, keepdims=True)

    for s in (1, 2, 3, 4, 0):
        for t in range(4):
            z_of = (z + rel[t]) % 4
            for core in range(2):
                j = s * 8 + 2 * t + core
                both = jnp.maximum(row_line[j:j + 1, :], jnp.max(col_best[j], axis=0, keepdims=True))
                part[s * 2 + z_of // 2, pl.ds(2 * (z_of % 2) + core, 1), :] = both
        for half in range(2):
            copy = remote(part.at[s * 2 + half], parts_got.at[place[s] * 2 + h], r_send.at[s * 2 + half],
                          r_recv.at[place[s] * 2 + h], (owner_grp, held[s] * 2 + half))
            copy.start()

    ids_copy.wait_send()
    for half in range(2):
        for copy in (swap(1, half), swap(2, half), relay_in(half), relay_out(half)):
            copy.wait_send()

    @pl.loop(0, STEPS)
    def _(t):
        for d in range(4):
            forward(d, t).wait_send()
        for s in range(SLOTS):
            pl.when(sibling_need[s] == 1)(lambda s=s: share(s, t).wait_send())

    best = None
    for k in range(2 * SLOTS):
        got = remote(parts_got.at[k], parts_got.at[k], r_send.at[k], r_recv.at[k], sibling)
        got.wait_recv()
        best = parts_got[k] if best is None else jnp.maximum(best, parts_got[k])
    out[...] = best

    for s in range(SLOTS):
        for half in range(2):
            copy = remote(part.at[s * 2 + half], parts_got.at[place[s] * 2 + h], r_send.at[s * 2 + half],
                          r_recv.at[place[s] * 2 + h], (owner_grp, held[s] * 2 + half))
            copy.wait_send()


def on_device(embeddings, cluster_ids):
    emb = embeddings.reshape(4, 128, D)
    ids = cluster_ids.reshape(128, 128)
    dma = pltpu.SemaphoreType.DMA
    best = pl.pallas_call(
        kernel,
        out_shape=jax.ShapeDtypeStruct((4, 128), jnp.float32),
        in_specs=[pl.BlockSpec(memory_space=pl.ANY), pl.BlockSpec(memory_space=pl.ANY)],
        out_specs=pl.BlockSpec(memory_space=pltpu.VMEM),
        scratch_shapes=[
            pltpu.VMEM((SLOTS, 1024, D), jnp.bfloat16),
            pltpu.VMEM((3, 128, D), jnp.bfloat16),
            pltpu.VMEM((4, 128, D), jnp.float32),
            pltpu.VMEM((128, 128), jnp.int32),
            pltpu.VMEM((SLOTS * 8, 128, 128), jnp.float32),
            pltpu.VMEM((128, 128), jnp.float32),
            pltpu.VMEM((SLOTS * 8, 128, 128), jnp.float32),
            pltpu.VMEM((SLOTS * 8, 8, 128), jnp.float32),
            pltpu.VMEM((SLOTS * 8, 128), jnp.float32),
            pltpu.VMEM((2 * SLOTS, 4, 128), jnp.float32),
            pltpu.VMEM((2 * SLOTS, 4, 128), jnp.float32),
            pltpu.VMEM((128, D), jnp.bfloat16),
            dma((4,)), dma, dma, dma((3, 2)), dma((3, 2)), dma((2, 2)), dma((2,)), dma((4, STEPS)), dma((4, STEPS)),
            dma((SLOTS, 8)), dma((SLOTS, 8)), dma((2 * SLOTS,)), dma((2 * SLOTS,)),
        ],
        compiler_params=pltpu.CompilerParams(
            collective_id=0, has_side_effects=True, vmem_limit_bytes=55168 * 1024),
        cost_estimate=pl.CostEstimate(flops=7 * 10**9, bytes_accessed=2 * 10**6, transcendentals=0),
        name="best_match",
    )(emb, ids)
    return best.reshape(1, 512)


def solution(mesh):
    placed = (P(None, "grp", "blk", None, None), P("grp", None))
    return jax.shard_map(
        on_device, mesh=mesh, in_specs=placed, out_specs=P("grp", "blk"), check_vma=False
    )
```

```python
import functools

import jax
import jax.numpy as jnp
from jax import lax
from jax.experimental import pallas as pl
from jax.experimental.pallas import tpu as pltpu
from jax.sharding import PartitionSpec as P

MESH = pl.DeviceIdType.MESH
D = 768
SLOTS = 5
PIECE = 64
STEPS = 8

SRC = [[4, 0, 0, 2], [0, 4, 0, 1], [0, 0, 0, 2], [0, 0, 0, 1], [4, 0, 0, 2], [0, 4, 0, 1], [0, 0, 1, 2],
       [0, 0, 2, 1], [4, 0, 0, 0], [0, 4, 0, 0], [0, 1, 0, 3], [2, 0, 0, 3], [4, 0, 0, 0], [0, 4, 0, 0],
       [0, 0, 4, 0], [0, 0, 4, 0]]
DEP = [[2, 1, 2, 1], [1, 2, 2, 1], [1, 1, 2, 2], [1, 1, 2, 2], [2, 1, 1, 1], [1, 2, 1, 1], [1, 1, 2, 1],
       [1, 1, 2, 1], [2, 2, 1, 1], [2, 2, 1, 1], [1, 1, 1, 2], [1, 1, 1, 2], [2, 1, 2, 1], [1, 2, 2, 1],
       [1, 1, 2, 1], [1, 1, 2, 1]]
BLK = [[13, 3, 7, 12], [2, 12, 6, 13], [3, 1, 5, 10], [0, 2, 4, 11], [1, 7, 8, 0], [6, 0, 9, 1], [7, 5, 14, 2],
       [4, 6, 15, 3], [5, 10, 12, 4], [11, 4, 13, 5], [11, 9, 14, 7], [8, 10, 15, 6], [9, 15, 3, 8], [14, 8, 2, 9],
       [15, 13, 1, 10], [12, 14, 0, 11]]
IDX = [[1, 1, 1, 1], [1, 2, 1, 2], [2, 1, 1, 1], [1, 2, 1, 1], [2, 2, 1, 2], [2, 3, 1, 3], [3, 2, 1, 3],
       [2, 3, 1, 3], [3, 2, 3, 3], [2, 4, 3, 4], [3, 2, 2, 4], [2, 3, 2, 4], [3, 3, 4, 3], [3, 4, 4, 4],
       [4, 4, 4, 4], [4, 4, 4, 4]]
HOLD = [[0, 3, 4, 5, 15], [1, 2, 4, 5, 14], [2, 1, 3, 6, 13], [3, 0, 2, 7, 12], [4, 3, 7, 8, 9], [5, 2, 6, 8, 9],
        [6, 1, 5, 7, 11], [7, 0, 4, 6, 10], [8, 4, 11, 12, 13], [9, 5, 10, 12, 13], [10, 2, 8, 11, 14],
        [11, 3, 9, 10, 15], [12, 0, 1, 8, 15], [13, 0, 1, 9, 14], [14, 6, 10, 13, 15], [15, 7, 11, 12, 14]]
PAIRS = [[[(2, 4), (3, 4), (3, 1)], [(0, 2), (0, 3), (2, 3)]], [[(3, 2), (3, 4), (2, 4)], [(0, 1), (1, 3), (0, 3)]],
         [[(2, 1), (1, 3), (2, 3)], [(0, 4), (1, 4), (3, 4)]], [[(1, 2), (2, 3), (3, 4)], [(2, 0), (2, 4), (0, 4)]],
         [[(2, 3), (1, 2), (1, 3)], [(4, 3), (4, 0), (1, 0), (4, 1)]],
         [[(1, 3), (2, 1), (2, 3)], [(4, 3), (0, 3), (2, 0)]],
         [[(4, 1), (4, 2), (2, 3)], [(2, 1), (0, 1), (2, 0), (0, 3)]],
         [[(4, 2), (1, 2), (2, 3)], [(4, 1), (1, 0), (0, 3)]],
         [[(4, 3), (4, 2), (2, 3)], [(4, 0), (1, 0), (1, 3), (4, 1)]],
         [[(4, 3), (4, 1), (1, 3)], [(0, 3), (2, 0), (2, 3)]], [[(2, 1), (4, 2), (4, 1)], [(2, 0), (4, 0), (4, 3)]],
         [[(1, 0), (4, 1), (4, 0)], [(1, 2), (2, 0), (4, 2)]], [[(4, 2), (3, 4), (3, 1)], [(4, 0), (1, 0), (1, 2)]],
         [[(3, 2), (3, 4), (2, 4)], [(4, 1), (2, 0), (2, 1)]], [[(4, 2), (2, 1), (4, 1)], [(4, 0), (2, 0), (3, 4)]],
         [[(4, 1), (1, 2), (4, 2)], [(1, 0), (2, 0), (4, 0)]]]
EARLY = [[1, 1], [0, 1], [1, 0], [1, 1], [1, 2], [1, 2], [2, 3], [2, 2], [1, 1], [1, 1], [1, 1], [1, 2], [1, 1],
         [0, 1], [3, 2], [3, 3]]
NEED = [[[1, 2, 3, 4], [0, 2, 3]], [[2, 3, 4], [0, 1, 3]], [[1, 2, 3], [0, 1, 3, 4]], [[1, 2, 3, 4], [0, 2, 4]],
        [[1, 2, 3], [0, 1, 3, 4]], [[1, 2, 3], [0, 2, 3, 4]], [[1, 2, 3, 4], [0, 1, 2, 3]],
        [[1, 2, 3, 4], [0, 1, 3, 4]], [[2, 3, 4], [0, 1, 3, 4]], [[1, 3, 4], [0, 2, 3]], [[1, 2, 4], [0, 2, 3, 4]],
        [[0, 1, 4], [0, 1, 2, 4]], [[1, 2, 3, 4], [0, 1, 2, 4]], [[2, 3, 4], [0, 1, 2, 4]],
        [[1, 2, 4], [0, 2, 3, 4]], [[1, 2, 4], [0, 1, 2, 4]]]

REL = (0, 3, 1, 2)


def word(digits, base):
    total = 0
    for digit in reversed(digits):
        total = total * base + digit
    return total


def look_up(index, words):
    got = jnp.int32(words[0])
    for k in range(1, len(words)):
        got = jnp.where(index == k, jnp.int32(words[k]), got)
    return got


def digits_of(value, base, count):
    out = []
    for _ in range(count):
        out.append(value % base)
        value = value // base
    return out


def pick(values, index):
    got = values[0]
    for k in range(1, len(values)):
        got = jnp.where(index == k, values[k], got)
    return got


def kernel(emb, ids_in, out, x, units, stage, ids_got, ids_rows, ids_cols, row_best, col_best, row_line, part, parts_got,
           relay,
           load_sem, id_send, id_recv, z_send, z_recv, relay_send, relay_recv, f_send, f_recv, c_send, c_recv, r_send, r_recv):
    grp, blk = lax.axis_index("grp"), lax.axis_index("blk")
    h, zl = grp % 2, grp // 2
    p, zh = blk // 2, blk % 2
    z = zh * 2 + zl
    px, py = p % 4, p // 4

    def device(z_of, core, chip):
        return ((z_of % 2) * 2 + core, chip * 2 + z_of // 2)

    def group_of(z_of):
        return (1 - z_of % 2) * 2 + z_of // 2

    near = [py * 4 + (px + 1) % 4, py * 4 + (px + 3) % 4, ((py + 1) % 4) * 4 + px, ((py + 3) % 4) * 4 + px]
    first = look_up(p, [word(SRC[c], 8) + 4096 * word(DEP[c], 4) for c in range(16)])
    src = digits_of(first, 8, 4)
    dep = digits_of(first // 4096, 4, 4)
    held = [p] + digits_of(look_up(p, [word(BLK[c], 16) for c in range(16)]), 16, 4)
    third = look_up(p, [word(IDX[c], 8) + 4096 * word(HOLD[c][1:], 16) for c in range(16)])
    place = [jnp.int32(0)] + digits_of(third, 8, 4)
    holders = [p] + digits_of(third // 4096, 16, 4)
    lists = []
    for c in range(16):
        for core in range(2):
            flat = [slot for pair in PAIRS[c][core] for slot in pair]
            lists.append(len(PAIRS[c][core]) + 8 * EARLY[c][core] + 64 * word(flat + [0] * (8 - len(flat)), 8))
    todo = look_up(p * 2 + h, lists)
    pair_count, early_count = todo % 8, todo // 8 % 8
    todo = digits_of(todo // 64, 8, 8)

    needs = [[sum(1 << slot for slot in NEED[c][core]) for core in range(2)] for c in range(16)]
    need = digits_of(look_up(p * 2 + h, [needs[c][core] for c in range(16) for core in range(2)]), 2, SLOTS)
    sibling_need = digits_of(look_up(p * 2 + h, [needs[c][1 - core] for c in range(16) for core in range(2)]), 2, SLOTS)

    sibling = device(z, 1 - h, p)
    owner_grp = group_of(z)
    from_z = 2 * h + 1 - zl
    ids_from = device(2 * h + 1 - zl, zh, p)

    def load(k):
        return pltpu.make_async_copy(emb.at[group_of((z + pick((0, 1, 3, 2), k)) % 4)], stage.at[k], load_sem.at[k])

    for k in range(4):
        load(k).start()
    barrier = pltpu.get_barrier_semaphore()
    for rel in (1, 3):
        pl.semaphore_signal(barrier, inc=1, device_id=device((z + rel) % 4, h, p), device_id_type=MESH)
    for d in range(4):
        pl.semaphore_signal(barrier, inc=1, device_id=device(z, h, near[d]), device_id_type=MESH)
    pl.semaphore_signal(barrier, inc=1, device_id=sibling, device_id_type=MESH)
    pl.semaphore_signal(barrier, inc=1, device_id=ids_from, device_id_type=MESH)
    for k in range(SLOTS):
        for core in range(2):
            pl.semaphore_signal(barrier, inc=1, device_id=device(from_z, core, holders[k]), device_id_type=MESH)

    def normalised(k):
        v = stage[k]
        total = jnp.sum(v * v, axis=-1, keepdims=True)
        return (v / jnp.sqrt(total + 1e-06)).astype(jnp.bfloat16)

    load(0).wait()
    own_rows = pl.multiple_of(h * 128, 128)
    x[0, pl.ds(own_rows, 128), :] = normalised(0)
    pl.semaphore_wait(barrier, 18)

    def remote(src_ref, dst_ref, send_sem, recv_sem, to):
        return pltpu.make_async_remote_copy(
            src_ref=src_ref, dst_ref=dst_ref, send_sem=send_sem, recv_sem=recv_sem, device_id=to, device_id_type=MESH)

    def part_rows(t):
        return pl.ds(pl.multiple_of((t // 2) * 256 + h * 128 + (t % 2) * PIECE, PIECE), PIECE)

    def forward(d, t):
        rows = part_rows(t)
        return remote(x.at[src[d], rows, :], x.at[1 + (d ^ 1), rows, :], f_send.at[d, t], f_recv.at[d ^ 1, t],
                      device(z, h, near[d]))

    def arrival(s, t):
        rows = part_rows(t)
        return remote(x.at[s, rows, :], x.at[s, rows, :], f_send.at[s - 1, t], f_recv.at[s - 1, t],
                      device(z, h, near[s - 1]))

    def swap(k, half):
        rows = pl.ds(pl.multiple_of(k * 256 + h * 128 + half * 64, 64), 64)
        return remote(units.at[k - 1, pl.ds(half * 64, 64), :], x.at[0, rows, :], z_send.at[k - 1, half],
                      z_recv.at[k - 1, half], device((z + pick((1, 3), k - 1)) % 4, h, p))

    between = device((z + jnp.where(h == 0, 1, 3)) % 4, h, p)

    def relay_in(half):
        rows = pl.ds(half * 64, 64)
        return remote(units.at[2, rows, :], relay.at[rows, :], relay_send.at[0, half], relay_recv.at[half], between)

    def relay_out(half):
        rows = pl.ds(pl.multiple_of(3 * 256 + h * 128 + half * 64, 64), 64)
        return remote(relay.at[pl.ds(half * 64, 64), :], x.at[0, rows, :], relay_send.at[1, half], z_recv.at[2, half],
                      between)

    def share_rows(t, core):
        return pl.ds(pl.multiple_of((t // 2) * 256 + core * 128 + (t % 2) * 64, 64), 64)

    def share(s, t):
        rows = share_rows(t, h)
        return remote(x.at[s, rows, :], x.at[s, rows, :], c_send.at[s, t], c_recv.at[s, t], sibling)

    def shared(s, t):
        rows = share_rows(t, 1 - h)
        return remote(x.at[s, rows, :], x.at[s, rows, :], c_send.at[s, t], c_recv.at[s, t], sibling)

    def give(s, t):
        pl.when(sibling_need[s] == 1)(lambda: share(s, t).start())

    def send_own(t):
        for d in range(4):
            pl.when(src[d] == 0)(lambda d=d: forward(d, t).start())

    def send_held(t):
        for d in range(4):
            pl.when(src[d] != 0)(lambda d=d: forward(d, t).start())

    def receive(links, t):
        for s in range(1, SLOTS):
            pl.when(dep[s - 1] == links)(lambda s=s: arrival(s, t).wait_recv())

    def give_held(links, t):
        for s in range(1, SLOTS):
            pl.when(dep[s - 1] == links)(lambda s=s: give(s, t))

    for t in range(2):
        send_own(t)
    @pl.loop(1, 4)
    def _(k):
        load(k).wait()
        units[k - 1] = normalised(k)
        for half in range(2):
            pl.when(k < 3)(lambda half=half: swap(k, half).start())
            pl.when(k == 3)(lambda half=half: relay_in(half).start())

    ids_copy = remote(ids_in, ids_got, id_send, id_recv, device(from_z, zh, p))
    ids_copy.start()
    give(0, 0)
    give(0, 1)
    def strip(a, t, b, count, diagonal=False):
        sim = lax.dot_general(x[a, 256 * t:256 * t + 256, :], x[b, 0:256 * count, :], (((1,), (1,)), ((), ())),
                              preferred_element_type=jnp.float32)
        for r in range(4):
            unit, first_row = a * 8 + 2 * t + r // 2, 64 * (r % 2)
            row_ids = ids_rows[unit, first_row:first_row + 64]
            best = row_best[unit, first_row:first_row + 64]
            for c in range(2 * count):
                keep = row_ids == ids_cols[pl.ds(b * 8 + c, 1), :]
                if diagonal and c // 2 == t:
                    row = lax.broadcasted_iota(jnp.int32, (64, 128), 0) + 64 * r
                    col = lax.broadcasted_iota(jnp.int32, (64, 128), 1) + 128 * (c % 2)
                    keep = jnp.logical_and(keep, row != col)
                kept = jnp.where(keep, sim[64 * r:64 * r + 64, 128 * c:128 * c + 128], jnp.float32(-1.0))
                down = jnp.max(kept.reshape(8, 8, 128), axis=0)
                col_best[b * 8 + c] = jnp.maximum(col_best[b * 8 + c], down)
                best = jnp.maximum(best, kept)
            row_best[unit, first_row:first_row + 64] = best

    def compare(t, j):
        a, b = todo[0], todo[1]
        for k in range(1, 4):
            a = jnp.where(j == k, todo[2 * k], a)
            b = jnp.where(j == k, todo[2 * k + 1], b)
        strip(a, t, b, t + 1)
        if t:
            strip(b, t, a, t)

    def own_pair(t):
        pl.when(h == 1)(lambda: strip(0, t, 0, t + 1, diagonal=True))

    def finish_rows(t):
        for s in range(SLOTS):
            @pl.when(need[s] == 1)
            def _():
                for core in range(2):
                    unit = s * 8 + 2 * t + core
                    row_line[unit:unit + 1, :] = jnp.max(row_best[unit].T, axis=0, keepdims=True)

    def wait_shared(m, links):
        for s in range(SLOTS):
            there = need[s] == 1
            if s == 0:
                if links:
                    continue
            elif links:
                there = jnp.logical_and(there, dep[s - 1] == links)
            else:
                continue

            @pl.when(there)
            def _():
                for half in range(2):
                    shared(s, 2 * m + half).wait_recv()

    def own_piece_ready(t):
        send_own(t)
        give(0, t)

    def pass_on(k):
        receive(1, k - 1)
        send_held(k - 1)
        give_held(1, k - 1)

    def take(t):
        receive(2, t)
        give_held(2, t)

    pass_on(1)
    swap(1, 0).wait_recv()
    own_piece_ready(2)
    pass_on(2)
    swap(1, 1).wait_recv()
    own_piece_ready(3)
    swap(2, 0).wait_recv()
    own_piece_ready(4)

    ids_copy.wait_recv()
    ids_cols[...] = jnp.zeros_like(ids_cols)
    for s in range(SLOTS):
        for t in range(4):
            for core in range(2):
                unit = held[s] * 8 + 2 * ((z + REL[t]) % 4) + core
                ids_cols[pl.ds(s * 8 + 2 * t + core, 1), :] = ids_got[pl.ds(unit, 1), :].astype(jnp.float32)
    turned = ids_cols[...].T
    for j in range(SLOTS * 8):
        ids_rows[j] = jnp.broadcast_to(turned[:, j:j + 1], (128, 128))

    pass_on(3)
    for half in range(2):
        relay_in(half).wait_recv()
        relay_out(half).start()
    swap(2, 1).wait_recv()
    own_piece_ready(5)
    @pl.loop(0, SLOTS * 8)
    def _(j):
        row_best[j] = jnp.full((128, 128), -1.0, jnp.float32)
        col_best[j] = jnp.full((8, 128), -1.0, jnp.float32)
    row_line[...] = jnp.full_like(row_line, -1.0)

    take(0)
    pass_on(4)
    for m in (0, 1):
        wait_shared(m, 0)
        own_pair(m)
    take(1)
    pass_on(5)
    for half in range(2):
        relay_out(half).wait_recv()
        own_piece_ready(6 + half)
    wait_shared(0, 1)
    wait_shared(0, 2)

    @pl.loop(0, pair_count)
    def _(j):
        compare(0, j)
    take(2)
    pass_on(6)
    for m in (2, 3):
        wait_shared(m, 0)
        own_pair(m)
    take(3)

    @pl.loop(0, 2)
    def _(k):
        pass_on(7 + k)

        @pl.when(k == 0)
        def _():
            wait_shared(1, 1)
            wait_shared(1, 2)

        @pl.loop(2 * k, jnp.minimum(2 * k + 2, pair_count))
        def _(j):
            compare(1, j)
        take(4 + k)
    finish_rows(0)

    for m in (2, 3):
        wait_shared(m, 1)

        @pl.loop(0, pair_count)
        def _(j):
            pl.when(j == early_count)(lambda: wait_shared(m, 2))
            compare(m, j)
        if m == 2:
            finish_rows(1)
            take(6)
            finish_rows(2)
            take(7)
    for s in range(SLOTS):
        for core in range(2):
            unit = s * 8 + 6 + core
            row_line[unit:unit + 1, :] = jnp.max(row_best[unit].T, axis=0, keepdims=True)

    for s in (1, 2, 3, 4, 0):
        for t in range(4):
            z_of = (z + REL[t]) % 4
            for core in range(2):
                j = s * 8 + 2 * t + core
                both = jnp.maximum(row_line[j:j + 1, :], jnp.max(col_best[j], axis=0, keepdims=True))
                part[s * 2 + z_of // 2, pl.ds(2 * (z_of % 2) + core, 1), :] = both
        for half in range(2):
            copy = remote(part.at[s * 2 + half], parts_got.at[place[s] * 2 + h], r_send.at[s * 2 + half],
                          r_recv.at[place[s] * 2 + h], (owner_grp, held[s] * 2 + half))
            copy.start()

    ids_copy.wait_send()
    for half in range(2):
        for copy in (swap(1, half), swap(2, half), relay_in(half), relay_out(half)):
            copy.wait_send()

    @pl.loop(0, STEPS)
    def _(t):
        for d in range(4):
            forward(d, t).wait_send()
        for s in range(SLOTS):
            pl.when(sibling_need[s] == 1)(lambda s=s: share(s, t).wait_send())

    best = None
    for k in range(2 * SLOTS):
        got = remote(parts_got.at[k], parts_got.at[k], r_send.at[k], r_recv.at[k], sibling)
        got.wait_recv()
        best = parts_got[k] if best is None else jnp.maximum(best, parts_got[k])
    out[...] = best

    for s in range(SLOTS):
        for half in range(2):
            copy = remote(part.at[s * 2 + half], parts_got.at[place[s] * 2 + h], r_send.at[s * 2 + half],
                          r_recv.at[place[s] * 2 + h], (owner_grp, held[s] * 2 + half))
            copy.wait_send()


def on_device(embeddings, cluster_ids):
    emb = embeddings.reshape(4, 128, D)
    ids = cluster_ids.reshape(128, 128)
    dma = pltpu.SemaphoreType.DMA
    best = pl.pallas_call(
        kernel,
        out_shape=jax.ShapeDtypeStruct((4, 128), jnp.float32),
        in_specs=[pl.BlockSpec(memory_space=pl.ANY), pl.BlockSpec(memory_space=pl.ANY)],
        out_specs=pl.BlockSpec(memory_space=pltpu.VMEM),
        scratch_shapes=[
            pltpu.VMEM((SLOTS, 1024, D), jnp.bfloat16),
            pltpu.VMEM((3, 128, D), jnp.bfloat16),
            pltpu.VMEM((4, 128, D), jnp.float32),
            pltpu.VMEM((128, 128), jnp.int32),
            pltpu.VMEM((SLOTS * 8, 128, 128), jnp.float32),
            pltpu.VMEM((128, 128), jnp.float32),
            pltpu.VMEM((SLOTS * 8, 128, 128), jnp.float32),
            pltpu.VMEM((SLOTS * 8, 8, 128), jnp.float32),
            pltpu.VMEM((SLOTS * 8, 128), jnp.float32),
            pltpu.VMEM((2 * SLOTS, 4, 128), jnp.float32),
            pltpu.VMEM((2 * SLOTS, 4, 128), jnp.float32),
            pltpu.VMEM((128, D), jnp.bfloat16),
            dma((4,)), dma, dma, dma((3, 2)), dma((3, 2)), dma((2, 2)), dma((2,)), dma((4, STEPS)), dma((4, STEPS)),
            dma((SLOTS, 8)), dma((SLOTS, 8)), dma((2 * SLOTS,)), dma((2 * SLOTS,)),
        ],
        compiler_params=pltpu.CompilerParams(
            collective_id=0, has_side_effects=True, vmem_limit_bytes=55168 * 1024),
        cost_estimate=pl.CostEstimate(flops=7 * 10**9, bytes_accessed=2 * 10**6, transcendentals=0),
        name="best_match",
    )(emb, ids)
    return best.reshape(1, 512)


def solution(mesh):
    placed = (P(None, "grp", "blk", None, None), P("grp", None))
    return jax.shard_map(
        on_device, mesh=mesh, in_specs=placed, out_specs=P("grp", "blk"), check_vma=False
    )
```

```python
import functools

import jax
import jax.numpy as jnp
from jax import lax
from jax.experimental import pallas as pl
from jax.experimental.pallas import tpu as pltpu
from jax.sharding import PartitionSpec as P

MESH = pl.DeviceIdType.MESH
D = 768
SLOTS = 5
PIECE = 64
STEPS = 8

SRC = [[4, 0, 0, 2], [0, 4, 0, 1], [0, 0, 0, 2], [0, 0, 0, 1], [4, 0, 0, 2], [0, 4, 0, 1], [0, 0, 1, 2],
       [0, 0, 2, 1], [4, 0, 0, 0], [0, 4, 0, 0], [0, 1, 0, 3], [2, 0, 0, 3], [4, 0, 0, 0], [0, 4, 0, 0],
       [0, 0, 4, 0], [0, 0, 4, 0]]
DEP = [[2, 1, 2, 1], [1, 2, 2, 1], [1, 1, 2, 2], [1, 1, 2, 2], [2, 1, 1, 1], [1, 2, 1, 1], [1, 1, 2, 1],
       [1, 1, 2, 1], [2, 2, 1, 1], [2, 2, 1, 1], [1, 1, 1, 2], [1, 1, 1, 2], [2, 1, 2, 1], [1, 2, 2, 1],
       [1, 1, 2, 1], [1, 1, 2, 1]]
BLK = [[13, 3, 7, 12], [2, 12, 6, 13], [3, 1, 5, 10], [0, 2, 4, 11], [1, 7, 8, 0], [6, 0, 9, 1], [7, 5, 14, 2],
       [4, 6, 15, 3], [5, 10, 12, 4], [11, 4, 13, 5], [11, 9, 14, 7], [8, 10, 15, 6], [9, 15, 3, 8], [14, 8, 2, 9],
       [15, 13, 1, 10], [12, 14, 0, 11]]
IDX = [[1, 1, 1, 1], [1, 2, 1, 2], [2, 1, 1, 1], [1, 2, 1, 1], [2, 2, 1, 2], [2, 3, 1, 3], [3, 2, 1, 3],
       [2, 3, 1, 3], [3, 2, 3, 3], [2, 4, 3, 4], [3, 2, 2, 4], [2, 3, 2, 4], [3, 3, 4, 3], [3, 4, 4, 4],
       [4, 4, 4, 4], [4, 4, 4, 4]]
HOLD = [[0, 3, 4, 5, 15], [1, 2, 4, 5, 14], [2, 1, 3, 6, 13], [3, 0, 2, 7, 12], [4, 3, 7, 8, 9], [5, 2, 6, 8, 9],
        [6, 1, 5, 7, 11], [7, 0, 4, 6, 10], [8, 4, 11, 12, 13], [9, 5, 10, 12, 13], [10, 2, 8, 11, 14],
        [11, 3, 9, 10, 15], [12, 0, 1, 8, 15], [13, 0, 1, 9, 14], [14, 6, 10, 13, 15], [15, 7, 11, 12, 14]]
PAIRS = [[[(2, 4), (3, 4), (4, 1)], [(0, 2), (3, 1), (0, 3)]], [[(3, 2), (3, 4)], [(0, 1), (1, 3), (0, 3)]],
         [[(2, 1), (1, 3), (3, 4)], [(0, 1), (0, 4), (1, 4)]], [[(1, 2), (2, 3), (2, 4)], [(0, 4), (3, 4)]],
         [[(2, 3), (1, 2), (1, 3)], [(4, 3), (4, 0), (1, 0), (4, 1)]],
         [[(1, 3), (2, 1), (2, 3)], [(4, 3), (4, 0), (0, 3), (2, 0)]],
         [[(4, 1), (4, 2), (2, 3)], [(2, 1), (2, 0), (0, 1), (0, 3)]],
         [[(4, 2), (1, 2), (2, 3)], [(4, 1), (4, 0), (1, 0), (0, 3)]],
         [[(4, 3), (4, 2), (2, 3)], [(4, 0), (1, 0), (1, 3), (4, 1)]],
         [[(4, 3), (4, 1), (1, 3)], [(0, 3), (2, 0), (2, 3)]], [[(2, 1), (4, 2), (4, 1)], [(2, 0), (4, 0), (4, 3)]],
         [[(1, 0), (4, 1), (4, 0)], [(1, 2), (2, 0), (4, 2)]], [[(4, 0), (3, 4), (3, 1)], [(4, 2), (1, 0), (1, 2)]],
         [[(3, 2), (3, 4), (2, 4)], [(4, 1), (2, 0), (2, 1)]], [[(4, 2), (2, 1), (4, 1)], [(4, 0), (2, 0), (3, 4)]],
         [[(4, 1), (1, 2), (4, 2)], [(1, 0), (4, 0), (2, 0)]]]
EARLY = [[1, 1], [0, 1], [1, 1], [1, 0], [1, 2], [1, 3], [2, 3], [2, 3], [1, 1], [1, 1], [1, 1], [1, 2], [1, 1],
         [0, 1], [3, 2], [3, 3]]
NEED = [[[1, 2, 3, 4], [0, 1, 2, 3]], [[2, 3, 4], [0, 1, 3]], [[1, 2, 3, 4], [0, 1, 4]], [[1, 2, 3, 4], [0, 3, 4]],
        [[1, 2, 3], [0, 1, 3, 4]], [[1, 2, 3], [0, 2, 3, 4]], [[1, 2, 3, 4], [0, 1, 2, 3]],
        [[1, 2, 3, 4], [0, 1, 3, 4]], [[2, 3, 4], [0, 1, 3, 4]], [[1, 3, 4], [0, 2, 3]], [[1, 2, 4], [0, 2, 3, 4]],
        [[0, 1, 4], [0, 1, 2, 4]], [[0, 1, 3, 4], [0, 1, 2, 4]], [[2, 3, 4], [0, 1, 2, 4]],
        [[1, 2, 4], [0, 2, 3, 4]], [[1, 2, 4], [0, 1, 2, 4]]]

REL = (0, 3, 1, 2)


def word(digits, base):
    total = 0
    for digit in reversed(digits):
        total = total * base + digit
    return total


def look_up(index, words):
    got = jnp.int32(words[0])
    for k in range(1, len(words)):
        got = jnp.where(index == k, jnp.int32(words[k]), got)
    return got


def digits_of(value, base, count):
    out = []
    for _ in range(count):
        out.append(value % base)
        value = value // base
    return out


def pick(values, index):
    got = values[0]
    for k in range(1, len(values)):
        got = jnp.where(index == k, values[k], got)
    return got


def kernel(emb, ids_in, out, x, units, stage, ids_got, ids_rows, ids_cols, row_best, col_best, row_line, part, parts_got,
           relay,
           load_sem, id_send, id_recv, z_send, z_recv, relay_send, relay_recv, f_send, f_recv, c_send, c_recv, r_send, r_recv):
    grp, blk = lax.axis_index("grp"), lax.axis_index("blk")
    h, zl = grp % 2, grp // 2
    p, zh = blk // 2, blk % 2
    z = zh * 2 + zl
    px, py = p % 4, p // 4

    def device(z_of, core, chip):
        return ((z_of % 2) * 2 + core, chip * 2 + z_of // 2)

    def group_of(z_of):
        return (1 - z_of % 2) * 2 + z_of // 2

    near = [py * 4 + (px + 1) % 4, py * 4 + (px + 3) % 4, ((py + 1) % 4) * 4 + px, ((py + 3) % 4) * 4 + px]
    first = look_up(p, [word(SRC[c], 8) + 4096 * word(DEP[c], 4) for c in range(16)])
    src = digits_of(first, 8, 4)
    dep = digits_of(first // 4096, 4, 4)
    held = [p] + digits_of(look_up(p, [word(BLK[c], 16) for c in range(16)]), 16, 4)
    third = look_up(p, [word(IDX[c], 8) + 4096 * word(HOLD[c][1:], 16) for c in range(16)])
    place = [jnp.int32(0)] + digits_of(third, 8, 4)
    holders = [p] + digits_of(third // 4096, 16, 4)
    lists = []
    for c in range(16):
        for core in range(2):
            flat = [slot for pair in PAIRS[c][core] for slot in pair]
            lists.append(len(PAIRS[c][core]) + 8 * EARLY[c][core] + 64 * word(flat + [0] * (8 - len(flat)), 8))
    todo = look_up(p * 2 + h, lists)
    pair_count, early_count = todo % 8, todo // 8 % 8
    todo = digits_of(todo // 64, 8, 8)

    needs = [[sum(1 << slot for slot in NEED[c][core]) for core in range(2)] for c in range(16)]
    need = digits_of(look_up(p * 2 + h, [needs[c][core] for c in range(16) for core in range(2)]), 2, SLOTS)
    sibling_need = digits_of(look_up(p * 2 + h, [needs[c][1 - core] for c in range(16) for core in range(2)]), 2, SLOTS)

    sibling = device(z, 1 - h, p)
    owner_grp = group_of(z)
    from_z = 2 * h + 1 - zl
    ids_from = device(2 * h + 1 - zl, zh, p)

    def load(k):
        return pltpu.make_async_copy(emb.at[group_of((z + pick((0, 1, 3, 2), k)) % 4)], stage.at[k], load_sem.at[k])

    for k in range(4):
        load(k).start()
    barrier = pltpu.get_barrier_semaphore()
    for rel in (1, 3):
        pl.semaphore_signal(barrier, inc=1, device_id=device((z + rel) % 4, h, p), device_id_type=MESH)
    for d in range(4):
        pl.semaphore_signal(barrier, inc=1, device_id=device(z, h, near[d]), device_id_type=MESH)
    pl.semaphore_signal(barrier, inc=1, device_id=sibling, device_id_type=MESH)
    pl.semaphore_signal(barrier, inc=1, device_id=ids_from, device_id_type=MESH)
    for k in range(SLOTS):
        for core in range(2):
            pl.semaphore_signal(barrier, inc=1, device_id=device(from_z, core, holders[k]), device_id_type=MESH)

    def normalised(k):
        v = stage[k]
        total = jnp.sum(v * v, axis=-1, keepdims=True)
        return (v / jnp.sqrt(total + 1e-06)).astype(jnp.bfloat16)

    load(0).wait()
    own_rows = pl.multiple_of(h * 128, 128)
    x[0, pl.ds(own_rows, 128), :] = normalised(0)
    pl.semaphore_wait(barrier, 18)

    def remote(src_ref, dst_ref, send_sem, recv_sem, to):
        return pltpu.make_async_remote_copy(
            src_ref=src_ref, dst_ref=dst_ref, send_sem=send_sem, recv_sem=recv_sem, device_id=to, device_id_type=MESH)

    def part_rows(t):
        return pl.ds(pl.multiple_of((t // 2) * 256 + h * 128 + (t % 2) * PIECE, PIECE), PIECE)

    def forward(d, t):
        rows = part_rows(t)
        return remote(x.at[src[d], rows, :], x.at[1 + (d ^ 1), rows, :], f_send.at[d, t], f_recv.at[d ^ 1, t],
                      device(z, h, near[d]))

    def arrival(s, t):
        rows = part_rows(t)
        return remote(x.at[s, rows, :], x.at[s, rows, :], f_send.at[s - 1, t], f_recv.at[s - 1, t],
                      device(z, h, near[s - 1]))

    def swap(k, half):
        rows = pl.ds(pl.multiple_of(k * 256 + h * 128 + half * 64, 64), 64)
        return remote(units.at[k - 1, pl.ds(half * 64, 64), :], x.at[0, rows, :], z_send.at[k - 1, half],
                      z_recv.at[k - 1, half], device((z + pick((1, 3), k - 1)) % 4, h, p))

    between = device((z + jnp.where(h == 0, 1, 3)) % 4, h, p)

    def relay_in(half):
        rows = pl.ds(half * 64, 64)
        return remote(units.at[2, rows, :], relay.at[rows, :], relay_send.at[0, half], relay_recv.at[half], between)

    def relay_out(half):
        rows = pl.ds(pl.multiple_of(3 * 256 + h * 128 + half * 64, 64), 64)
        return remote(relay.at[pl.ds(half * 64, 64), :], x.at[0, rows, :], relay_send.at[1, half], z_recv.at[2, half],
                      between)

    def share_rows(t, core):
        return pl.ds(pl.multiple_of((t // 2) * 256 + core * 128 + (t % 2) * 64, 64), 64)

    def share(s, t):
        rows = share_rows(t, h)
        return remote(x.at[s, rows, :], x.at[s, rows, :], c_send.at[s, t], c_recv.at[s, t], sibling)

    def shared(s, t):
        rows = share_rows(t, 1 - h)
        return remote(x.at[s, rows, :], x.at[s, rows, :], c_send.at[s, t], c_recv.at[s, t], sibling)

    def give(s, t):
        pl.when(sibling_need[s] == 1)(lambda: share(s, t).start())

    def send_own(t):
        for d in range(4):
            pl.when(src[d] == 0)(lambda d=d: forward(d, t).start())

    def send_held(t):
        for d in range(4):
            pl.when(src[d] != 0)(lambda d=d: forward(d, t).start())

    def receive(links, t):
        for s in range(1, SLOTS):
            pl.when(dep[s - 1] == links)(lambda s=s: arrival(s, t).wait_recv())

    def give_held(links, t):
        for s in range(1, SLOTS):
            pl.when(dep[s - 1] == links)(lambda s=s: give(s, t))

    for t in range(2):
        send_own(t)
    @pl.loop(1, 4)
    def _(k):
        load(k).wait()
        units[k - 1] = normalised(k)
        for half in range(2):
            pl.when(k < 3)(lambda half=half: swap(k, half).start())
            pl.when(k == 3)(lambda half=half: relay_in(half).start())

    ids_copy = remote(ids_in, ids_got, id_send, id_recv, device(from_z, zh, p))
    ids_copy.start()
    give(0, 0)
    give(0, 1)
    def strip(a, t, b, count, diagonal=False):
        sim = lax.dot_general(x[a, 256 * t:256 * t + 256, :], x[b, 0:256 * count, :], (((1,), (1,)), ((), ())),
                              preferred_element_type=jnp.float32)
        for r in range(4):
            unit, first_row = a * 8 + 2 * t + r // 2, 64 * (r % 2)
            row_ids = ids_rows[unit, first_row:first_row + 64]
            best = row_best[unit, first_row:first_row + 64]
            for c in range(2 * count):
                keep = row_ids == ids_cols[pl.ds(b * 8 + c, 1), :]
                if diagonal and c // 2 == t:
                    row = lax.broadcasted_iota(jnp.int32, (64, 128), 0) + 64 * r
                    col = lax.broadcasted_iota(jnp.int32, (64, 128), 1) + 128 * (c % 2)
                    keep = jnp.logical_and(keep, row != col)
                kept = jnp.where(keep, sim[64 * r:64 * r + 64, 128 * c:128 * c + 128], jnp.float32(-1.0))
                down = jnp.max(kept.reshape(8, 8, 128), axis=0)
                col_best[b * 8 + c] = jnp.maximum(col_best[b * 8 + c], down)
                best = jnp.maximum(best, kept)
            row_best[unit, first_row:first_row + 64] = best

    def compare(t, j):
        a, b = todo[0], todo[1]
        for k in range(1, 4):
            a = jnp.where(j == k, todo[2 * k], a)
            b = jnp.where(j == k, todo[2 * k + 1], b)
        strip(a, t, b, t + 1)
        if t:
            strip(b, t, a, t)

    def own_pair(t):
        pl.when(h == 1)(lambda: strip(0, t, 0, t + 1, diagonal=True))

    def finish_rows(t):
        for s in range(SLOTS):
            @pl.when(need[s] == 1)
            def _():
                for core in range(2):
                    unit = s * 8 + 2 * t + core
                    row_line[unit:unit + 1, :] = jnp.max(row_best[unit].T, axis=0, keepdims=True)

    def wait_shared(m, links):
        for s in range(SLOTS):
            there = need[s] == 1
            if s == 0:
                if links:
                    continue
            elif links:
                there = jnp.logical_and(there, dep[s - 1] == links)
            else:
                continue

            @pl.when(there)
            def _():
                for half in range(2):
                    shared(s, 2 * m + half).wait_recv()

    def own_piece_ready(t):
        send_own(t)
        give(0, t)

    def pass_on(k):
        receive(1, k - 1)
        send_held(k - 1)
        give_held(1, k - 1)

    def take(t):
        receive(2, t)
        give_held(2, t)

    pass_on(1)
    swap(1, 0).wait_recv()
    own_piece_ready(2)
    pass_on(2)
    swap(1, 1).wait_recv()
    own_piece_ready(3)
    swap(2, 0).wait_recv()
    own_piece_ready(4)

    ids_copy.wait_recv()
    ids_cols[...] = jnp.zeros_like(ids_cols)
    for s in range(SLOTS):
        for t in range(4):
            for core in range(2):
                unit = held[s] * 8 + 2 * ((z + REL[t]) % 4) + core
                ids_cols[pl.ds(s * 8 + 2 * t + core, 1), :] = ids_got[pl.ds(unit, 1), :].astype(jnp.float32)
    turned = ids_cols[...].T
    for j in range(SLOTS * 8):
        ids_rows[j] = jnp.broadcast_to(turned[:, j:j + 1], (128, 128))

    pass_on(3)
    for half in range(2):
        relay_in(half).wait_recv()
        relay_out(half).start()
    swap(2, 1).wait_recv()
    own_piece_ready(5)
    @pl.loop(0, SLOTS * 8)
    def _(j):
        row_best[j] = jnp.full((128, 128), -1.0, jnp.float32)
        col_best[j] = jnp.full((8, 128), -1.0, jnp.float32)
    row_line[...] = jnp.full_like(row_line, -1.0)

    take(0)
    pass_on(4)
    for m in (0, 1):
        wait_shared(m, 0)
        own_pair(m)
    take(1)
    pass_on(5)
    for half in range(2):
        relay_out(half).wait_recv()
        own_piece_ready(6 + half)
    wait_shared(0, 1)
    wait_shared(0, 2)

    @pl.loop(0, pair_count)
    def _(j):
        compare(0, j)
    take(2)
    pass_on(6)
    for m in (2, 3):
        wait_shared(m, 0)
        own_pair(m)
    take(3)

    @pl.loop(0, 2)
    def _(k):
        pass_on(7 + k)

        @pl.when(k == 0)
        def _():
            wait_shared(1, 1)
            wait_shared(1, 2)

        @pl.loop(2 * k, jnp.minimum(2 * k + 2, pair_count))
        def _(j):
            compare(1, j)
        take(4 + k)
    finish_rows(0)

    for m in (2, 3):
        wait_shared(m, 1)

        @pl.loop(0, pair_count)
        def _(j):
            pl.when(j == early_count)(lambda: wait_shared(m, 2))
            compare(m, j)
        if m == 2:
            finish_rows(1)
            take(6)
            finish_rows(2)
            take(7)
    for s in range(SLOTS):
        for core in range(2):
            unit = s * 8 + 6 + core
            row_line[unit:unit + 1, :] = jnp.max(row_best[unit].T, axis=0, keepdims=True)

    for s in (1, 2, 3, 4, 0):
        for t in range(4):
            z_of = (z + REL[t]) % 4
            for core in range(2):
                j = s * 8 + 2 * t + core
                both = jnp.maximum(row_line[j:j + 1, :], jnp.max(col_best[j], axis=0, keepdims=True))
                part[s * 2 + z_of // 2, pl.ds(2 * (z_of % 2) + core, 1), :] = both
        for half in range(2):
            copy = remote(part.at[s * 2 + half], parts_got.at[place[s] * 2 + h], r_send.at[s * 2 + half],
                          r_recv.at[place[s] * 2 + h], (owner_grp, held[s] * 2 + half))
            copy.start()

    ids_copy.wait_send()
    for half in range(2):
        for copy in (swap(1, half), swap(2, half), relay_in(half), relay_out(half)):
            copy.wait_send()

    @pl.loop(0, STEPS)
    def _(t):
        for d in range(4):
            forward(d, t).wait_send()
        for s in range(SLOTS):
            pl.when(sibling_need[s] == 1)(lambda s=s: share(s, t).wait_send())

    best = None
    for k in range(2 * SLOTS):
        got = remote(parts_got.at[k], parts_got.at[k], r_send.at[k], r_recv.at[k], sibling)
        got.wait_recv()
        best = parts_got[k] if best is None else jnp.maximum(best, parts_got[k])
    out[...] = best

    for s in range(SLOTS):
        for half in range(2):
            copy = remote(part.at[s * 2 + half], parts_got.at[place[s] * 2 + h], r_send.at[s * 2 + half],
                          r_recv.at[place[s] * 2 + h], (owner_grp, held[s] * 2 + half))
            copy.wait_send()


def on_device(embeddings, cluster_ids):
    emb = embeddings.reshape(4, 128, D)
    ids = cluster_ids.reshape(128, 128)
    dma = pltpu.SemaphoreType.DMA
    best = pl.pallas_call(
        kernel,
        out_shape=jax.ShapeDtypeStruct((4, 128), jnp.float32),
        in_specs=[pl.BlockSpec(memory_space=pl.ANY), pl.BlockSpec(memory_space=pl.ANY)],
        out_specs=pl.BlockSpec(memory_space=pltpu.VMEM),
        scratch_shapes=[
            pltpu.VMEM((SLOTS, 1024, D), jnp.bfloat16),
            pltpu.VMEM((3, 128, D), jnp.bfloat16),
            pltpu.VMEM((4, 128, D), jnp.float32),
            pltpu.VMEM((128, 128), jnp.int32),
            pltpu.VMEM((SLOTS * 8, 128, 128), jnp.float32),
            pltpu.VMEM((128, 128), jnp.float32),
            pltpu.VMEM((SLOTS * 8, 128, 128), jnp.float32),
            pltpu.VMEM((SLOTS * 8, 8, 128), jnp.float32),
            pltpu.VMEM((SLOTS * 8, 128), jnp.float32),
            pltpu.VMEM((2 * SLOTS, 4, 128), jnp.float32),
            pltpu.VMEM((2 * SLOTS, 4, 128), jnp.float32),
            pltpu.VMEM((128, D), jnp.bfloat16),
            dma((4,)), dma, dma, dma((3, 2)), dma((3, 2)), dma((2, 2)), dma((2,)), dma((4, STEPS)), dma((4, STEPS)),
            dma((SLOTS, 8)), dma((SLOTS, 8)), dma((2 * SLOTS,)), dma((2 * SLOTS,)),
        ],
        compiler_params=pltpu.CompilerParams(
            collective_id=0, has_side_effects=True, vmem_limit_bytes=55168 * 1024),
        cost_estimate=pl.CostEstimate(flops=7 * 10**9, bytes_accessed=2 * 10**6, transcendentals=0),
        name="best_match",
    )(emb, ids)
    return best.reshape(1, 512)


def solution(mesh):
    placed = (P(None, "grp", "blk", None, None), P("grp", None))
    return jax.shard_map(
        on_device, mesh=mesh, in_specs=placed, out_specs=P("grp", "blk"), check_vma=False
    )
```
